32 devices in a mesh: head: 4 (over y, x), node: 8 (over z, core).
Axes of the slice: x: 2, y: 2, z: 4, core: 2. Of those that a mesh axis runs over, the one named last changes fastest.
Arguments:
- prev_state: float32 [98304, 84], P('node'), may hold values from -6 to 6
- target: float32 [98304, 84], P('node')
- noise_eps: float32 [98304, 84], P('node'), may hold values from -6 to 6
- noise_level: int32 [1], replicated, may hold values from 0 to 999
- valid_count: int32 [8], P('node'), may hold values from 1 to 2048, as said below
- neighbours: int32 [16384, 16], P('node'), may hold values from 0 to 16383, as said below
- nbr_count: int32 [16384], P('node'), may hold values from 8 to 16
- pix_node: int32 [98304], P('node'), may hold values from 0 to 16383, as said below
- pix_read: int32 [98304, 3], P('node'), may hold values from 0 to 16383, as said below
- w_enc: float32 [168, 512], replicated, may hold values from -0.1875 to 0.1875
- w_cond: float32 [32, 2048], replicated, may hold values from -1 to 1
- w_dec: float32 [512, 84], replicated, may hold values from -0.25 to 0.25
- layer_w: float32 [3, 512, 2048], P(None, 'node', 'head'), may hold values from -0.25 to 0.25
- soap_first: float32 [3, 512, 2048], P(None, 'node', 'head'), may hold values from -9.536743e-06 to 9.536743e-06
- soap_second: float32 [3, 512, 2048], P(None, 'node', 'head'), may hold values from 1.57566e-12 to 6.30264e-12
- soap_basis: float32 [3, 4, 512, 512], P(None, 'head')
- soap_stats: float32 [3, 4, 512, 512], P(None, 'head')
- enc_first: float32 [168, 512], replicated, may hold values from -9.536743e-06 to 9.536743e-06
- enc_second: float32 [168, 512], replicated, may hold values from 1.57566e-12 to 6.30264e-12
- cond_first: float32 [32, 2048], replicated, may hold values from -9.536743e-06 to 9.536743e-06
- cond_second: float32 [32, 2048], replicated, may hold values from 1.57566e-12 to 6.30264e-12
- dec_first: float32 [512, 84], replicated, may hold values from -9.536743e-06 to 9.536743e-06
- dec_second: float32 [512, 84], replicated, may hold values from 1.57566e-12 to 6.30264e-12
Outputs:
- loss_sum: float32 [1], replicated
- loss_count: float32 [1], replicated
- grad_norm: float32 [1], replicated
- layer_w_new: float32 [3, 512, 2048], P(None, 'node', 'head')
- soap_first_new: float32 [3, 512, 2048], P(None, 'node', 'head')
- soap_second_new: float32 [3, 512, 2048], P(None, 'node', 'head')
- soap_basis_new: float32 [3, 4, 512, 512], P(None, 'head')
- soap_stats_new: float32 [3, 4, 512, 512], P(None, 'head')
- w_enc_new: float32 [168, 512], replicated
- enc_first_new: float32 [168, 512], replicated
- enc_second_new: float32 [168, 512], replicated
- w_cond_new: float32 [32, 2048], replicated
- cond_first_new: float32 [32, 2048], replicated
- cond_second_new: float32 [32, 2048], replicated
- w_dec_new: float32 [512, 84], replicated
- dec_first_new: float32 [512, 84], replicated
- dec_second_new: float32 [512, 84], replicated
The draws below stay inside these ranges and needn't reach their ends.
Inputs may be any that keep to these rules, and one draw needn't show every extreme that they name: `pix_node`: pixel p encodes into a node of block p // 12288 of 2048 nodes. `pix_read`: pixel p reads three nodes of block p // 12288. The neighbours of a node of block b lie in blocks b - 1, b and b + 1 of 2048 nodes, cyclically. `valid_count`: the last block's nodes are all valid.
All inputs are finite; a program needn't handle non-finite values.
Results may differ from the reference program's by a relative error of at most 0.0074.
Values may be sent and summed in bfloat16 or wider, within the bound.
A program may use at most 320 MiB of HBM per device.

```python
import math
import jax
import jax.numpy as jnp
from jax import lax

D = 512
HEADS = 4
HD = 128
FF = 2048
VARS = 84
NF = 32
NBR = 16
PPN = 6
LEVELS = 1000
STEP = 10
NODES_DEV = 2048
PIX_DEV = 12288
NODES = 16384
PIX = 98304
N_NODE = 8


def draw_target(key, part):
    key = jax.random.fold_in(key, 11)
    key_scale, key_values = jax.random.split(key)
    spread = jnp.exp(jax.random.uniform(key_scale, (VARS,), jnp.float32, -1.0, 1.0))
    values_drawn = jax.random.normal(key_values, (PIX, VARS), jnp.float32)
    return values_drawn * spread


def draw_valid_count(key, part):
    key = jax.random.fold_in(key, 12)
    blocks = NODES // NODES_DEV
    block_rank = jnp.arange(blocks, dtype=jnp.int32)
    baseline = NODES_DEV // 3 + (NODES_DEV - NODES_DEV // 3) * block_rank // max(blocks - 1, 1)
    wobble = max(NODES_DEV // 8, 1)
    jitter = jax.random.randint(key, (blocks,), -wobble, wobble + 1)
    counts = jnp.clip(baseline + jitter, 1, NODES_DEV)
    return counts.at[blocks - 1].set(NODES_DEV).astype(jnp.int32)


def draw_neighbours(key, part):
    key = jax.random.fold_in(key, 13)
    block_start = jnp.arange(NODES, dtype=jnp.int32) // NODES_DEV * NODES_DEV
    offsets = jax.random.randint(key, (NODES, NBR), -NODES_DEV, 2 * NODES_DEV)
    return ((block_start[:, None] + offsets + NODES) % NODES).astype(jnp.int32)


def draw_pix_node(key, part):
    key = jax.random.fold_in(key, 14)
    key_one, key_two = jax.random.split(key)
    first_pick = jax.random.randint(key_one, (PIX,), 0, NODES_DEV)
    second_pick = jax.random.randint(key_two, (PIX,), 0, NODES_DEV)
    local_pick = jnp.minimum(first_pick, second_pick)
    local_pick = local_pick.at[PIX_DEV - 1::PIX_DEV].set(NODES_DEV - 1)
    block_start = jnp.arange(PIX, dtype=jnp.int32) // PIX_DEV * NODES_DEV
    return (block_start + local_pick).astype(jnp.int32)


def draw_pix_read(key, part):
    key = jax.random.fold_in(key, 15)
    picks = jax.random.randint(key, (PIX, 3), 0, NODES_DEV)
    block_start = jnp.arange(PIX, dtype=jnp.int32) // PIX_DEV * NODES_DEV
    return (block_start[:, None] + picks).astype(jnp.int32)


def draw_soap_basis(key, part):
    key = jax.random.fold_in(key, 16)
    block_cols = FF // HEADS
    shape_all = (3, HEADS, block_cols, block_cols)
    noise_part = jax.random.normal(key, shape_all, jnp.float32)
    return jnp.eye(block_cols, dtype=jnp.float32) + noise_part * (0.5 / block_cols ** 0.5)


def draw_soap_stats(key, part):
    key = jax.random.fold_in(key, 17)
    key_diag, key_off = jax.random.split(key)
    block_cols = FF // HEADS
    unit_base = D / (200000.0 * (3 * D * FF + 3 * VARS * D + 4 * NF * D))
    diag_vals = unit_base * jnp.exp(jax.random.uniform(key_diag, (3, HEADS, block_cols), jnp.float32, 0.0, 1.386))
    raw_off = jax.random.normal(key_off, (3, HEADS, block_cols, block_cols), jnp.float32)
    symmetric = (raw_off + jnp.swapaxes(raw_off, 2, 3)) * (0.25 * unit_base / block_cols ** 0.5)
    return symmetric + diag_vals[..., None] * jnp.eye(block_cols, dtype=jnp.float32)


def plant(array, stream_key, least, top_value):
    dims = array.shape
    index_at = [jax.random.randint(jax.random.fold_in(stream_key, axis), (), 0, dims[axis]) for axis in range(len(dims))]
    array = array.at[tuple(index_at)].set(least)
    longest = dims.index(max(dims))
    index_at[longest] = (index_at[longest] + 1) % dims[longest]
    return array.at[tuple(index_at)].set(top_value)


def shard_levels(stream_key, extent, cuts, smallest, largest):
    gain = 1.0
    for axis_at, blocks in cuts:
        heights = jax.random.uniform(jax.random.fold_in(jax.random.fold_in(stream_key, 6), axis_at), (blocks,), jnp.float32, smallest / len(cuts), largest / len(cuts))
        gain = gain * jnp.repeat(jnp.exp(heights), extent[axis_at] // blocks).reshape((-1,) + (1,) * (len(extent) - 1 - axis_at))
    return gain


def noise(rng, dims, scale, most, pieces=(), kind=jnp.bfloat16):
    entries = scale * jax.random.normal(rng, dims, jnp.float32)
    if pieces:
        entries = entries * shard_levels(rng, dims, pieces, -0.22, 0.18)
    return jnp.clip(entries, -most, most).astype(kind)


def setup_inputs(seed: int = 0) -> dict:
    key_list = jax.random.split(jax.random.key(seed), 24)
    return {
        "prev_state": noise(key_list[0], (PIX, VARS), 1.0, 6.0, ((0, 8),), jnp.float32),
        "target": draw_target(jax.random.fold_in(key_list[23], 71), 0),
        "noise_eps": noise(key_list[2], (PIX, VARS), 1.0, 6.0, ((0, 8),), jnp.float32),
        "noise_level": jax.random.randint(key_list[3], (1,), 0, LEVELS).astype(jnp.int32),
        "valid_count": draw_valid_count(jax.random.fold_in(key_list[23], 71), 0),
        "neighbours": draw_neighbours(jax.random.fold_in(key_list[23], 71), 0),
        "nbr_count": plant(jax.random.randint(key_list[6], (NODES,), NBR // 2, NBR + 1), jax.random.fold_in(key_list[6], 1), NBR // 2, NBR).astype(jnp.int32),
        "pix_node": draw_pix_node(jax.random.fold_in(key_list[23], 71), 0),
        "pix_read": draw_pix_read(jax.random.fold_in(key_list[23], 71), 0),
        "w_enc": noise(key_list[9], (2 * VARS, D), (2 * VARS * PPN) ** -0.5, 0.1875, (), jnp.float32),
        "w_cond": noise(key_list[10], (NF, 4 * D), NF ** -0.5, 1.0, (), jnp.float32),
        "w_dec": noise(key_list[11], (D, VARS), D ** -0.5, 0.25, (), jnp.float32),
        "layer_w": noise(key_list[12], (3, D, FF), D ** -0.5, 0.25, ((1, 8), (2, 4)), jnp.float32),
        "soap_first": noise(key_list[13], (3, D, FF), (1 / (900 * (3 * D * FF + 3 * VARS * D + 4 * NF * D) ** 0.5)), 9.5367431640625e-06, ((1, 8), (2, 4)), jnp.float32),
        "soap_second": jnp.clip(jnp.exp(math.log(6.302639833644097e-12) - 1.3862944 * jax.random.uniform(key_list[14], (3, D, FF), jnp.float32) ** shard_levels(key_list[14], (3, D, FF), ((1, 8), (2, 4)), -0.2, 0.2)), 1.5756599584110242e-12, 6.302639833644097e-12),
        "soap_basis": draw_soap_basis(jax.random.fold_in(key_list[23], 71), 0),
        "soap_stats": draw_soap_stats(jax.random.fold_in(key_list[23], 71), 0),
        "enc_first": noise(key_list[17], (2 * VARS, D), (1 / (900 * (3 * D * FF + 3 * VARS * D + 4 * NF * D) ** 0.5)), 9.5367431640625e-06, (), jnp.float32),
        "enc_second": jnp.clip(jnp.exp(jax.random.uniform(key_list[18], (2 * VARS, D), jnp.float32, math.log(1.5756599584110242e-12), math.log(6.302639833644097e-12))), 1.5756599584110242e-12, 6.302639833644097e-12),
        "cond_first": noise(key_list[19], (NF, 4 * D), (1 / (900 * (3 * D * FF + 3 * VARS * D + 4 * NF * D) ** 0.5)), 9.5367431640625e-06, (), jnp.float32),
        "cond_second": jnp.clip(jnp.exp(jax.random.uniform(key_list[20], (NF, 4 * D), jnp.float32, math.log(1.5756599584110242e-12), math.log(6.302639833644097e-12))), 1.5756599584110242e-12, 6.302639833644097e-12),
        "dec_first": noise(key_list[21], (D, VARS), (1 / (900 * (3 * D * FF + 3 * VARS * D + 4 * NF * D) ** 0.5)), 9.5367431640625e-06, (), jnp.float32),
        "dec_second": jnp.clip(jnp.exp(jax.random.uniform(key_list[22], (D, VARS), jnp.float32, math.log(1.5756599584110242e-12), math.log(6.302639833644097e-12))), 1.5756599584110242e-12, 6.302639833644097e-12),
    }


highest = lax.Precision.HIGHEST
clip_limit = 0.01
beta_first = 0.9
beta_second = 0.95
beta_stats = 0.95
adam_epsilon = 1e-08
rate_layer = 0.02
rate_small = 0.05
decay_rate = 0.1
norm_eps = 1e-05

@jax.custom_vjp
def low(v):
    return lax.optimization_barrier(v.astype(jnp.bfloat16)).astype(jnp.float32)

@jax.custom_vjp
def low_back(v):
    return v

def low_keep(v):
    return (low(v), None)

def low_pass(kept, grad):
    return (grad,)

def back_keep(v):
    return (v, None)

def back_low(kept, grad):
    return (low(grad),)
low.defvjp(low_keep, low_pass)
low_back.defvjp(back_keep, back_low)

def noise_terms(noise_level):
    level_frac = noise_level[0].astype(jnp.float32) / (LEVELS - 1)
    noise_sigma = 0.05 * jnp.exp(level_frac * math.log(40.0))
    frequency = 1.0 + jnp.arange(NF // 2).astype(jnp.float32)
    phase_angle = jnp.log(noise_sigma) * frequency
    return (noise_sigma, jnp.concatenate([jnp.sin(phase_angle), jnp.cos(phase_angle)]))

def standardize(values_in):
    row_mean = lax.optimization_barrier(jnp.mean(values_in, -1, keepdims=True))
    centered = values_in - row_mean
    return centered * lax.rsqrt(lax.optimization_barrier(jnp.mean(centered * centered, -1, keepdims=True)) + norm_eps)

def adam_small(weight, grad_item, first, second):
    first_new = beta_first * first + (1 - beta_first) * grad_item
    second_new = beta_second * second + (1 - beta_second) * grad_item * grad_item
    ratio = first_new / (1 - beta_first ** STEP) / (jnp.sqrt(second_new / (1 - beta_second ** STEP)) + adam_epsilon)
    return (weight - rate_small * (ratio + decay_rate * weight), first_new, second_new)

def reference(prev_state, target, noise_eps, noise_level, valid_count, neighbours, nbr_count, pix_node, pix_read, w_enc, w_cond, w_dec, layer_w, soap_first, soap_second, soap_basis, soap_stats, enc_first, enc_second, cond_first, cond_second, dec_first, dec_second):
    noise_sigma, noise_feat = noise_terms(noise_level)
    sig_sq = noise_sigma * noise_sigma
    input_scale = lax.rsqrt(sig_sq + 1.0)
    skip_scale = 1.0 / (sig_sq + 1.0)
    output_scale = noise_sigma * lax.rsqrt(sig_sq + 1.0)
    loss_scale = (sig_sq + 1.0) / sig_sq
    noisy = target + noise_sigma * noise_eps
    block_of = (jnp.arange(PIX) // PIX_DEV).astype(jnp.int32)
    node_local = pix_node - block_of * NODES_DEV
    valid_mask = (node_local < valid_count[block_of]).astype(jnp.float32)[:, None]
    residual = target - prev_state
    count_sum = jnp.sum(valid_mask)
    var_weight = 1.0 / (lax.optimization_barrier(jnp.sum(valid_mask * residual * residual, 0)) / count_sum + norm_eps)
    loss_count = count_sum * VARS
    node_in = jax.ops.segment_sum(low(jnp.concatenate([prev_state, input_scale * noisy], 1)), pix_node, NODES)
    live_mask = jnp.arange(NBR)[None, :] < nbr_count[:, None]
    score_scale = 1.0 / math.sqrt(HD)

    def forward(params):
        enc_weight, cond_weight, dec_weight, layer_weight = params
        modulation = jnp.dot(noise_feat[None, :], cond_weight, precision=highest)[0]
        scale_one, shift_one, scale_two, shift_two = jnp.split(modulation, 4)
        h_zero = jnp.dot(node_in, low(enc_weight), precision=highest)
        norm_one = low(standardize(h_zero) * (1 + scale_one) + shift_one)
        layer_low = low(layer_weight)
        attn_w = layer_low[0].reshape(D, HEADS, 4, HD)

        def project(column):
            flat = jnp.dot(norm_one, attn_w[:, :, column, :].reshape(D, HEADS * HD), precision=highest)
            return low(low_back(flat)).reshape(NODES, HEADS, HD)
        query_all = project(0)
        key_all = project(1)
        value_all = project(2)

        def attend(block_args):
            query_block, index_block, mask_block = block_args
            key_near = key_all[index_block]
            value_near = value_all[index_block]
            scores = jnp.einsum('nhe,njhe->nhj', query_block, key_near, precision=highest) * score_scale
            scores = jnp.where(mask_block[:, None, :], scores, -1e+30)
            attn_probs = jax.nn.softmax(scores, axis=-1)
            return jnp.einsum('nhj,njhe->nhe', low(attn_probs), value_near, precision=highest)
        mixed_all = lax.map(jax.checkpoint(attend), (query_all.reshape(N_NODE, NODES_DEV, HEADS, HD), neighbours.reshape(N_NODE, NODES_DEV, NBR), live_mask.reshape(N_NODE, NODES_DEV, NBR)))
        mixed_all = low(low_back(mixed_all.reshape(NODES, HEADS * HD)))
        w_out = attn_w[:, :, 3, :].reshape(D, HEADS * HD)
        h_one = h_zero + low_back(jnp.dot(mixed_all, w_out.T, precision=highest))
        norm_two = low(standardize(h_one) * (1 + scale_two) + shift_two)
        up_proj = low_back(jnp.dot(norm_two, layer_low[1], precision=highest))
        act_low = low(jax.nn.silu(up_proj))
        h_two = h_one + low_back(jnp.dot(act_low, layer_low[2].T, precision=highest))
        final_low = low(standardize(h_two))
        decoded = low_back(jnp.dot(final_low, low(dec_weight), precision=highest))
        pixel_field = (decoded[pix_read[:, 0]] + decoded[pix_read[:, 1]] + decoded[pix_read[:, 2]]) / 3.0
        pixel_error = skip_scale * noisy + output_scale * pixel_field - target
        return jnp.sum(valid_mask * loss_scale * var_weight * pixel_error * pixel_error)
    loss_sum, pullback = jax.vjp(forward, (w_enc, w_cond, w_dec, layer_w))
    grad_enc, grad_cond, grad_dec, grad_layer = pullback(1.0 / loss_count)[0]
    total_sq = sum((jnp.sum(grad_item * grad_item) for grad_item in (grad_enc, grad_cond, grad_dec, grad_layer)))
    grad_norm = jnp.sqrt(total_sq)
    clip_factor = clip_limit / jnp.maximum(grad_norm, clip_limit)
    block_cols = FF // HEADS
    clipped = (clip_factor * grad_layer).reshape(3, D, HEADS, block_cols)
    rotated = jnp.einsum('idhb,ihbc->idhc', clipped, soap_basis, precision=highest).reshape(3, D, FF)
    first_new = beta_first * soap_first + (1 - beta_first) * rotated
    second_new = beta_second * soap_second + (1 - beta_second) * rotated * rotated
    direction = first_new / (1 - beta_first ** STEP) / (jnp.sqrt(second_new / (1 - beta_second ** STEP)) + adam_epsilon)
    step_back = jnp.einsum('idhc,ihbc->idhb', direction.reshape(3, D, HEADS, block_cols), soap_basis, precision=highest).reshape(3, D, FF)
    layer_new = layer_w - rate_layer * (step_back + decay_rate * layer_w)
    stat_new = jnp.einsum('idhb,idhc->ihbc', clipped, clipped, precision=highest)
    stats_new = beta_stats * soap_stats + (1 - beta_stats) * stat_new
    product = jnp.einsum('ihbc,ihcd->ihbd', stats_new, soap_basis, precision=highest)
    gram_matrix = jnp.einsum('ihbc,ihbd->ihcd', product, product, precision=highest)
    chol_lower = jnp.linalg.cholesky(gram_matrix)
    basis_new = jnp.swapaxes(lax.linalg.triangular_solve(chol_lower, jnp.swapaxes(product, 2, 3), left_side=True, lower=True), 2, 3)
    enc_new = adam_small(w_enc, clip_factor * grad_enc, enc_first, enc_second)
    cond_new = adam_small(w_cond, clip_factor * grad_cond, cond_first, cond_second)
    dec_new = adam_small(w_dec, clip_factor * grad_dec, dec_first, dec_second)
    return (jnp.reshape(loss_sum, (1,)), jnp.reshape(loss_count, (1,)), jnp.reshape(grad_norm, (1,)), layer_new, first_new, second_new, basis_new, stats_new, enc_new[0], enc_new[1], enc_new[2], cond_new[0], cond_new[1], cond_new[2], dec_new[0], dec_new[1], dec_new[2])
```

```python
import functools
import math

import jax
import jax.numpy as jnp
from jax import lax
from jax.experimental import pallas as pl
from jax.experimental.pallas import tpu as pltpu
from jax.sharding import PartitionSpec as P

HD = 128
VARS = 84
NF = 32
NBR = 16
LEVELS = 1000
STEP = 10

SLOT = 128
SLIM = 96
GROUP = 256 // NBR
BLOCK = 128

highest = lax.Precision.HIGHEST
clip_limit = 0.01
beta_first = 0.9
beta_second = 0.95
beta_stats = 0.95
adam_epsilon = 1e-08
rate_layer = 0.02
rate_small = 0.05
decay_rate = 0.1
norm_eps = 1e-05

f32 = jnp.float32
bf16 = jnp.bfloat16
MIB = 2**20


def passed_along(x, axis, by):
    length = lax.axis_size(axis)
    return lax.ppermute(x, axis, [(i, (i + by) % length) for i in range(length)])


def noise_terms(noise_level):
    level_frac = noise_level[0].astype(f32) / (LEVELS - 1)
    noise_sigma = 0.05 * jnp.exp(level_frac * math.log(40.0))
    frequency = 1.0 + jnp.arange(NF // 2).astype(f32)
    phase_angle = jnp.log(noise_sigma) * frequency
    return (noise_sigma, jnp.concatenate([jnp.sin(phase_angle), jnp.cos(phase_angle)]))


def standardize(values_in):
    row_mean = jnp.mean(values_in, -1, keepdims=True)
    centered = values_in - row_mean
    inv_std = lax.rsqrt(jnp.mean(centered * centered, -1, keepdims=True) + norm_eps)
    return (centered * inv_std, inv_std)


def norm_back(normed, inv_std, grad_in):
    return inv_std * (
        grad_in
        - jnp.mean(grad_in, -1, keepdims=True)
        - normed * jnp.mean(grad_in * normed, -1, keepdims=True)
    )


def contract(left, right, left_dim, right_dim, precision=None):
    return lax.dot_general(
        left,
        right,
        (((left_dim,), (right_dim,)), ((), ())),
        preferred_element_type=f32,
        precision=precision,
    )


def halves(x):
    high = x.astype(bf16)
    return high, (x - high.astype(f32)).astype(bf16)


def thirds(x):
    high = x.astype(bf16)
    rest = x - high.astype(f32)
    return (high, *halves(rest))


def fold_lanes(x, op=jnp.add):
    parts = [x[:, i : i + 128] for i in range(0, x.shape[1], 128)]
    while len(parts) > 1:
        parts = [op(*parts[i : i + 2]) if i + 1 < len(parts) else parts[i] for i in range(0, len(parts), 2)]
    return parts[0]


def adam_small(weight, grad_item, first, second):
    first_new = beta_first * first + (1 - beta_first) * grad_item
    second_new = beta_second * second + (1 - beta_second) * grad_item * grad_item
    ratio = (
        first_new
        / (1 - beta_first**STEP)
        / (jnp.sqrt(second_new / (1 - beta_second**STEP)) + adam_epsilon)
    )
    return (weight - rate_small * (ratio + decay_rate * weight), first_new, second_new)


def smem():
    return pl.BlockSpec(memory_space=pltpu.SMEM)


def whole(shape):
    zeros = (0,) * len(shape)
    return pl.BlockSpec(tuple(shape), lambda *_: zeros)


def params(mib=48):
    return pltpu.CompilerParams(vmem_limit_bytes=mib * MIB)


def encode_kernel(place_ref, scale_ref, node_ref, prev_ref, target_ref, eps_ref, in_ref, stat_ref, pix):
    step = pl.program_id(0)
    rows = in_ref.shape[0]
    tile = node_ref.shape[1]

    @pl.when(step == 0)
    def _():
        pix[...] = jnp.zeros_like(pix)
        in_ref[...] = jnp.zeros_like(in_ref)
        stat_ref[...] = jnp.zeros_like(stat_ref)

    prev = prev_ref[...]
    target = target_ref[...]
    noisy = target + scale_ref[0] * eps_ref[...]
    pix[:VARS] = prev.astype(bf16)
    pix[SLOT : SLOT + VARS] = (scale_ref[1] * noisy).astype(bf16)
    node = node_ref[...] - place_ref[0]
    mine = node - place_ref[1]
    spot = lax.broadcasted_iota(jnp.int32, (rows, tile), 0)
    onehot = (spot == mine).astype(f32).astype(bf16)
    in_ref[...] += contract(onehot, pix[...], 1, 1)
    valid = (node < place_ref[2]).astype(f32)
    residual = target - prev
    stat_ref[:VARS] += fold_lanes(valid * residual * residual)
    stat_ref[SLIM - 1 : SLIM] += fold_lanes(valid)


def encode(place, scales, node_row, prev, target, eps, rows, tile):
    pixels = prev.shape[1]
    pixel_block = pl.BlockSpec((VARS, tile), lambda i: (0, i))
    return pl.pallas_call(
        encode_kernel,
        grid=(pixels // tile,),
        in_specs=[smem(), smem(), pl.BlockSpec((1, tile), lambda i: (0, i))] + [pixel_block] * 3,
        out_specs=[whole((rows, 2 * SLOT)), whole((SLIM, 128))],
        out_shape=[
            jax.ShapeDtypeStruct((rows, 2 * SLOT), f32),
            jax.ShapeDtypeStruct((SLIM, 128), f32),
        ],
        scratch_shapes=[pltpu.VMEM((2 * SLOT, tile), bf16)],
        compiler_params=params(),
        name="encode",
    )(place, scales, node_row, prev, target, eps)


def enter_kernel(in_ref, w_ref, mod_ref, zero_ref, norm_ref):
    w = w_ref[...]
    h_zero = sum(contract(part, w, 1, 0) for part in thirds(in_ref[...]))
    zero_ref[...] = h_zero
    normed, _ = standardize(h_zero)
    norm_ref[...] = (normed * (1 + mod_ref[0:1]) + mod_ref[1:2]).astype(bf16)


def enter(node_in, w_enc, modulation):
    rows, width = node_in.shape[0], w_enc.shape[1]
    return pl.pallas_call(
        enter_kernel,
        out_shape=[
            jax.ShapeDtypeStruct((rows, width), f32),
            jax.ShapeDtypeStruct((rows, width), bf16),
        ],
        compiler_params=params(),
        name="enter",
    )(node_in, w_enc, modulation)


def project_kernel(norm_ref, w_ref, q_ref, kv_ref):
    out = contract(norm_ref[...], w_ref[...], 1, 0).astype(bf16)
    q_ref[...] = out[:, :HD]
    kv_ref[...] = out[:, HD : 3 * HD]


def project(norm_all, w_attn, tile):
    nodes, width = norm_all.shape
    return pl.pallas_call(
        project_kernel,
        grid=(nodes // tile,),
        in_specs=[
            pl.BlockSpec((tile, width), lambda i: (i, 0)),
            pl.BlockSpec((width, 3 * HD), lambda i: (0, 0)),
        ],
        out_specs=[
            pl.BlockSpec((tile, HD), lambda i: (i, 0)),
            pl.BlockSpec((tile, 2 * HD), lambda i: (i, 0)),
        ],
        out_shape=[
            jax.ShapeDtypeStruct((nodes, HD), bf16),
            jax.ShapeDtypeStruct((nodes, 2 * HD), bf16),
        ],
        compiler_params=params(),
        name="project",
    )(norm_all, w_attn)


def count_kernel(slot_ref, count_ref):
    groups = slot_ref.shape[0]
    bands = count_ref.shape[1] // 256
    lane = lax.broadcasted_iota(jnp.int32, (GROUP, 256), 1)
    sub = lax.broadcasted_iota(jnp.int32, (GROUP, 256), 0)
    own = lane // NBR == sub
    spot = lax.broadcasted_iota(jnp.int32, (256, 256), 0)
    for g in range(groups):
        row = slot_ref[g : g + 1]
        band = jnp.where(own, row >> 8, -1)
        left = jnp.concatenate([(band == t).astype(f32).astype(bf16) for t in range(bands)], 0)
        right = (spot == (row & 255)).astype(f32).astype(bf16)
        found = contract(left, right, 1, 1).astype(bf16)
        for t in range(bands):
            count_ref[g * GROUP : (g + 1) * GROUP, t * 256 : (t + 1) * 256] = found[
                t * GROUP : (t + 1) * GROUP
            ]


def count_slots(slots, reach, tile_groups):
    groups = slots.shape[0]
    return pl.pallas_call(
        count_kernel,
        grid=(groups // tile_groups,),
        in_specs=[pl.BlockSpec((tile_groups, 256), lambda i: (i, 0))],
        out_specs=pl.BlockSpec((tile_groups * GROUP, reach), lambda i: (i, 0)),
        out_shape=jax.ShapeDtypeStruct((groups * GROUP, reach), bf16),
        compiler_params=params(),
        name="count_slots",
    )(slots)


def attend_kernel(q_ref, below_ref, here_ref, above_ref, count_ref, e_ref, mix_ref, low_ref, s_scr, chunk):
    tile = q_ref.shape[0]
    nodes = here_ref.shape[0]
    q = q_ref[...]
    top = jnp.full((tile, 128), -1e30, f32)
    for b, kv_ref in enumerate((below_ref, here_ref, above_ref)):
        for at in range(0, nodes, chunk):
            cols = slice(b * nodes + at, b * nodes + at + chunk)
            s = contract(q, kv_ref[at : at + chunk, :HD], 1, 1)
            s = jnp.where(count_ref[:, cols].astype(f32) > 0, s, -1e30)
            s_scr[:, cols] = s
            top = jnp.maximum(top, fold_lanes(s, jnp.maximum))
    top = jnp.max(top, 1, keepdims=True)
    factor = math.log2(math.e) / math.sqrt(HD)
    total = jnp.zeros((tile, 128), f32)
    mixed = jnp.zeros((tile, HD), f32)
    for b, kv_ref in enumerate((below_ref, here_ref, above_ref)):
        for at in range(0, nodes, chunk):
            cols = slice(b * nodes + at, b * nodes + at + chunk)
            e = count_ref[:, cols].astype(f32) * jnp.exp2((s_scr[:, cols] - top) * factor)
            total += fold_lanes(e)
            e = e.astype(bf16)
            e_ref[:, cols] = e
            mixed += contract(e, kv_ref[at : at + chunk, HD:], 1, 0)
    inverse = 1.0 / jnp.sum(total, 1, keepdims=True)
    mixed = mixed * inverse
    mix_ref[:, :HD] = mixed
    mix_ref[:, HD:] = jnp.broadcast_to(inverse, (tile, HD))
    low_ref[...] = mixed.astype(bf16)


def attend(query, below, here, above, counts, tile, chunk):
    nodes, reach = counts.shape
    row = lambda width: pl.BlockSpec((tile, width), lambda i: (i, 0))
    return pl.pallas_call(
        functools.partial(attend_kernel, chunk=chunk),
        grid=(nodes // tile,),
        in_specs=[row(HD)] + [whole((nodes, 2 * HD))] * 3 + [row(reach)],
        out_specs=[row(reach), row(2 * HD), row(HD)],
        out_shape=[
            jax.ShapeDtypeStruct((nodes, reach), bf16),
            jax.ShapeDtypeStruct((nodes, 2 * HD), f32),
            jax.ShapeDtypeStruct((nodes, HD), bf16),
        ],
        scratch_shapes=[pltpu.VMEM((tile, reach), f32)],
        compiler_params=params(60),
        name="attend",
    )(query, below, here, above, counts)


def attend_back_kernel(
    q_ref, d_ref, mix_ref, e_ref, below_ref, here_ref, above_ref, dq_ref, low_ref, self_ref, high_ref, dk, dv, chunk
):
    step = pl.program_id(0)
    tile = q_ref.shape[0]
    nodes = here_ref.shape[0]

    @pl.when(step == 0)
    def _():
        dk[...] = jnp.zeros_like(dk)
        dv[...] = jnp.zeros_like(dv)

    grad = d_ref[...]
    wide = grad.astype(f32)
    inverse = mix_ref[:, HD : HD + 1]
    delta = jnp.sum(wide * mix_ref[:, :HD], 1, keepdims=True)
    gain = inverse * (1.0 / math.sqrt(HD))
    q_turned = q_ref[...].T
    d_turned = (wide * inverse).astype(bf16).T
    dq = jnp.zeros((tile, HD), f32)
    for b, kv_ref in enumerate((below_ref, here_ref, above_ref)):
        for at in range(0, nodes, chunk):
            cols = slice(b * nodes + at, b * nodes + at + chunk)
            key = kv_ref[at : at + chunk, :HD]
            dp = contract(grad, kv_ref[at : at + chunk, HD:], 1, 1)
            e = e_ref[:, cols]
            ds = (e.astype(f32) * ((dp - delta) * gain)).astype(bf16)
            dq += contract(ds, key, 1, 0)
            dk[:, cols] += contract(q_turned, ds, 1, 0)
            dv[:, cols] += contract(d_turned, e, 1, 0)
    dq_ref[...] = dq.astype(bf16)

    @pl.when(step == pl.num_programs(0) - 1)
    def _():
        for b, ref in enumerate((low_ref, self_ref, high_ref)):
            cols = slice(b * nodes, (b + 1) * nodes)
            ref[:HD] = dk[:, cols].astype(ref.dtype)
            ref[HD:] = dv[:, cols].astype(ref.dtype)


def attend_back(query, grad, mix, e, below, here, above, tile, chunk):
    nodes, reach = e.shape
    row = lambda width: pl.BlockSpec((tile, width), lambda i: (i, 0))
    return pl.pallas_call(
        functools.partial(attend_back_kernel, chunk=chunk),
        grid=(nodes // tile,),
        in_specs=[row(HD), row(HD), row(2 * HD), row(reach)] + [whole((nodes, 2 * HD))] * 3,
        out_specs=[row(HD)] + [whole((2 * HD, nodes))] * 3,
        out_shape=[
            jax.ShapeDtypeStruct((nodes, HD), bf16),
            jax.ShapeDtypeStruct((2 * HD, nodes), bf16),
            jax.ShapeDtypeStruct((2 * HD, nodes), f32),
            jax.ShapeDtypeStruct((2 * HD, nodes), bf16),
        ],
        scratch_shapes=[pltpu.VMEM((HD, reach), f32)] * 2,
        compiler_params=params(60),
        name="attend_back",
    )(query, grad, mix, e, below, here, above)


def forward_kernel(mixed_ref, zero_ref, w_ref, mod_ref, wdec_ref, one_ref, two_ref, norm_ref, up_ref, act_ref, dec_ref):
    heads, width = w_ref.shape[0], w_ref.shape[1]
    h_one = zero_ref[...] + sum(
        contract(mixed_ref[h], w_ref[h, :, 2 * width :], 1, 1) for h in range(heads)
    )
    one_ref[...] = h_one
    normed, _ = standardize(h_one)
    norm_two = (normed * (1 + mod_ref[2:3]) + mod_ref[3:4]).astype(bf16)
    norm_ref[...] = norm_two
    h_two = h_one
    for h in range(heads):
        up = contract(norm_two, w_ref[h, :, :width], 1, 0)
        up_ref[h] = up
        act = (up * jax.nn.sigmoid(up)).astype(bf16)
        act_ref[h] = act
        h_two = h_two + contract(act, w_ref[h, :, width : 2 * width], 1, 1)
    two_ref[...] = h_two
    final = standardize(h_two)[0].astype(bf16)
    high, low = halves(contract(wdec_ref[...], final, 1, 1))
    dec_ref[:SLIM] = high
    dec_ref[SLIM:] = low


def forward(mixed, h_zero, w_big, modulation, w_dec, tile):
    heads, rows = mixed.shape[:2]
    width = h_zero.shape[1]
    row = pl.BlockSpec((tile, width), lambda i: (i, 0))
    stack = lambda w: pl.BlockSpec((heads, tile, w), lambda i: (0, i, 0))
    return pl.pallas_call(
        forward_kernel,
        grid=(rows // tile,),
        in_specs=[stack(HD), row, whole(w_big.shape), whole(modulation.shape), whole(w_dec.shape)],
        out_specs=[row, row, row, stack(width), stack(width), pl.BlockSpec((2 * SLIM, tile), lambda i: (0, i))],
        out_shape=[
            jax.ShapeDtypeStruct((rows, width), f32),
            jax.ShapeDtypeStruct((rows, width), f32),
            jax.ShapeDtypeStruct((rows, width), bf16),
            jax.ShapeDtypeStruct((heads, rows, width), f32),
            jax.ShapeDtypeStruct((heads, rows, width), bf16),
            jax.ShapeDtypeStruct((2 * SLIM, rows), bf16),
        ],
        compiler_params=params(),
        name="forward",
    )(mixed, h_zero, w_big, modulation, w_dec)


def pixel_kernel(place_ref, scale_ref, node_ref, read_ref, target_ref, eps_ref, weight_ref, dec_ref, loss_ref, d_ref, hits, turned, total):
    step = pl.program_id(0)
    heads, _, rows = dec_ref.shape
    tile = target_ref.shape[1]

    @pl.when(step == 0)
    def _():
        turned[...] = jnp.zeros_like(turned)
        total[...] = jnp.zeros_like(total)
        loss_ref[...] = jnp.zeros_like(loss_ref)

    reads = read_ref[...] - place_ref[0]
    field = jnp.zeros((2 * SLIM, tile), f32)
    for h in range(heads):
        spot = lax.broadcasted_iota(jnp.int32, (rows, tile), 0) + h * rows
        hit = sum((spot == reads[k : k + 1]).astype(f32) for k in range(3)).astype(bf16)
        hits[h * rows : (h + 1) * rows] = hit
        field += contract(dec_ref[h], hit, 1, 0)
    field = (field[:VARS] + field[SLIM : SLIM + VARS]) / 3.0
    target = target_ref[...]
    noisy = target + scale_ref[0] * eps_ref[...]
    error = scale_ref[2] * noisy + scale_ref[3] * field - target
    valid = (node_ref[...] - place_ref[0] < place_ref[2]).astype(f32)
    weighted = valid * weight_ref[:, 0:1]
    loss_ref[:VARS] += fold_lanes(weighted * error * error)
    high, low = halves(scale_ref[4] * weighted * error)
    turned[:VARS] = high
    turned[SLOT : SLOT + VARS] = low
    total[...] += contract(hits[...], turned[...], 1, 1)

    @pl.when(step == pl.num_programs(0) - 1)
    def _():
        d_ref[...] = total[:, :SLOT] + total[:, SLOT:]


def pixels_back(place, scales, node_row, read_rows, target, eps, weight, decoded, tile):
    heads, _, rows = decoded.shape
    count = target.shape[1] // heads
    steps = count // tile
    at = lambda i, place: (0, place[3] * steps + i)
    fixed = lambda shape: pl.BlockSpec(tuple(shape), lambda i, place: (0,) * len(shape))
    return pl.pallas_call(
        pixel_kernel,
        grid_spec=pltpu.PrefetchScalarGridSpec(
            num_scalar_prefetch=1,
            grid=(steps,),
            in_specs=[
                smem(),
                pl.BlockSpec((1, tile), at),
                pl.BlockSpec((3, tile), at),
                pl.BlockSpec((VARS, tile), at),
                pl.BlockSpec((VARS, tile), at),
                fixed(weight.shape),
                fixed(decoded.shape),
            ],
            out_specs=[fixed((SLIM, 128)), fixed((heads * rows, SLOT))],
            scratch_shapes=[
                pltpu.VMEM((heads * rows, tile), bf16),
                pltpu.VMEM((2 * SLOT, tile), bf16),
                pltpu.VMEM((heads * rows, 2 * SLOT), f32),
            ],
        ),
        out_shape=[
            jax.ShapeDtypeStruct((SLIM, 128), f32),
            jax.ShapeDtypeStruct((heads * rows, SLOT), f32),
        ],
        compiler_params=params(),
        name="pixels_back",
    )(place, scales, node_row, read_rows, target, eps, weight, decoded)


def backward_kernel(
    d_ref, two_ref, one_ref, norm_ref, up_ref, act_ref, mixed_ref, w_ref, mod_ref, wdec_ref,
    done_ref, dmix_ref, grad_ref, gdec_ref, gmod_ref,
):
    heads, width = w_ref.shape[0], w_ref.shape[1]
    step = pl.program_id(0)

    @pl.when(step == 0)
    def _():
        grad_ref[...] = jnp.zeros_like(grad_ref)
        gdec_ref[...] = jnp.zeros_like(gdec_ref)
        gmod_ref[...] = jnp.zeros_like(gmod_ref)

    d_dec = sum(d_ref[h] for h in range(heads)).astype(bf16)
    normed_two, inv_two = standardize(two_ref[...])
    final = normed_two.astype(bf16)
    gdec_ref[...] += contract(d_dec[:, :SLIM], final, 0, 0)
    d_two = norm_back(normed_two, inv_two, contract(d_dec[:, :SLIM], wdec_ref[...], 1, 0))
    d_low = d_two.astype(bf16)
    norm_two = norm_ref[...]
    d_mid = jnp.zeros_like(d_two)
    for h in range(heads):
        act = act_ref[h]
        up = up_ref[h]
        d_act = contract(d_low, w_ref[h, :, width : 2 * width], 1, 0)
        gating = jax.nn.sigmoid(up)
        d_up = (d_act * gating * (1 + up * (1 - gating))).astype(bf16)
        grad_ref[h, :, :width] += contract(norm_two, d_up, 0, 0)
        grad_ref[h, :, width : 2 * width] += contract(d_low, act, 0, 0)
        d_mid += contract(d_up, w_ref[h, :, :width], 1, 1)
    normed_one, inv_one = standardize(one_ref[...])
    gmod_ref[0:1] += jnp.sum(d_mid * normed_one, 0, keepdims=True)
    gmod_ref[1:2] += jnp.sum(d_mid, 0, keepdims=True)
    d_one = d_two + norm_back(normed_one, inv_one, d_mid * (1 + mod_ref[2:3]))
    done_ref[...] = d_one
    one_low = d_one.astype(bf16)
    for h in range(heads):
        dmix_ref[h] = contract(one_low, w_ref[h, :, 2 * width :], 1, 0).astype(bf16)
        grad_ref[h, :, 2 * width :] += contract(one_low, mixed_ref[h], 0, 0)


def backward(d_dec, h_two, h_one, norm_two, up, act, mixed, w_big, modulation, w_dec, tile):
    heads, rows = mixed.shape[:2]
    width = h_one.shape[1]
    row = lambda w: pl.BlockSpec((tile, w), lambda i: (i, 0))
    stack = lambda w: pl.BlockSpec((heads, tile, w), lambda i: (0, i, 0))
    return pl.pallas_call(
        backward_kernel,
        grid=(rows // tile,),
        in_specs=[
            stack(SLOT),
            row(width),
            row(width),
            row(width),
            stack(width),
            stack(width),
            stack(HD),
            whole(w_big.shape),
            whole(modulation.shape),
            whole(w_dec.shape),
        ],
        out_specs=[row(width), stack(HD), whole(w_big.shape), whole((SLIM, width)), whole((8, width))],
        out_shape=[
            jax.ShapeDtypeStruct((rows, width), f32),
            jax.ShapeDtypeStruct((heads, rows, HD), bf16),
            jax.ShapeDtypeStruct(w_big.shape, f32),
            jax.ShapeDtypeStruct((SLIM, width), f32),
            jax.ShapeDtypeStruct((8, width), f32),
        ],
        compiler_params=params(56),
        name="backward",
    )(d_dec, h_two, h_one, norm_two, up, act, mixed, w_big, modulation, w_dec)


def unproject_kernel(dq_ref, self_ref, down_ref, up_ref, norm_ref, w_ref, dn_ref, grad_ref):
    step = pl.program_id(0)

    @pl.when(step == 0)
    def _():
        grad_ref[...] = jnp.zeros_like(grad_ref)

    kv = self_ref[...] + down_ref[...].astype(f32) + up_ref[...].astype(f32)
    both = jnp.concatenate([dq_ref[...], kv.astype(bf16).T], 1)
    dn_ref[...] = contract(both, w_ref[...], 1, 1).astype(bf16)
    grad_ref[...] += contract(norm_ref[...], both, 0, 0)


def unproject(dq, kv_self, from_below, from_above, norm_all, w_attn, tile):
    nodes, width = norm_all.shape
    row = lambda w: pl.BlockSpec((tile, w), lambda i: (i, 0))
    col = pl.BlockSpec((2 * HD, tile), lambda i: (0, i))
    return pl.pallas_call(
        unproject_kernel,
        grid=(nodes // tile,),
        in_specs=[row(HD), col, col, col, row(width), pl.BlockSpec((width, 3 * HD), lambda i: (0, 0))],
        out_specs=[row(width), whole((width, 3 * HD))],
        out_shape=[
            jax.ShapeDtypeStruct((nodes, width), bf16),
            jax.ShapeDtypeStruct((width, 3 * HD), f32),
        ],
        compiler_params=params(),
        name="unproject",
    )(dq, kv_self, from_below, from_above, norm_all, w_attn)


def leave_kernel(dn_ref, zero_ref, done_ref, in_ref, mod_ref, genc_ref, gmod_ref):
    heads = dn_ref.shape[0]
    d_norm = sum(dn_ref[h].astype(f32) for h in range(heads))
    normed, inv = standardize(zero_ref[...])
    gmod_ref[0:1] = jnp.sum(d_norm * normed, 0, keepdims=True)
    gmod_ref[1:2] = jnp.sum(d_norm, 0, keepdims=True)
    gmod_ref[2:] = jnp.zeros_like(gmod_ref[2:])
    d_zero = done_ref[...] + norm_back(normed, inv, d_norm * (1 + mod_ref[0:1]))
    genc_ref[...] = contract(in_ref[...].T, d_zero, 1, 0, highest)


def leave(d_norm, h_zero, d_one, node_in, modulation):
    width = h_zero.shape[1]
    return pl.pallas_call(
        leave_kernel,
        out_shape=[
            jax.ShapeDtypeStruct((2 * SLOT, width), f32),
            jax.ShapeDtypeStruct((8, width), f32),
        ],
        compiler_params=params(),
        name="leave",
    )(d_norm, h_zero, d_one, node_in, modulation)


def eliminate(blocks):
    size = blocks[0].shape[0]
    tiles = [[b[8 * i : 8 * i + 8] for i in range(size // 8)] for b in blocks]
    lane = lax.broadcasted_iota(jnp.int32, (8, size), 1)
    sub = lax.broadcasted_iota(jnp.int32, (8, size), 0)
    pivots = [jnp.zeros((1, size), f32) for _ in blocks]
    for j in range(size):
        first, inside = divmod(j, 8)
        for m in range(len(blocks)):
            row = tiles[m][first][inside : inside + 1]
            pivot = row[:, j : j + 1]
            here = lane[:1] == j
            pivots[m] = jnp.where(here, pivot, pivots[m])
            scaled = jnp.where(here, 1.0, row) * (1.0 / pivot)
            for i in range(first, size // 8):
                old = tiles[m][i]
                new = jnp.where(lane == j, 0.0, old) - old[:, j : j + 1] * scaled
                if i == first:
                    new = jnp.where(
                        sub > inside, new, jnp.where((sub == inside) & (lane == j), 1.0, old)
                    )
                tiles[m][i] = new
    return [jnp.concatenate(t, 0) for t in tiles], pivots


def renew_kernel(gram_ref, product_ref, out_ref, both):
    count, size = gram_ref.shape[:2]
    k = pl.program_id(0)

    @pl.when(k == 0)
    def _():
        both[:, :size] = gram_ref[...]
        both[:, size:] = product_ref[...]

    at = pl.ds(pl.multiple_of(k * BLOCK, BLOCK), BLOCK)
    factors, pivots = eliminate([both[m, at, at] for m in range(count)])
    below = lax.broadcasted_iota(jnp.int32, (size, BLOCK), 0) >= (k + 1) * BLOCK
    lower = lax.broadcasted_iota(jnp.int32, (BLOCK, BLOCK), 1) <= lax.broadcasted_iota(
        jnp.int32, (BLOCK, BLOCK), 0
    )
    for m in range(count):
        factor = jnp.where(lower, factors[m], 0.0)
        panel = contract(both[m, :, at], factor, 1, 1, highest) * lax.rsqrt(pivots[m])
        out_ref[m] = panel[size:]

        @pl.when(k < size // BLOCK - 1)
        def _():
            left = jnp.where(below, panel[:size], 0.0)
            both[m] -= contract(jnp.concatenate([left, panel[size:]], 0), left, 1, 1, highest)


def renew(gram, product):
    count, size = gram.shape[:2]
    return pl.pallas_call(
        renew_kernel,
        grid=(size // BLOCK,),
        in_specs=[whole(gram.shape), whole(gram.shape)],
        out_specs=pl.BlockSpec((count, size, BLOCK), lambda k: (0, 0, k)),
        out_shape=jax.ShapeDtypeStruct(gram.shape, f32),
        scratch_shapes=[pltpu.VMEM((count, 2 * size, size), f32)],
        compiler_params=params(),
        name="renew",
    )(gram, product)


def local(
    prev_state,
    target,
    noise_eps,
    noise_level,
    valid_count,
    neighbours,
    nbr_count,
    pix_node,
    pix_read,
    w_enc,
    w_cond,
    w_dec,
    layer_w,
    soap_first,
    soap_second,
    soap_basis,
    soap_stats,
    enc_first,
    enc_second,
    cond_first,
    cond_second,
    dec_first,
    dec_second,
):
    nodes = nbr_count.shape[0]
    groups = lax.axis_size("node")
    heads = lax.axis_size("head")
    rows = nodes // heads
    reach = 3 * nodes
    block_start = lax.axis_index("node") * nodes
    quarter = lax.axis_index("head")
    width = w_enc.shape[1]
    both = ("head", "node")

    low_w = layer_w.astype(bf16)
    w_attn = lax.all_gather(low_w[0], "node", axis=0, tiled=True)
    big_share = jnp.concatenate([low_w[1], low_w[2], low_w[0, :, 3 * HD :]], 1)
    w_big = lax.all_gather(big_share, both, axis=0, tiled=True).reshape(heads, width, -1)

    noise_sigma, noise_feat = noise_terms(noise_level)
    sig_sq = noise_sigma * noise_sigma
    input_scale = lax.rsqrt(sig_sq + 1.0)
    skip_scale = 1.0 / (sig_sq + 1.0)
    output_scale = noise_sigma * lax.rsqrt(sig_sq + 1.0)
    loss_scale = (sig_sq + 1.0) / sig_sq
    modulation = jnp.dot(noise_feat[None, :], w_cond, precision=highest).reshape(4, width)

    prev_t, target_t, eps_t = prev_state.T, target.T, noise_eps.T
    node_row = pix_node.reshape(1, -1)
    read_rows = pix_read.T
    place = jnp.stack([block_start, quarter * rows, valid_count[0], quarter]).astype(jnp.int32)
    node_in, stat = encode(
        place, jnp.stack([noise_sigma, input_scale]), node_row, prev_t, target_t, eps_t, rows, 1024
    )
    stat_sum = lax.psum(jnp.sum(stat, 1), "node")
    count_sum = stat_sum[SLIM - 1]
    var_weight = 1.0 / (stat_sum[:VARS] / count_sum + norm_eps)
    loss_count = count_sum * VARS

    pad_enc = jnp.zeros((2, SLOT, width), bf16)
    pad_enc = pad_enc.at[:, :VARS].set(w_enc.astype(bf16).reshape(2, VARS, width))
    h_zero, norm_one = enter(node_in, pad_enc.reshape(2 * SLOT, width), modulation)
    norm_all = lax.all_gather(norm_one, "head", axis=0, tiled=True)
    query, keyval = project(norm_all, w_attn, 512)
    below = passed_along(keyval, "node", 1)
    above = passed_along(keyval, "node", -1)

    relative = (neighbours - block_start + nodes) % (nodes * groups)
    live = jnp.arange(NBR)[None, :] < nbr_count[:, None]
    slots = jnp.where(live, relative, -1).reshape(nodes // GROUP, 256)
    counts = count_slots(slots, reach, 8)
    e, mix, mixed_low = attend(query, below, keyval, above, counts, 128, 512)
    mixed = lax.all_to_all(mixed_low.reshape(heads, rows, HD), "head", 0, 0)

    w_dec_t = jnp.zeros((SLIM, width), bf16).at[:VARS].set(w_dec.T.astype(bf16))
    h_one, h_two, norm_two, up, act, dec = forward(mixed, h_zero, w_big, modulation, w_dec_t, 256)
    decoded = lax.all_gather(dec, "head", axis=0)
    scales = jnp.stack(
        [noise_sigma, input_scale, skip_scale, output_scale, output_scale * (2.0 / loss_count) / 3.0]
    )
    weight = jnp.broadcast_to((loss_scale * var_weight)[:, None], (VARS, 128))
    loss_part, d_part = pixels_back(
        place, scales, node_row, read_rows, target_t, eps_t, weight, decoded, 512
    )
    d_dec = lax.all_to_all(d_part.reshape(heads, rows, SLOT), "head", 0, 0)
    d_one, d_mixed, grad_big, grad_dec, gmod_two = backward(
        d_dec, h_two, h_one, norm_two, up, act, mixed, w_big, modulation, w_dec_t, 256
    )
    big_share = lax.psum_scatter(
        grad_big.reshape(heads * width, -1), both, scatter_dimension=0, tiled=True
    )
    d_mixed = lax.all_to_all(d_mixed, "head", 0, 0).reshape(nodes, HD)
    dq, kv_low, kv_self, kv_high = attend_back(
        query, d_mixed, mix, e, below, keyval, above, 256, 512
    )
    from_above = passed_along(kv_low, "node", -1)
    from_below = passed_along(kv_high, "node", 1)
    dn_part, grad_qkv = unproject(dq, kv_self, from_below, from_above, norm_all, w_attn, 512)
    qkv_share = lax.psum_scatter(grad_qkv, "node", scatter_dimension=0, tiled=True)
    d_norm = lax.all_to_all(dn_part.reshape(heads, rows, width), "head", 0, 0)
    grad_enc, gmod_one = leave(d_norm, h_zero, d_one, node_in, modulation)

    grad_enc = jnp.concatenate([grad_enc[:VARS], grad_enc[SLOT : SLOT + VARS]], 0)
    d_mod = jnp.concatenate([gmod_one[:2], gmod_two[:2]], 0)
    grad_enc, d_mod, grad_dec = lax.psum((grad_enc, d_mod, grad_dec[:VARS]), both)
    grad_cond = noise_feat[:, None] * d_mod.reshape(1, -1)
    layer_share = jnp.stack(
        [
            jnp.concatenate([qkv_share, big_share[:, 2 * width :]], 1),
            big_share[:, :width],
            big_share[:, width : 2 * width],
        ]
    )
    small_sq = (
        jnp.sum(grad_enc * grad_enc) + jnp.sum(grad_cond * grad_cond) + jnp.sum(grad_dec * grad_dec)
    )
    total_sq, loss_sum = lax.psum((jnp.sum(layer_share * layer_share), jnp.sum(loss_part[:VARS])), both)
    grad_norm = jnp.sqrt(total_sq + small_sq)
    clip_factor = clip_limit / jnp.maximum(grad_norm, clip_limit)
    clipped = clip_factor * layer_share
    grad_full = lax.all_gather(layer_share, "node", axis=1, tiled=True)
    raw_stat = jnp.einsum("idb,idc->ibc", grad_full, grad_full, precision=highest)
    stat_new = clip_factor * (clip_factor * raw_stat)
    basis_old = soap_basis[:, 0]
    rotated = jnp.einsum("idb,ibc->idc", clipped, basis_old, precision=highest)
    first_new = beta_first * soap_first + (1 - beta_first) * rotated
    second_new = beta_second * soap_second + (1 - beta_second) * rotated * rotated
    direction = (
        first_new
        / (1 - beta_first**STEP)
        / (jnp.sqrt(second_new / (1 - beta_second**STEP)) + adam_epsilon)
    )
    step_back = jnp.einsum("idc,ibc->idb", direction, basis_old, precision=highest)
    layer_new = layer_w - rate_layer * (step_back + decay_rate * layer_w)
    stats_new = beta_stats * soap_stats[:, 0] + (1 - beta_stats) * stat_new
    product = jnp.einsum("ibc,icd->ibd", stats_new, basis_old, precision=highest)
    gram_matrix = jnp.einsum("ibc,ibd->icd", product, product, precision=highest)
    basis_new = renew(gram_matrix, product)
    enc_new = adam_small(w_enc, clip_factor * grad_enc, enc_first, enc_second)
    cond_new = adam_small(w_cond, clip_factor * grad_cond, cond_first, cond_second)
    dec_new = adam_small(w_dec.T, clip_factor * grad_dec, dec_first.T, dec_second.T)
    return (
        jnp.reshape(loss_sum, (1,)),
        jnp.reshape(loss_count, (1,)),
        jnp.reshape(grad_norm, (1,)),
        layer_new,
        first_new,
        second_new,
        basis_new[:, None],
        stats_new[:, None],
        *enc_new,
        *cond_new,
        *(x.T for x in dec_new),
    )


def solution(mesh):
    pixel = P("node", None)
    layer = P(None, "node", "head")
    basis = P(None, "head", None, None)
    placed = (
        *(pixel,) * 3,
        P(),
        P("node"),
        P("node", None),
        P("node"),
        P("node"),
        P("node", None),
        *(P(),) * 3,
        *(layer,) * 3,
        *(basis,) * 2,
        *(P(),) * 6,
    )
    return jax.shard_map(
        local,
        mesh=mesh,
        in_specs=placed,
        out_specs=(*(P(),) * 3, *(layer,) * 3, *(basis,) * 2, *(P(),) * 9),
        check_vma=False,
    )
```

```python
import functools
import math

import jax
import jax.numpy as jnp
from jax import lax
from jax.experimental import pallas as pl
from jax.experimental.pallas import tpu as pltpu
from jax.sharding import PartitionSpec as P

HD = 128
VARS = 84
NF = 32
NBR = 16
LEVELS = 1000
STEP = 10

SLOT = 128
SLIM = 96
GROUP = 256 // NBR
BLOCK = 128

highest = lax.Precision.HIGHEST
clip_limit = 0.01
beta_first = 0.9
beta_second = 0.95
beta_stats = 0.95
adam_epsilon = 1e-08
rate_layer = 0.02
rate_small = 0.05
decay_rate = 0.1
norm_eps = 1e-05

f32 = jnp.float32
bf16 = jnp.bfloat16
MIB = 2**20


def passed_along(x, axis, by):
    length = lax.axis_size(axis)
    return lax.ppermute(x, axis, [(i, (i + by) % length) for i in range(length)])


def noise_terms(noise_level):
    level_frac = noise_level[0].astype(f32) / (LEVELS - 1)
    noise_sigma = 0.05 * jnp.exp(level_frac * math.log(40.0))
    frequency = 1.0 + jnp.arange(NF // 2).astype(f32)
    phase_angle = jnp.log(noise_sigma) * frequency
    return (noise_sigma, jnp.concatenate([jnp.sin(phase_angle), jnp.cos(phase_angle)]))


def standardize(values_in):
    row_mean = jnp.mean(values_in, -1, keepdims=True)
    centered = values_in - row_mean
    inv_std = lax.rsqrt(jnp.mean(centered * centered, -1, keepdims=True) + norm_eps)
    return (centered * inv_std, inv_std)


def norm_back(normed, inv_std, grad_in):
    return inv_std * (
        grad_in
        - jnp.mean(grad_in, -1, keepdims=True)
        - normed * jnp.mean(grad_in * normed, -1, keepdims=True)
    )


def contract(left, right, left_dim, right_dim, precision=None):
    return lax.dot_general(
        left,
        right,
        (((left_dim,), (right_dim,)), ((), ())),
        preferred_element_type=f32,
        precision=precision,
    )


def halves(x):
    high = x.astype(bf16)
    return high, (x - high.astype(f32)).astype(bf16)


def thirds(x):
    high = x.astype(bf16)
    rest = x - high.astype(f32)
    return (high, *halves(rest))


def fold_lanes(x, op=jnp.add):
    parts = [x[:, i : i + 128] for i in range(0, x.shape[1], 128)]
    while len(parts) > 1:
        parts = [op(*parts[i : i + 2]) if i + 1 < len(parts) else parts[i] for i in range(0, len(parts), 2)]
    return parts[0]


def adam_small(weight, grad_item, first, second):
    first_new = beta_first * first + (1 - beta_first) * grad_item
    second_new = beta_second * second + (1 - beta_second) * grad_item * grad_item
    ratio = (
        first_new
        / (1 - beta_first**STEP)
        / (jnp.sqrt(second_new / (1 - beta_second**STEP)) + adam_epsilon)
    )
    return (weight - rate_small * (ratio + decay_rate * weight), first_new, second_new)


def smem():
    return pl.BlockSpec(memory_space=pltpu.SMEM)


def whole(shape):
    zeros = (0,) * len(shape)
    return pl.BlockSpec(tuple(shape), lambda *_: zeros)


def params(mib=48):
    return pltpu.CompilerParams(vmem_limit_bytes=mib * MIB)


def encode_kernel(place_ref, scale_ref, node_ref, prev_ref, target_ref, eps_ref, in_ref, stat_ref, pix):
    step = pl.program_id(0)
    rows = in_ref.shape[0]
    tile = node_ref.shape[1]

    @pl.when(step == 0)
    def _():
        pix[...] = jnp.zeros_like(pix)
        in_ref[...] = jnp.zeros_like(in_ref)
        stat_ref[...] = jnp.zeros_like(stat_ref)

    prev = prev_ref[...]
    target = target_ref[...]
    noisy = target + scale_ref[0] * eps_ref[...]
    pix[:VARS] = prev.astype(bf16)
    pix[SLOT : SLOT + VARS] = (scale_ref[1] * noisy).astype(bf16)
    node = node_ref[...] - place_ref[0]
    mine = node - place_ref[1]
    spot = lax.broadcasted_iota(jnp.int32, (rows, tile), 0)
    onehot = (spot == mine).astype(f32).astype(bf16)
    in_ref[...] += contract(onehot, pix[...], 1, 1)
    valid = (node < place_ref[2]).astype(f32)
    residual = target - prev
    stat_ref[:VARS] += fold_lanes(valid * residual * residual)
    stat_ref[SLIM - 1 : SLIM] += fold_lanes(valid)


def encode(place, scales, node_row, prev, target, eps, rows, tile):
    pixels = prev.shape[1]
    pixel_block = pl.BlockSpec((VARS, tile), lambda i: (0, i))
    return pl.pallas_call(
        encode_kernel,
        grid=(pixels // tile,),
        in_specs=[smem(), smem(), pl.BlockSpec((1, tile), lambda i: (0, i))] + [pixel_block] * 3,
        out_specs=[whole((rows, 2 * SLOT)), whole((SLIM, 128))],
        out_shape=[
            jax.ShapeDtypeStruct((rows, 2 * SLOT), f32),
            jax.ShapeDtypeStruct((SLIM, 128), f32),
        ],
        scratch_shapes=[pltpu.VMEM((2 * SLOT, tile), bf16)],
        compiler_params=params(),
        name="encode",
    )(place, scales, node_row, prev, target, eps)


def enter_kernel(in_ref, w_ref, mod_ref, zero_ref, norm_ref):
    w = w_ref[...]
    h_zero = sum(contract(part, w, 1, 0) for part in thirds(in_ref[...]))
    zero_ref[...] = h_zero
    normed, _ = standardize(h_zero)
    norm_ref[...] = (normed * (1 + mod_ref[0:1]) + mod_ref[1:2]).astype(bf16)


def enter(node_in, w_enc, modulation):
    rows, width = node_in.shape[0], w_enc.shape[1]
    return pl.pallas_call(
        enter_kernel,
        out_shape=[
            jax.ShapeDtypeStruct((rows, width), f32),
            jax.ShapeDtypeStruct((rows, width), bf16),
        ],
        compiler_params=params(),
        name="enter",
    )(node_in, w_enc, modulation)


def project_kernel(norm_ref, w_ref, q_ref, kv_ref):
    out = contract(norm_ref[...], w_ref[...], 1, 0).astype(bf16)
    q_ref[...] = out[:, :HD]
    kv_ref[...] = out[:, HD : 3 * HD]


def project(norm_all, w_attn, tile):
    nodes, width = norm_all.shape
    return pl.pallas_call(
        project_kernel,
        grid=(nodes // tile,),
        in_specs=[
            pl.BlockSpec((tile, width), lambda i: (i, 0)),
            pl.BlockSpec((width, 3 * HD), lambda i: (0, 0)),
        ],
        out_specs=[
            pl.BlockSpec((tile, HD), lambda i: (i, 0)),
            pl.BlockSpec((tile, 2 * HD), lambda i: (i, 0)),
        ],
        out_shape=[
            jax.ShapeDtypeStruct((nodes, HD), bf16),
            jax.ShapeDtypeStruct((nodes, 2 * HD), bf16),
        ],
        compiler_params=params(),
        name="project",
    )(norm_all, w_attn)


def count_kernel(slot_ref, count_ref):
    groups = slot_ref.shape[0]
    bands = count_ref.shape[1] // 256
    lane = lax.broadcasted_iota(jnp.int32, (GROUP, 256), 1)
    sub = lax.broadcasted_iota(jnp.int32, (GROUP, 256), 0)
    own = lane // NBR == sub
    spot = lax.broadcasted_iota(jnp.int32, (256, 256), 0)
    for g in range(groups):
        row = slot_ref[g : g + 1]
        band = jnp.where(own, row >> 8, -1)
        left = jnp.concatenate([(band == t).astype(f32).astype(bf16) for t in range(bands)], 0)
        right = (spot == (row & 255)).astype(f32).astype(bf16)
        found = contract(left, right, 1, 1).astype(bf16)
        for t in range(bands):
            count_ref[g * GROUP : (g + 1) * GROUP, t * 256 : (t + 1) * 256] = found[
                t * GROUP : (t + 1) * GROUP
            ]


def count_slots(slots, reach, tile_groups):
    groups = slots.shape[0]
    return pl.pallas_call(
        count_kernel,
        grid=(groups // tile_groups,),
        in_specs=[pl.BlockSpec((tile_groups, 256), lambda i: (i, 0))],
        out_specs=pl.BlockSpec((tile_groups * GROUP, reach), lambda i: (i, 0)),
        out_shape=jax.ShapeDtypeStruct((groups * GROUP, reach), bf16),
        compiler_params=params(),
        name="count_slots",
    )(slots)


def attend_kernel(q_ref, below_ref, here_ref, above_ref, count_ref, e_ref, mix_ref, low_ref, s_scr, chunk):
    tile = q_ref.shape[0]
    nodes = here_ref.shape[0]
    q = q_ref[...]
    top = jnp.full((tile, 128), -1e30, f32)
    for b, kv_ref in enumerate((below_ref, here_ref, above_ref)):
        for at in range(0, nodes, chunk):
            cols = slice(b * nodes + at, b * nodes + at + chunk)
            s = contract(q, kv_ref[at : at + chunk, :HD], 1, 1)
            s = jnp.where(count_ref[:, cols].astype(f32) > 0, s, -1e30)
            s_scr[:, cols] = s
            top = jnp.maximum(top, fold_lanes(s, jnp.maximum))
    top = jnp.max(top, 1, keepdims=True)
    factor = math.log2(math.e) / math.sqrt(HD)
    total = jnp.zeros((tile, 128), f32)
    mixed = jnp.zeros((tile, HD), f32)
    for b, kv_ref in enumerate((below_ref, here_ref, above_ref)):
        for at in range(0, nodes, chunk):
            cols = slice(b * nodes + at, b * nodes + at + chunk)
            e = count_ref[:, cols].astype(f32) * jnp.exp2((s_scr[:, cols] - top) * factor)
            total += fold_lanes(e)
            e = e.astype(bf16)
            e_ref[:, cols] = e
            mixed += contract(e, kv_ref[at : at + chunk, HD:], 1, 0)
    inverse = 1.0 / jnp.sum(total, 1, keepdims=True)
    mixed = mixed * inverse
    mix_ref[:, :HD] = mixed
    mix_ref[:, HD:] = jnp.broadcast_to(inverse, (tile, HD))
    low_ref[...] = mixed.astype(bf16)


def attend(query, below, here, above, counts, tile, chunk):
    nodes, reach = counts.shape
    row = lambda width: pl.BlockSpec((tile, width), lambda i: (i, 0))
    return pl.pallas_call(
        functools.partial(attend_kernel, chunk=chunk),
        grid=(nodes // tile,),
        in_specs=[row(HD)] + [whole((nodes, 2 * HD))] * 3 + [row(reach)],
        out_specs=[row(reach), row(2 * HD), row(HD)],
        out_shape=[
            jax.ShapeDtypeStruct((nodes, reach), bf16),
            jax.ShapeDtypeStruct((nodes, 2 * HD), f32),
            jax.ShapeDtypeStruct((nodes, HD), bf16),
        ],
        scratch_shapes=[pltpu.VMEM((tile, reach), f32)],
        compiler_params=params(60),
        name="attend",
    )(query, below, here, above, counts)


def attend_back_kernel(
    q_ref, d_ref, mix_ref, e_ref, below_ref, here_ref, above_ref, dq_ref, low_ref, self_ref, high_ref, dk, dv, chunk
):
    step = pl.program_id(0)
    tile = q_ref.shape[0]
    nodes = here_ref.shape[0]

    @pl.when(step == 0)
    def _():
        dk[...] = jnp.zeros_like(dk)
        dv[...] = jnp.zeros_like(dv)

    grad = d_ref[...]
    wide = grad.astype(f32)
    inverse = mix_ref[:, HD : HD + 1]
    delta = jnp.sum(wide * mix_ref[:, :HD], 1, keepdims=True)
    gain = inverse * (1.0 / math.sqrt(HD))
    q_turned = q_ref[...].T
    d_turned = (wide * inverse).astype(bf16).T
    dq = jnp.zeros((tile, HD), f32)
    for b, kv_ref in enumerate((below_ref, here_ref, above_ref)):
        for at in range(0, nodes, chunk):
            cols = slice(b * nodes + at, b * nodes + at + chunk)
            key = kv_ref[at : at + chunk, :HD]
            dp = contract(grad, kv_ref[at : at + chunk, HD:], 1, 1)
            e = e_ref[:, cols]
            ds = (e.astype(f32) * ((dp - delta) * gain)).astype(bf16)
            dq += contract(ds, key, 1, 0)
            dk[:, cols] += contract(q_turned, ds, 1, 0)
            dv[:, cols] += contract(d_turned, e, 1, 0)
    dq_ref[...] = dq.astype(bf16)

    @pl.when(step == pl.num_programs(0) - 1)
    def _():
        for b, ref in enumerate((low_ref, self_ref, high_ref)):
            cols = slice(b * nodes, (b + 1) * nodes)
            ref[:HD] = dk[:, cols].astype(ref.dtype)
            ref[HD:] = dv[:, cols].astype(ref.dtype)


def attend_back(query, grad, mix, e, below, here, above, tile, chunk):
    nodes, reach = e.shape
    row = lambda width: pl.BlockSpec((tile, width), lambda i: (i, 0))
    return pl.pallas_call(
        functools.partial(attend_back_kernel, chunk=chunk),
        grid=(nodes // tile,),
        in_specs=[row(HD), row(HD), row(2 * HD), row(reach)] + [whole((nodes, 2 * HD))] * 3,
        out_specs=[row(HD)] + [whole((2 * HD, nodes))] * 3,
        out_shape=[
            jax.ShapeDtypeStruct((nodes, HD), bf16),
            jax.ShapeDtypeStruct((2 * HD, nodes), bf16),
            jax.ShapeDtypeStruct((2 * HD, nodes), f32),
            jax.ShapeDtypeStruct((2 * HD, nodes), bf16),
        ],
        scratch_shapes=[pltpu.VMEM((HD, reach), f32)] * 2,
        compiler_params=params(60),
        name="attend_back",
    )(query, grad, mix, e, below, here, above)


def forward_kernel(mixed_ref, zero_ref, w_ref, mod_ref, wdec_ref, one_ref, two_ref, norm_ref, up_ref, act_ref, dec_ref):
    heads, width = w_ref.shape[0], w_ref.shape[1]
    h_one = zero_ref[...] + sum(
        contract(mixed_ref[h], w_ref[h, :, 2 * width :], 1, 1) for h in range(heads)
    )
    one_ref[...] = h_one
    normed, _ = standardize(h_one)
    norm_two = (normed * (1 + mod_ref[2:3]) + mod_ref[3:4]).astype(bf16)
    norm_ref[...] = norm_two
    h_two = h_one
    for h in range(heads):
        up = contract(norm_two, w_ref[h, :, :width], 1, 0)
        up_ref[h] = up
        act = (up * jax.nn.sigmoid(up)).astype(bf16)
        act_ref[h] = act
        h_two = h_two + contract(act, w_ref[h, :, width : 2 * width], 1, 1)
    two_ref[...] = h_two
    final = standardize(h_two)[0].astype(bf16)
    high, low = halves(contract(wdec_ref[...], final, 1, 1))
    dec_ref[:SLIM] = high
    dec_ref[SLIM:] = low


def forward(mixed, h_zero, w_big, modulation, w_dec, tile):
    heads, rows = mixed.shape[:2]
    width = h_zero.shape[1]
    row = pl.BlockSpec((tile, width), lambda i: (i, 0))
    stack = lambda w: pl.BlockSpec((heads, tile, w), lambda i: (0, i, 0))
    return pl.pallas_call(
        forward_kernel,
        grid=(rows // tile,),
        in_specs=[stack(HD), row, whole(w_big.shape), whole(modulation.shape), whole(w_dec.shape)],
        out_specs=[row, row, row, stack(width), stack(width), pl.BlockSpec((2 * SLIM, tile), lambda i: (0, i))],
        out_shape=[
            jax.ShapeDtypeStruct((rows, width), f32),
            jax.ShapeDtypeStruct((rows, width), f32),
            jax.ShapeDtypeStruct((rows, width), bf16),
            jax.ShapeDtypeStruct((heads, rows, width), f32),
            jax.ShapeDtypeStruct((heads, rows, width), bf16),
            jax.ShapeDtypeStruct((2 * SLIM, rows), bf16),
        ],
        compiler_params=params(),
        name="forward",
    )(mixed, h_zero, w_big, modulation, w_dec)


def pixel_kernel(place_ref, scale_ref, node_ref, read_ref, target_ref, eps_ref, weight_ref, dec_ref, loss_ref, d_ref, hits, turned, total):
    step = pl.program_id(0)
    heads, _, rows = dec_ref.shape
    tile = target_ref.shape[1]

    @pl.when(step == 0)
    def _():
        turned[...] = jnp.zeros_like(turned)
        total[...] = jnp.zeros_like(total)
        loss_ref[...] = jnp.zeros_like(loss_ref)

    reads = read_ref[...] - place_ref[0]
    field = jnp.zeros((2 * SLIM, tile), f32)
    for h in range(heads):
        spot = lax.broadcasted_iota(jnp.int32, (rows, tile), 0) + h * rows
        hit = sum((spot == reads[k : k + 1]).astype(f32) for k in range(3)).astype(bf16)
        hits[h * rows : (h + 1) * rows] = hit
        field += contract(dec_ref[h], hit, 1, 0)
    field = (field[:VARS] + field[SLIM : SLIM + VARS]) / 3.0
    target = target_ref[...]
    noisy = target + scale_ref[0] * eps_ref[...]
    error = scale_ref[2] * noisy + scale_ref[3] * field - target
    valid = (node_ref[...] - place_ref[0] < place_ref[2]).astype(f32)
    weighted = valid * weight_ref[:, 0:1]
    loss_ref[:VARS] += fold_lanes(weighted * error * error)
    high, low = halves(scale_ref[4] * weighted * error)
    turned[:VARS] = high
    turned[SLOT : SLOT + VARS] = low
    total[...] += contract(hits[...], turned[...], 1, 1)

    @pl.when(step == pl.num_programs(0) - 1)
    def _():
        d_ref[...] = total[:, :SLOT] + total[:, SLOT:]


def pixels_back(place, scales, node_row, read_rows, target, eps, weight, decoded, tile):
    heads, _, rows = decoded.shape
    count = target.shape[1] // heads
    steps = count // tile
    at = lambda i, place: (0, place[3] * steps + i)
    fixed = lambda shape: pl.BlockSpec(tuple(shape), lambda i, place: (0,) * len(shape))
    return pl.pallas_call(
        pixel_kernel,
        grid_spec=pltpu.PrefetchScalarGridSpec(
            num_scalar_prefetch=1,
            grid=(steps,),
            in_specs=[
                smem(),
                pl.BlockSpec((1, tile), at),
                pl.BlockSpec((3, tile), at),
                pl.BlockSpec((VARS, tile), at),
                pl.BlockSpec((VARS, tile), at),
                fixed(weight.shape),
                fixed(decoded.shape),
            ],
            out_specs=[fixed((SLIM, 128)), fixed((heads * rows, SLOT))],
            scratch_shapes=[
                pltpu.VMEM((heads * rows, tile), bf16),
                pltpu.VMEM((2 * SLOT, tile), bf16),
                pltpu.VMEM((heads * rows, 2 * SLOT), f32),
            ],
        ),
        out_shape=[
            jax.ShapeDtypeStruct((SLIM, 128), f32),
            jax.ShapeDtypeStruct((heads * rows, SLOT), f32),
        ],
        compiler_params=params(),
        name="pixels_back",
    )(place, scales, node_row, read_rows, target, eps, weight, decoded)


def backward_kernel(
    d_ref, two_ref, one_ref, norm_ref, up_ref, act_ref, mixed_ref, w_ref, mod_ref, wdec_ref,
    done_ref, dmix_ref, grad_ref, gdec_ref, gmod_ref,
):
    heads, width = w_ref.shape[0], w_ref.shape[1]
    step = pl.program_id(0)

    @pl.when(step == 0)
    def _():
        grad_ref[...] = jnp.zeros_like(grad_ref)
        gdec_ref[...] = jnp.zeros_like(gdec_ref)
        gmod_ref[...] = jnp.zeros_like(gmod_ref)

    d_dec = sum(d_ref[h] for h in range(heads)).astype(bf16)
    normed_two, inv_two = standardize(two_ref[...])
    final = normed_two.astype(bf16)
    gdec_ref[...] += contract(d_dec[:, :SLIM], final, 0, 0)
    d_two = norm_back(normed_two, inv_two, contract(d_dec[:, :SLIM], wdec_ref[...], 1, 0))
    d_low = d_two.astype(bf16)
    norm_two = norm_ref[...]
    d_mid = jnp.zeros_like(d_two)
    for h in range(heads):
        act = act_ref[h]
        up = up_ref[h]
        d_act = contract(d_low, w_ref[h, :, width : 2 * width], 1, 0)
        gating = jax.nn.sigmoid(up)
        d_up = (d_act * gating * (1 + up * (1 - gating))).astype(bf16)
        grad_ref[h, :, :width] += contract(norm_two, d_up, 0, 0)
        grad_ref[h, :, width : 2 * width] += contract(d_low, act, 0, 0)
        d_mid += contract(d_up, w_ref[h, :, :width], 1, 1)
    normed_one, inv_one = standardize(one_ref[...])
    gmod_ref[0:1] += jnp.sum(d_mid * normed_one, 0, keepdims=True)
    gmod_ref[1:2] += jnp.sum(d_mid, 0, keepdims=True)
    d_one = d_two + norm_back(normed_one, inv_one, d_mid * (1 + mod_ref[2:3]))
    done_ref[...] = d_one
    one_low = d_one.astype(bf16)
    for h in range(heads):
        dmix_ref[h] = contract(one_low, w_ref[h, :, 2 * width :], 1, 0).astype(bf16)
        grad_ref[h, :, 2 * width :] += contract(one_low, mixed_ref[h], 0, 0)


def backward(d_dec, h_two, h_one, norm_two, up, act, mixed, w_big, modulation, w_dec, tile):
    heads, rows = mixed.shape[:2]
    width = h_one.shape[1]
    row = lambda w: pl.BlockSpec((tile, w), lambda i: (i, 0))
    stack = lambda w: pl.BlockSpec((heads, tile, w), lambda i: (0, i, 0))
    return pl.pallas_call(
        backward_kernel,
        grid=(rows // tile,),
        in_specs=[
            stack(SLOT),
            row(width),
            row(width),
            row(width),
            stack(width),
            stack(width),
            stack(HD),
            whole(w_big.shape),
            whole(modulation.shape),
            whole(w_dec.shape),
        ],
        out_specs=[row(width), stack(HD), whole(w_big.shape), whole((SLIM, width)), whole((8, width))],
        out_shape=[
            jax.ShapeDtypeStruct((rows, width), f32),
            jax.ShapeDtypeStruct((heads, rows, HD), bf16),
            jax.ShapeDtypeStruct(w_big.shape, f32),
            jax.ShapeDtypeStruct((SLIM, width), f32),
            jax.ShapeDtypeStruct((8, width), f32),
        ],
        compiler_params=params(56),
        name="backward",
    )(d_dec, h_two, h_one, norm_two, up, act, mixed, w_big, modulation, w_dec)


def unproject_kernel(dq_ref, self_ref, down_ref, up_ref, norm_ref, w_ref, dn_ref, grad_ref):
    step = pl.program_id(0)

    @pl.when(step == 0)
    def _():
        grad_ref[...] = jnp.zeros_like(grad_ref)

    kv = self_ref[...] + down_ref[...].astype(f32) + up_ref[...].astype(f32)
    both = jnp.concatenate([dq_ref[...], kv.astype(bf16).T], 1)
    dn_ref[...] = contract(both, w_ref[...], 1, 1).astype(bf16)
    grad_ref[...] += contract(norm_ref[...], both, 0, 0)


def unproject(dq, kv_self, from_below, from_above, norm_all, w_attn, tile):
    nodes, width = norm_all.shape
    row = lambda w: pl.BlockSpec((tile, w), lambda i: (i, 0))
    col = pl.BlockSpec((2 * HD, tile), lambda i: (0, i))
    return pl.pallas_call(
        unproject_kernel,
        grid=(nodes // tile,),
        in_specs=[row(HD), col, col, col, row(width), pl.BlockSpec((width, 3 * HD), lambda i: (0, 0))],
        out_specs=[row(width), whole((width, 3 * HD))],
        out_shape=[
            jax.ShapeDtypeStruct((nodes, width), bf16),
            jax.ShapeDtypeStruct((width, 3 * HD), f32),
        ],
        compiler_params=params(),
        name="unproject",
    )(dq, kv_self, from_below, from_above, norm_all, w_attn)


def settle_kernel(
    feat_ref, dn_ref, zero_ref, done_ref, in_ref, mod_ref, gdec_ref, gmod_ref, qkv_ref, big_ref, loss_ref,
    small_ref, share_ref, full_ref, sums_ref,
    parts, spread, inbox, pay, heard, q_low, q_box, sems,
):
    heads = dn_ref.shape[0]
    nodes = q_low.shape[0]
    world = inbox.shape[0]
    head, node = lax.axis_index("head"), lax.axis_index("node")
    me = head * nodes + node
    share_rows = share_ref.shape[0]
    a_send, a_recv, q_send, q_recv, b_send, b_recv, f_send, f_recv = (sems.at[i] for i in range(8))

    def where(other):
        return {"head": other // nodes, "node": other % nodes}

    barrier = pltpu.get_barrier_semaphore()

    def greet(off, carry):
        pl.semaphore_signal(barrier, inc=1, device_id=where((me + off) % world))
        return carry

    lax.fori_loop(1, world, greet, 0)
    for t in range(nodes):
        q_low[t] = qkv_ref[t * share_rows : (t + 1) * share_rows].astype(bf16)
    pl.semaphore_wait(barrier, world - 1)

    def q_copy(off):
        other = (node + off) % nodes
        return pltpu.make_async_remote_copy(
            src_ref=q_low.at[other],
            dst_ref=q_box.at[node],
            send_sem=q_send.at[other],
            recv_sem=q_recv.at[node],
            device_id={"node": other},
        )

    def q_arrived(off):
        other = (node + off) % nodes
        return pltpu.make_async_remote_copy(
            src_ref=q_low.at[other],
            dst_ref=q_box.at[other],
            send_sem=q_send.at[other],
            recv_sem=q_recv.at[other],
            device_id={"node": other},
        )

    def each(count, act):
        def body(off, carry):
            act(off)
            return carry

        lax.fori_loop(1, count, body, 0)

    each(nodes, lambda off: q_copy(off).start())

    d_norm = sum(dn_ref[h].astype(f32) for h in range(heads))
    normed, inv = standardize(zero_ref[...])
    d_zero = done_ref[...] + norm_back(normed, inv, d_norm * (1 + mod_ref[0:1]))
    g_enc = contract(in_ref[...].T, d_zero, 1, 0, highest)
    parts[...] = jnp.zeros_like(parts)
    parts[:VARS] = g_enc[:VARS]
    parts[VARS : 2 * VARS] = g_enc[SLOT : SLOT + VARS]
    parts[2 * VARS : 3 * VARS] = gdec_ref[:VARS]
    at = 3 * VARS
    parts[at : at + 1] = jnp.sum(d_norm * normed, 0, keepdims=True)
    parts[at + 1 : at + 2] = jnp.sum(d_norm, 0, keepdims=True)
    parts[at + 2 : at + 4] = gmod_ref[0:2]
    for t in range(world):
        spread[t] = parts[8 * t : 8 * t + 8]

    def a_copy(off, slot):
        other = (me + off) % world
        return pltpu.make_async_remote_copy(
            src_ref=spread.at[other],
            dst_ref=inbox.at[slot(other)],
            send_sem=a_send.at[other],
            recv_sem=a_recv.at[slot(other)],
            device_id=where(other),
        )

    def b_copy(off, slot):
        other = (me + off) % world
        return pltpu.make_async_remote_copy(
            src_ref=pay,
            dst_ref=heard.at[slot(other)],
            send_sem=b_send.at[other],
            recv_sem=b_recv.at[slot(other)],
            device_id=where(other),
        )

    mine = lambda other: me
    theirs = lambda other: other
    each(world, lambda off: a_copy(off, mine).start())

    each(nodes, lambda off: q_arrived(off).wait_recv())
    q_box[node] = q_low[node]
    share = sum(q_box[t].astype(f32) for t in range(nodes))
    share_ref[...] = share
    each(nodes, lambda off: q_copy(off).wait_send())
    q_low[0] = share.astype(bf16)

    def f_copy(off, slot):
        other = (node + off) % nodes
        return pltpu.make_async_remote_copy(
            src_ref=q_low.at[0],
            dst_ref=full_ref.at[slot(other)],
            send_sem=f_send.at[other],
            recv_sem=f_recv.at[slot(other)],
            device_id={"node": other},
        )

    each(nodes, lambda off: f_copy(off, lambda other: node).start())
    full_ref[node] = share.astype(bf16)

    each(world, lambda off: a_copy(off, theirs).wait_recv())
    inbox[me] = spread[me]
    own = sum(inbox[t] for t in range(world))
    row = lax.broadcasted_iota(jnp.int32, own.shape, 0) + 8 * me
    weighted = own * own * jnp.where(row >= 3 * VARS, feat_ref[0], 1.0)
    total = jnp.sum(weighted) + jnp.sum(share * share) + jnp.sum(big_ref[...] * big_ref[...])
    loss = jnp.sum(loss_ref[:VARS])
    width = own.shape[1]
    pay[:, :width] = own
    line = lax.broadcasted_iota(jnp.int32, (8, 128), 0)
    pay[:, width:] = jnp.where(line == 0, total, jnp.where(line == 1, loss, 0.0))
    each(world, lambda off: b_copy(off, mine).start())
    heard[me] = pay[...]
    each(world, lambda off: b_copy(off, theirs).wait_recv())
    for t in range(world):
        small_ref[8 * t : 8 * t + 8] = heard[t, :, :width]
    sums_ref[...] = sum(heard[t, :, width:] for t in range(world))
    each(nodes, lambda off: f_copy(off, lambda other: other).wait_recv())
    each(world, lambda off: a_copy(off, mine).wait_send())
    each(world, lambda off: b_copy(off, mine).wait_send())
    each(nodes, lambda off: f_copy(off, lambda other: node).wait_send())


def settle(feat_sq, d_norm, h_zero, d_one, node_in, modulation, grad_dec, gmod_two, grad_qkv, big_share, loss, nodes):
    heads, rows, width = d_norm.shape
    world = heads * nodes
    share = (grad_qkv.shape[0] // nodes, grad_qkv.shape[1])
    return pl.pallas_call(
        settle_kernel,
        in_specs=[smem()] + [pl.BlockSpec(memory_space=pltpu.VMEM)] * 10,
        out_specs=[pl.BlockSpec(memory_space=pltpu.VMEM)] * 4,
        out_shape=[
            jax.ShapeDtypeStruct((8 * world, width), f32),
            jax.ShapeDtypeStruct(share, f32),
            jax.ShapeDtypeStruct((nodes, *share), bf16),
            jax.ShapeDtypeStruct((8, 128), f32),
        ],
        scratch_shapes=[
            pltpu.VMEM((8 * world, width), f32),
            pltpu.VMEM((world, 8, width), f32),
            pltpu.VMEM((world, 8, width), f32),
            pltpu.VMEM((8, width + 128), f32),
            pltpu.VMEM((world, 8, width + 128), f32),
            pltpu.VMEM((nodes, *share), bf16),
            pltpu.VMEM((nodes, *share), bf16),
            pltpu.SemaphoreType.DMA((8, world)),
        ],
        compiler_params=pltpu.CompilerParams(
            vmem_limit_bytes=48 * MIB, collective_id=1, has_side_effects=True
        ),
        name="settle",
    )(feat_sq, d_norm, h_zero, d_one, node_in, modulation, grad_dec, gmod_two, grad_qkv, big_share, loss)


def eliminate(blocks):
    size = blocks[0].shape[0]
    tiles = [[b[8 * i : 8 * i + 8] for i in range(size // 8)] for b in blocks]
    lane = lax.broadcasted_iota(jnp.int32, (8, size), 1)
    sub = lax.broadcasted_iota(jnp.int32, (8, size), 0)
    pivots = [jnp.zeros((1, size), f32) for _ in blocks]
    for j in range(size):
        first, inside = divmod(j, 8)
        for m in range(len(blocks)):
            row = tiles[m][first][inside : inside + 1]
            pivot = row[:, j : j + 1]
            here = lane[:1] == j
            pivots[m] = jnp.where(here, pivot, pivots[m])
            scaled = jnp.where(here, 1.0, row) * (1.0 / pivot)
            for i in range(first, size // 8):
                old = tiles[m][i]
                new = jnp.where(lane == j, 0.0, old) - old[:, j : j + 1] * scaled
                if i == first:
                    new = jnp.where(
                        sub > inside, new, jnp.where((sub == inside) & (lane == j), 1.0, old)
                    )
                tiles[m][i] = new
    return [jnp.concatenate(t, 0) for t in tiles], pivots


def renew_kernel(gram_ref, product_ref, out_ref, both):
    count, size = gram_ref.shape[:2]
    k = pl.program_id(0)

    @pl.when(k == 0)
    def _():
        both[:, :size] = gram_ref[...]
        both[:, size:] = product_ref[...]

    at = pl.ds(pl.multiple_of(k * BLOCK, BLOCK), BLOCK)
    factors, pivots = eliminate([both[m, at, at] for m in range(count)])
    below = lax.broadcasted_iota(jnp.int32, (size, BLOCK), 0) >= (k + 1) * BLOCK
    lower = lax.broadcasted_iota(jnp.int32, (BLOCK, BLOCK), 1) <= lax.broadcasted_iota(
        jnp.int32, (BLOCK, BLOCK), 0
    )
    for m in range(count):
        factor = jnp.where(lower, factors[m], 0.0)
        panel = contract(both[m, :, at], factor, 1, 1, highest) * lax.rsqrt(pivots[m])
        out_ref[m] = panel[size:]

        @pl.when(k < size // BLOCK - 1)
        def _():
            left = jnp.where(below, panel[:size], 0.0)
            both[m] -= contract(jnp.concatenate([left, panel[size:]], 0), left, 1, 1, highest)


def renew(gram, product):
    count, size = gram.shape[:2]
    return pl.pallas_call(
        renew_kernel,
        grid=(size // BLOCK,),
        in_specs=[whole(gram.shape), whole(gram.shape)],
        out_specs=pl.BlockSpec((count, size, BLOCK), lambda k: (0, 0, k)),
        out_shape=jax.ShapeDtypeStruct(gram.shape, f32),
        scratch_shapes=[pltpu.VMEM((count, 2 * size, size), f32)],
        compiler_params=params(),
        name="renew",
    )(gram, product)


def local(
    prev_state,
    target,
    noise_eps,
    noise_level,
    valid_count,
    neighbours,
    nbr_count,
    pix_node,
    pix_read,
    w_enc,
    w_cond,
    w_dec,
    layer_w,
    soap_first,
    soap_second,
    soap_basis,
    soap_stats,
    enc_first,
    enc_second,
    cond_first,
    cond_second,
    dec_first,
    dec_second,
):
    nodes = nbr_count.shape[0]
    groups = lax.axis_size("node")
    heads = lax.axis_size("head")
    rows = nodes // heads
    reach = 3 * nodes
    block_start = lax.axis_index("node") * nodes
    quarter = lax.axis_index("head")
    width = w_enc.shape[1]
    both = ("head", "node")

    low_w = layer_w.astype(bf16)
    w_attn = lax.all_gather(low_w[0], "node", axis=0, tiled=True)
    big_share = jnp.concatenate([low_w[1], low_w[2], low_w[0, :, 3 * HD :]], 1)
    w_big = lax.all_gather(big_share, both, axis=0, tiled=True).reshape(heads, width, -1)

    noise_sigma, noise_feat = noise_terms(noise_level)
    sig_sq = noise_sigma * noise_sigma
    input_scale = lax.rsqrt(sig_sq + 1.0)
    skip_scale = 1.0 / (sig_sq + 1.0)
    output_scale = noise_sigma * lax.rsqrt(sig_sq + 1.0)
    loss_scale = (sig_sq + 1.0) / sig_sq
    modulation = jnp.dot(noise_feat[None, :], w_cond, precision=highest).reshape(4, width)

    prev_t, target_t, eps_t = prev_state.T, target.T, noise_eps.T
    node_row = pix_node.reshape(1, -1)
    read_rows = pix_read.T
    place = jnp.stack([block_start, quarter * rows, valid_count[0], quarter]).astype(jnp.int32)
    node_in, stat = encode(
        place, jnp.stack([noise_sigma, input_scale]), node_row, prev_t, target_t, eps_t, rows, 1024
    )
    stat_sum = lax.psum(jnp.sum(stat, 1), "node")
    count_sum = stat_sum[SLIM - 1]
    var_weight = 1.0 / (stat_sum[:VARS] / count_sum + norm_eps)
    loss_count = count_sum * VARS

    pad_enc = jnp.zeros((2, SLOT, width), bf16)
    pad_enc = pad_enc.at[:, :VARS].set(w_enc.astype(bf16).reshape(2, VARS, width))
    h_zero, norm_one = enter(node_in, pad_enc.reshape(2 * SLOT, width), modulation)
    norm_all = lax.all_gather(norm_one, "head", axis=0, tiled=True)
    query, keyval = project(norm_all, w_attn, 512)
    below = passed_along(keyval, "node", 1)
    above = passed_along(keyval, "node", -1)

    relative = (neighbours - block_start + nodes) % (nodes * groups)
    live = jnp.arange(NBR)[None, :] < nbr_count[:, None]
    slots = jnp.where(live, relative, -1).reshape(nodes // GROUP, 256)
    counts = count_slots(slots, reach, 8)
    e, mix, mixed_low = attend(query, below, keyval, above, counts, 128, 512)
    mixed = lax.all_to_all(mixed_low.reshape(heads, rows, HD), "head", 0, 0)

    w_dec_t = jnp.zeros((SLIM, width), bf16).at[:VARS].set(w_dec.T.astype(bf16))
    h_one, h_two, norm_two, up, act, dec = forward(mixed, h_zero, w_big, modulation, w_dec_t, 256)
    decoded = lax.all_gather(dec, "head", axis=0)
    scales = jnp.stack(
        [noise_sigma, input_scale, skip_scale, output_scale, output_scale * (2.0 / loss_count) / 3.0]
    )
    weight = jnp.broadcast_to((loss_scale * var_weight)[:, None], (VARS, 128))
    loss_part, d_part = pixels_back(
        place, scales, node_row, read_rows, target_t, eps_t, weight, decoded, 512
    )
    d_dec = lax.all_to_all(d_part.reshape(heads, rows, SLOT), "head", 0, 0)
    d_one, d_mixed, grad_big, grad_dec, gmod_two = backward(
        d_dec, h_two, h_one, norm_two, up, act, mixed, w_big, modulation, w_dec_t, 256
    )
    big_share = lax.psum_scatter(
        grad_big.reshape(heads * width, -1), both, scatter_dimension=0, tiled=True
    )
    d_mixed = lax.all_to_all(d_mixed, "head", 0, 0).reshape(nodes, HD)
    dq, kv_low, kv_self, kv_high = attend_back(
        query, d_mixed, mix, e, below, keyval, above, 256, 512
    )
    from_above = passed_along(kv_low, "node", -1)
    from_below = passed_along(kv_high, "node", 1)
    dn_part, grad_qkv = unproject(dq, kv_self, from_below, from_above, norm_all, w_attn, 512)
    d_norm = lax.all_to_all(dn_part.reshape(heads, rows, width), "head", 0, 0)
    feat_sq = jnp.sum(noise_feat * noise_feat).reshape(1)
    small, qkv_share, qkv_full, sums = settle(
        feat_sq, d_norm, h_zero, d_one, node_in, modulation, grad_dec, gmod_two, grad_qkv, big_share,
        loss_part, groups,
    )
    grad_enc = small[: 2 * VARS]
    grad_dec = small[2 * VARS : 3 * VARS]
    grad_cond = noise_feat[:, None] * small[3 * VARS : 3 * VARS + 4].reshape(1, -1)
    layer_share = jnp.stack(
        [
            jnp.concatenate([qkv_share, big_share[:, 2 * width :]], 1),
            big_share[:, :width],
            big_share[:, width : 2 * width],
        ]
    )
    grad_norm = jnp.sqrt(sums[0, 0])
    loss_sum = sums[1, 0]
    clip_factor = clip_limit / jnp.maximum(grad_norm, clip_limit)
    clipped = clip_factor * layer_share
    big_full = lax.all_gather(big_share.astype(bf16), "node", axis=0, tiled=True)
    grad_full = jnp.stack(
        [
            jnp.concatenate([qkv_full.reshape(width, -1), big_full[:, 2 * width :]], 1),
            big_full[:, :width],
            big_full[:, width : 2 * width],
        ]
    )
    raw_stat = jnp.einsum("idb,idc->ibc", grad_full, grad_full, preferred_element_type=f32)
    stat_new = clip_factor * (clip_factor * raw_stat)
    basis_old = soap_basis[:, 0]
    rotated = jnp.einsum("idb,ibc->idc", clipped, basis_old, precision=highest)
    first_new = beta_first * soap_first + (1 - beta_first) * rotated
    second_new = beta_second * soap_second + (1 - beta_second) * rotated * rotated
    direction = (
        first_new
        / (1 - beta_first**STEP)
        / (jnp.sqrt(second_new / (1 - beta_second**STEP)) + adam_epsilon)
    )
    step_back = jnp.einsum("idc,ibc->idb", direction, basis_old, precision=highest)
    layer_new = layer_w - rate_layer * (step_back + decay_rate * layer_w)
    stats_new = beta_stats * soap_stats[:, 0] + (1 - beta_stats) * stat_new
    product = jnp.einsum("ibc,icd->ibd", stats_new, basis_old, precision=highest)
    gram_matrix = jnp.einsum("ibc,ibd->icd", product, product, precision=highest)
    basis_new = renew(gram_matrix, product)
    enc_new = adam_small(w_enc, clip_factor * grad_enc, enc_first, enc_second)
    cond_new = adam_small(w_cond, clip_factor * grad_cond, cond_first, cond_second)
    dec_new = adam_small(w_dec.T, clip_factor * grad_dec, dec_first.T, dec_second.T)
    return (
        jnp.reshape(loss_sum, (1,)),
        jnp.reshape(loss_count, (1,)),
        jnp.reshape(grad_norm, (1,)),
        layer_new,
        first_new,
        second_new,
        basis_new[:, None],
        stats_new[:, None],
        *enc_new,
        *cond_new,
        *(x.T for x in dec_new),
    )


def solution(mesh):
    pixel = P("node", None)
    layer = P(None, "node", "head")
    basis = P(None, "head", None, None)
    placed = (
        *(pixel,) * 3,
        P(),
        P("node"),
        P("node", None),
        P("node"),
        P("node"),
        P("node", None),
        *(P(),) * 3,
        *(layer,) * 3,
        *(basis,) * 2,
        *(P(),) * 6,
    )
    return jax.shard_map(
        local,
        mesh=mesh,
        in_specs=placed,
        out_specs=(*(P(),) * 3, *(layer,) * 3, *(basis,) * 2, *(P(),) * 9),
        check_vma=False,
    )
```

```python
import functools
import math

import jax
import jax.numpy as jnp
from jax import lax
from jax.experimental import pallas as pl
from jax.experimental.pallas import tpu as pltpu
from jax.sharding import PartitionSpec as P

HD = 128
VARS = 84
NF = 32
NBR = 16
LEVELS = 1000
STEP = 10

SLOT = 128
SLIM = 96
GROUP = 256 // NBR
BLOCK = 128
STRIP = 16

highest = lax.Precision.HIGHEST
clip_limit = 0.01
beta_first = 0.9
beta_second = 0.95
beta_stats = 0.95
adam_epsilon = 1e-08
rate_layer = 0.02
rate_small = 0.05
decay_rate = 0.1
norm_eps = 1e-05

f32 = jnp.float32
bf16 = jnp.bfloat16
MIB = 2**20


def passed_along(x, axis, by):
    length = lax.axis_size(axis)
    return lax.ppermute(x, axis, [(i, (i + by) % length) for i in range(length)])


def noise_terms(noise_level):
    level_frac = noise_level[0].astype(f32) / (LEVELS - 1)
    noise_sigma = 0.05 * jnp.exp(level_frac * math.log(40.0))
    frequency = 1.0 + jnp.arange(NF // 2).astype(f32)
    phase_angle = jnp.log(noise_sigma) * frequency
    return (noise_sigma, jnp.concatenate([jnp.sin(phase_angle), jnp.cos(phase_angle)]))


def standardize(values_in):
    row_mean = jnp.mean(values_in, -1, keepdims=True)
    centered = values_in - row_mean
    inv_std = lax.rsqrt(jnp.mean(centered * centered, -1, keepdims=True) + norm_eps)
    return (centered * inv_std, inv_std)


def norm_back(normed, inv_std, grad_in):
    return inv_std * (
        grad_in
        - jnp.mean(grad_in, -1, keepdims=True)
        - normed * jnp.mean(grad_in * normed, -1, keepdims=True)
    )


def contract(left, right, left_dim, right_dim, precision=None):
    return lax.dot_general(
        left,
        right,
        (((left_dim,), (right_dim,)), ((), ())),
        preferred_element_type=f32,
        precision=precision,
    )


def halves(x):
    high = x.astype(bf16)
    return high, (x - high.astype(f32)).astype(bf16)


def thirds(x):
    high = x.astype(bf16)
    rest = x - high.astype(f32)
    return (high, *halves(rest))


def fold_lanes(x, op=jnp.add):
    parts = [x[:, i : i + 128] for i in range(0, x.shape[1], 128)]
    while len(parts) > 1:
        parts = [op(*parts[i : i + 2]) if i + 1 < len(parts) else parts[i] for i in range(0, len(parts), 2)]
    return parts[0]


def adam_small(weight, grad_item, first, second):
    first_new = beta_first * first + (1 - beta_first) * grad_item
    second_new = beta_second * second + (1 - beta_second) * grad_item * grad_item
    ratio = (
        first_new
        / (1 - beta_first**STEP)
        / (jnp.sqrt(second_new / (1 - beta_second**STEP)) + adam_epsilon)
    )
    return (weight - rate_small * (ratio + decay_rate * weight), first_new, second_new)


def smem():
    return pl.BlockSpec(memory_space=pltpu.SMEM)


def whole(shape):
    zeros = (0,) * len(shape)
    return pl.BlockSpec(tuple(shape), lambda *_: zeros)


def params(mib=48):
    return pltpu.CompilerParams(vmem_limit_bytes=mib * MIB)


def remote(mib, identity):
    return pltpu.CompilerParams(
        vmem_limit_bytes=mib * MIB, collective_id=identity, has_side_effects=True
    )


def vmem():
    return pl.BlockSpec(memory_space=pltpu.VMEM)


def each(count, act, start=1):
    def body(off, carry):
        act(off)
        return carry

    lax.fori_loop(start, count, body, 0)


def meet(axes):
    barrier = pltpu.get_barrier_semaphore()
    total = 0
    for axis in axes:
        count, me = lax.axis_size(axis), lax.axis_index(axis)
        total += count - 1
        each(
            count,
            lambda off: pl.semaphore_signal(barrier, inc=1, device_id={axis: (me + off) % count}),
        )
    pl.semaphore_wait(barrier, total)


class Spread:
    def __init__(self, axis, source, target, sends, receives):
        self.axis, self.source, self.target = axis, source, target
        self.sends, self.receives = sends, receives
        self.count, self.me = lax.axis_size(axis), lax.axis_index(axis)

    def copy(self, other, slot):
        return pltpu.make_async_remote_copy(
            src_ref=self.source(other),
            dst_ref=self.target(slot),
            send_sem=self.sends.at[other],
            recv_sem=self.receives.at[slot],
            device_id={self.axis: other},
        )

    def other(self, off):
        return (self.me + off) % self.count

    def start(self, off):
        self.copy(self.other(off), self.me).start()

    def arrived(self, off):
        self.copy(self.other(off), self.other(off)).wait_recv()

    def sent(self, off):
        self.copy(self.other(off), self.me).wait_send()

    def all(self, act):
        each(self.count, getattr(self, act))


def encode_kernel(
    place_ref, scale_ref, node_ref, prev_ref, target_ref, eps_ref, w_ref, in_ref, stat_ref, all_ref, pix, box, sems
):
    step = pl.program_id(0)
    rows = in_ref.shape[0]
    tile = node_ref.shape[1]
    weights = Spread("node", lambda _: w_ref, lambda i: box.at[i], sems.at[0], sems.at[1])

    @pl.when(step == 0)
    def _():
        meet(["node"])
        weights.all("start")
        box[weights.me] = w_ref[...]
        pix[...] = jnp.zeros_like(pix)
        in_ref[...] = jnp.zeros_like(in_ref)
        stat_ref[...] = jnp.zeros_like(stat_ref)

    prev = prev_ref[...]
    target = target_ref[...]
    noisy = target + scale_ref[0] * eps_ref[...]
    pix[:VARS] = prev.astype(bf16)
    pix[SLOT : SLOT + VARS] = (scale_ref[1] * noisy).astype(bf16)
    node = node_ref[...] - place_ref[0]
    mine = node - place_ref[1]
    spot = lax.broadcasted_iota(jnp.int32, (rows, tile), 0)
    onehot = (spot == mine).astype(f32).astype(bf16)
    in_ref[...] += contract(onehot, pix[...], 1, 1)
    valid = (node < place_ref[2]).astype(f32)
    residual = target - prev
    stat_ref[:VARS] += fold_lanes(valid * residual * residual)
    stat_ref[SLIM - 1 : SLIM] += fold_lanes(valid)

    @pl.when(step == pl.num_programs(0) - 1)
    def _():
        weights.all("arrived")
        all_ref[...] = box[...]
        weights.all("sent")


def encode(place, scales, node_row, prev, target, eps, w_share, rows, tile, nodes):
    pixels = prev.shape[1]
    gathered = (nodes, *w_share.shape)
    pixel_block = pl.BlockSpec((VARS, tile), lambda i: (0, i))
    return pl.pallas_call(
        encode_kernel,
        grid=(pixels // tile,),
        in_specs=[smem(), smem(), pl.BlockSpec((1, tile), lambda i: (0, i))]
        + [pixel_block] * 3
        + [whole(w_share.shape)],
        out_specs=[whole((rows, 2 * SLOT)), whole((SLIM, 128)), whole(gathered)],
        out_shape=[
            jax.ShapeDtypeStruct((rows, 2 * SLOT), f32),
            jax.ShapeDtypeStruct((SLIM, 128), f32),
            jax.ShapeDtypeStruct(gathered, bf16),
        ],
        scratch_shapes=[
            pltpu.VMEM((2 * SLOT, tile), bf16),
            pltpu.VMEM(gathered, bf16),
            pltpu.SemaphoreType.DMA((2, nodes)),
        ],
        compiler_params=remote(48, 2),
        name="encode",
    )(place, scales, node_row, prev, target, eps, w_share)


def count_tile(slots, put, bands):
    lane = lax.broadcasted_iota(jnp.int32, (GROUP, 256), 1)
    sub = lax.broadcasted_iota(jnp.int32, (GROUP, 256), 0)
    own = lane // NBR == sub
    spot = lax.broadcasted_iota(jnp.int32, (256, 256), 0)
    for g in range(slots.shape[0]):
        row = slots[g : g + 1]
        band = jnp.where(own, row >> 8, -1)
        left = jnp.concatenate([(band == t).astype(f32).astype(bf16) for t in range(bands)], 0)
        right = (spot == (row & 255)).astype(f32).astype(bf16)
        found = contract(left, right, 1, 1).astype(bf16)
        for t in range(bands):
            put(g, t, found[t * GROUP : (t + 1) * GROUP])


def open_kernel(
    in_ref, wenc_ref, mod_ref, stat_ref, w_ref, slot_ref,
    zero_ref, norm_ref, q_ref, here_ref, below_ref, above_ref, sum_ref, count_ref,
    norm_box, stat_own, stat_box, kv, low_box, high_box, tiles, head_sems, stat_sems, halo_sems, out_sems,
):
    heads, rows, _ = norm_box.shape
    head, node = lax.axis_index("head"), lax.axis_index("node")
    nodes = lax.axis_size("node")
    depth = tiles.shape[1]
    steps = count_ref.shape[0] // depth
    stat_own[...] = jnp.broadcast_to(
        jnp.sum(stat_ref[...], 1, keepdims=True), stat_own.shape
    )
    meet(["head", "node"])

    stats = Spread("node", lambda _: stat_own, lambda i: stat_box.at[i], stat_sems.at[0], stat_sems.at[1])
    stats.all("start")
    w_enc = wenc_ref[...]
    h_zero = sum(contract(part, w_enc, 1, 0) for part in thirds(in_ref[...]))
    zero_ref[...] = h_zero
    normed, _ = standardize(h_zero)
    norm_box[head] = (normed * (1 + mod_ref[0:1]) + mod_ref[1:2]).astype(bf16)
    norms = Spread(
        "head", lambda _: norm_box.at[head], lambda i: norm_box.at[i], head_sems.at[0], head_sems.at[1]
    )
    norms.all("start")

    def halo(block):
        return [
            pltpu.make_async_remote_copy(
                src_ref=kv.at[block],
                dst_ref=box.at[block],
                send_sem=halo_sems.at[2 * side, block],
                recv_sem=halo_sems.at[2 * side + 1, block],
                device_id={"node": (node + by) % nodes},
            )
            for side, (box, by) in enumerate(((low_box, 1), (high_box, nodes - 1)))
        ]

    def project(block):
        out = contract(norm_box[block], w_ref[:, : 3 * HD], 1, 0).astype(bf16)
        q_ref[block] = out[:, :HD]
        kv[block] = out[:, HD:]
        for copy in halo(block):
            copy.start()

    def count(step):
        slot = step % 2

        @pl.when(step >= 2)
        def _():
            count_out(step - 2).wait()

        per = depth // GROUP
        slots = slot_ref[pl.ds(pl.multiple_of(step * per, per), per)]

        def put(g, t, found):
            tiles[slot, g * GROUP : (g + 1) * GROUP, t * 256 : (t + 1) * 256] = found

        count_tile(slots, put, tiles.shape[2] // 256)
        count_out(step).start()

    def count_out(step):
        return pltpu.make_async_copy(
            tiles.at[step % 2],
            count_ref.at[pl.ds(pl.multiple_of(step * depth, depth), depth)],
            out_sems.at[step % 2],
        )

    project(head)
    each(steps // 2, count, 0)

    def next_block(off):
        norms.arrived(off)
        project(norms.other(off))

    each(heads, next_block)
    norm_ref[...] = norm_box[...]
    here_ref[...] = kv[...]
    each(steps, count, steps // 2)
    each(steps, lambda step: count_out(step).wait(), steps - 2)
    stats.all("arrived")
    sum_ref[...] = sum(jnp.where(t == node, stat_own[...], stat_box[t]) for t in range(nodes))

    def finish(block):
        for copy in halo(block):
            copy.wait()

    each(heads, finish, 0)
    below_ref[...] = low_box[...]
    above_ref[...] = high_box[...]
    norms.all("sent")
    stats.all("sent")


def open_nodes(node_in, w_enc, modulation, stat, w_attn, slots, heads, groups, reach):
    rows, width = node_in.shape[0], w_enc.shape[1]
    depth = 8 * GROUP
    block = lambda w: jax.ShapeDtypeStruct((heads, rows, w), bf16)
    return pl.pallas_call(
        open_kernel,
        in_specs=[vmem()] * 6,
        out_specs=[vmem()] * 7 + [pl.BlockSpec(memory_space=pl.ANY)],
        out_shape=[
            jax.ShapeDtypeStruct((rows, width), f32),
            block(width),
            block(HD),
            block(2 * HD),
            block(2 * HD),
            block(2 * HD),
            jax.ShapeDtypeStruct((SLIM, 128), f32),
            jax.ShapeDtypeStruct((heads * rows, reach), bf16),
        ],
        scratch_shapes=[
            pltpu.VMEM((heads, rows, width), bf16),
            pltpu.VMEM((SLIM, 128), f32),
            pltpu.VMEM((groups, SLIM, 128), f32),
            pltpu.VMEM((heads, rows, 2 * HD), bf16),
            pltpu.VMEM((heads, rows, 2 * HD), bf16),
            pltpu.VMEM((heads, rows, 2 * HD), bf16),
            pltpu.VMEM((2, depth, reach), bf16),
            pltpu.SemaphoreType.DMA((2, heads)),
            pltpu.SemaphoreType.DMA((2, groups)),
            pltpu.SemaphoreType.DMA((4, heads)),
            pltpu.SemaphoreType.DMA((2,)),
        ],
        compiler_params=remote(56, 3),
        name="open_nodes",
    )(node_in, w_enc, modulation, stat, w_attn, slots)


def attend_kernel(
    q_ref, below_ref, here_ref, above_ref, count_ref, e_ref, mix_ref, out_ref, s_scr, own, box, sems, chunk
):
    step = pl.program_id(0)
    steps = pl.num_programs(0)
    head = lax.axis_index("head")
    tile = q_ref.shape[0]
    per = box.shape[1] // tile

    def copy(target, source, part):
        at = pl.ds(pl.multiple_of(part * tile, tile), tile)
        return pltpu.make_async_remote_copy(
            src_ref=own.at[target, at],
            dst_ref=box.at[source, at],
            send_sem=sems.at[0, target, part],
            recv_sem=sems.at[1, source, part],
            device_id={"head": target},
        )

    @pl.when(step == 0)
    def _():
        meet(["head"])

    nodes = here_ref.shape[0]
    q = q_ref[...]
    top = jnp.full((tile, 128), -1e30, f32)
    for b, kv_ref in enumerate((below_ref, here_ref, above_ref)):
        for at in range(0, nodes, chunk):
            cols = slice(b * nodes + at, b * nodes + at + chunk)
            s = contract(q, kv_ref[at : at + chunk, :HD], 1, 1)
            s = jnp.where(count_ref[:, cols].astype(f32) > 0, s, -1e30)
            s_scr[:, cols] = s
            top = jnp.maximum(top, fold_lanes(s, jnp.maximum))
    top = jnp.max(top, 1, keepdims=True)
    factor = math.log2(math.e) / math.sqrt(HD)
    total = jnp.zeros((tile, 128), f32)
    mixed = jnp.zeros((tile, HD), f32)
    for b, kv_ref in enumerate((below_ref, here_ref, above_ref)):
        for at in range(0, nodes, chunk):
            cols = slice(b * nodes + at, b * nodes + at + chunk)
            e = count_ref[:, cols].astype(f32) * jnp.exp2((s_scr[:, cols] - top) * factor)
            total += fold_lanes(e)
            e = e.astype(bf16)
            e_ref[:, cols] = e
            mixed += contract(e, kv_ref[at : at + chunk, HD:], 1, 0)
    inverse = 1.0 / jnp.sum(total, 1, keepdims=True)
    mixed = mixed * inverse
    mix_ref[:, :HD] = mixed
    mix_ref[:, HD:] = jnp.broadcast_to(inverse, (tile, HD))
    target, part = step // per, step % per
    at = pl.ds(pl.multiple_of(part * tile, tile), tile)
    low = mixed.astype(bf16)
    own[target, at] = low

    @pl.when(target == head)
    def _():
        box[head, at] = low

    @pl.when(target != head)
    def _():
        copy(target, head, part).start()

    @pl.when(step == steps - 1)
    def _():
        heads = box.shape[0]

        def finish(off):
            other = (head + off) % heads
            for p in range(per):
                copy(other, other, p).wait_recv()
                copy(other, head, p).wait_send()

        each(heads, finish)
        out_ref[...] = box[...]


def attend(query, below, here, above, counts, heads, tile, chunk):
    nodes, reach = counts.shape
    rows = nodes // heads
    row = lambda width: pl.BlockSpec((tile, width), lambda i: (i, 0))
    return pl.pallas_call(
        functools.partial(attend_kernel, chunk=chunk),
        grid=(nodes // tile,),
        in_specs=[row(HD)] + [whole((nodes, 2 * HD))] * 3 + [row(reach)],
        out_specs=[row(reach), row(2 * HD), whole((heads, rows, HD))],
        out_shape=[
            jax.ShapeDtypeStruct((nodes, reach), bf16),
            jax.ShapeDtypeStruct((nodes, 2 * HD), f32),
            jax.ShapeDtypeStruct((heads, rows, HD), bf16),
        ],
        scratch_shapes=[
            pltpu.VMEM((tile, reach), f32),
            pltpu.VMEM((heads, rows, HD), bf16),
            pltpu.VMEM((heads, rows, HD), bf16),
            pltpu.SemaphoreType.DMA((2, heads, rows // tile)),
        ],
        compiler_params=remote(60, 4),
        name="attend",
    )(query, below, here, above, counts)


def attend_back_kernel(
    q_ref, d_ref, mix_ref, e_ref, below_ref, here_ref, above_ref, dq_ref, low_ref, self_ref, high_ref, dk, dv, chunk
):
    step = pl.program_id(0)
    tile = q_ref.shape[0]
    nodes = here_ref.shape[0]

    @pl.when(step == 0)
    def _():
        dk[...] = jnp.zeros_like(dk)
        dv[...] = jnp.zeros_like(dv)

    grad = d_ref[...]
    wide = grad.astype(f32)
    inverse = mix_ref[:, HD : HD + 1]
    delta = jnp.sum(wide * mix_ref[:, :HD], 1, keepdims=True)
    gain = inverse * (1.0 / math.sqrt(HD))
    q_turned = q_ref[...].T
    d_turned = (wide * inverse).astype(bf16).T
    dq = jnp.zeros((tile, HD), f32)
    for b, kv_ref in enumerate((below_ref, here_ref, above_ref)):
        for at in range(0, nodes, chunk):
            cols = slice(b * nodes + at, b * nodes + at + chunk)
            key = kv_ref[at : at + chunk, :HD]
            dp = contract(grad, kv_ref[at : at + chunk, HD:], 1, 1)
            e = e_ref[:, cols]
            ds = (e.astype(f32) * ((dp - delta) * gain)).astype(bf16)
            dq += contract(ds, key, 1, 0)
            dk[:, cols] += contract(q_turned, ds, 1, 0)
            dv[:, cols] += contract(d_turned, e, 1, 0)
    dq_ref[...] = dq.astype(bf16)

    @pl.when(step == pl.num_programs(0) - 1)
    def _():
        for b, ref in enumerate((low_ref, self_ref, high_ref)):
            cols = slice(b * nodes, (b + 1) * nodes)
            ref[:HD] = dk[:, cols].astype(ref.dtype)
            ref[HD:] = dv[:, cols].astype(ref.dtype)


def attend_back(query, grad, mix, e, below, here, above, tile, chunk):
    nodes, reach = e.shape
    row = lambda width: pl.BlockSpec((tile, width), lambda i: (i, 0))
    return pl.pallas_call(
        functools.partial(attend_back_kernel, chunk=chunk),
        grid=(nodes // tile,),
        in_specs=[row(HD), row(HD), row(2 * HD), row(reach)] + [whole((nodes, 2 * HD))] * 3,
        out_specs=[row(HD)] + [whole((2 * HD, nodes))] * 3,
        out_shape=[
            jax.ShapeDtypeStruct((nodes, HD), bf16),
            jax.ShapeDtypeStruct((2 * HD, nodes), bf16),
            jax.ShapeDtypeStruct((2 * HD, nodes), f32),
            jax.ShapeDtypeStruct((2 * HD, nodes), bf16),
        ],
        scratch_shapes=[pltpu.VMEM((HD, reach), f32)] * 2,
        compiler_params=params(60),
        name="attend_back",
    )(query, grad, mix, e, below, here, above)


def forward_kernel(mixed_ref, zero_ref, w_ref, mod_ref, wdec_ref, one_ref, two_ref, norm_ref, up_ref, act_ref, dec_ref):
    heads, width = w_ref.shape[0], w_ref.shape[1]
    h_one = zero_ref[...] + sum(
        contract(mixed_ref[h], w_ref[h, :, 2 * width :], 1, 1) for h in range(heads)
    )
    one_ref[...] = h_one
    normed, _ = standardize(h_one)
    norm_two = (normed * (1 + mod_ref[2:3]) + mod_ref[3:4]).astype(bf16)
    norm_ref[...] = norm_two
    h_two = h_one
    for h in range(heads):
        up = contract(norm_two, w_ref[h, :, :width], 1, 0)
        up_ref[h] = up
        act = (up * jax.nn.sigmoid(up)).astype(bf16)
        act_ref[h] = act
        h_two = h_two + contract(act, w_ref[h, :, width : 2 * width], 1, 1)
    two_ref[...] = h_two
    final = standardize(h_two)[0].astype(bf16)
    high, low = halves(contract(wdec_ref[...], final, 1, 1))
    dec_ref[:SLIM] = high
    dec_ref[SLIM:] = low


def forward(mixed, h_zero, w_big, modulation, w_dec, tile):
    heads, rows = mixed.shape[:2]
    width = h_zero.shape[1]
    row = pl.BlockSpec((tile, width), lambda i: (i, 0))
    stack = lambda w: pl.BlockSpec((heads, tile, w), lambda i: (0, i, 0))
    return pl.pallas_call(
        forward_kernel,
        grid=(rows // tile,),
        in_specs=[stack(HD), row, whole(w_big.shape), whole(modulation.shape), whole(w_dec.shape)],
        out_specs=[row, row, row, stack(width), stack(width), pl.BlockSpec((2 * SLIM, tile), lambda i: (0, i))],
        out_shape=[
            jax.ShapeDtypeStruct((rows, width), f32),
            jax.ShapeDtypeStruct((rows, width), f32),
            jax.ShapeDtypeStruct((rows, width), bf16),
            jax.ShapeDtypeStruct((heads, rows, width), f32),
            jax.ShapeDtypeStruct((heads, rows, width), bf16),
            jax.ShapeDtypeStruct((2 * SLIM, rows), bf16),
        ],
        compiler_params=params(),
        name="forward",
    )(mixed, h_zero, w_big, modulation, w_dec)


def pixel_kernel(place_ref, scale_ref, node_ref, read_ref, target_ref, eps_ref, weight_ref, dec_ref, loss_ref, d_ref, hits, turned, total):
    step = pl.program_id(0)
    heads, _, rows = dec_ref.shape
    tile = target_ref.shape[1]

    @pl.when(step == 0)
    def _():
        turned[...] = jnp.zeros_like(turned)
        total[...] = jnp.zeros_like(total)
        loss_ref[...] = jnp.zeros_like(loss_ref)

    reads = read_ref[...] - place_ref[0]
    field = jnp.zeros((2 * SLIM, tile), f32)
    for h in range(heads):
        spot = lax.broadcasted_iota(jnp.int32, (rows, tile), 0) + h * rows
        hit = sum((spot == reads[k : k + 1]).astype(f32) for k in range(3)).astype(bf16)
        hits[h * rows : (h + 1) * rows] = hit
        field += contract(dec_ref[h], hit, 1, 0)
    field = (field[:VARS] + field[SLIM : SLIM + VARS]) / 3.0
    target = target_ref[...]
    noisy = target + scale_ref[0] * eps_ref[...]
    error = scale_ref[2] * noisy + scale_ref[3] * field - target
    valid = (node_ref[...] - place_ref[0] < place_ref[2]).astype(f32)
    weighted = valid * weight_ref[:, 0:1]
    loss_ref[:VARS] += fold_lanes(weighted * error * error)
    high, low = halves(scale_ref[4] * weighted * error)
    turned[:VARS] = high
    turned[SLOT : SLOT + VARS] = low
    total[...] += contract(hits[...], turned[...], 1, 1)

    @pl.when(step == pl.num_programs(0) - 1)
    def _():
        d_ref[...] = total[:, :SLOT] + total[:, SLOT:]


def pixels_back(place, scales, node_row, read_rows, target, eps, weight, decoded, tile):
    heads, _, rows = decoded.shape
    count = target.shape[1] // heads
    steps = count // tile
    at = lambda i, place: (0, place[3] * steps + i)
    fixed = lambda shape: pl.BlockSpec(tuple(shape), lambda i, place: (0,) * len(shape))
    return pl.pallas_call(
        pixel_kernel,
        grid_spec=pltpu.PrefetchScalarGridSpec(
            num_scalar_prefetch=1,
            grid=(steps,),
            in_specs=[
                smem(),
                pl.BlockSpec((1, tile), at),
                pl.BlockSpec((3, tile), at),
                pl.BlockSpec((VARS, tile), at),
                pl.BlockSpec((VARS, tile), at),
                fixed(weight.shape),
                fixed(decoded.shape),
            ],
            out_specs=[fixed((SLIM, 128)), fixed((heads * rows, SLOT))],
            scratch_shapes=[
                pltpu.VMEM((heads * rows, tile), bf16),
                pltpu.VMEM((2 * SLOT, tile), bf16),
                pltpu.VMEM((heads * rows, 2 * SLOT), f32),
            ],
        ),
        out_shape=[
            jax.ShapeDtypeStruct((SLIM, 128), f32),
            jax.ShapeDtypeStruct((heads * rows, SLOT), f32),
        ],
        compiler_params=params(),
        name="pixels_back",
    )(place, scales, node_row, read_rows, target, eps, weight, decoded)


def backward_kernel(
    d_ref, two_ref, one_ref, norm_ref, up_ref, act_ref, mixed_ref, w_ref, mod_ref, wdec_ref,
    done_ref, dmix_ref, grad_ref, gdec_ref, gmod_ref,
):
    heads, width = w_ref.shape[0], w_ref.shape[1]
    step = pl.program_id(0)

    @pl.when(step == 0)
    def _():
        grad_ref[...] = jnp.zeros_like(grad_ref)
        gdec_ref[...] = jnp.zeros_like(gdec_ref)
        gmod_ref[...] = jnp.zeros_like(gmod_ref)

    d_dec = sum(d_ref[h] for h in range(heads)).astype(bf16)
    normed_two, inv_two = standardize(two_ref[...])
    final = normed_two.astype(bf16)
    gdec_ref[...] += contract(d_dec[:, :SLIM], final, 0, 0)
    d_two = norm_back(normed_two, inv_two, contract(d_dec[:, :SLIM], wdec_ref[...], 1, 0))
    d_low = d_two.astype(bf16)
    norm_two = norm_ref[...]
    d_mid = jnp.zeros_like(d_two)
    for h in range(heads):
        act = act_ref[h]
        up = up_ref[h]
        d_act = contract(d_low, w_ref[h, :, width : 2 * width], 1, 0)
        gating = jax.nn.sigmoid(up)
        d_up = (d_act * gating * (1 + up * (1 - gating))).astype(bf16)
        grad_ref[h, :, :width] += contract(norm_two, d_up, 0, 0)
        grad_ref[h, :, width : 2 * width] += contract(d_low, act, 0, 0)
        d_mid += contract(d_up, w_ref[h, :, :width], 1, 1)
    normed_one, inv_one = standardize(one_ref[...])
    gmod_ref[0:1] += jnp.sum(d_mid * normed_one, 0, keepdims=True)
    gmod_ref[1:2] += jnp.sum(d_mid, 0, keepdims=True)
    d_one = d_two + norm_back(normed_one, inv_one, d_mid * (1 + mod_ref[2:3]))
    done_ref[...] = d_one
    one_low = d_one.astype(bf16)
    for h in range(heads):
        dmix_ref[h] = contract(one_low, w_ref[h, :, 2 * width :], 1, 0).astype(bf16)
        grad_ref[h, :, 2 * width :] += contract(one_low, mixed_ref[h], 0, 0)


def backward(d_dec, h_two, h_one, norm_two, up, act, mixed, w_big, modulation, w_dec, tile):
    heads, rows = mixed.shape[:2]
    width = h_one.shape[1]
    row = lambda w: pl.BlockSpec((tile, w), lambda i: (i, 0))
    stack = lambda w: pl.BlockSpec((heads, tile, w), lambda i: (0, i, 0))
    return pl.pallas_call(
        backward_kernel,
        grid=(rows // tile,),
        in_specs=[
            stack(SLOT),
            row(width),
            row(width),
            row(width),
            stack(width),
            stack(width),
            stack(HD),
            whole(w_big.shape),
            whole(modulation.shape),
            whole(w_dec.shape),
        ],
        out_specs=[row(width), stack(HD), whole(w_big.shape), whole((SLIM, width)), whole((8, width))],
        out_shape=[
            jax.ShapeDtypeStruct((rows, width), f32),
            jax.ShapeDtypeStruct((heads, rows, HD), bf16),
            jax.ShapeDtypeStruct(w_big.shape, f32),
            jax.ShapeDtypeStruct((SLIM, width), f32),
            jax.ShapeDtypeStruct((8, width), f32),
        ],
        compiler_params=params(56),
        name="backward",
    )(d_dec, h_two, h_one, norm_two, up, act, mixed, w_big, modulation, w_dec)


def unproject_kernel(dq_ref, self_ref, down_ref, up_ref, norm_ref, w_ref, dn_ref, grad_ref):
    step = pl.program_id(0)

    @pl.when(step == 0)
    def _():
        grad_ref[...] = jnp.zeros_like(grad_ref)

    kv = self_ref[...] + down_ref[...].astype(f32) + up_ref[...].astype(f32)
    both = jnp.concatenate([dq_ref[...], kv.astype(bf16).T], 1)
    dn_ref[...] = contract(both, w_ref[...], 1, 1).astype(bf16)
    grad_ref[...] += contract(norm_ref[...], both, 0, 0)


def unproject(dq, kv_self, from_below, from_above, norm_all, w_attn, tile):
    nodes, width = norm_all.shape
    row = lambda w: pl.BlockSpec((tile, w), lambda i: (i, 0))
    col = pl.BlockSpec((2 * HD, tile), lambda i: (0, i))
    return pl.pallas_call(
        unproject_kernel,
        grid=(nodes // tile,),
        in_specs=[row(HD), col, col, col, row(width), pl.BlockSpec((width, 3 * HD), lambda i: (0, 0))],
        out_specs=[row(width), whole((width, 3 * HD))],
        out_shape=[
            jax.ShapeDtypeStruct((nodes, width), bf16),
            jax.ShapeDtypeStruct((width, 3 * HD), f32),
        ],
        compiler_params=params(),
        name="unproject",
    )(dq, kv_self, from_below, from_above, norm_all, w_attn)


def settle_kernel(
    feat_ref, dn_ref, zero_ref, done_ref, in_ref, mod_ref, gdec_ref, gmod_ref, qkv_ref, big_ref, loss_ref,
    small_ref, share_ref, full_ref, sums_ref,
    parts, spread, inbox, pay, heard, q_low, q_box, sems,
):
    heads = dn_ref.shape[0]
    nodes = q_low.shape[0]
    world = inbox.shape[0]
    head, node = lax.axis_index("head"), lax.axis_index("node")
    me = head * nodes + node
    share_rows = share_ref.shape[0]
    a_send, a_recv, q_send, q_recv, b_send, b_recv, f_send, f_recv = (sems.at[i] for i in range(8))

    def where(other):
        return {"head": other // nodes, "node": other % nodes}

    barrier = pltpu.get_barrier_semaphore()

    def greet(off, carry):
        pl.semaphore_signal(barrier, inc=1, device_id=where((me + off) % world))
        return carry

    lax.fori_loop(1, world, greet, 0)
    for t in range(nodes):
        q_low[t] = qkv_ref[t * share_rows : (t + 1) * share_rows].astype(bf16)
    pl.semaphore_wait(barrier, world - 1)

    def q_copy(off):
        other = (node + off) % nodes
        return pltpu.make_async_remote_copy(
            src_ref=q_low.at[other],
            dst_ref=q_box.at[node],
            send_sem=q_send.at[other],
            recv_sem=q_recv.at[node],
            device_id={"node": other},
        )

    def q_arrived(off):
        other = (node + off) % nodes
        return pltpu.make_async_remote_copy(
            src_ref=q_low.at[other],
            dst_ref=q_box.at[other],
            send_sem=q_send.at[other],
            recv_sem=q_recv.at[other],
            device_id={"node": other},
        )

    def each(count, act):
        def body(off, carry):
            act(off)
            return carry

        lax.fori_loop(1, count, body, 0)

    each(nodes, lambda off: q_copy(off).start())

    d_norm = sum(dn_ref[h].astype(f32) for h in range(heads))
    normed, inv = standardize(zero_ref[...])
    d_zero = done_ref[...] + norm_back(normed, inv, d_norm * (1 + mod_ref[0:1]))
    g_enc = contract(in_ref[...].T, d_zero, 1, 0, highest)
    parts[...] = jnp.zeros_like(parts)
    parts[:VARS] = g_enc[:VARS]
    parts[VARS : 2 * VARS] = g_enc[SLOT : SLOT + VARS]
    parts[2 * VARS : 3 * VARS] = gdec_ref[:VARS]
    at = 3 * VARS
    parts[at : at + 1] = jnp.sum(d_norm * normed, 0, keepdims=True)
    parts[at + 1 : at + 2] = jnp.sum(d_norm, 0, keepdims=True)
    parts[at + 2 : at + 4] = gmod_ref[0:2]
    for t in range(world):
        spread[t] = parts[8 * t : 8 * t + 8]

    def a_copy(off, slot):
        other = (me + off) % world
        return pltpu.make_async_remote_copy(
            src_ref=spread.at[other],
            dst_ref=inbox.at[slot(other)],
            send_sem=a_send.at[other],
            recv_sem=a_recv.at[slot(other)],
            device_id=where(other),
        )

    def b_copy(off, slot):
        other = (me + off) % world
        return pltpu.make_async_remote_copy(
            src_ref=pay,
            dst_ref=heard.at[slot(other)],
            send_sem=b_send.at[other],
            recv_sem=b_recv.at[slot(other)],
            device_id=where(other),
        )

    mine = lambda other: me
    theirs = lambda other: other
    each(world, lambda off: a_copy(off, mine).start())

    each(nodes, lambda off: q_arrived(off).wait_recv())
    q_box[node] = q_low[node]
    share = sum(q_box[t].astype(f32) for t in range(nodes))
    share_ref[...] = share
    each(nodes, lambda off: q_copy(off).wait_send())
    q_low[0] = share.astype(bf16)

    def f_copy(off, slot):
        other = (node + off) % nodes
        return pltpu.make_async_remote_copy(
            src_ref=q_low.at[0],
            dst_ref=full_ref.at[slot(other)],
            send_sem=f_send.at[other],
            recv_sem=f_recv.at[slot(other)],
            device_id={"node": other},
        )

    each(nodes, lambda off: f_copy(off, lambda other: node).start())
    full_ref[node] = share.astype(bf16)

    each(world, lambda off: a_copy(off, theirs).wait_recv())
    inbox[me] = spread[me]
    own = sum(inbox[t] for t in range(world))
    row = lax.broadcasted_iota(jnp.int32, own.shape, 0) + 8 * me
    weighted = own * own * jnp.where(row >= 3 * VARS, feat_ref[0], 1.0)
    total = jnp.sum(weighted) + jnp.sum(share * share) + jnp.sum(big_ref[...] * big_ref[...])
    loss = jnp.sum(loss_ref[:VARS])
    width = own.shape[1]
    pay[:, :width] = own
    line = lax.broadcasted_iota(jnp.int32, (8, 128), 0)
    pay[:, width:] = jnp.where(line == 0, total, jnp.where(line == 1, loss, 0.0))
    each(world, lambda off: b_copy(off, mine).start())
    heard[me] = pay[...]
    each(world, lambda off: b_copy(off, theirs).wait_recv())
    for t in range(world):
        small_ref[8 * t : 8 * t + 8] = heard[t, :, :width]
    sums_ref[...] = sum(heard[t, :, width:] for t in range(world))
    each(nodes, lambda off: f_copy(off, lambda other: other).wait_recv())
    each(world, lambda off: a_copy(off, mine).wait_send())
    each(world, lambda off: b_copy(off, mine).wait_send())
    each(nodes, lambda off: f_copy(off, lambda other: node).wait_send())


def settle(feat_sq, d_norm, h_zero, d_one, node_in, modulation, grad_dec, gmod_two, grad_qkv, big_share, loss, nodes):
    heads, rows, width = d_norm.shape
    world = heads * nodes
    share = (grad_qkv.shape[0] // nodes, grad_qkv.shape[1])
    return pl.pallas_call(
        settle_kernel,
        in_specs=[smem()] + [pl.BlockSpec(memory_space=pltpu.VMEM)] * 10,
        out_specs=[pl.BlockSpec(memory_space=pltpu.VMEM)] * 4,
        out_shape=[
            jax.ShapeDtypeStruct((8 * world, width), f32),
            jax.ShapeDtypeStruct(share, f32),
            jax.ShapeDtypeStruct((nodes, *share), bf16),
            jax.ShapeDtypeStruct((8, 128), f32),
        ],
        scratch_shapes=[
            pltpu.VMEM((8 * world, width), f32),
            pltpu.VMEM((world, 8, width), f32),
            pltpu.VMEM((world, 8, width), f32),
            pltpu.VMEM((8, width + 128), f32),
            pltpu.VMEM((world, 8, width + 128), f32),
            pltpu.VMEM((nodes, *share), bf16),
            pltpu.VMEM((nodes, *share), bf16),
            pltpu.SemaphoreType.DMA((8, world)),
        ],
        compiler_params=pltpu.CompilerParams(
            vmem_limit_bytes=48 * MIB, collective_id=1, has_side_effects=True
        ),
        name="settle",
    )(feat_sq, d_norm, h_zero, d_one, node_in, modulation, grad_dec, gmod_two, grad_qkv, big_share, loss)


def eliminate(work, done):
    count = work.shape[0]
    lane = lax.broadcasted_iota(jnp.int32, (1, BLOCK), 1)
    sub = lax.broadcasted_iota(jnp.int32, (STRIP, BLOCK), 0)
    pivots = [jnp.ones((1, BLOCK), f32) for _ in range(count)]
    both = lambda x: jnp.concatenate([x, x], 1)
    for at in range(0, BLOCK, STRIP):
        strip = slice(at, at + STRIP)
        rows = [work[m, strip] for m in range(count)]
        columns = [
            [jnp.broadcast_to(rows[m][:, at + k : at + k + 1], (STRIP, BLOCK)) for k in range(STRIP)]
            for m in range(count)
        ]
        scale = [jnp.ones((STRIP, BLOCK), f32) for _ in range(count)]
        for r in range(STRIP):
            for m in range(count):
                column = columns[m][r]
                pivot = jnp.broadcast_to(column[r : r + 1], (STRIP, BLOCK))
                factor = jnp.where(sub > r, column * (1.0 / pivot), 0.0)
                scale[m] = jnp.where(sub == r, pivot, scale[m])
                for k in range(r + 1, STRIP):
                    columns[m][k] = columns[m][k] - factor * columns[m][k][r : r + 1]
                pivots[m] = jnp.where(lane == at + r, pivot[:1], pivots[m])
                rows[m] = rows[m] - both(factor) * rows[m][r : r + 1]
        for m in range(count):
            done[m, strip] = rows[m][:, BLOCK:]
            if at + STRIP < BLOCK:
                high, mid, low = thirds(rows[m] * both(lax.rsqrt(scale[m])))
                left = jnp.concatenate([high, high, mid, mid, high, low], 0)[:, :BLOCK]
                right = jnp.concatenate([high, mid, high, mid, low, high], 0)
                rest = slice(at + STRIP, BLOCK)
                work[m, rest] -= contract(left, right, 0, 0)[rest]
    return pivots


def renew_kernel(gram_ref, product_ref, out_ref, gram, both, work, done):
    count, size = gram_ref.shape[:2]
    k = pl.program_id(0)

    @pl.when(k == 0)
    def _():
        gram[...] = gram_ref[...]
        both[...] = product_ref[...]

    at = pl.ds(pl.multiple_of(k * BLOCK, BLOCK), BLOCK)
    unit = lax.broadcasted_iota(jnp.int32, (BLOCK, BLOCK), 0) == lax.broadcasted_iota(
        jnp.int32, (BLOCK, BLOCK), 1
    )
    for m in range(count):
        work[m, :, :BLOCK] = gram[m, at, at]
        work[m, :, BLOCK:] = unit.astype(f32)
    roots = [lax.rsqrt(p) for p in eliminate(work, done)]
    for step in range(size // BLOCK):

        @pl.when(k == step)
        def _(here=slice(step * BLOCK, (step + 1) * BLOCK), rest=(step + 1) * BLOCK):
            for m in range(count):
                factor = done[m]
                panel = contract(both[m, :, here], factor, 1, 1, highest) * roots[m]
                out_ref[m] = panel
                if rest < size:
                    left = contract(gram[m, rest:, here], factor, 1, 1, highest) * roots[m]
                    both[m, :, rest:] -= contract(panel, left, 1, 1, highest)
                    gram[m, rest:, rest:] -= contract(left, left, 1, 1, highest)


def renew(gram, product):
    count, size = gram.shape[:2]
    return pl.pallas_call(
        renew_kernel,
        grid=(size // BLOCK,),
        in_specs=[whole(gram.shape), whole(gram.shape)],
        out_specs=pl.BlockSpec((count, size, BLOCK), lambda k: (0, 0, k)),
        out_shape=jax.ShapeDtypeStruct(gram.shape, f32),
        scratch_shapes=[
            pltpu.VMEM((count, size, size), f32),
            pltpu.VMEM((count, size, size), f32),
            pltpu.VMEM((count, BLOCK, 2 * BLOCK), f32),
            pltpu.VMEM((count, BLOCK, BLOCK), f32),
        ],
        compiler_params=params(),
        name="renew",
    )(gram, product)


def local(
    prev_state,
    target,
    noise_eps,
    noise_level,
    valid_count,
    neighbours,
    nbr_count,
    pix_node,
    pix_read,
    w_enc,
    w_cond,
    w_dec,
    layer_w,
    soap_first,
    soap_second,
    soap_basis,
    soap_stats,
    enc_first,
    enc_second,
    cond_first,
    cond_second,
    dec_first,
    dec_second,
):
    nodes = nbr_count.shape[0]
    groups = lax.axis_size("node")
    heads = lax.axis_size("head")
    rows = nodes // heads
    reach = 3 * nodes
    block_start = lax.axis_index("node") * nodes
    quarter = lax.axis_index("head")
    width = w_enc.shape[1]
    both = ("head", "node")

    low_w = layer_w.astype(bf16)
    big_share = jnp.concatenate([low_w[1], low_w[2], low_w[0, :, 3 * HD :]], 1)
    w_big = lax.all_gather(big_share, both, axis=0, tiled=True).reshape(heads, width, -1)

    noise_sigma, noise_feat = noise_terms(noise_level)
    sig_sq = noise_sigma * noise_sigma
    input_scale = lax.rsqrt(sig_sq + 1.0)
    skip_scale = 1.0 / (sig_sq + 1.0)
    output_scale = noise_sigma * lax.rsqrt(sig_sq + 1.0)
    loss_scale = (sig_sq + 1.0) / sig_sq
    modulation = jnp.dot(noise_feat[None, :], w_cond, precision=highest).reshape(4, width)

    prev_t, target_t, eps_t = prev_state.T, target.T, noise_eps.T
    node_row = pix_node.reshape(1, -1)
    read_rows = pix_read.T
    place = jnp.stack([block_start, quarter * rows, valid_count[0], quarter]).astype(jnp.int32)
    node_in, stat, w_attn = encode(
        place, jnp.stack([noise_sigma, input_scale]), node_row, prev_t, target_t, eps_t, low_w[0], rows, 1024, groups
    )
    w_attn = w_attn.reshape(width, -1)

    relative = (neighbours - block_start + nodes) % (nodes * groups)
    live = jnp.arange(NBR)[None, :] < nbr_count[:, None]
    slots = jnp.where(live, relative, -1).reshape(nodes // GROUP, 256)
    pad_enc = jnp.zeros((2, SLOT, width), bf16)
    pad_enc = pad_enc.at[:, :VARS].set(w_enc.astype(bf16).reshape(2, VARS, width))
    h_zero, norm_all, query, keyval, below, above, stat, counts = open_nodes(
        node_in, pad_enc.reshape(2 * SLOT, width), modulation, stat, w_attn, slots, heads, groups, reach
    )
    norm_all, query, keyval, below, above = (
        x.reshape(nodes, -1) for x in (norm_all, query, keyval, below, above)
    )
    stat_sum = stat[:, 0]
    count_sum = stat_sum[SLIM - 1]
    var_weight = 1.0 / (stat_sum[:VARS] / count_sum + norm_eps)
    loss_count = count_sum * VARS
    e, mix, mixed = attend(query, below, keyval, above, counts, heads, 128, 512)

    w_dec_t = jnp.zeros((SLIM, width), bf16).at[:VARS].set(w_dec.T.astype(bf16))
    h_one, h_two, norm_two, up, act, dec = forward(mixed, h_zero, w_big, modulation, w_dec_t, 256)
    decoded = lax.all_gather(dec, "head", axis=0)
    scales = jnp.stack(
        [noise_sigma, input_scale, skip_scale, output_scale, output_scale * (2.0 / loss_count) / 3.0]
    )
    weight = jnp.broadcast_to((loss_scale * var_weight)[:, None], (VARS, 128))
    loss_part, d_part = pixels_back(
        place, scales, node_row, read_rows, target_t, eps_t, weight, decoded, 512
    )
    d_dec = lax.all_to_all(d_part.reshape(heads, rows, SLOT), "head", 0, 0)
    d_one, d_mixed, grad_big, grad_dec, gmod_two = backward(
        d_dec, h_two, h_one, norm_two, up, act, mixed, w_big, modulation, w_dec_t, 256
    )
    big_share = lax.psum_scatter(
        grad_big.reshape(heads * width, -1), both, scatter_dimension=0, tiled=True
    )
    d_mixed = lax.all_to_all(d_mixed, "head", 0, 0).reshape(nodes, HD)
    dq, kv_low, kv_self, kv_high = attend_back(
        query, d_mixed, mix, e, below, keyval, above, 256, 512
    )
    from_above = passed_along(kv_low, "node", -1)
    from_below = passed_along(kv_high, "node", 1)
    dn_part, grad_qkv = unproject(dq, kv_self, from_below, from_above, norm_all, w_attn, 512)
    d_norm = lax.all_to_all(dn_part.reshape(heads, rows, width), "head", 0, 0)
    feat_sq = jnp.sum(noise_feat * noise_feat).reshape(1)
    small, qkv_share, qkv_full, sums = settle(
        feat_sq, d_norm, h_zero, d_one, node_in, modulation, grad_dec, gmod_two, grad_qkv, big_share,
        loss_part, groups,
    )
    grad_enc = small[: 2 * VARS]
    grad_dec = small[2 * VARS : 3 * VARS]
    grad_cond = noise_feat[:, None] * small[3 * VARS : 3 * VARS + 4].reshape(1, -1)
    layer_share = jnp.stack(
        [
            jnp.concatenate([qkv_share, big_share[:, 2 * width :]], 1),
            big_share[:, :width],
            big_share[:, width : 2 * width],
        ]
    )
    grad_norm = jnp.sqrt(sums[0, 0])
    loss_sum = sums[1, 0]
    clip_factor = clip_limit / jnp.maximum(grad_norm, clip_limit)
    clipped = clip_factor * layer_share
    big_full = lax.all_gather(big_share.astype(bf16), "node", axis=0, tiled=True)
    grad_full = jnp.stack(
        [
            jnp.concatenate([qkv_full.reshape(width, -1), big_full[:, 2 * width :]], 1),
            big_full[:, :width],
            big_full[:, width : 2 * width],
        ]
    )
    raw_stat = jnp.einsum("idb,idc->ibc", grad_full, grad_full, preferred_element_type=f32)
    stat_new = clip_factor * (clip_factor * raw_stat)
    basis_old = soap_basis[:, 0]
    rotated = jnp.einsum("idb,ibc->idc", clipped, basis_old, precision=highest)
    first_new = beta_first * soap_first + (1 - beta_first) * rotated
    second_new = beta_second * soap_second + (1 - beta_second) * rotated * rotated
    direction = (
        first_new
        / (1 - beta_first**STEP)
        / (jnp.sqrt(second_new / (1 - beta_second**STEP)) + adam_epsilon)
    )
    step_back = jnp.einsum("idc,ibc->idb", direction, basis_old, precision=highest)
    layer_new = layer_w - rate_layer * (step_back + decay_rate * layer_w)
    stats_new = beta_stats * soap_stats[:, 0] + (1 - beta_stats) * stat_new
    product = jnp.einsum("ibc,icd->ibd", stats_new, basis_old, precision=highest)
    gram_matrix = jnp.einsum("ibc,ibd->icd", product, product, precision=highest)
    basis_new = renew(gram_matrix, product)
    enc_new = adam_small(w_enc, clip_factor * grad_enc, enc_first, enc_second)
    cond_new = adam_small(w_cond, clip_factor * grad_cond, cond_first, cond_second)
    dec_new = adam_small(w_dec.T, clip_factor * grad_dec, dec_first.T, dec_second.T)
    return (
        jnp.reshape(loss_sum, (1,)),
        jnp.reshape(loss_count, (1,)),
        jnp.reshape(grad_norm, (1,)),
        layer_new,
        first_new,
        second_new,
        basis_new[:, None],
        stats_new[:, None],
        *enc_new,
        *cond_new,
        *(x.T for x in dec_new),
    )


def solution(mesh):
    pixel = P("node", None)
    layer = P(None, "node", "head")
    basis = P(None, "head", None, None)
    placed = (
        *(pixel,) * 3,
        P(),
        P("node"),
        P("node", None),
        P("node"),
        P("node"),
        P("node", None),
        *(P(),) * 3,
        *(layer,) * 3,
        *(basis,) * 2,
        *(P(),) * 6,
    )
    return jax.shard_map(
        local,
        mesh=mesh,
        in_specs=placed,
        out_specs=(*(P(),) * 3, *(layer,) * 3, *(basis,) * 2, *(P(),) * 9),
        check_vma=False,
    )
```

```python
import functools
import math

import jax
import jax.numpy as jnp
from jax import lax
from jax.experimental import pallas as pl
from jax.experimental.pallas import tpu as pltpu
from jax.sharding import PartitionSpec as P

HD = 128
VARS = 84
NF = 32
NBR = 16
LEVELS = 1000
STEP = 10

SLOT = 128
SLIM = 96
GROUP = 256 // NBR
BLOCK = 128
STRIP = 16
PAIR_STEP = 4
HEAD_STEP = 21

highest = lax.Precision.HIGHEST
clip_limit = 0.01
beta_first = 0.9
beta_second = 0.95
beta_stats = 0.95
adam_epsilon = 1e-08
rate_layer = 0.02
rate_small = 0.05
decay_rate = 0.1
norm_eps = 1e-05

f32 = jnp.float32
bf16 = jnp.bfloat16
MIB = 2**20


def passed_along(x, axis, by):
    length = lax.axis_size(axis)
    return lax.ppermute(x, axis, [(i, (i + by) % length) for i in range(length)])


def noise_terms(noise_level):
    level_frac = noise_level[0].astype(f32) / (LEVELS - 1)
    noise_sigma = 0.05 * jnp.exp(level_frac * math.log(40.0))
    frequency = 1.0 + jnp.arange(NF // 2).astype(f32)
    phase_angle = jnp.log(noise_sigma) * frequency
    return (noise_sigma, jnp.concatenate([jnp.sin(phase_angle), jnp.cos(phase_angle)]))


def standardize(values_in):
    row_mean = jnp.mean(values_in, -1, keepdims=True)
    centered = values_in - row_mean
    inv_std = lax.rsqrt(jnp.mean(centered * centered, -1, keepdims=True) + norm_eps)
    return (centered * inv_std, inv_std)


def norm_back(normed, inv_std, grad_in):
    return inv_std * (
        grad_in
        - jnp.mean(grad_in, -1, keepdims=True)
        - normed * jnp.mean(grad_in * normed, -1, keepdims=True)
    )


def contract(left, right, left_dim, right_dim, precision=None):
    return lax.dot_general(
        left,
        right,
        (((left_dim,), (right_dim,)), ((), ())),
        preferred_element_type=f32,
        precision=precision,
    )


def halves(x):
    high = x.astype(bf16)
    return high, (x - high.astype(f32)).astype(bf16)


def thirds(x):
    high = x.astype(bf16)
    rest = x - high.astype(f32)
    return (high, *halves(rest))


def fold_lanes(x, op=jnp.add):
    parts = [x[:, i : i + 128] for i in range(0, x.shape[1], 128)]
    while len(parts) > 1:
        parts = [op(*parts[i : i + 2]) if i + 1 < len(parts) else parts[i] for i in range(0, len(parts), 2)]
    return parts[0]


def adam_small(weight, grad_item, first, second):
    first_new = beta_first * first + (1 - beta_first) * grad_item
    second_new = beta_second * second + (1 - beta_second) * grad_item * grad_item
    ratio = (
        first_new
        / (1 - beta_first**STEP)
        / (jnp.sqrt(second_new / (1 - beta_second**STEP)) + adam_epsilon)
    )
    return (weight - rate_small * (ratio + decay_rate * weight), first_new, second_new)


def QKV(width):
    return slice(2 * width, 2 * width + 3 * HD)


def OUT(width):
    return slice(2 * width + 3 * HD, 2 * width + 4 * HD)


def smem():
    return pl.BlockSpec(memory_space=pltpu.SMEM)


def whole(shape):
    zeros = (0,) * len(shape)
    return pl.BlockSpec(tuple(shape), lambda *_: zeros)


def params(mib=48):
    return pltpu.CompilerParams(vmem_limit_bytes=mib * MIB)


def remote(mib, identity):
    return pltpu.CompilerParams(
        vmem_limit_bytes=mib * MIB, collective_id=identity, has_side_effects=True
    )


def vmem():
    return pl.BlockSpec(memory_space=pltpu.VMEM)


def each(count, act, start=1):
    def body(off, carry):
        act(off)
        return carry

    lax.fori_loop(start, count, body, 0)


def meet(axes):
    barrier = pltpu.get_barrier_semaphore()
    total = 0
    for axis in axes:
        count, me = lax.axis_size(axis), lax.axis_index(axis)
        total += count - 1
        each(
            count,
            lambda off: pl.semaphore_signal(barrier, inc=1, device_id={axis: (me + off) % count}),
        )
    pl.semaphore_wait(barrier, total)


class Spread:
    def __init__(self, group, source, target, sends, receives):
        self.count, self.me, self.where = group
        self.source, self.target = source, target
        self.sends, self.receives = sends, receives

    def copy(self, other, slot):
        return pltpu.make_async_remote_copy(
            src_ref=self.source(other),
            dst_ref=self.target(slot),
            send_sem=self.sends.at[other],
            recv_sem=self.receives.at[slot],
            device_id=self.where(other),
        )

    def other(self, off):
        return (self.me + off) % self.count

    def start(self, off):
        self.copy(self.other(off), self.me).start()

    def arrived(self, off):
        self.copy(self.other(off), self.other(off)).wait_recv()

    def sent(self, off):
        self.copy(self.other(off), self.me).wait_send()

    def all(self, act):
        each(self.count, getattr(self, act))


def along(axis):
    return lax.axis_size(axis), lax.axis_index(axis), lambda other: {axis: other}


def pairs():
    node = lax.axis_index("node")
    place, pair = node % 2, node // 2
    within = (2, place, lambda other: {"node": 2 * pair + other})
    across = (lax.axis_size("node") // 2, pair, lambda other: {"node": 2 * other + place})
    return within, across


def encode_kernel(
    place_ref, scale_ref, node_ref, prev_ref, target_ref, eps_ref, w_ref, in_ref, stat_ref, all_ref, pix, box, sems
):
    step = pl.program_id(0)
    rows = in_ref.shape[0]
    tile = node_ref.shape[1]
    weights = Spread(along("node"), lambda _: w_ref, lambda i: box.at[i], sems.at[0], sems.at[1])

    @pl.when(step == 0)
    def _():
        meet(["node"])
        weights.all("start")
        box[weights.me] = w_ref[...]
        pix[...] = jnp.zeros_like(pix)
        in_ref[...] = jnp.zeros_like(in_ref)
        stat_ref[...] = jnp.zeros_like(stat_ref)

    prev = prev_ref[...]
    target = target_ref[...]
    noisy = target + scale_ref[0] * eps_ref[...]
    pix[:VARS] = prev.astype(bf16)
    pix[SLOT : SLOT + VARS] = (scale_ref[1] * noisy).astype(bf16)
    node = node_ref[...] - place_ref[0]
    mine = node - place_ref[1]
    spot = lax.broadcasted_iota(jnp.int32, (rows, tile), 0)
    onehot = (spot == mine).astype(f32).astype(bf16)
    in_ref[...] += contract(onehot, pix[...], 1, 1)
    valid = (node < place_ref[2]).astype(f32)
    residual = target - prev
    stat_ref[:VARS] += fold_lanes(valid * residual * residual)
    stat_ref[SLIM - 1 : SLIM] += fold_lanes(valid)

    @pl.when(step == pl.num_programs(0) - 1)
    def _():
        weights.all("arrived")
        all_ref[...] = box[...]
        weights.all("sent")


def encode(place, scales, node_row, prev, target, eps, w_share, rows, tile, nodes):
    pixels = prev.shape[1]
    gathered = (nodes, *w_share.shape)
    pixel_block = pl.BlockSpec((VARS, tile), lambda i: (0, i))
    return pl.pallas_call(
        encode_kernel,
        grid=(pixels // tile,),
        in_specs=[smem(), smem(), pl.BlockSpec((1, tile), lambda i: (0, i))]
        + [pixel_block] * 3
        + [whole(w_share.shape)],
        out_specs=[whole((rows, 2 * SLOT)), whole((SLIM, 128)), whole(gathered)],
        out_shape=[
            jax.ShapeDtypeStruct((rows, 2 * SLOT), f32),
            jax.ShapeDtypeStruct((SLIM, 128), f32),
            jax.ShapeDtypeStruct(gathered, bf16),
        ],
        scratch_shapes=[
            pltpu.VMEM((2 * SLOT, tile), bf16),
            pltpu.VMEM(gathered, bf16),
            pltpu.SemaphoreType.DMA((2, nodes)),
        ],
        compiler_params=remote(48, 2),
        name="encode",
    )(place, scales, node_row, prev, target, eps, w_share)


def count_tile(slots, put, bands):
    lane = lax.broadcasted_iota(jnp.int32, (GROUP, 256), 1)
    sub = lax.broadcasted_iota(jnp.int32, (GROUP, 256), 0)
    own = lane // NBR == sub
    spot = lax.broadcasted_iota(jnp.int32, (256, 256), 0)
    for g in range(slots.shape[0]):
        row = slots[g : g + 1]
        band = jnp.where(own, row >> 8, -1)
        left = jnp.concatenate([(band == t).astype(f32).astype(bf16) for t in range(bands)], 0)
        right = (spot == (row & 255)).astype(f32).astype(bf16)
        found = contract(left, right, 1, 1).astype(bf16)
        for t in range(bands):
            put(g, t, found[t * GROUP : (t + 1) * GROUP])


def open_kernel(
    in_ref, wenc_ref, mod_ref, stat_ref, w_ref, slot_ref,
    zero_ref, norm_ref, q_ref, kv_ref, sum_ref, count_ref,
    norm_box, stat_own, stat_box, kv, low_box, high_box, tiles, head_sems, stat_sems, halo_sems, out_sems,
):
    heads, rows, _ = norm_box.shape
    head, node = lax.axis_index("head"), lax.axis_index("node")
    nodes = lax.axis_size("node")
    depth = tiles.shape[1]
    steps = count_ref.shape[0] // depth
    stat_own[...] = jnp.broadcast_to(
        jnp.sum(stat_ref[...], 1, keepdims=True), stat_own.shape
    )
    meet(["head", "node"])

    stats = Spread(along("node"), lambda _: stat_own, lambda i: stat_box.at[i], stat_sems.at[0], stat_sems.at[1])
    stats.all("start")
    w_enc = wenc_ref[...]
    h_zero = sum(contract(part, w_enc, 1, 0) for part in thirds(in_ref[...]))
    zero_ref[...] = h_zero
    normed, _ = standardize(h_zero)
    norm_box[head] = (normed * (1 + mod_ref[0:1]) + mod_ref[1:2]).astype(bf16)
    norms = Spread(
        along("head"), lambda _: norm_box.at[head], lambda i: norm_box.at[i], head_sems.at[0], head_sems.at[1]
    )
    norms.all("start")

    def halo(block):
        return [
            pltpu.make_async_remote_copy(
                src_ref=kv.at[block],
                dst_ref=box.at[block],
                send_sem=halo_sems.at[2 * side, block],
                recv_sem=halo_sems.at[2 * side + 1, block],
                device_id={"node": (node + by) % nodes},
            )
            for side, (box, by) in enumerate(((low_box, 1), (high_box, nodes - 1)))
        ]

    def project(block):
        out = contract(norm_box[block], w_ref[:, : 3 * HD], 1, 0).astype(bf16)
        q_ref[block] = out[:, :HD]
        kv[block] = out[:, HD:]
        for copy in halo(block):
            copy.start()

    def count(step):
        slot = step % 2

        @pl.when(step >= 2)
        def _():
            count_out(step - 2).wait()

        per = depth // GROUP
        slots = slot_ref[pl.ds(pl.multiple_of(step * per, per), per)]

        def put(g, t, found):
            tiles[slot, g * GROUP : (g + 1) * GROUP, t * 256 : (t + 1) * 256] = found

        count_tile(slots, put, tiles.shape[2] // 256)
        count_out(step).start()

    def count_out(step):
        return pltpu.make_async_copy(
            tiles.at[step % 2],
            count_ref.at[pl.ds(pl.multiple_of(step * depth, depth), depth)],
            out_sems.at[step % 2],
        )

    project(head)
    each(steps // 2, count, 0)

    def next_block(off):
        norms.arrived(off)
        project(norms.other(off))

    each(heads, next_block)
    norm_ref[...] = norm_box[...]
    kv_ref[1] = kv[...]
    each(steps, count, steps // 2)
    each(steps, lambda step: count_out(step).wait(), steps - 2)
    stats.all("arrived")
    sum_ref[...] = sum(jnp.where(t == node, stat_own[...], stat_box[t]) for t in range(nodes))

    def finish(block):
        for copy in halo(block):
            copy.wait()

    each(heads, finish, 0)
    kv_ref[0] = low_box[...]
    kv_ref[2] = high_box[...]
    norms.all("sent")
    stats.all("sent")


def open_nodes(node_in, w_enc, modulation, stat, w_attn, slots, heads, groups, reach):
    rows, width = node_in.shape[0], w_enc.shape[1]
    depth = 8 * GROUP
    block = lambda w: jax.ShapeDtypeStruct((heads, rows, w), bf16)
    return pl.pallas_call(
        open_kernel,
        in_specs=[vmem()] * 6,
        out_specs=[vmem()] * 5 + [pl.BlockSpec(memory_space=pl.ANY)],
        out_shape=[
            jax.ShapeDtypeStruct((rows, width), f32),
            block(width),
            block(HD),
            jax.ShapeDtypeStruct((3, heads, rows, 2 * HD), bf16),
            jax.ShapeDtypeStruct((SLIM, 128), f32),
            jax.ShapeDtypeStruct((heads * rows, reach), bf16),
        ],
        scratch_shapes=[
            pltpu.VMEM((heads, rows, width), bf16),
            pltpu.VMEM((SLIM, 128), f32),
            pltpu.VMEM((groups, SLIM, 128), f32),
            pltpu.VMEM((heads, rows, 2 * HD), bf16),
            pltpu.VMEM((heads, rows, 2 * HD), bf16),
            pltpu.VMEM((heads, rows, 2 * HD), bf16),
            pltpu.VMEM((2, depth, reach), bf16),
            pltpu.SemaphoreType.DMA((2, heads)),
            pltpu.SemaphoreType.DMA((2, groups)),
            pltpu.SemaphoreType.DMA((4, heads)),
            pltpu.SemaphoreType.DMA((2,)),
        ],
        compiler_params=remote(56, 3),
        name="open_nodes",
    )(node_in, w_enc, modulation, stat, w_attn, slots)


def attend_kernel(
    q_ref, kv_ref, count_ref, e_ref, mix_ref, out_ref, s_scr, own, box, sems, chunk
):
    step = pl.program_id(0)
    steps = pl.num_programs(0)
    head = lax.axis_index("head")
    tile = q_ref.shape[0]
    per = box.shape[1] // tile

    def copy(target, source, part):
        at = pl.ds(pl.multiple_of(part * tile, tile), tile)
        return pltpu.make_async_remote_copy(
            src_ref=own.at[target, at],
            dst_ref=box.at[source, at],
            send_sem=sems.at[0, target, part],
            recv_sem=sems.at[1, source, part],
            device_id={"head": target},
        )

    @pl.when(step == 0)
    def _():
        meet(["head"])

    nodes = kv_ref.shape[1]
    q = q_ref[...]
    top = jnp.full((tile, 128), -1e30, f32)
    for b in range(3):
        for at in range(0, nodes, chunk):
            cols = slice(b * nodes + at, b * nodes + at + chunk)
            s = contract(q, kv_ref[b, at : at + chunk, :HD], 1, 1)
            s = jnp.where(count_ref[:, cols].astype(f32) > 0, s, -1e30)
            s_scr[:, cols] = s
            top = jnp.maximum(top, fold_lanes(s, jnp.maximum))
    top = jnp.max(top, 1, keepdims=True)
    factor = math.log2(math.e) / math.sqrt(HD)
    total = jnp.zeros((tile, 128), f32)
    mixed = jnp.zeros((tile, HD), f32)
    for b in range(3):
        for at in range(0, nodes, chunk):
            cols = slice(b * nodes + at, b * nodes + at + chunk)
            e = count_ref[:, cols].astype(f32) * jnp.exp2((s_scr[:, cols] - top) * factor)
            total += fold_lanes(e)
            e = e.astype(bf16)
            e_ref[:, cols] = e
            mixed += contract(e, kv_ref[b, at : at + chunk, HD:], 1, 0)
    inverse = 1.0 / jnp.sum(total, 1, keepdims=True)
    mixed = mixed * inverse
    mix_ref[:, :HD] = mixed
    mix_ref[:, HD:] = jnp.broadcast_to(inverse, (tile, HD))
    target, part = step // per, step % per
    at = pl.ds(pl.multiple_of(part * tile, tile), tile)
    low = mixed.astype(bf16)
    own[target, at] = low

    @pl.when(target == head)
    def _():
        box[head, at] = low

    @pl.when(target != head)
    def _():
        copy(target, head, part).start()

    @pl.when(step == steps - 1)
    def _():
        heads = box.shape[0]

        def finish(off):
            other = (head + off) % heads
            for p in range(per):
                copy(other, other, p).wait_recv()
                copy(other, head, p).wait_send()

        each(heads, finish)
        out_ref[...] = box[...]


def attend(query, keyval, counts, heads, tile, chunk):
    nodes, reach = counts.shape
    rows = nodes // heads
    row = lambda width: pl.BlockSpec((tile, width), lambda i: (i, 0))
    return pl.pallas_call(
        functools.partial(attend_kernel, chunk=chunk),
        grid=(nodes // tile,),
        in_specs=[row(HD), whole(keyval.shape), row(reach)],
        out_specs=[row(reach), row(2 * HD), whole((heads, rows, HD))],
        out_shape=[
            jax.ShapeDtypeStruct((nodes, reach), bf16),
            jax.ShapeDtypeStruct((nodes, 2 * HD), f32),
            jax.ShapeDtypeStruct((heads, rows, HD), bf16),
        ],
        scratch_shapes=[
            pltpu.VMEM((tile, reach), f32),
            pltpu.VMEM((heads, rows, HD), bf16),
            pltpu.VMEM((heads, rows, HD), bf16),
            pltpu.SemaphoreType.DMA((2, heads, rows // tile)),
        ],
        compiler_params=remote(60, 4),
        name="attend",
    )(query, keyval, counts)


def attend_back_kernel(
    q_ref, d_ref, mix_ref, e_ref, kv_ref, norm_ref, big_ref,
    dq_ref, dkv_ref, grad_ref, share_ref,
    dk, dv, dq, low_own, high_own, low_box, high_box, dq_own, dq_box, dkv_own, dkv_box,
    pair_box, pair_sum, head_box, across_own, across_box,
    halo_sems, dq_sems, dkv_sems, pair_sems, head_sems, across_sems,
    chunk,
):
    turn, part = pl.program_id(0), pl.program_id(1)
    parts = pl.num_programs(1)
    step = turn * parts + part
    tile = q_ref.shape[0]
    nodes = kv_ref.shape[1]
    heads, rows, _ = dq_box.shape
    per = rows // tile
    head, node, groups = lax.axis_index("head"), lax.axis_index("node"), lax.axis_size("node")
    within, across = pairs()
    last = part == parts - 1

    place = within[1]
    pair_copy = pltpu.make_async_remote_copy(
        src_ref=big_ref.at[1 - place],
        dst_ref=pair_box,
        send_sem=pair_sems.at[0],
        recv_sem=pair_sems.at[1],
        device_id=within[2](1 - place),
    )
    over_heads = Spread(
        along("head"), lambda o: pair_sum.at[o], lambda i: head_box.at[i], head_sems.at[0], head_sems.at[1]
    )
    over_pairs = Spread(
        across, lambda o: across_own.at[o], lambda i: across_box.at[i], across_sems.at[0], across_sems.at[1]
    )
    count = across[0]

    def halo(own, box, side, by):
        return pltpu.make_async_remote_copy(
            src_ref=own,
            dst_ref=box,
            send_sem=halo_sems.at[0, side],
            recv_sem=halo_sems.at[1, side],
            device_id={"node": (node + by) % groups},
        )

    to_below = halo(low_own, low_box, 0, groups - 1)
    to_above = halo(high_own, high_box, 1, 1)

    def dq_copy(target, source, piece):
        at = pl.ds(pl.multiple_of(piece * tile, tile), tile)
        return pltpu.make_async_remote_copy(
            src_ref=dq_own.at[target, at],
            dst_ref=dq_box.at[source, at],
            send_sem=dq_sems.at[0, target, piece],
            recv_sem=dq_sems.at[1, source, piece],
            device_id={"head": target},
        )

    dkv_spread = Spread(
        along("head"), lambda o: dkv_own.at[o], lambda i: dkv_box.at[i], dkv_sems.at[0], dkv_sems.at[1]
    )

    @pl.when(step == 0)
    def _():
        meet(["head", "node"])
        pair_copy.start()

    @pl.when(step == PAIR_STEP)
    def _():
        pair_copy.wait()

        def add(h):
            for z in range(count):
                pair_sum[h, z] = (
                    big_ref[place, h, z].astype(f32) + pair_box[h, z].astype(f32)
                ).astype(bf16)

        each(heads, add, 0)
        over_heads.all("start")
        head_box[head] = pair_sum[head]

    @pl.when(step == HEAD_STEP)
    def _():
        over_heads.all("arrived")

        def add(z):
            across_own[z] = sum(head_box[h, z].astype(f32) for h in range(heads)).astype(bf16)

        each(count, add, 0)
        over_pairs.all("start")
        across_box[across[1]] = across_own[across[1]]

    @pl.when(part == 0)
    def _():
        dk[...] = jnp.zeros_like(dk)
        dv[...] = jnp.zeros_like(dv)

    grad = d_ref[...]
    wide = grad.astype(f32)
    inverse = mix_ref[:, HD : HD + 1]
    delta = jnp.sum(wide * mix_ref[:, :HD], 1, keepdims=True)
    gain = inverse * (1.0 / math.sqrt(HD))
    q_turned = q_ref[...].T
    d_turned = (wide * inverse).astype(bf16).T
    here = pl.ds(pl.multiple_of(part * tile, tile), tile)
    dq_here = jnp.where(turn == 0, 0.0, dq[here])
    for at in range(0, nodes, chunk):
        cols = slice(at, at + chunk)
        dp = contract(grad, kv_ref[0, cols, HD:], 1, 1)
        e = e_ref[:, cols]
        ds = (e.astype(f32) * ((dp - delta) * gain)).astype(bf16)
        dq_here += contract(ds, kv_ref[0, cols, :HD], 1, 0)
        dk[:, cols] += contract(q_turned, ds, 1, 0)
        dv[:, cols] += contract(d_turned, e, 1, 0)
    dq[here] = dq_here

    for which, own, copy in ((0, low_own, to_below), (1, high_own, to_above)):

        @pl.when(last & (turn == which))
        def _(own=own, copy=copy):
            own[:HD] = dk[...].astype(bf16)
            own[HD:] = dv[...].astype(bf16)
            copy.start()

    @pl.when(turn == 2)
    def _():
        target, piece = part // per, part % per
        at = pl.ds(pl.multiple_of(piece * tile, tile), tile)
        low = dq_here.astype(bf16)
        dq_own[target, at] = low

        @pl.when(target == head)
        def _():
            dq_box[head, at] = low

        @pl.when(target != head)
        def _():
            dq_copy(target, head, piece).start()

    @pl.when(last & (turn == 2))
    def _():
        to_below.wait()
        to_above.wait()
        for h in range(heads):
            cols = slice(h * rows, (h + 1) * rows)
            for half, acc in enumerate((dk, dv)):
                lines = slice(half * HD, (half + 1) * HD)
                total = acc[:, cols] + low_box[lines, cols].astype(f32) + high_box[lines, cols].astype(f32)
                dkv_own[h, lines] = total.astype(bf16)
        dkv_spread.all("start")
        dkv_box[head] = dkv_own[head]
        grad_q = sum(
            contract(norm_ref[h * rows : (h + 1) * rows], dq_own[h], 0, 0) for h in range(heads)
        )
        grad_kv = sum(
            contract(dkv_own[h], norm_ref[h * rows : (h + 1) * rows], 1, 0) for h in range(heads)
        )
        grad_ref[:, :HD] = grad_q
        grad_ref[:, HD:] = grad_kv.T
        over_pairs.all("arrived")
        share_ref[...] = sum(across_box[z].astype(f32) for z in range(count))

        def finish(off):
            other = (head + off) % heads
            for p in range(per):
                dq_copy(other, other, p).wait_recv()
                dq_copy(other, head, p).wait_send()

        each(heads, finish)
        dkv_spread.all("arrived")
        dq_ref[...] = dq_box[...]
        dkv_ref[...] = dkv_box[...]
        dkv_spread.all("sent")
        over_heads.all("sent")
        over_pairs.all("sent")


def attend_back(query, grad, mix, e, keyval, norm_all, grad_big, heads, tile, chunk):
    nodes, reach = e.shape
    rows, width = nodes // heads, norm_all.shape[1]
    parts = nodes // tile
    _, _, count, share, across = grad_big.shape
    row = lambda width: pl.BlockSpec((tile, width), lambda j, i: (i, 0))
    pair = (heads, count, share, across)
    dma = lambda *shape: pltpu.SemaphoreType.DMA(shape)
    order = lambda j: 2 * j % 3
    return pl.pallas_call(
        functools.partial(attend_back_kernel, chunk=chunk),
        grid=(3, parts),
        in_specs=[
            row(HD),
            row(HD),
            row(2 * HD),
            pl.BlockSpec((tile, nodes), lambda j, i: (i, order(j))),
            pl.BlockSpec((1, nodes, 2 * HD), lambda j, i: (order(j), 0, 0)),
            vmem(),
            vmem(),
        ],
        out_specs=[
            whole((heads, rows, HD)),
            whole((heads, 2 * HD, rows)),
            whole((width, 3 * HD)),
            whole((share, across)),
        ],
        out_shape=[
            jax.ShapeDtypeStruct((heads, rows, HD), bf16),
            jax.ShapeDtypeStruct((heads, 2 * HD, rows), bf16),
            jax.ShapeDtypeStruct((width, 3 * HD), f32),
            jax.ShapeDtypeStruct((share, across), f32),
        ],
        scratch_shapes=[
            pltpu.VMEM((HD, nodes), f32),
            pltpu.VMEM((HD, nodes), f32),
            pltpu.VMEM((nodes, HD), f32),
            *[pltpu.VMEM((2 * HD, nodes), bf16)] * 4,
            *[pltpu.VMEM((heads, rows, HD), bf16)] * 2,
            *[pltpu.VMEM((heads, 2 * HD, rows), bf16)] * 2,
            *[pltpu.VMEM(pair, bf16)] * 3,
            *[pltpu.VMEM(pair[1:], bf16)] * 2,
            dma(2, 2),
            dma(2, heads, rows // tile),
            dma(2, heads),
            dma(2),
            dma(2, heads),
            dma(2, count),
        ],
        compiler_params=remote(60, 5),
        name="attend_back",
    )(query, grad, mix, e, keyval, norm_all, grad_big)


def forward_kernel(mixed_ref, zero_ref, w_ref, mod_ref, wdec_ref, one_ref, two_ref, norm_ref, up_ref, act_ref, dec_ref):
    heads, width = w_ref.shape[0], w_ref.shape[1]
    h_one = zero_ref[...] + sum(
        contract(mixed_ref[h], w_ref[h, :, OUT(width)], 1, 1) for h in range(heads)
    )
    one_ref[...] = h_one
    normed, _ = standardize(h_one)
    norm_two = (normed * (1 + mod_ref[2:3]) + mod_ref[3:4]).astype(bf16)
    norm_ref[...] = norm_two
    h_two = h_one
    for h in range(heads):
        up = contract(norm_two, w_ref[h, :, :width], 1, 0)
        up_ref[h] = up
        act = (up * jax.nn.sigmoid(up)).astype(bf16)
        act_ref[h] = act
        h_two = h_two + contract(act, w_ref[h, :, width : 2 * width], 1, 1)
    two_ref[...] = h_two
    final = standardize(h_two)[0].astype(bf16)
    high, low = halves(contract(wdec_ref[...], final, 1, 1))
    dec_ref[:SLIM] = high
    dec_ref[SLIM:] = low


def forward(mixed, h_zero, w_big, modulation, w_dec, tile):
    heads, rows = mixed.shape[:2]
    width = h_zero.shape[1]
    row = pl.BlockSpec((tile, width), lambda i: (i, 0))
    stack = lambda w: pl.BlockSpec((heads, tile, w), lambda i: (0, i, 0))
    return pl.pallas_call(
        forward_kernel,
        grid=(rows // tile,),
        in_specs=[stack(HD), row, whole(w_big.shape), whole(modulation.shape), whole(w_dec.shape)],
        out_specs=[row, row, row, stack(width), stack(width), pl.BlockSpec((2 * SLIM, tile), lambda i: (0, i))],
        out_shape=[
            jax.ShapeDtypeStruct((rows, width), f32),
            jax.ShapeDtypeStruct((rows, width), f32),
            jax.ShapeDtypeStruct((rows, width), bf16),
            jax.ShapeDtypeStruct((heads, rows, width), f32),
            jax.ShapeDtypeStruct((heads, rows, width), bf16),
            jax.ShapeDtypeStruct((2 * SLIM, rows), bf16),
        ],
        compiler_params=params(),
        name="forward",
    )(mixed, h_zero, w_big, modulation, w_dec)


def pixel_kernel(place_ref, scale_ref, node_ref, read_ref, target_ref, eps_ref, weight_ref, dec_ref, loss_ref, d_ref, hits, turned, total):
    step = pl.program_id(0)
    heads, _, rows = dec_ref.shape
    tile = target_ref.shape[1]

    @pl.when(step == 0)
    def _():
        turned[...] = jnp.zeros_like(turned)
        total[...] = jnp.zeros_like(total)
        loss_ref[...] = jnp.zeros_like(loss_ref)

    reads = read_ref[...] - place_ref[0]
    field = jnp.zeros((2 * SLIM, tile), f32)
    for h in range(heads):
        spot = lax.broadcasted_iota(jnp.int32, (rows, tile), 0) + h * rows
        hit = sum((spot == reads[k : k + 1]).astype(f32) for k in range(3)).astype(bf16)
        hits[h * rows : (h + 1) * rows] = hit
        field += contract(dec_ref[h], hit, 1, 0)
    field = (field[:VARS] + field[SLIM : SLIM + VARS]) / 3.0
    target = target_ref[...]
    noisy = target + scale_ref[0] * eps_ref[...]
    error = scale_ref[2] * noisy + scale_ref[3] * field - target
    valid = (node_ref[...] - place_ref[0] < place_ref[2]).astype(f32)
    weighted = valid * weight_ref[:, 0:1]
    loss_ref[:VARS] += fold_lanes(weighted * error * error)
    high, low = halves(scale_ref[4] * weighted * error)
    turned[:VARS] = high
    turned[SLOT : SLOT + VARS] = low
    total[...] += contract(hits[...], turned[...], 1, 1)

    @pl.when(step == pl.num_programs(0) - 1)
    def _():
        d_ref[...] = total[:, :SLOT] + total[:, SLOT:]


def pixels_back(place, scales, node_row, read_rows, target, eps, weight, decoded, tile):
    heads, _, rows = decoded.shape
    count = target.shape[1] // heads
    steps = count // tile
    at = lambda i, place: (0, place[3] * steps + i)
    fixed = lambda shape: pl.BlockSpec(tuple(shape), lambda i, place: (0,) * len(shape))
    return pl.pallas_call(
        pixel_kernel,
        grid_spec=pltpu.PrefetchScalarGridSpec(
            num_scalar_prefetch=1,
            grid=(steps,),
            in_specs=[
                smem(),
                pl.BlockSpec((1, tile), at),
                pl.BlockSpec((3, tile), at),
                pl.BlockSpec((VARS, tile), at),
                pl.BlockSpec((VARS, tile), at),
                fixed(weight.shape),
                fixed(decoded.shape),
            ],
            out_specs=[fixed((SLIM, 128)), fixed((heads * rows, SLOT))],
            scratch_shapes=[
                pltpu.VMEM((heads * rows, tile), bf16),
                pltpu.VMEM((2 * SLOT, tile), bf16),
                pltpu.VMEM((heads * rows, 2 * SLOT), f32),
            ],
        ),
        out_shape=[
            jax.ShapeDtypeStruct((SLIM, 128), f32),
            jax.ShapeDtypeStruct((heads * rows, SLOT), f32),
        ],
        compiler_params=params(),
        name="pixels_back",
    )(place, scales, node_row, read_rows, target, eps, weight, decoded)


def backward_kernel(
    d_ref, two_ref, one_ref, norm_ref, up_ref, act_ref, mixed_ref, w_ref, mod_ref, wdec_ref,
    done_ref, dmix_ref, big_ref, gdec_ref, gmod_ref, grad_ref,
):
    heads, width = w_ref.shape[0], w_ref.shape[1]
    step = pl.program_id(0)

    @pl.when(step == 0)
    def _():
        grad_ref[...] = jnp.zeros_like(grad_ref)
        gdec_ref[...] = jnp.zeros_like(gdec_ref)
        gmod_ref[...] = jnp.zeros_like(gmod_ref)

    d_dec = sum(d_ref[h] for h in range(heads)).astype(bf16)
    normed_two, inv_two = standardize(two_ref[...])
    final = normed_two.astype(bf16)
    gdec_ref[...] += contract(d_dec[:, :SLIM], final, 0, 0)
    d_two = norm_back(normed_two, inv_two, contract(d_dec[:, :SLIM], wdec_ref[...], 1, 0))
    d_low = d_two.astype(bf16)
    norm_two = norm_ref[...]
    d_mid = jnp.zeros_like(d_two)
    for h in range(heads):
        act = act_ref[h]
        up = up_ref[h]
        d_act = contract(d_low, w_ref[h, :, width : 2 * width], 1, 0)
        gating = jax.nn.sigmoid(up)
        d_up = (d_act * gating * (1 + up * (1 - gating))).astype(bf16)
        grad_ref[h, :, :width] += contract(norm_two, d_up, 0, 0)
        grad_ref[h, :, width : 2 * width] += contract(d_low, act, 0, 0)
        d_mid += contract(d_up, w_ref[h, :, :width], 1, 1)
    normed_one, inv_one = standardize(one_ref[...])
    gmod_ref[0:1] += jnp.sum(d_mid * normed_one, 0, keepdims=True)
    gmod_ref[1:2] += jnp.sum(d_mid, 0, keepdims=True)
    d_one = d_two + norm_back(normed_one, inv_one, d_mid * (1 + mod_ref[2:3]))
    done_ref[...] = d_one
    one_low = d_one.astype(bf16)
    for h in range(heads):
        dmix_ref[h] = contract(one_low, w_ref[h, :, OUT(width)], 1, 0).astype(bf16)
        grad_ref[h, :, 2 * width :] += contract(one_low, mixed_ref[h], 0, 0)

    @pl.when(step == pl.num_programs(0) - 1)
    def _():
        _, _, count, share, _ = big_ref.shape
        for c in range(2):
            for h in range(heads):
                for z in range(count):
                    at = (2 * z + c) * share
                    big_ref[c, h, z] = grad_ref[h, at : at + share].astype(bf16)


def backward(d_dec, h_two, h_one, norm_two, up, act, mixed, w_big, modulation, w_dec, groups, tile):
    heads, rows = mixed.shape[:2]
    width = h_one.shape[1]
    grads = (heads, width, 2 * width + HD)
    big = (2, heads, groups // 2, width // groups, grads[2])
    row = lambda w: pl.BlockSpec((tile, w), lambda i: (i, 0))
    stack = lambda w: pl.BlockSpec((heads, tile, w), lambda i: (0, i, 0))
    return pl.pallas_call(
        backward_kernel,
        grid=(rows // tile,),
        in_specs=[
            stack(SLOT),
            row(width),
            row(width),
            row(width),
            stack(width),
            stack(width),
            stack(HD),
            whole(w_big.shape),
            whole(modulation.shape),
            whole(w_dec.shape),
        ],
        out_specs=[row(width), stack(HD), whole(big), whole((SLIM, width)), whole((8, width))],
        out_shape=[
            jax.ShapeDtypeStruct((rows, width), f32),
            jax.ShapeDtypeStruct((heads, rows, HD), bf16),
            jax.ShapeDtypeStruct(big, bf16),
            jax.ShapeDtypeStruct((SLIM, width), f32),
            jax.ShapeDtypeStruct((8, width), f32),
        ],
        scratch_shapes=[pltpu.VMEM(grads, f32)],
        compiler_params=params(56),
        name="backward",
    )(d_dec, h_two, h_one, norm_two, up, act, mixed, w_big, modulation, w_dec)


def settle_kernel(
    feat_ref, dq_ref, dkv_ref, w_ref, zero_ref, done_ref, in_ref, mod_ref, gdec_ref, gmod_ref, qkv_ref, big_ref, loss_ref,
    small_ref, share_ref, full_ref, bigfull_ref, sums_ref,
    q_low, q_pair, q_sum, q_box, q_share, q_full, big_low, big_full,
    parts, part_box, part_sum, part_own, pay, heard, tally, tallies,
    pair_sems, q_sems, f_sems, big_sems, a_sems, n_sems, b_sems, t_sems,
):
    heads, width = w_ref.shape[0], w_ref.shape[1]
    share_rows = share_ref.shape[0]
    head, node = lax.axis_index("head"), lax.axis_index("node")
    groups = heard.shape[0]
    within, across = pairs()
    place, pair, count = within[1], across[1], across[0]

    def to_other(source, target, index):
        return pltpu.make_async_remote_copy(
            src_ref=source,
            dst_ref=target,
            send_sem=pair_sems.at[0, index],
            recv_sem=pair_sems.at[1, index],
            device_id=within[2](1 - place),
        )

    for c in range(2):
        for z in range(count):
            at = (2 * z + c) * share_rows
            q_low[c, z] = qkv_ref[at : at + share_rows].astype(bf16)
    big_low[...] = big_ref[...].astype(bf16)
    meet(["head", "node"])
    q_pairs = to_other(q_low.at[1 - place], q_pair, 0)
    q_pairs.start()

    d_norm = sum(
        contract(dq_ref[h], w_ref[h, :, 2 * width : 2 * width + HD], 1, 1)
        + contract(dkv_ref[h], w_ref[h, :, 2 * width + HD : 2 * width + 3 * HD], 0, 1)
        for h in range(heads)
    )
    normed, inv = standardize(zero_ref[...])
    d_zero = done_ref[...] + norm_back(normed, inv, d_norm * (1 + mod_ref[0:1]))

    q_pairs.wait()
    for z in range(count):
        q_sum[z] = (q_low[place, z].astype(f32) + q_pair[z].astype(f32)).astype(bf16)
    q_over = Spread(across, lambda o: q_sum.at[o], lambda i: q_box.at[i], q_sems.at[0], q_sems.at[1])
    q_over.all("start")
    q_box[pair] = q_sum[pair]

    g_enc = contract(in_ref[...].T, d_zero, 1, 0, highest)
    parts[...] = jnp.zeros_like(parts)
    flat = parts.reshape(parts.shape[0] * parts.shape[1], width)
    flat[:VARS] = g_enc[:VARS]
    flat[VARS : 2 * VARS] = g_enc[SLOT : SLOT + VARS]
    flat[2 * VARS : 3 * VARS] = gdec_ref[:VARS]
    at = 3 * VARS
    flat[at : at + 1] = jnp.sum(d_norm * normed, 0, keepdims=True)
    flat[at + 1 : at + 2] = jnp.sum(d_norm, 0, keepdims=True)
    flat[at + 2 : at + 4] = gmod_ref[0:2]
    over_heads = Spread(
        along("head"), lambda o: parts.at[o], lambda i: part_box.at[i], a_sems.at[0], a_sems.at[1]
    )
    over_heads.all("start")
    part_box[head] = parts[head]

    q_over.all("arrived")
    share = sum(q_box[z].astype(f32) for z in range(count))
    share_ref[...] = share
    q_share[...] = share.astype(bf16)
    q_full[place, pair] = share.astype(bf16)
    f_over = Spread(
        across, lambda _: q_share, lambda i: q_full.at[place, i], f_sems.at[0], f_sems.at[1]
    )
    f_over.all("start")

    over_heads.all("arrived")
    total = sum(part_box[h] for h in range(heads))
    for t in range(groups):
        part_sum[t] = total[8 * t : 8 * t + 8]
    over_nodes = Spread(
        along("node"), lambda o: part_sum.at[o], lambda i: part_own.at[i], n_sems.at[0], n_sems.at[1]
    )
    over_nodes.all("start")
    part_own[node] = part_sum[node]

    big_over = Spread(
        across, lambda _: big_low, lambda i: big_full.at[place, i], big_sems.at[0], big_sems.at[1]
    )
    big_full[place, pair] = big_low[...]

    squares = jnp.sum(share * share) + jnp.sum(big_ref[...] * big_ref[...])
    loss = jnp.sum(loss_ref[:VARS])
    over_nodes.all("arrived")
    own = sum(part_own[t] for t in range(groups))
    row = lax.broadcasted_iota(jnp.int32, own.shape, 0) + 8 * (head * groups + node)
    squares += jnp.sum(own * own * jnp.where(row >= 3 * VARS, feat_ref[0], 1.0))
    line = lax.broadcasted_iota(jnp.int32, (8, 128), 0)
    pay[:, :width] = own
    pay[:, width:] = jnp.where(line == 0, squares, jnp.where(line == 1, loss, 0.0))
    back = Spread(along("node"), lambda _: pay, lambda i: heard.at[i], b_sems.at[0], b_sems.at[1])
    back.all("start")
    heard[node] = pay[...]
    big_over.all("start")

    f_over.all("arrived")
    q_rest = to_other(q_full.at[place], q_full.at[place], 1)
    q_rest.start()

    back.all("arrived")
    tally[...] = sum(heard[t, :, width:] for t in range(groups))
    tell = Spread(along("head"), lambda _: tally, lambda i: tallies.at[i], t_sems.at[0], t_sems.at[1])
    tell.all("start")
    tallies[head] = tally[...]
    for t in range(groups):
        small_ref[8 * t : 8 * t + 8] = heard[t, :, :width]
    tell.all("arrived")
    sums_ref[...] = sum(tallies[h] for h in range(heads))

    big_over.all("arrived")
    big_rest = to_other(big_full.at[place], big_full.at[place], 2)
    big_rest.start()
    q_rest.wait_send()
    to_other(q_full.at[1 - place], q_full.at[1 - place], 1).wait_recv()
    for c in range(2):
        for z in range(count):
            full_ref[2 * z + c] = q_full[c, z]
    big_rest.wait_send()
    to_other(big_full.at[1 - place], big_full.at[1 - place], 2).wait_recv()
    for c in range(2):
        for z in range(count):
            bigfull_ref[2 * z + c] = big_full[c, z]
    for spread in (q_over, over_heads, f_over, over_nodes, back, big_over, tell):
        spread.all("sent")


def settle(feat_sq, dq, dkv, w_big, h_zero, d_one, node_in, modulation, grad_dec, gmod_two, grad_qkv, big_share, loss, groups):
    heads, rows, _ = dq.shape
    width = h_zero.shape[1]
    count = groups // 2
    share = (grad_qkv.shape[0] // groups, grad_qkv.shape[1])
    big = big_share.shape
    low = lambda *shape: pltpu.VMEM(shape, bf16)
    full = lambda *shape: pltpu.VMEM(shape, f32)
    dma = lambda *shape: pltpu.SemaphoreType.DMA(shape)
    return pl.pallas_call(
        settle_kernel,
        in_specs=[smem()] + [vmem()] * 12,
        out_specs=[vmem()] * 5,
        out_shape=[
            jax.ShapeDtypeStruct((8 * groups, width), f32),
            jax.ShapeDtypeStruct(share, f32),
            jax.ShapeDtypeStruct((groups, *share), bf16),
            jax.ShapeDtypeStruct((groups, *big), bf16),
            jax.ShapeDtypeStruct((8, 128), f32),
        ],
        scratch_shapes=[
            low(2, count, *share),
            low(count, *share),
            low(count, *share),
            low(count, *share),
            low(*share),
            low(2, count, *share),
            low(*big),
            low(2, count, *big),
            full(heads, 8 * groups, width),
            full(heads, 8 * groups, width),
            full(groups, 8, width),
            full(groups, 8, width),
            full(8, width + 128),
            full(groups, 8, width + 128),
            full(8, 128),
            full(heads, 8, 128),
            dma(2, 3),
            dma(2, count),
            dma(2, count),
            dma(2, count),
            dma(2, heads),
            dma(2, groups),
            dma(2, groups),
            dma(2, heads),
        ],
        compiler_params=remote(56, 1),
        name="settle",
    )(feat_sq, dq, dkv, w_big, h_zero, d_one, node_in, modulation, grad_dec, gmod_two, grad_qkv, big_share, loss)


def eliminate(work, done):
    count = work.shape[0]
    lane = lax.broadcasted_iota(jnp.int32, (1, BLOCK), 1)
    sub = lax.broadcasted_iota(jnp.int32, (STRIP, BLOCK), 0)
    pivots = [jnp.ones((1, BLOCK), f32) for _ in range(count)]
    both = lambda x: jnp.concatenate([x, x], 1)
    for at in range(0, BLOCK, STRIP):
        strip = slice(at, at + STRIP)
        rows = [work[m, strip] for m in range(count)]
        columns = [
            [jnp.broadcast_to(rows[m][:, at + k : at + k + 1], (STRIP, BLOCK)) for k in range(STRIP)]
            for m in range(count)
        ]
        scale = [jnp.ones((STRIP, BLOCK), f32) for _ in range(count)]
        for r in range(STRIP):
            for m in range(count):
                column = columns[m][r]
                pivot = jnp.broadcast_to(column[r : r + 1], (STRIP, BLOCK))
                factor = jnp.where(sub > r, column * (1.0 / pivot), 0.0)
                scale[m] = jnp.where(sub == r, pivot, scale[m])
                for k in range(r + 1, STRIP):
                    columns[m][k] = columns[m][k] - factor * columns[m][k][r : r + 1]
                pivots[m] = jnp.where(lane == at + r, pivot[:1], pivots[m])
                rows[m] = rows[m] - both(factor) * rows[m][r : r + 1]
        for m in range(count):
            done[m, strip] = rows[m][:, BLOCK:]
            if at + STRIP < BLOCK:
                high, mid, low = thirds(rows[m] * both(lax.rsqrt(scale[m])))
                left = jnp.concatenate([high, high, mid, mid, high, low], 0)[:, :BLOCK]
                right = jnp.concatenate([high, mid, high, mid, low, high], 0)
                rest = slice(at + STRIP, BLOCK)
                work[m, rest] -= contract(left, right, 0, 0)[rest]
    return pivots


def renew_kernel(gram_ref, product_ref, out_ref, gram, both, work, done):
    count, size = gram_ref.shape[:2]
    k = pl.program_id(0)

    @pl.when(k == 0)
    def _():
        gram[...] = gram_ref[...]
        both[...] = product_ref[...]

    at = pl.ds(pl.multiple_of(k * BLOCK, BLOCK), BLOCK)
    unit = lax.broadcasted_iota(jnp.int32, (BLOCK, BLOCK), 0) == lax.broadcasted_iota(
        jnp.int32, (BLOCK, BLOCK), 1
    )
    for m in range(count):
        work[m, :, :BLOCK] = gram[m, at, at]
        work[m, :, BLOCK:] = unit.astype(f32)
    roots = [lax.rsqrt(p) for p in eliminate(work, done)]
    for step in range(size // BLOCK):

        @pl.when(k == step)
        def _(here=slice(step * BLOCK, (step + 1) * BLOCK), rest=(step + 1) * BLOCK):
            for m in range(count):
                factor = done[m]
                panel = contract(both[m, :, here], factor, 1, 1, highest) * roots[m]
                out_ref[m] = panel
                if rest < size:
                    left = contract(gram[m, rest:, here], factor, 1, 1, highest) * roots[m]
                    both[m, :, rest:] -= contract(panel, left, 1, 1, highest)
                    gram[m, rest:, rest:] -= contract(left, left, 1, 1, highest)


def renew(gram, product):
    count, size = gram.shape[:2]
    return pl.pallas_call(
        renew_kernel,
        grid=(size // BLOCK,),
        in_specs=[whole(gram.shape), whole(gram.shape)],
        out_specs=pl.BlockSpec((count, size, BLOCK), lambda k: (0, 0, k)),
        out_shape=jax.ShapeDtypeStruct(gram.shape, f32),
        scratch_shapes=[
            pltpu.VMEM((count, size, size), f32),
            pltpu.VMEM((count, size, size), f32),
            pltpu.VMEM((count, BLOCK, 2 * BLOCK), f32),
            pltpu.VMEM((count, BLOCK, BLOCK), f32),
        ],
        compiler_params=params(),
        name="renew",
    )(gram, product)


def local(
    prev_state,
    target,
    noise_eps,
    noise_level,
    valid_count,
    neighbours,
    nbr_count,
    pix_node,
    pix_read,
    w_enc,
    w_cond,
    w_dec,
    layer_w,
    soap_first,
    soap_second,
    soap_basis,
    soap_stats,
    enc_first,
    enc_second,
    cond_first,
    cond_second,
    dec_first,
    dec_second,
):
    nodes = nbr_count.shape[0]
    groups = lax.axis_size("node")
    heads = lax.axis_size("head")
    rows = nodes // heads
    reach = 3 * nodes
    block_start = lax.axis_index("node") * nodes
    quarter = lax.axis_index("head")
    width = w_enc.shape[1]
    both = ("head", "node")

    low_w = layer_w.astype(bf16)
    big_share = jnp.concatenate([low_w[1], low_w[2], low_w[0]], 1)
    w_big = lax.all_gather(big_share, both, axis=0, tiled=True).reshape(heads, width, -1)

    noise_sigma, noise_feat = noise_terms(noise_level)
    sig_sq = noise_sigma * noise_sigma
    input_scale = lax.rsqrt(sig_sq + 1.0)
    skip_scale = 1.0 / (sig_sq + 1.0)
    output_scale = noise_sigma * lax.rsqrt(sig_sq + 1.0)
    loss_scale = (sig_sq + 1.0) / sig_sq
    modulation = jnp.dot(noise_feat[None, :], w_cond, precision=highest).reshape(4, width)

    prev_t, target_t, eps_t = prev_state.T, target.T, noise_eps.T
    node_row = pix_node.reshape(1, -1)
    read_rows = pix_read.T
    place = jnp.stack([block_start, quarter * rows, valid_count[0], quarter]).astype(jnp.int32)
    node_in, stat, w_attn = encode(
        place, jnp.stack([noise_sigma, input_scale]), node_row, prev_t, target_t, eps_t, low_w[0], rows, 1024, groups
    )
    w_attn = w_attn.reshape(width, -1)

    relative = (neighbours - block_start + nodes) % (nodes * groups)
    live = jnp.arange(NBR)[None, :] < nbr_count[:, None]
    slots = jnp.where(live, relative, -1).reshape(nodes // GROUP, 256)
    pad_enc = jnp.zeros((2, SLOT, width), bf16)
    pad_enc = pad_enc.at[:, :VARS].set(w_enc.astype(bf16).reshape(2, VARS, width))
    h_zero, norm_all, query, keyval, stat, counts = open_nodes(
        node_in, pad_enc.reshape(2 * SLOT, width), modulation, stat, w_attn, slots, heads, groups, reach
    )
    norm_all, query = norm_all.reshape(nodes, -1), query.reshape(nodes, -1)
    keyval = keyval.reshape(3, nodes, -1)
    stat_sum = stat[:, 0]
    count_sum = stat_sum[SLIM - 1]
    var_weight = 1.0 / (stat_sum[:VARS] / count_sum + norm_eps)
    loss_count = count_sum * VARS
    e, mix, mixed = attend(query, keyval, counts, heads, 128, 512)

    w_dec_t = jnp.zeros((SLIM, width), bf16).at[:VARS].set(w_dec.T.astype(bf16))
    h_one, h_two, norm_two, up, act, dec = forward(mixed, h_zero, w_big, modulation, w_dec_t, 256)
    decoded = lax.all_gather(dec, "head", axis=0)
    scales = jnp.stack(
        [noise_sigma, input_scale, skip_scale, output_scale, output_scale * (2.0 / loss_count) / 3.0]
    )
    weight = jnp.broadcast_to((loss_scale * var_weight)[:, None], (VARS, 128))
    loss_part, d_part = pixels_back(
        place, scales, node_row, read_rows, target_t, eps_t, weight, decoded, 512
    )
    d_dec = lax.all_to_all(d_part.reshape(heads, rows, SLOT), "head", 0, 0)
    d_one, d_mixed, grad_big, grad_dec, gmod_two = backward(
        d_dec, h_two, h_one, norm_two, up, act, mixed, w_big, modulation, w_dec_t, groups, 256
    )
    d_mixed = lax.all_to_all(d_mixed, "head", 0, 0).reshape(nodes, HD)
    dq, dkv, grad_qkv, big_share = attend_back(
        query, d_mixed, mix, e, keyval, norm_all, grad_big, heads, 256, 512
    )
    feat_sq = jnp.sum(noise_feat * noise_feat).reshape(1)
    small, qkv_share, qkv_full, big_full, sums = settle(
        feat_sq, dq, dkv, w_big, h_zero, d_one, node_in, modulation, grad_dec, gmod_two, grad_qkv, big_share,
        loss_part, groups,
    )
    small = lax.all_gather(small, "head", axis=0, tiled=True)
    big_full = big_full.reshape(width, -1)
    grad_enc = small[: 2 * VARS]
    grad_dec = small[2 * VARS : 3 * VARS]
    grad_cond = noise_feat[:, None] * small[3 * VARS : 3 * VARS + 4].reshape(1, -1)
    layer_share = jnp.stack(
        [
            jnp.concatenate([qkv_share, big_share[:, 2 * width :]], 1),
            big_share[:, :width],
            big_share[:, width : 2 * width],
        ]
    )
    grad_norm = jnp.sqrt(sums[0, 0])
    loss_sum = sums[1, 0]
    clip_factor = clip_limit / jnp.maximum(grad_norm, clip_limit)
    clipped = clip_factor * layer_share
    grad_full = jnp.stack(
        [
            jnp.concatenate([qkv_full.reshape(width, -1), big_full[:, 2 * width :]], 1),
            big_full[:, :width],
            big_full[:, width : 2 * width],
        ]
    )
    raw_stat = jnp.einsum("idb,idc->ibc", grad_full, grad_full, preferred_element_type=f32)
    stat_new = clip_factor * (clip_factor * raw_stat)
    basis_old = soap_basis[:, 0]
    rotated = jnp.einsum("idb,ibc->idc", clipped, basis_old, precision=highest)
    first_new = beta_first * soap_first + (1 - beta_first) * rotated
    second_new = beta_second * soap_second + (1 - beta_second) * rotated * rotated
    direction = (
        first_new
        / (1 - beta_first**STEP)
        / (jnp.sqrt(second_new / (1 - beta_second**STEP)) + adam_epsilon)
    )
    step_back = jnp.einsum("idc,ibc->idb", direction, basis_old, precision=highest)
    layer_new = layer_w - rate_layer * (step_back + decay_rate * layer_w)
    stats_new = beta_stats * soap_stats[:, 0] + (1 - beta_stats) * stat_new
    product = jnp.einsum("ibc,icd->ibd", stats_new, basis_old, precision=highest)
    gram_matrix = jnp.einsum("ibc,ibd->icd", product, product, precision=highest)
    basis_new = renew(gram_matrix, product)
    enc_new = adam_small(w_enc, clip_factor * grad_enc, enc_first, enc_second)
    cond_new = adam_small(w_cond, clip_factor * grad_cond, cond_first, cond_second)
    dec_new = adam_small(w_dec.T, clip_factor * grad_dec, dec_first.T, dec_second.T)
    return (
        jnp.reshape(loss_sum, (1,)),
        jnp.reshape(loss_count, (1,)),
        jnp.reshape(grad_norm, (1,)),
        layer_new,
        first_new,
        second_new,
        basis_new[:, None],
        stats_new[:, None],
        *enc_new,
        *cond_new,
        *(x.T for x in dec_new),
    )


def solution(mesh):
    pixel = P("node", None)
    layer = P(None, "node", "head")
    basis = P(None, "head", None, None)
    placed = (
        *(pixel,) * 3,
        P(),
        P("node"),
        P("node", None),
        P("node"),
        P("node"),
        P("node", None),
        *(P(),) * 3,
        *(layer,) * 3,
        *(basis,) * 2,
        *(P(),) * 6,
    )
    return jax.shard_map(
        local,
        mesh=mesh,
        in_specs=placed,
        out_specs=(*(P(),) * 3, *(layer,) * 3, *(basis,) * 2, *(P(),) * 9),
        check_vma=False,
    )
```

```python
import functools
import math

import jax
import jax.numpy as jnp
from jax import lax
from jax.experimental import pallas as pl
from jax.experimental.pallas import tpu as pltpu
from jax.sharding import PartitionSpec as P

HD = 128
VARS = 84
NF = 32
NBR = 16
LEVELS = 1000
STEP = 10

SLOT = 128
SLIM = 96
GROUP = 256 // NBR
BLOCK = 128
STRIP = 16
HEAD_STEP = 17

highest = lax.Precision.HIGHEST
clip_limit = 0.01
beta_first = 0.9
beta_second = 0.95
beta_stats = 0.95
adam_epsilon = 1e-08
rate_layer = 0.02
rate_small = 0.05
decay_rate = 0.1
norm_eps = 1e-05

f32 = jnp.float32
bf16 = jnp.bfloat16
MIB = 2**20


def passed_along(x, axis, by):
    length = lax.axis_size(axis)
    return lax.ppermute(x, axis, [(i, (i + by) % length) for i in range(length)])


def noise_terms(noise_level):
    level_frac = noise_level[0].astype(f32) / (LEVELS - 1)
    noise_sigma = 0.05 * jnp.exp(level_frac * math.log(40.0))
    frequency = 1.0 + jnp.arange(NF // 2).astype(f32)
    phase_angle = jnp.log(noise_sigma) * frequency
    return (noise_sigma, jnp.concatenate([jnp.sin(phase_angle), jnp.cos(phase_angle)]))


def standardize(values_in):
    row_mean = jnp.mean(values_in, -1, keepdims=True)
    centered = values_in - row_mean
    inv_std = lax.rsqrt(jnp.mean(centered * centered, -1, keepdims=True) + norm_eps)
    return (centered * inv_std, inv_std)


def norm_back(normed, inv_std, grad_in):
    return inv_std * (
        grad_in
        - jnp.mean(grad_in, -1, keepdims=True)
        - normed * jnp.mean(grad_in * normed, -1, keepdims=True)
    )


def contract(left, right, left_dim, right_dim, precision=None):
    return lax.dot_general(
        left,
        right,
        (((left_dim,), (right_dim,)), ((), ())),
        preferred_element_type=f32,
        precision=precision,
    )


def halves(x):
    high = x.astype(bf16)
    return high, (x - high.astype(f32)).astype(bf16)


def thirds(x):
    high = x.astype(bf16)
    rest = x - high.astype(f32)
    return (high, *halves(rest))


def fold_lanes(x, op=jnp.add):
    parts = [x[:, i : i + 128] for i in range(0, x.shape[1], 128)]
    while len(parts) > 1:
        parts = [op(*parts[i : i + 2]) if i + 1 < len(parts) else parts[i] for i in range(0, len(parts), 2)]
    return parts[0]


def adam_small(weight, grad_item, first, second):
    first_new = beta_first * first + (1 - beta_first) * grad_item
    second_new = beta_second * second + (1 - beta_second) * grad_item * grad_item
    ratio = (
        first_new
        / (1 - beta_first**STEP)
        / (jnp.sqrt(second_new / (1 - beta_second**STEP)) + adam_epsilon)
    )
    return (weight - rate_small * (ratio + decay_rate * weight), first_new, second_new)


def smem():
    return pl.BlockSpec(memory_space=pltpu.SMEM)


def whole(shape):
    zeros = (0,) * len(shape)
    return pl.BlockSpec(tuple(shape), lambda *_: zeros)


def params(mib=48):
    return pltpu.CompilerParams(vmem_limit_bytes=mib * MIB)


def remote(mib, identity):
    return pltpu.CompilerParams(
        vmem_limit_bytes=mib * MIB, collective_id=identity, has_side_effects=True
    )


def vmem():
    return pl.BlockSpec(memory_space=pltpu.VMEM)


def hbm():
    return pl.BlockSpec(memory_space=pl.ANY)


def each(count, act, start=1):
    def body(off, carry):
        act(off)
        return carry

    lax.fori_loop(start, count, body, 0)


def meet(axes):
    barrier = pltpu.get_barrier_semaphore()
    total = 0
    for axis in axes:
        count, me = lax.axis_size(axis), lax.axis_index(axis)
        total += count - 1
        each(
            count,
            lambda off: pl.semaphore_signal(barrier, inc=1, device_id={axis: (me + off) % count}),
        )
    pl.semaphore_wait(barrier, total)


class Spread:
    def __init__(self, group, source, target, sends, receives):
        self.count, self.me, self.where = group
        self.source, self.target = source, target
        self.sends, self.receives = sends, receives

    def copy(self, other, slot):
        return pltpu.make_async_remote_copy(
            src_ref=self.source(other),
            dst_ref=self.target(slot),
            send_sem=self.sends.at[other],
            recv_sem=self.receives.at[slot],
            device_id=self.where(other),
        )

    def other(self, off):
        return (self.me + off) % self.count

    def start(self, off):
        self.copy(self.other(off), self.me).start()

    def arrived(self, off):
        self.copy(self.other(off), self.other(off)).wait_recv()

    def sent(self, off):
        self.copy(self.other(off), self.me).wait_send()

    def all(self, act):
        each(self.count, getattr(self, act))


def along(axis):
    return lax.axis_size(axis), lax.axis_index(axis), lambda other: {axis: other}


def pairs():
    node = lax.axis_index("node")
    place, pair = node % 2, node // 2
    within = (2, place, lambda other: {"node": 2 * pair + other})
    across = (lax.axis_size("node") // 2, pair, lambda other: {"node": 2 * other + place})
    return within, across


def encode_kernel(
    place_ref, scale_ref, node_ref, prev_ref, target_ref, eps_ref, w_ref, in_ref, stat_ref, own_ref, all_ref,
    pix, box, pair_box, sems, pair_sems
):
    step = pl.program_id(0)
    rows = in_ref.shape[0]
    tile = node_ref.shape[1]
    within, across = pairs()
    place = within[1]
    weights = Spread(across, lambda _: w_ref, lambda i: box.at[i], sems.at[0], sems.at[1])
    swap = pltpu.make_async_remote_copy(
        src_ref=box,
        dst_ref=pair_box,
        send_sem=pair_sems.at[0],
        recv_sem=pair_sems.at[1],
        device_id=within[2](1 - place),
    )

    @pl.when(step == 0)
    def _():
        meet(["node"])
        weights.all("start")
        box[weights.me] = w_ref[...]
        pix[...] = jnp.zeros_like(pix)
        in_ref[...] = jnp.zeros_like(in_ref)
        stat_ref[...] = jnp.zeros_like(stat_ref)

    @pl.when(step == pl.num_programs(0) - 2)
    def _():
        weights.all("arrived")
        swap.start()

    prev = prev_ref[...]
    target = target_ref[...]
    noisy = target + scale_ref[0] * eps_ref[...]
    pix[:VARS] = prev.astype(bf16)
    pix[SLOT : SLOT + VARS] = (scale_ref[1] * noisy).astype(bf16)
    node = node_ref[...] - place_ref[0]
    mine = node - place_ref[1]
    spot = lax.broadcasted_iota(jnp.int32, (rows, tile), 0)
    onehot = (spot == mine).astype(f32).astype(bf16)
    in_ref[...] += contract(onehot, pix[...], 1, 1)
    valid = (node < place_ref[2]).astype(f32)
    residual = target - prev
    stat_ref[:VARS] += fold_lanes(valid * residual * residual)
    stat_ref[SLIM - 1 : SLIM] += fold_lanes(valid)

    @pl.when(step == pl.num_programs(0) - 1)
    def _():
        swap.wait()
        own_ref[...] = box[...]
        all_ref[:, place] = box[...]
        all_ref[:, 1 - place] = pair_box[...]
        weights.all("sent")


def encode(place, scales, node_row, prev, target, eps, w_share, rows, tile, nodes):
    pixels = prev.shape[1]
    column = (nodes // 2, *w_share.shape)
    gathered = (nodes // 2, 2, *w_share.shape)
    pixel_block = pl.BlockSpec((VARS, tile), lambda i: (0, i))
    return pl.pallas_call(
        encode_kernel,
        grid=(pixels // tile,),
        in_specs=[smem(), smem(), pl.BlockSpec((1, tile), lambda i: (0, i))]
        + [pixel_block] * 3
        + [whole(w_share.shape)],
        out_specs=[whole((rows, 2 * SLOT)), whole((SLIM, 128)), whole(column), whole(gathered)],
        out_shape=[
            jax.ShapeDtypeStruct((rows, 2 * SLOT), f32),
            jax.ShapeDtypeStruct((SLIM, 128), f32),
            jax.ShapeDtypeStruct(column, bf16),
            jax.ShapeDtypeStruct(gathered, bf16),
        ],
        scratch_shapes=[
            pltpu.VMEM((2 * SLOT, tile), bf16),
            pltpu.VMEM(column, bf16),
            pltpu.VMEM(column, bf16),
            pltpu.SemaphoreType.DMA((2, nodes // 2)),
            pltpu.SemaphoreType.DMA((2,)),
        ],
        compiler_params=remote(48, 2),
        name="encode",
    )(place, scales, node_row, prev, target, eps, w_share)


def count_tile(band_rows, spot_rows, put, bands):
    lane = lax.broadcasted_iota(jnp.int32, (GROUP, 256), 1)
    sub = lax.broadcasted_iota(jnp.int32, (GROUP, 256), 0)
    own = lane % GROUP == sub
    widen = (lane // GROUP == sub).astype(f32).astype(bf16)
    all_bands = contract(band_rows, widen, 0, 0)
    all_spots = contract(spot_rows, widen, 0, 0)
    spot = lax.broadcasted_iota(jnp.int32, (256, 256), 0).astype(f32)
    for g in range(band_rows.shape[1] // GROUP):
        nodes = slice(g * GROUP, (g + 1) * GROUP)
        band = jnp.where(own, all_bands[nodes], -1.0)
        left = jnp.concatenate([(band == t).astype(f32).astype(bf16) for t in range(bands)], 0)
        row = jnp.sum(jnp.where(own, all_spots[nodes], 0.0), 0, keepdims=True)
        right = (spot == row).astype(f32).astype(bf16)
        found = contract(left, right, 1, 1).astype(bf16)
        for t in range(bands):
            put(g, t, found[t * GROUP : (t + 1) * GROUP])


def nearest_first(me, count):
    if count == 4:
        return [me + 1 - 2 * (me % 2), (me + 2) % 4, 3 - me]
    return [(me + k) % count for k in range(1, count)]


def open_kernel(
    in_ref, wenc_ref, mod_ref, stat_ref, w_ref, nbr_ref, live_ref,
    zero_ref, norm_ref, q_ref, kv_ref, sum_ref, count_ref,
    stat_own, stat_box, bands, spots, tiles, head_sems, stat_sems, halo_sems, out_sems,
):
    heads, rows, _ = norm_ref.shape
    head, node = lax.axis_index("head"), lax.axis_index("node")
    groups = lax.axis_size("node")
    depth = tiles.shape[1]
    nodes = count_ref.shape[0]
    steps = nodes // depth
    stat_own[...] = jnp.broadcast_to(jnp.sum(stat_ref[...], 1, keepdims=True), stat_own.shape)
    meet(["head", "node"])

    stats = Spread(along("node"), lambda _: stat_own, lambda i: stat_box.at[i], stat_sems.at[0], stat_sems.at[1])
    stats.all("start")
    w_enc = wenc_ref[...]
    h_zero = sum(contract(part, w_enc, 1, 0) for part in thirds(in_ref[...]))
    zero_ref[...] = h_zero
    normed, _ = standardize(h_zero)
    norm_ref[head] = (normed * (1 + mod_ref[0:1]) + mod_ref[1:2]).astype(bf16)
    norms = Spread(
        along("head"), lambda _: norm_ref.at[head], lambda i: norm_ref.at[i], head_sems.at[0], head_sems.at[1]
    )
    near = nearest_first(head, heads)
    for other in near[:2]:
        norms.copy(other, head).start()

    def halo(block):
        return [
            pltpu.make_async_remote_copy(
                src_ref=kv_ref.at[1, block],
                dst_ref=kv_ref.at[2 * side, block],
                send_sem=halo_sems.at[2 * side, block],
                recv_sem=halo_sems.at[2 * side + 1, block],
                device_id={"node": (node + by) % groups},
            )
            for side, by in enumerate((1, groups - 1))
        ]

    def project(block):
        out = contract(norm_ref[block], w_ref[:, : 3 * HD], 1, 0).astype(bf16)
        q_ref[block] = out[:, :HD]
        kv_ref[1, block] = out[:, HD:]
        for copy in halo(block):
            copy.start()

    def count(step):
        slot = step % 2

        @pl.when(step >= 2)
        def _():
            count_out(step - 2).wait()

        here = pl.ds(pl.multiple_of(step * depth, depth), depth)

        def put(g, t, found):
            tiles[slot, g * GROUP : (g + 1) * GROUP, t * 256 : (t + 1) * 256] = found

        count_tile(bands[:, here], spots[:, here], put, tiles.shape[2] // 256)
        count_out(step).start()

    def count_out(step):
        return pltpu.make_async_copy(
            tiles.at[step % 2],
            count_ref.at[pl.ds(pl.multiple_of(step * depth, depth), depth)],
            out_sems.at[step % 2],
        )

    project(head)
    total = nodes * groups
    relative = nbr_ref[...] - node * nodes + nodes
    relative = jnp.where(relative >= total, relative - total, relative)
    relative = jnp.where(relative < 0, relative + total, relative)
    live = lax.broadcasted_iota(jnp.int32, relative.shape, 0) < live_ref[...]
    bands[...] = jnp.where(live, relative >> 8, -1).astype(f32).astype(bf16)
    spots[...] = (relative & 255).astype(f32).astype(bf16)
    each(steps // 4, count, 0)

    norms.copy(near[0], near[0]).wait_recv()
    for other in near[2:]:
        norms.copy(other, head).start()
    project(near[0])
    norms.copy(near[1], near[1]).wait_recv()
    project(near[1])
    each(steps * 5 // 8, count, steps // 4)
    for other in near[2:]:
        norms.copy(other, other).wait_recv()
        project(other)
    each(steps, count, steps * 5 // 8)
    each(steps, lambda step: count_out(step).wait(), steps - 2)
    stats.all("arrived")
    sum_ref[...] = sum(jnp.where(t == node, stat_own[...], stat_box[t]) for t in range(groups))

    def finish(block):
        for copy in halo(block):
            copy.wait()

    each(heads, finish, 0)
    norms.all("sent")
    stats.all("sent")


def open_nodes(node_in, w_enc, modulation, stat, w_attn, neighbours, live, heads, groups):
    rows, width = node_in.shape[0], w_enc.shape[1]
    depth = 8 * GROUP
    reach = 3 * heads * rows
    block = lambda w: jax.ShapeDtypeStruct((heads, rows, w), bf16)
    return pl.pallas_call(
        open_kernel,
        in_specs=[vmem()] * 7,
        out_specs=[vmem()] * 5 + [pl.BlockSpec(memory_space=pl.ANY)],
        out_shape=[
            jax.ShapeDtypeStruct((rows, width), f32),
            block(width),
            block(HD),
            jax.ShapeDtypeStruct((3, heads, rows, 2 * HD), bf16),
            jax.ShapeDtypeStruct((SLIM, 128), f32),
            jax.ShapeDtypeStruct((heads * rows, reach), bf16),
        ],
        scratch_shapes=[
            pltpu.VMEM((SLIM, 128), f32),
            pltpu.VMEM((groups, SLIM, 128), f32),
            pltpu.VMEM((NBR, heads * rows), bf16),
            pltpu.VMEM((NBR, heads * rows), bf16),
            pltpu.VMEM((2, depth, reach), bf16),
            pltpu.SemaphoreType.DMA((2, heads)),
            pltpu.SemaphoreType.DMA((2, groups)),
            pltpu.SemaphoreType.DMA((4, heads)),
            pltpu.SemaphoreType.DMA((2,)),
        ],
        compiler_params=remote(56, 3),
        name="open_nodes",
    )(node_in, w_enc, modulation, stat, w_attn, neighbours, live)


def attend_kernel(
    q_ref, kv_ref, count_ref, column_ref, ffn_ref, e_ref, mix_ref, out_ref, attn_all, ffn_all, s_scr, own, box, sems,
    attn_sems, column_sems, ffn_sems, pair_sems, local_sems, chunk
):
    step = pl.program_id(0)
    steps = pl.num_programs(0)
    head = lax.axis_index("head")
    tile = q_ref.shape[0]
    per = box.shape[1] // tile

    def copy(target, source, part):
        at = pl.ds(pl.multiple_of(part * tile, tile), tile)
        return pltpu.make_async_remote_copy(
            src_ref=own.at[target, at],
            dst_ref=box.at[source, at],
            send_sem=sems.at[0, target, part],
            recv_sem=sems.at[1, source, part],
            device_id={"head": target},
        )

    within, across = pairs()
    place, pair = within[1], across[1]
    attn_heads = Spread(
        along("head"), lambda _: column_ref, lambda i: attn_all.at[i, :, place], attn_sems.at[0], attn_sems.at[1]
    )
    ffn_pairs = Spread(
        across, lambda _: ffn_ref, lambda i: ffn_all.at[head, i, place], column_sems.at[0], column_sems.at[1]
    )
    ffn_heads = Spread(
        along("head"),
        lambda _: ffn_all.at[head, :, place],
        lambda i: ffn_all.at[i, :, place],
        ffn_sems.at[0],
        ffn_sems.at[1],
    )
    stay = [
        pltpu.make_async_copy(column_ref, attn_all.at[head, :, place], local_sems.at[0]),
        pltpu.make_async_copy(ffn_ref, ffn_all.at[head, pair, place], local_sems.at[1]),
    ]

    def swap(h, which, side):
        array = (attn_all, ffn_all)[which]
        return pltpu.make_async_remote_copy(
            src_ref=array.at[h, :, side],
            dst_ref=array.at[h, :, side],
            send_sem=pair_sems.at[0, which, h],
            recv_sem=pair_sems.at[1, which, h],
            device_id=within[2](1 - place),
        )

    @pl.when(step == 0)
    def _():
        meet(["head", "node"])
        ffn_pairs.all("start")
        attn_heads.all("start")
        for copy in stay:
            copy.start()

    @pl.when(step == steps * 5 // 16)
    def _():
        ffn_pairs.all("arrived")
        for copy in stay:
            copy.wait()
        ffn_heads.all("start")

    @pl.when(step == steps * 14 // 16)
    def _():
        attn_heads.all("arrived")
        ffn_heads.all("arrived")

        def begin(h):
            for which in range(2):
                swap(h, which, place).start()

        each(box.shape[0], begin, 0)

    nodes = kv_ref.shape[1]
    q = q_ref[...]
    top = jnp.full((tile, 128), -1e30, f32)
    for b in range(3):
        for at in range(0, nodes, chunk):
            cols = slice(b * nodes + at, b * nodes + at + chunk)
            s = contract(q, kv_ref[b, at : at + chunk, :HD], 1, 1)
            s = jnp.where(count_ref[:, cols].astype(f32) > 0, s, -1e30)
            s_scr[:, cols] = s
            top = jnp.maximum(top, fold_lanes(s, jnp.maximum))
    top = jnp.max(top, 1, keepdims=True)
    factor = math.log2(math.e) / math.sqrt(HD)
    total = jnp.zeros((tile, 128), f32)
    mixed = jnp.zeros((tile, HD), f32)
    for b in range(3):
        for at in range(0, nodes, chunk):
            cols = slice(b * nodes + at, b * nodes + at + chunk)
            e = count_ref[:, cols].astype(f32) * jnp.exp2((s_scr[:, cols] - top) * factor)
            total += fold_lanes(e)
            e = e.astype(bf16)
            e_ref[:, cols] = e
            mixed += contract(e, kv_ref[b, at : at + chunk, HD:], 1, 0)
    inverse = 1.0 / jnp.sum(total, 1, keepdims=True)
    mixed = mixed * inverse
    mix_ref[:, :HD] = mixed
    mix_ref[:, HD:] = jnp.broadcast_to(inverse, (tile, HD))
    target, part = step // per, step % per
    at = pl.ds(pl.multiple_of(part * tile, tile), tile)
    low = mixed.astype(bf16)
    own[target, at] = low

    @pl.when(target == head)
    def _():
        box[head, at] = low

    @pl.when(target != head)
    def _():
        copy(target, head, part).start()

    @pl.when(step == steps - 1)
    def _():
        heads = box.shape[0]

        def finish(off):
            other = (head + off) % heads
            for p in range(per):
                copy(other, other, p).wait_recv()
                copy(other, head, p).wait_send()

        each(heads, finish)
        out_ref[...] = box[...]

        def end(h):
            for which in range(2):
                swap(h, which, place).wait_send()
                swap(h, which, 1 - place).wait_recv()

        each(heads, end, 0)
        for spread in (attn_heads, ffn_pairs, ffn_heads):
            spread.all("sent")


def attend(query, keyval, counts, column, ffn_share, heads, tile, chunk):
    nodes, reach = counts.shape
    rows = nodes // heads
    count = column.shape[0]
    dma = lambda *shape: pltpu.SemaphoreType.DMA(shape)
    row = lambda width: pl.BlockSpec((tile, width), lambda i: (i, 0))
    return pl.pallas_call(
        functools.partial(attend_kernel, chunk=chunk),
        grid=(nodes // tile,),
        in_specs=[row(HD), whole(keyval.shape), row(reach), hbm(), hbm()],
        out_specs=[row(reach), row(2 * HD), whole((heads, rows, HD)), hbm(), hbm()],
        out_shape=[
            jax.ShapeDtypeStruct((nodes, reach), bf16),
            jax.ShapeDtypeStruct((nodes, 2 * HD), f32),
            jax.ShapeDtypeStruct((heads, rows, HD), bf16),
            jax.ShapeDtypeStruct((heads, count, 2, *column.shape[1:]), bf16),
            jax.ShapeDtypeStruct((heads, count, 2, *ffn_share.shape), bf16),
        ],
        scratch_shapes=[
            pltpu.VMEM((tile, reach), f32),
            pltpu.VMEM((heads, rows, HD), bf16),
            pltpu.VMEM((heads, rows, HD), bf16),
            dma(2, heads, rows // tile),
            dma(2, heads),
            dma(2, count),
            dma(2, heads),
            dma(2, 2, heads),
            dma(2),
        ],
        compiler_params=remote(60, 4),
        name="attend",
    )(query, keyval, counts, column, ffn_share)


def attend_back_kernel(
    q_ref, d_ref, mix_ref, e_ref, kv_ref, norm_ref, pair_sum,
    dq_ref, dkv_ref, grad_ref, share_ref, full_ref,
    dk, dv, dq, low_own, high_own, low_box, high_box, dq_own, dq_box, dkv_own, dkv_box,
    head_box, across_own, across_box, share_low, full,
    halo_sems, dq_sems, dkv_sems, pair_sems, head_sems, across_sems, full_sems,
    chunk,
):
    turn, part = pl.program_id(0), pl.program_id(1)
    parts = pl.num_programs(1)
    step = turn * parts + part
    tile = q_ref.shape[0]
    nodes = kv_ref.shape[1]
    heads, rows, _ = dq_box.shape
    per = rows // tile
    head, node, groups = lax.axis_index("head"), lax.axis_index("node"), lax.axis_size("node")
    within, across = pairs()
    last = part == parts - 1

    place, pair = within[1], across[1]
    over_heads = Spread(
        along("head"), lambda o: pair_sum.at[o], lambda i: head_box.at[i], head_sems.at[0], head_sems.at[1]
    )
    over_pairs = Spread(
        across, lambda o: across_own.at[o], lambda i: across_box.at[i], across_sems.at[0], across_sems.at[1]
    )
    over_full = Spread(
        across, lambda _: share_low, lambda i: full.at[place, i], full_sems.at[0], full_sems.at[1]
    )
    count = across[0]

    def swap(side):
        return pltpu.make_async_remote_copy(
            src_ref=full.at[side],
            dst_ref=full.at[side],
            send_sem=pair_sems.at[0],
            recv_sem=pair_sems.at[1],
            device_id=within[2](1 - place),
        )

    def halo(own, box, side, by):
        return pltpu.make_async_remote_copy(
            src_ref=own,
            dst_ref=box,
            send_sem=halo_sems.at[0, side],
            recv_sem=halo_sems.at[1, side],
            device_id={"node": (node + by) % groups},
        )

    to_below = halo(low_own, low_box, 0, groups - 1)
    to_above = halo(high_own, high_box, 1, 1)

    def dq_copy(target, source, piece):
        at = pl.ds(pl.multiple_of(piece * tile, tile), tile)
        return pltpu.make_async_remote_copy(
            src_ref=dq_own.at[target, at],
            dst_ref=dq_box.at[source, at],
            send_sem=dq_sems.at[0, target, piece],
            recv_sem=dq_sems.at[1, source, piece],
            device_id={"head": target},
        )

    dkv_spread = Spread(
        along("head"), lambda o: dkv_own.at[o], lambda i: dkv_box.at[i], dkv_sems.at[0], dkv_sems.at[1]
    )

    @pl.when(step == 0)
    def _():
        meet(["head", "node"])
        over_heads.all("start")
        head_box[head] = pair_sum[head]

    @pl.when(step == HEAD_STEP)
    def _():
        over_heads.all("arrived")

        def add(z):
            across_own[z] = sum(head_box[h, z].astype(f32) for h in range(heads)).astype(bf16)

        each(count, add, 0)
        over_pairs.all("start")
        across_box[across[1]] = across_own[across[1]]

    @pl.when(part == 0)
    def _():
        dk[...] = jnp.zeros_like(dk)
        dv[...] = jnp.zeros_like(dv)

    grad = d_ref[...]
    wide = grad.astype(f32)
    inverse = mix_ref[:, HD : HD + 1]
    delta = jnp.sum(wide * mix_ref[:, :HD], 1, keepdims=True)
    gain = inverse * (1.0 / math.sqrt(HD))
    q_turned = q_ref[...].T
    d_turned = (wide * inverse).astype(bf16).T
    here = pl.ds(pl.multiple_of(part * tile, tile), tile)
    dq_here = jnp.where(turn == 0, 0.0, dq[here])
    for at in range(0, nodes, chunk):
        cols = slice(at, at + chunk)
        dp = contract(grad, kv_ref[0, cols, HD:], 1, 1)
        e = e_ref[:, cols]
        ds = (e.astype(f32) * ((dp - delta) * gain)).astype(bf16)
        dq_here += contract(ds, kv_ref[0, cols, :HD], 1, 0)
        dk[:, cols] += contract(q_turned, ds, 1, 0)
        dv[:, cols] += contract(d_turned, e, 1, 0)
    dq[here] = dq_here

    for which, own, copy in ((0, low_own, to_below), (1, high_own, to_above)):

        @pl.when(last & (turn == which))
        def _(own=own, copy=copy):
            own[:HD] = dk[...].astype(bf16)
            own[HD:] = dv[...].astype(bf16)
            copy.start()

    @pl.when(turn == 2)
    def _():
        target, piece = part // per, part % per
        at = pl.ds(pl.multiple_of(piece * tile, tile), tile)
        low = dq_here.astype(bf16)
        dq_own[target, at] = low

        @pl.when(target == head)
        def _():
            dq_box[head, at] = low

        @pl.when(target != head)
        def _():
            dq_copy(target, head, piece).start()

    @pl.when(last & (turn == 2))
    def _():
        to_below.wait()
        to_above.wait()
        for h in range(heads):
            cols = slice(h * rows, (h + 1) * rows)
            for half, acc in enumerate((dk, dv)):
                lines = slice(half * HD, (half + 1) * HD)
                total = acc[:, cols] + low_box[lines, cols].astype(f32) + high_box[lines, cols].astype(f32)
                dkv_own[h, lines] = total.astype(bf16)
        dkv_spread.all("start")
        dkv_box[head] = dkv_own[head]
        over_pairs.all("arrived")
        total = sum(across_box[z].astype(f32) for z in range(count))
        share_ref[...] = total
        share_low[...] = total.astype(bf16)
        over_full.all("start")
        full[place, pair] = total.astype(bf16)
        grad_q = sum(
            contract(norm_ref[h * rows : (h + 1) * rows], dq_own[h], 0, 0) for h in range(heads)
        )
        grad_kv = sum(
            contract(dkv_own[h], norm_ref[h * rows : (h + 1) * rows], 1, 0) for h in range(heads)
        )
        grad_ref[:, :HD] = grad_q
        grad_ref[:, HD:] = grad_kv.T

        def finish(off):
            other = (head + off) % heads
            for p in range(per):
                dq_copy(other, other, p).wait_recv()
                dq_copy(other, head, p).wait_send()

        each(heads, finish)
        over_full.all("arrived")
        swap(place).start()
        dkv_spread.all("arrived")
        dq_ref[...] = dq_box[...]
        dkv_ref[...] = dkv_box[...]
        swap(place).wait_send()
        swap(1 - place).wait_recv()
        for c in range(2):
            for z in range(count):
                full_ref[z, c] = full[c, z]
        for spread in (dkv_spread, over_heads, over_pairs, over_full):
            spread.all("sent")


def attend_back(query, grad, mix, e, keyval, norm_all, pair_sum, heads, tile, chunk):
    nodes, reach = e.shape
    rows, width = nodes // heads, norm_all.shape[1]
    parts = nodes // tile
    _, count, share, across = pair_sum.shape
    row = lambda width: pl.BlockSpec((tile, width), lambda j, i: (i, 0))
    pair = (heads, count, share, across)
    dma = lambda *shape: pltpu.SemaphoreType.DMA(shape)
    order = lambda j: 2 * j % 3
    return pl.pallas_call(
        functools.partial(attend_back_kernel, chunk=chunk),
        grid=(3, parts),
        in_specs=[
            row(HD),
            row(HD),
            row(2 * HD),
            pl.BlockSpec((tile, nodes), lambda j, i: (i, order(j))),
            pl.BlockSpec((1, nodes, 2 * HD), lambda j, i: (order(j), 0, 0)),
            vmem(),
            vmem(),
        ],
        out_specs=[
            whole((heads, rows, HD)),
            whole((heads, 2 * HD, rows)),
            whole((width, 3 * HD)),
            whole((share, across)),
            whole((count, 2, share, across)),
        ],
        out_shape=[
            jax.ShapeDtypeStruct((heads, rows, HD), bf16),
            jax.ShapeDtypeStruct((heads, 2 * HD, rows), bf16),
            jax.ShapeDtypeStruct((width, 3 * HD), f32),
            jax.ShapeDtypeStruct((share, across), f32),
            jax.ShapeDtypeStruct((count, 2, share, across), bf16),
        ],
        scratch_shapes=[
            pltpu.VMEM((HD, nodes), f32),
            pltpu.VMEM((HD, nodes), f32),
            pltpu.VMEM((nodes, HD), f32),
            *[pltpu.VMEM((2 * HD, nodes), bf16)] * 4,
            *[pltpu.VMEM((heads, rows, HD), bf16)] * 2,
            *[pltpu.VMEM((heads, 2 * HD, rows), bf16)] * 2,
            pltpu.VMEM(pair, bf16),
            *[pltpu.VMEM(pair[1:], bf16)] * 2,
            pltpu.VMEM((share, across), bf16),
            pltpu.VMEM((2, *pair[1:]), bf16),
            dma(2, 2),
            dma(2, heads, rows // tile),
            dma(2, heads),
            dma(2),
            dma(2, heads),
            dma(2, count),
            dma(2, count),
        ],
        compiler_params=remote(60, 5),
        name="attend_back",
    )(query, grad, mix, e, keyval, norm_all, pair_sum)


def middle_kernel(
    place_ref, scale_ref, mixed_ref, zero_ref, wa_ref, wf_ref, mod_ref, wdec_ref, weight_ref,
    node_ref, read_ref, target_ref, eps_ref,
    done_ref, dmix_ref, pair_ref, gdec_ref, gmod_ref, loss_ref,
    one_scr, two_scr, norm_scr, up_scr, act_scr, dec_box, hits, turned, total,
    d_own, d_box, dmix_own, dmix_box, grad, big, pair_box,
    dec_sems, d_sems, dmix_sems, pair_sems, out_sems,
    node_tiles, pixel_tiles,
):
    step = pl.program_id(0)
    heads, rows, _ = mixed_ref.shape
    width = zero_ref.shape[1]
    tile = rows // node_tiles
    head = lax.axis_index("head")
    within, _ = pairs()
    place = within[1]
    count, share = pair_ref.shape[1:3]
    pixel_end = node_tiles + pixel_tiles
    others = nearest_first(head, heads)

    def dec_copy(other, slot, t):
        cols = pl.ds(t * tile, tile)
        return pltpu.make_async_remote_copy(
            src_ref=dec_box.at[head, :, cols],
            dst_ref=dec_box.at[slot, :, cols],
            send_sem=dec_sems.at[0, other, t],
            recv_sem=dec_sems.at[1, slot, t],
            device_id={"head": other},
        )

    d_spread = Spread(along("head"), lambda o: d_own.at[o], lambda i: d_box.at[i], d_sems.at[0], d_sems.at[1])

    def dmix_copy(other, slot, t):
        lines = pl.ds(t * tile, tile)
        return pltpu.make_async_remote_copy(
            src_ref=dmix_own.at[other, lines],
            dst_ref=dmix_box.at[slot, lines],
            send_sem=dmix_sems.at[0, other, t],
            recv_sem=dmix_sems.at[1, slot, t],
            device_id={"head": other},
        )

    def pair_copy(h, part):
        cols = (pl.ds(0, 2 * width), pl.ds(2 * width, HD))[part]
        return pltpu.make_async_remote_copy(
            src_ref=big.at[1 - place, h, :, :, cols],
            dst_ref=pair_box.at[h, :, :, cols],
            send_sem=pair_sems.at[0, part, h],
            recv_sem=pair_sems.at[1, part, h],
            device_id=within[2](1 - place),
        )

    def pack(h, cols):
        for c in range(2):
            for z in range(count):
                at = (2 * z + c) * share
                big[c, h, z, :, cols] = grad[h, at : at + share, cols].astype(bf16)

    @pl.when(step == 0)
    def _():
        meet(["head", "node"])
        turned[...] = jnp.zeros_like(turned)
        total[...] = jnp.zeros_like(total)
        loss_ref[...] = jnp.zeros_like(loss_ref)
        gdec_ref[...] = jnp.zeros_like(gdec_ref)
        gmod_ref[...] = jnp.zeros_like(gmod_ref)

    for t in range(node_tiles):

        @pl.when(step == t)
        def _(t=t, lines=slice(t * tile, (t + 1) * tile)):
            h_one = zero_ref[lines] + sum(
                contract(mixed_ref[h, lines], wa_ref[h, :, 3 * HD :], 1, 1) for h in range(heads)
            )
            one_scr[lines] = h_one
            normed, _ = standardize(h_one)
            norm_two = (normed * (1 + mod_ref[2:3]) + mod_ref[3:4]).astype(bf16)
            norm_scr[lines] = norm_two
            h_two = h_one
            for h in range(heads):
                up = contract(norm_two, wf_ref[h, :, :width], 1, 0)
                up_scr[h, lines] = up
                act = (up * jax.nn.sigmoid(up)).astype(bf16)
                act_scr[h, lines] = act
                h_two = h_two + contract(act, wf_ref[h, :, width:], 1, 1)
            two_scr[lines] = h_two
            final = standardize(h_two)[0].astype(bf16)
            high, low = halves(contract(wdec_ref[...], final, 1, 1))
            dec_box[head, :SLIM, lines] = high
            dec_box[head, SLIM:, lines] = low
            for other in others:
                dec_copy(other, head, t).start()

    @pl.when((step >= node_tiles) & (step < pixel_end))
    def _():
        reads = read_ref[...] - place_ref[0]
        pixels = target_ref.shape[1]
        for h in range(heads):
            spot = lax.broadcasted_iota(jnp.int32, (rows, pixels), 0) + h * rows
            hit = sum((spot == reads[k : k + 1]).astype(f32) for k in range(3)).astype(bf16)
            hits[h * rows : (h + 1) * rows] = hit

        @pl.when(step == node_tiles)
        def _():
            for other in others:
                for t in range(node_tiles):
                    dec_copy(other, other, t).wait_recv()

        field = sum(contract(dec_box[h], hits[h * rows : (h + 1) * rows], 1, 0) for h in range(heads))
        field = (field[:VARS] + field[SLIM : SLIM + VARS]) / 3.0
        target = target_ref[...]
        noisy = target + scale_ref[0] * eps_ref[...]
        error = scale_ref[2] * noisy + scale_ref[3] * field - target
        valid = (node_ref[...] - place_ref[0] < place_ref[2]).astype(f32)
        weighted = valid * weight_ref[:, 0:1]
        loss_ref[:VARS] += fold_lanes(weighted * error * error)
        high, low = halves(scale_ref[4] * weighted * error)
        turned[:VARS] = high
        turned[SLOT : SLOT + VARS] = low
        total[...] += contract(hits[...], turned[...], 1, 1)

    @pl.when(step == pixel_end - 1)
    def _():
        for h in range(heads):
            lines = slice(h * rows, (h + 1) * rows)
            d_own[h] = (total[lines, :SLOT] + total[lines, SLOT:]).astype(bf16)
        for other in others:
            d_spread.copy(other, head).start()
        d_box[head] = d_own[head]

    for t in range(node_tiles):
        final_tile = t == node_tiles - 1

        @pl.when(step == pixel_end + t)
        def _(t=t, lines=slice(t * tile, (t + 1) * tile), final_tile=final_tile):
            normed_two, inv_two = standardize(two_scr[lines])
            final = normed_two.astype(bf16)
            normed_one, inv_one = standardize(one_scr[lines])
            if t == 0:
                for other in others:
                    d_spread.copy(other, other).wait_recv()
            d_dec = sum(d_box[h, lines].astype(f32) for h in range(heads)).astype(bf16)[:, :SLIM]
            gdec_ref[...] += contract(d_dec, final, 0, 0)
            d_two = norm_back(normed_two, inv_two, contract(d_dec, wdec_ref[...], 1, 0))
            d_low = d_two.astype(bf16)
            norm_two = norm_scr[lines]
            d_mid = jnp.zeros_like(d_two)

            def add(h, cols, value):
                if t == 0:
                    grad[h, :, cols] = value
                else:
                    grad[h, :, cols] += value

            for h in range(heads):
                up = up_scr[h, lines]
                d_act = contract(d_low, wf_ref[h, :, width:], 1, 0)
                gating = jax.nn.sigmoid(up)
                d_up = (d_act * gating * (1 + up * (1 - gating))).astype(bf16)
                add(h, slice(0, width), contract(norm_two, d_up, 0, 0))
                add(h, slice(width, 2 * width), contract(d_low, act_scr[h, lines], 0, 0))
                if final_tile:
                    pack(h, slice(0, 2 * width))
                    pair_copy(h, 0).start()
                d_mid += contract(d_up, wf_ref[h, :, :width], 1, 1)
            gmod_ref[0:1] += jnp.sum(d_mid * normed_one, 0, keepdims=True)
            gmod_ref[1:2] += jnp.sum(d_mid, 0, keepdims=True)
            d_one = d_two + norm_back(normed_one, inv_one, d_mid * (1 + mod_ref[2:3]))
            done_ref[lines] = d_one
            one_low = d_one.astype(bf16)
            for h in range(heads):
                dmix_own[h, lines] = contract(one_low, wa_ref[h, :, 3 * HD :], 1, 0).astype(bf16)
            for other in others:
                dmix_copy(other, head, t).start()
            dmix_box[head, lines] = dmix_own[head, lines]
            for h in range(heads):
                add(h, slice(2 * width, 2 * width + HD), contract(one_low, mixed_ref[h, lines], 0, 0))
                if final_tile:
                    pack(h, slice(2 * width, 2 * width + HD))
                    pair_copy(h, 1).start()
            if final_tile:
                for h in range(heads):
                    for part in range(2):
                        pair_copy(h, part).wait_recv()
                    for z in range(count):
                        pair_ref[h, z] = (
                            big[place, h, z].astype(f32) + pair_box[h, z].astype(f32)
                        ).astype(bf16)
                for other in others:
                    for u in range(node_tiles):
                        dmix_copy(other, other, u).wait_recv()
                dmix_ref[...] = dmix_box[...]
                for other in others:
                    d_spread.copy(other, head).wait_send()
                    for u in range(node_tiles):
                        dec_copy(other, head, u).wait_send()
                        dmix_copy(other, head, u).wait_send()
                for h in range(heads):
                    for part in range(2):
                        pair_copy(h, part).wait_send()


def middle(place, scales, mixed, h_zero, w_attn, w_ffn, modulation, w_dec, weight, node_row, read_rows, target, eps, groups):
    heads, rows, _ = mixed.shape
    width = h_zero.shape[1]
    node_tiles, pixels = 2, target.shape[1] // heads
    tile = 512
    pixel_tiles = pixels // tile
    share, count = width // groups, groups // 2
    grads = 2 * width + HD
    pair = (heads, count, share, grads)
    low = lambda *shape: pltpu.VMEM(shape, bf16)
    full = lambda *shape: pltpu.VMEM(shape, f32)
    dma = lambda *shape: pltpu.SemaphoreType.DMA(shape)

    def at(i):
        part = jnp.clip(i - node_tiles, 0, pixel_tiles - 1)
        return 0, lax.axis_index("head") * pixel_tiles + part

    piece = lambda lines: pl.BlockSpec((lines, tile), at)
    return pl.pallas_call(
        functools.partial(middle_kernel, node_tiles=node_tiles, pixel_tiles=pixel_tiles),
        grid=(2 * node_tiles + pixel_tiles,),
        in_specs=[smem(), smem()] + [vmem()] * 7 + [piece(1), piece(3), piece(VARS), piece(VARS)],
        out_specs=[
            whole((rows, width)),
            whole((heads, rows, HD)),
            whole(pair),
            whole((SLIM, width)),
            whole((8, width)),
            whole((SLIM, 128)),
        ],
        out_shape=[
            jax.ShapeDtypeStruct((rows, width), f32),
            jax.ShapeDtypeStruct((heads, rows, HD), bf16),
            jax.ShapeDtypeStruct(pair, bf16),
            jax.ShapeDtypeStruct((SLIM, width), f32),
            jax.ShapeDtypeStruct((8, width), f32),
            jax.ShapeDtypeStruct((SLIM, 128), f32),
        ],
        scratch_shapes=[
            full(rows, width),
            full(rows, width),
            low(rows, width),
            full(heads, rows, width),
            low(heads, rows, width),
            low(heads, 2 * SLIM, rows),
            low(heads * rows, tile),
            low(2 * SLOT, tile),
            full(heads * rows, 2 * SLOT),
            low(heads, rows, SLOT),
            low(heads, rows, SLOT),
            low(heads, rows, HD),
            low(heads, rows, HD),
            full(heads, width, grads),
            low(2, *pair),
            low(*pair),
            dma(2, heads, node_tiles),
            dma(2, heads),
            dma(2, heads, node_tiles),
            dma(2, 2, heads),
            dma(2, heads),
        ],
        compiler_params=remote(62, 7),
        name="middle",
    )(
        place, scales, mixed, h_zero, w_attn, w_ffn, modulation, w_dec, weight, node_row, read_rows, target, eps
    )


def settle_kernel(
    feat_ref, dq_ref, dkv_ref, w_ref, zero_ref, done_ref, in_ref, mod_ref, gdec_ref, gmod_ref, qkv_ref, big_ref, loss_ref,
    small_ref, share_ref, full_ref, sums_ref,
    q_low, q_pair, q_sum, q_box, q_share, q_full,
    parts, part_box, part_sum, part_own, pay, heard, tally, tallies,
    pair_sems, q_sems, f_sems, a_sems, n_sems, b_sems, t_sems,
):
    heads, width = w_ref.shape[0], w_ref.shape[1]
    share_rows = share_ref.shape[0]
    head, node = lax.axis_index("head"), lax.axis_index("node")
    groups = heard.shape[0]
    within, across = pairs()
    place, pair, count = within[1], across[1], across[0]

    def to_other(source, target, index):
        return pltpu.make_async_remote_copy(
            src_ref=source,
            dst_ref=target,
            send_sem=pair_sems.at[0, index],
            recv_sem=pair_sems.at[1, index],
            device_id=within[2](1 - place),
        )

    for c in range(2):
        for z in range(count):
            at = (2 * z + c) * share_rows
            q_low[c, z] = qkv_ref[at : at + share_rows].astype(bf16)
    meet(["head", "node"])
    q_pairs = to_other(q_low.at[1 - place], q_pair, 0)
    q_pairs.start()

    d_norm = sum(
        contract(dq_ref[h], w_ref[h, :, :HD], 1, 1)
        + contract(dkv_ref[h], w_ref[h, :, HD : 3 * HD], 0, 1)
        for h in range(heads)
    )
    normed, inv = standardize(zero_ref[...])
    d_zero = done_ref[...] + norm_back(normed, inv, d_norm * (1 + mod_ref[0:1]))

    q_pairs.wait()
    for z in range(count):
        q_sum[z] = (q_low[place, z].astype(f32) + q_pair[z].astype(f32)).astype(bf16)
    q_over = Spread(across, lambda o: q_sum.at[o], lambda i: q_box.at[i], q_sems.at[0], q_sems.at[1])
    q_over.all("start")
    q_box[pair] = q_sum[pair]

    g_enc = contract(in_ref[...].T, d_zero, 1, 0, highest)
    parts[...] = jnp.zeros_like(parts)
    flat = parts.reshape(parts.shape[0] * parts.shape[1], width)
    flat[:VARS] = g_enc[:VARS]
    flat[VARS : 2 * VARS] = g_enc[SLOT : SLOT + VARS]
    flat[2 * VARS : 3 * VARS] = gdec_ref[:VARS]
    at = 3 * VARS
    flat[at : at + 1] = jnp.sum(d_norm * normed, 0, keepdims=True)
    flat[at + 1 : at + 2] = jnp.sum(d_norm, 0, keepdims=True)
    flat[at + 2 : at + 4] = gmod_ref[0:2]
    over_heads = Spread(
        along("head"), lambda o: parts.at[o], lambda i: part_box.at[i], a_sems.at[0], a_sems.at[1]
    )
    over_heads.all("start")
    part_box[head] = parts[head]

    q_over.all("arrived")
    share = sum(q_box[z].astype(f32) for z in range(count))
    share_ref[...] = share
    q_share[...] = share.astype(bf16)
    q_full[place, pair] = share.astype(bf16)
    f_over = Spread(
        across, lambda _: q_share, lambda i: q_full.at[place, i], f_sems.at[0], f_sems.at[1]
    )
    f_over.all("start")

    over_heads.all("arrived")
    total = sum(part_box[h] for h in range(heads))
    for t in range(groups):
        part_sum[t] = total[8 * t : 8 * t + 8]
    over_nodes = Spread(
        along("node"), lambda o: part_sum.at[o], lambda i: part_own.at[i], n_sems.at[0], n_sems.at[1]
    )
    over_nodes.all("start")
    part_own[node] = part_sum[node]

    squares = jnp.sum(share * share) + jnp.sum(big_ref[...] * big_ref[...])
    loss = jnp.sum(loss_ref[:VARS])
    over_nodes.all("arrived")
    own = sum(part_own[t] for t in range(groups))
    row = lax.broadcasted_iota(jnp.int32, own.shape, 0) + 8 * (head * groups + node)
    squares += jnp.sum(own * own * jnp.where(row >= 3 * VARS, feat_ref[0], 1.0))
    line = lax.broadcasted_iota(jnp.int32, (8, 128), 0)
    pay[:, :width] = own
    pay[:, width:] = jnp.where(line == 0, squares, jnp.where(line == 1, loss, 0.0))
    back = Spread(along("node"), lambda _: pay, lambda i: heard.at[i], b_sems.at[0], b_sems.at[1])
    back.all("start")
    heard[node] = pay[...]

    f_over.all("arrived")
    q_rest = to_other(q_full.at[place], q_full.at[place], 1)
    q_rest.start()

    back.all("arrived")
    tally[...] = sum(heard[t, :, width:] for t in range(groups))
    tell = Spread(along("head"), lambda _: tally, lambda i: tallies.at[i], t_sems.at[0], t_sems.at[1])
    tell.all("start")
    tallies[head] = tally[...]
    for t in range(groups):
        small_ref[8 * t : 8 * t + 8] = heard[t, :, :width]
    tell.all("arrived")
    sums_ref[...] = sum(tallies[h] for h in range(heads))

    q_rest.wait_send()
    to_other(q_full.at[1 - place], q_full.at[1 - place], 1).wait_recv()
    for c in range(2):
        for z in range(count):
            full_ref[2 * z + c] = q_full[c, z]
    for spread in (q_over, over_heads, f_over, over_nodes, back, tell):
        spread.all("sent")


def settle(feat_sq, dq, dkv, w_attn, h_zero, d_one, node_in, modulation, grad_dec, gmod_two, grad_qkv, big_share, loss, groups):
    heads, rows, _ = dq.shape
    width = h_zero.shape[1]
    count = groups // 2
    share = (grad_qkv.shape[0] // groups, grad_qkv.shape[1])
    low = lambda *shape: pltpu.VMEM(shape, bf16)
    full = lambda *shape: pltpu.VMEM(shape, f32)
    dma = lambda *shape: pltpu.SemaphoreType.DMA(shape)
    return pl.pallas_call(
        settle_kernel,
        in_specs=[smem()] + [vmem()] * 12,
        out_specs=[vmem()] * 4,
        out_shape=[
            jax.ShapeDtypeStruct((8 * groups, width), f32),
            jax.ShapeDtypeStruct(share, f32),
            jax.ShapeDtypeStruct((groups, *share), bf16),
            jax.ShapeDtypeStruct((8, 128), f32),
        ],
        scratch_shapes=[
            low(2, count, *share),
            low(count, *share),
            low(count, *share),
            low(count, *share),
            low(*share),
            low(2, count, *share),
            full(heads, 8 * groups, width),
            full(heads, 8 * groups, width),
            full(groups, 8, width),
            full(groups, 8, width),
            full(8, width + 128),
            full(groups, 8, width + 128),
            full(8, 128),
            full(heads, 8, 128),
            dma(2, 2),
            dma(2, count),
            dma(2, count),
            dma(2, heads),
            dma(2, groups),
            dma(2, groups),
            dma(2, heads),
        ],
        compiler_params=remote(56, 1),
        name="settle",
    )(feat_sq, dq, dkv, w_attn, h_zero, d_one, node_in, modulation, grad_dec, gmod_two, grad_qkv, big_share, loss)


def eliminate(work, done):
    count = work.shape[0]
    lane = lax.broadcasted_iota(jnp.int32, (1, BLOCK), 1)
    sub = lax.broadcasted_iota(jnp.int32, (STRIP, BLOCK), 0)
    pivots = [jnp.ones((1, BLOCK), f32) for _ in range(count)]
    both = lambda x: jnp.concatenate([x, x], 1)
    for at in range(0, BLOCK, STRIP):
        strip = slice(at, at + STRIP)
        rows = [work[m, strip] for m in range(count)]
        columns = [
            [jnp.broadcast_to(rows[m][:, at + k : at + k + 1], (STRIP, BLOCK)) for k in range(STRIP)]
            for m in range(count)
        ]
        scale = [jnp.ones((STRIP, BLOCK), f32) for _ in range(count)]
        for r in range(STRIP):
            for m in range(count):
                column = columns[m][r]
                pivot = jnp.broadcast_to(column[r : r + 1], (STRIP, BLOCK))
                factor = jnp.where(sub > r, column * (1.0 / pivot), 0.0)
                scale[m] = jnp.where(sub == r, pivot, scale[m])
                for k in range(r + 1, STRIP):
                    columns[m][k] = columns[m][k] - factor * columns[m][k][r : r + 1]
                pivots[m] = jnp.where(lane == at + r, pivot[:1], pivots[m])
                rows[m] = rows[m] - both(factor) * rows[m][r : r + 1]
        for m in range(count):
            done[m, strip] = rows[m][:, BLOCK:]
            if at + STRIP < BLOCK:
                high, mid, low = thirds(rows[m] * both(lax.rsqrt(scale[m])))
                left = jnp.concatenate([high, high, mid, mid, high, low], 0)[:, :BLOCK]
                right = jnp.concatenate([high, mid, high, mid, low, high], 0)
                rest = slice(at + STRIP, BLOCK)
                work[m, rest] -= contract(left, right, 0, 0)[rest]
    return pivots


def renew_kernel(gram_ref, product_ref, small_ref, out_ref, all_ref, gram, both, work, done, box, sems):
    count, size = gram_ref.shape[:2]
    k = pl.program_id(0)

    head = lax.axis_index("head")
    smalls = Spread(along("head"), lambda _: small_ref, lambda i: box.at[i], sems.at[0], sems.at[1])

    @pl.when(k == 0)
    def _():
        gram[...] = gram_ref[...]
        both[...] = product_ref[...]
        meet(["head"])
        smalls.all("start")
        box[head] = small_ref[...]

    @pl.when(k == pl.num_programs(0) - 1)
    def _():
        smalls.all("arrived")
        all_ref[...] = box[...]
        smalls.all("sent")

    at = pl.ds(pl.multiple_of(k * BLOCK, BLOCK), BLOCK)
    unit = lax.broadcasted_iota(jnp.int32, (BLOCK, BLOCK), 0) == lax.broadcasted_iota(
        jnp.int32, (BLOCK, BLOCK), 1
    )
    for m in range(count):
        work[m, :, :BLOCK] = gram[m, at, at]
        work[m, :, BLOCK:] = unit.astype(f32)
    roots = [lax.rsqrt(p) for p in eliminate(work, done)]
    for step in range(size // BLOCK):

        @pl.when(k == step)
        def _(here=slice(step * BLOCK, (step + 1) * BLOCK), rest=(step + 1) * BLOCK):
            for m in range(count):
                factor = done[m]
                panel = contract(both[m, :, here], factor, 1, 1, highest) * roots[m]
                out_ref[m] = panel
                if rest < size:
                    left = contract(gram[m, rest:, here], factor, 1, 1, highest) * roots[m]
                    both[m, :, rest:] -= contract(panel, left, 1, 1, highest)
                    gram[m, rest:, rest:] -= contract(left, left, 1, 1, highest)


def renew(gram, product, small, heads):
    count, size = gram.shape[:2]
    gathered = (heads, *small.shape)
    return pl.pallas_call(
        renew_kernel,
        grid=(size // BLOCK,),
        in_specs=[whole(gram.shape), whole(gram.shape), whole(small.shape)],
        out_specs=[pl.BlockSpec((count, size, BLOCK), lambda k: (0, 0, k)), whole(gathered)],
        out_shape=[jax.ShapeDtypeStruct(gram.shape, f32), jax.ShapeDtypeStruct(gathered, f32)],
        scratch_shapes=[
            pltpu.VMEM((count, size, size), f32),
            pltpu.VMEM((count, size, size), f32),
            pltpu.VMEM((count, BLOCK, 2 * BLOCK), f32),
            pltpu.VMEM((count, BLOCK, BLOCK), f32),
            pltpu.VMEM(gathered, f32),
            pltpu.SemaphoreType.DMA((2, heads)),
        ],
        compiler_params=remote(48, 6),
        name="renew",
    )(gram, product, small)


def local(
    prev_state,
    target,
    noise_eps,
    noise_level,
    valid_count,
    neighbours,
    nbr_count,
    pix_node,
    pix_read,
    w_enc,
    w_cond,
    w_dec,
    layer_w,
    soap_first,
    soap_second,
    soap_basis,
    soap_stats,
    enc_first,
    enc_second,
    cond_first,
    cond_second,
    dec_first,
    dec_second,
):
    nodes = nbr_count.shape[0]
    groups = lax.axis_size("node")
    heads = lax.axis_size("head")
    rows = nodes // heads
    block_start = lax.axis_index("node") * nodes
    quarter = lax.axis_index("head")
    width = w_enc.shape[1]
    both = ("head", "node")

    low_w = layer_w.astype(bf16)
    ffn_share = jnp.concatenate([low_w[1], low_w[2]], 1)
    noise_sigma, noise_feat = noise_terms(noise_level)
    sig_sq = noise_sigma * noise_sigma
    input_scale = lax.rsqrt(sig_sq + 1.0)
    skip_scale = 1.0 / (sig_sq + 1.0)
    output_scale = noise_sigma * lax.rsqrt(sig_sq + 1.0)
    loss_scale = (sig_sq + 1.0) / sig_sq
    modulation = jnp.dot(noise_feat[None, :], w_cond, precision=highest).reshape(4, width)

    prev_t, target_t, eps_t = prev_state.T, target.T, noise_eps.T
    node_row = pix_node.reshape(1, -1)
    read_rows = pix_read.T
    place = jnp.stack([block_start, quarter * rows, valid_count[0], quarter]).astype(jnp.int32)
    node_in, stat, column, w_attn = encode(
        place, jnp.stack([noise_sigma, input_scale]), node_row, prev_t, target_t, eps_t, low_w[0], rows, 1024, groups
    )
    w_attn = w_attn.reshape(width, -1)

    pad_enc = jnp.zeros((2, SLOT, width), bf16)
    pad_enc = pad_enc.at[:, :VARS].set(w_enc.astype(bf16).reshape(2, VARS, width))
    h_zero, norm_all, query, keyval, stat, counts = open_nodes(
        node_in, pad_enc.reshape(2 * SLOT, width), modulation, stat, w_attn, neighbours.T,
        nbr_count.reshape(1, -1), heads, groups,
    )
    norm_all, query = norm_all.reshape(nodes, -1), query.reshape(nodes, -1)
    keyval = keyval.reshape(3, nodes, -1)
    stat_sum = stat[:, 0]
    count_sum = stat_sum[SLIM - 1]
    var_weight = 1.0 / (stat_sum[:VARS] / count_sum + norm_eps)
    loss_count = count_sum * VARS
    e, mix, mixed, attn_all, ffn_all = attend(query, keyval, counts, column, ffn_share, heads, 128, 512)
    attn_all = attn_all.reshape(heads, width, -1)
    ffn_all = ffn_all.reshape(heads, width, -1)

    w_dec_t = jnp.zeros((SLIM, width), bf16).at[:VARS].set(w_dec.T.astype(bf16))
    scales = jnp.stack(
        [noise_sigma, input_scale, skip_scale, output_scale, output_scale * (2.0 / loss_count) / 3.0]
    )
    weight = jnp.broadcast_to((loss_scale * var_weight)[:, None], (VARS, 128))
    d_one, d_mixed, pair_sum, grad_dec, gmod_two, loss_part = middle(
        place, scales, mixed, h_zero, attn_all, ffn_all, modulation, w_dec_t, weight, node_row, read_rows,
        target_t, eps_t, groups,
    )
    d_mixed = d_mixed.reshape(nodes, HD)
    dq, dkv, grad_qkv, big_share, big_full = attend_back(
        query, d_mixed, mix, e, keyval, norm_all, pair_sum, heads, 256, 512
    )
    feat_sq = jnp.sum(noise_feat * noise_feat).reshape(1)
    small, qkv_share, qkv_full, sums = settle(
        feat_sq, dq, dkv, attn_all, h_zero, d_one, node_in, modulation, grad_dec, gmod_two, grad_qkv, big_share,
        loss_part, groups,
    )
    big_full = big_full.reshape(width, -1)
    layer_share = jnp.stack(
        [
            jnp.concatenate([qkv_share, big_share[:, 2 * width :]], 1),
            big_share[:, :width],
            big_share[:, width : 2 * width],
        ]
    )
    grad_norm = jnp.sqrt(sums[0, 0])
    loss_sum = sums[1, 0]
    clip_factor = clip_limit / jnp.maximum(grad_norm, clip_limit)
    clipped = clip_factor * layer_share
    grad_full = jnp.stack(
        [
            jnp.concatenate([qkv_full.reshape(width, -1), big_full[:, 2 * width :]], 1),
            big_full[:, :width],
            big_full[:, width : 2 * width],
        ]
    )
    raw_stat = jnp.einsum("idb,idc->ibc", grad_full, grad_full, preferred_element_type=f32)
    stat_new = clip_factor * (clip_factor * raw_stat)
    basis_old = soap_basis[:, 0]
    rotated = jnp.einsum("idb,ibc->idc", clipped, basis_old, precision=highest)
    first_new = beta_first * soap_first + (1 - beta_first) * rotated
    second_new = beta_second * soap_second + (1 - beta_second) * rotated * rotated
    direction = (
        first_new
        / (1 - beta_first**STEP)
        / (jnp.sqrt(second_new / (1 - beta_second**STEP)) + adam_epsilon)
    )
    step_back = jnp.einsum("idc,ibc->idb", direction, basis_old, precision=highest)
    layer_new = layer_w - rate_layer * (step_back + decay_rate * layer_w)
    stats_new = beta_stats * soap_stats[:, 0] + (1 - beta_stats) * stat_new
    product = jnp.einsum("ibc,icd->ibd", stats_new, basis_old, precision=highest)
    gram_matrix = jnp.einsum("ibc,ibd->icd", product, product, precision=highest)
    basis_new, small = renew(gram_matrix, product, small, heads)
    small = small.reshape(-1, width)
    grad_enc = small[: 2 * VARS]
    grad_dec = small[2 * VARS : 3 * VARS]
    grad_cond = noise_feat[:, None] * small[3 * VARS : 3 * VARS + 4].reshape(1, -1)
    enc_new = adam_small(w_enc, clip_factor * grad_enc, enc_first, enc_second)
    cond_new = adam_small(w_cond, clip_factor * grad_cond, cond_first, cond_second)
    dec_new = adam_small(w_dec.T, clip_factor * grad_dec, dec_first.T, dec_second.T)
    return (
        jnp.reshape(loss_sum, (1,)),
        jnp.reshape(loss_count, (1,)),
        jnp.reshape(grad_norm, (1,)),
        layer_new,
        first_new,
        second_new,
        basis_new[:, None],
        stats_new[:, None],
        *enc_new,
        *cond_new,
        *(x.T for x in dec_new),
    )


def solution(mesh):
    pixel = P("node", None)
    layer = P(None, "node", "head")
    basis = P(None, "head", None, None)
    placed = (
        *(pixel,) * 3,
        P(),
        P("node"),
        P("node", None),
        P("node"),
        P("node"),
        P("node", None),
        *(P(),) * 3,
        *(layer,) * 3,
        *(basis,) * 2,
        *(P(),) * 6,
    )
    return jax.shard_map(
        local,
        mesh=mesh,
        in_specs=placed,
        out_specs=(*(P(),) * 3, *(layer,) * 3, *(basis,) * 2, *(P(),) * 9),
        check_vma=False,
    )
```

```python
import functools
import math

import jax
import jax.numpy as jnp
from jax import lax
from jax.experimental import pallas as pl
from jax.experimental.pallas import tpu as pltpu
from jax.sharding import PartitionSpec as P

HD = 128
VARS = 84
NF = 32
NBR = 16
LEVELS = 1000
STEP = 10

SLOT = 128
SLIM = 96
GROUP = 256 // NBR
BLOCK = 128
STRIP = 16
HEAD_STEP = 17

highest = lax.Precision.HIGHEST
clip_limit = 0.01
beta_first = 0.9
beta_second = 0.95
beta_stats = 0.95
adam_epsilon = 1e-08
rate_layer = 0.02
rate_small = 0.05
decay_rate = 0.1
norm_eps = 1e-05

f32 = jnp.float32
bf16 = jnp.bfloat16
MIB = 2**20


def passed_along(x, axis, by):
    length = lax.axis_size(axis)
    return lax.ppermute(x, axis, [(i, (i + by) % length) for i in range(length)])


def noise_terms(noise_level):
    level_frac = noise_level[0].astype(f32) / (LEVELS - 1)
    noise_sigma = 0.05 * jnp.exp(level_frac * math.log(40.0))
    frequency = 1.0 + jnp.arange(NF // 2).astype(f32)
    phase_angle = jnp.log(noise_sigma) * frequency
    return (noise_sigma, jnp.concatenate([jnp.sin(phase_angle), jnp.cos(phase_angle)]))


def standardize(values_in):
    row_mean = jnp.mean(values_in, -1, keepdims=True)
    centered = values_in - row_mean
    inv_std = lax.rsqrt(jnp.mean(centered * centered, -1, keepdims=True) + norm_eps)
    return (centered * inv_std, inv_std)


def norm_back(normed, inv_std, grad_in):
    return inv_std * (
        grad_in
        - jnp.mean(grad_in, -1, keepdims=True)
        - normed * jnp.mean(grad_in * normed, -1, keepdims=True)
    )


def contract(left, right, left_dim, right_dim, precision=None):
    return lax.dot_general(
        left,
        right,
        (((left_dim,), (right_dim,)), ((), ())),
        preferred_element_type=f32,
        precision=precision,
    )


def halves(x):
    high = x.astype(bf16)
    return high, (x - high.astype(f32)).astype(bf16)


def thirds(x):
    high = x.astype(bf16)
    rest = x - high.astype(f32)
    return (high, *halves(rest))


def fold_lanes(x, op=jnp.add):
    parts = [x[:, i : i + 128] for i in range(0, x.shape[1], 128)]
    while len(parts) > 1:
        parts = [op(*parts[i : i + 2]) if i + 1 < len(parts) else parts[i] for i in range(0, len(parts), 2)]
    return parts[0]


def adam_small(weight, grad_item, first, second):
    first_new = beta_first * first + (1 - beta_first) * grad_item
    second_new = beta_second * second + (1 - beta_second) * grad_item * grad_item
    ratio = (
        first_new
        / (1 - beta_first**STEP)
        / (jnp.sqrt(second_new / (1 - beta_second**STEP)) + adam_epsilon)
    )
    return (weight - rate_small * (ratio + decay_rate * weight), first_new, second_new)


def smem():
    return pl.BlockSpec(memory_space=pltpu.SMEM)


def whole(shape):
    zeros = (0,) * len(shape)
    return pl.BlockSpec(tuple(shape), lambda *_: zeros)


def params(mib=48):
    return pltpu.CompilerParams(vmem_limit_bytes=mib * MIB)


def remote(mib, identity):
    return pltpu.CompilerParams(
        vmem_limit_bytes=mib * MIB, collective_id=identity, has_side_effects=True
    )


def vmem():
    return pl.BlockSpec(memory_space=pltpu.VMEM)


def hbm():
    return pl.BlockSpec(memory_space=pl.ANY)


def each(count, act, start=1):
    def body(off, carry):
        act(off)
        return carry

    lax.fori_loop(start, count, body, 0)


def meet(axes):
    barrier = pltpu.get_barrier_semaphore()
    total = 0
    for axis in axes:
        count, me = lax.axis_size(axis), lax.axis_index(axis)
        total += count - 1
        each(
            count,
            lambda off: pl.semaphore_signal(barrier, inc=1, device_id={axis: (me + off) % count}),
        )
    pl.semaphore_wait(barrier, total)


class Spread:
    def __init__(self, group, source, target, sends, receives):
        self.count, self.me, self.where = group
        self.source, self.target = source, target
        self.sends, self.receives = sends, receives

    def copy(self, other, slot):
        return pltpu.make_async_remote_copy(
            src_ref=self.source(other),
            dst_ref=self.target(slot),
            send_sem=self.sends.at[other],
            recv_sem=self.receives.at[slot],
            device_id=self.where(other),
        )

    def other(self, off):
        return (self.me + off) % self.count

    def start(self, off):
        self.copy(self.other(off), self.me).start()

    def arrived(self, off):
        self.copy(self.other(off), self.other(off)).wait_recv()

    def sent(self, off):
        self.copy(self.other(off), self.me).wait_send()

    def all(self, act):
        each(self.count, getattr(self, act))


def along(axis):
    return lax.axis_size(axis), lax.axis_index(axis), lambda other: {axis: other}


def pairs():
    node = lax.axis_index("node")
    place, pair = node % 2, node // 2
    within = (2, place, lambda other: {"node": 2 * pair + other})
    across = (lax.axis_size("node") // 2, pair, lambda other: {"node": 2 * other + place})
    return within, across


class Relay:
    def __init__(self, part, sems):
        me = lax.axis_index("head")
        self.me, self.near, self.across = me, (me + 1 - 2 * (me % 2), (me + 2) % 4), 3 - me
        self.part, self.sems = part, sems

    def copy(self, kind, target, slot, half):
        return pltpu.make_async_remote_copy(
            src_ref=self.part(slot, half),
            dst_ref=self.part(slot, half),
            send_sem=self.sems.at[0, kind, half],
            recv_sem=self.sems.at[1, kind, half],
            device_id={"head": target},
        )

    def start(self, halves=((0, 0), (1, 1), (0, 1), (1, 0))):
        for side, half in halves:
            self.copy(side, self.near[side], self.me, half).start()

    def hand_on(self, side):
        self.copy(side, self.near[side], self.near[side], side).wait_recv()
        self.copy(2, self.near[1 - side], self.near[side], side).start()

    def arrived(self, side):
        self.copy(side, self.near[side], self.near[side], 1 - side).wait_recv()

    def arrived_across(self):
        for half in range(2):
            self.copy(2, self.near[half], self.across, half).wait_recv()

    def sent(self):
        for half in range(2):
            for side in range(2):
                self.copy(side, self.near[side], self.me, half).wait_send()
            self.copy(2, self.near[1 - half], self.near[half], half).wait_send()


def encode_kernel(
    place_ref, scale_ref, node_ref, prev_ref, target_ref, eps_ref, w_ref,
    in_ref, stat_ref, own_ref, all_ref,
    pix, box, pair_box, sems, pair_sems,
):
    step = pl.program_id(0)
    rows = in_ref.shape[0]
    tile = node_ref.shape[1]
    within, across = pairs()
    place = within[1]
    weights = Spread(across, lambda _: w_ref, lambda i: box.at[i], sems.at[0], sems.at[1])
    swap = pltpu.make_async_remote_copy(
        src_ref=box,
        dst_ref=pair_box,
        send_sem=pair_sems.at[0],
        recv_sem=pair_sems.at[1],
        device_id=within[2](1 - place),
    )

    @pl.when(step == 0)
    def _():
        meet(["node"])
        weights.all("start")
        box[weights.me] = w_ref[...]
        pix[...] = jnp.zeros_like(pix)
        in_ref[...] = jnp.zeros_like(in_ref)
        stat_ref[...] = jnp.zeros_like(stat_ref)

    @pl.when(step == pl.num_programs(0) - 2)
    def _():
        weights.all("arrived")
        swap.start()

    prev = prev_ref[...]
    target = target_ref[...]
    noisy = target + scale_ref[0] * eps_ref[...]
    pix[:VARS] = prev.astype(bf16)
    pix[SLOT : SLOT + VARS] = (scale_ref[1] * noisy).astype(bf16)
    node = node_ref[...] - place_ref[0]
    mine = node - place_ref[1]
    spot = lax.broadcasted_iota(jnp.int32, (rows, tile), 0)
    onehot = (spot == mine).astype(f32).astype(bf16)
    in_ref[...] += contract(onehot, pix[...], 1, 1)
    valid = (node < place_ref[2]).astype(f32)
    residual = target - prev
    stat_ref[:VARS] += fold_lanes(valid * residual * residual)
    stat_ref[SLIM - 1 : SLIM] += fold_lanes(valid)

    @pl.when(step == pl.num_programs(0) - 1)
    def _():
        swap.wait()
        own_ref[...] = box[...]
        all_ref[:, place] = box[...]
        all_ref[:, 1 - place] = pair_box[...]
        weights.all("sent")


def encode(place, scales, node_row, prev, target, eps, w_share, rows, tile, nodes):
    pixels = prev.shape[1]
    column = (nodes // 2, *w_share.shape)
    gathered = (nodes // 2, 2, *w_share.shape)
    pixel_block = pl.BlockSpec((VARS, tile), lambda i: (0, i))
    return pl.pallas_call(
        encode_kernel,
        grid=(pixels // tile,),
        in_specs=[smem(), smem(), pl.BlockSpec((1, tile), lambda i: (0, i))]
        + [pixel_block] * 3
        + [whole(w_share.shape)],
        out_specs=[whole((rows, 2 * SLOT)), whole((SLIM, 128)), whole(column), whole(gathered)],
        out_shape=[
            jax.ShapeDtypeStruct((rows, 2 * SLOT), f32),
            jax.ShapeDtypeStruct((SLIM, 128), f32),
            jax.ShapeDtypeStruct(column, bf16),
            jax.ShapeDtypeStruct(gathered, bf16),
        ],
        scratch_shapes=[
            pltpu.VMEM((2 * SLOT, tile), bf16),
            pltpu.VMEM(column, bf16),
            pltpu.VMEM(column, bf16),
            pltpu.SemaphoreType.DMA((2, nodes // 2)),
            pltpu.SemaphoreType.DMA((2,)),
        ],
        compiler_params=remote(48, 2),
        name="encode",
    )(place, scales, node_row, prev, target, eps, w_share)


def count_tile(band_rows, spot_rows, put, bands):
    lane = lax.broadcasted_iota(jnp.int32, (GROUP, 256), 1)
    sub = lax.broadcasted_iota(jnp.int32, (GROUP, 256), 0)
    own = lane % GROUP == sub
    widen = (lane // GROUP == sub).astype(f32).astype(bf16)
    all_bands = contract(band_rows, widen, 0, 0)
    all_spots = contract(spot_rows, widen, 0, 0)
    spot = lax.broadcasted_iota(jnp.int32, (256, 256), 0).astype(f32)
    for g in range(band_rows.shape[1] // GROUP):
        nodes = slice(g * GROUP, (g + 1) * GROUP)
        band = jnp.where(own, all_bands[nodes], -1.0)
        left = jnp.concatenate([(band == t).astype(f32).astype(bf16) for t in range(bands)], 0)
        row = jnp.sum(jnp.where(own, all_spots[nodes], 0.0), 0, keepdims=True)
        right = (spot == row).astype(f32).astype(bf16)
        found = contract(left, right, 1, 1).astype(bf16)
        for t in range(bands):
            put(g, t, found[t * GROUP : (t + 1) * GROUP])


def nearest_first(me, count):
    if count == 4:
        return [me + 1 - 2 * (me % 2), (me + 2) % 4, 3 - me]
    return [(me + k) % count for k in range(1, count)]


def open_kernel(
    in_ref, wenc_ref, mod_ref, stat_ref, w_ref, nbr_ref, live_ref,
    zero_ref, norm_ref, q_ref, kv_ref, sum_ref, count_ref,
    stat_own, stat_box, bands, spots, tiles, head_sems, stat_sems, halo_sems, out_sems,
):
    heads, rows, _ = norm_ref.shape
    head, node = lax.axis_index("head"), lax.axis_index("node")
    groups = lax.axis_size("node")
    depth = tiles.shape[1]
    nodes = count_ref.shape[0]
    steps = nodes // depth
    stat_own[...] = jnp.broadcast_to(jnp.sum(stat_ref[...], 1, keepdims=True), stat_own.shape)
    meet(["head", "node"])

    stats = Spread(along("node"), lambda _: stat_own, lambda i: stat_box.at[i], stat_sems.at[0], stat_sems.at[1])
    stats.all("start")
    w_enc = wenc_ref[...]
    h_zero = sum(contract(part, w_enc, 1, 0) for part in thirds(in_ref[...]))
    zero_ref[...] = h_zero
    normed, _ = standardize(h_zero)
    norm_ref[head] = (normed * (1 + mod_ref[0:1]) + mod_ref[1:2]).astype(bf16)
    half_rows = rows // 2
    norms = Relay(lambda slot, half: norm_ref.at[slot, pl.ds(half * half_rows, half_rows)], head_sems)
    norms.start()

    def halo(block):
        return [
            pltpu.make_async_remote_copy(
                src_ref=kv_ref.at[1, block],
                dst_ref=kv_ref.at[2 * side, block],
                send_sem=halo_sems.at[2 * side, block],
                recv_sem=halo_sems.at[2 * side + 1, block],
                device_id={"node": (node + by) % groups},
            )
            for side, by in enumerate((1, groups - 1))
        ]

    def project(block):
        out = contract(norm_ref[block], w_ref[:, : 3 * HD], 1, 0).astype(bf16)
        q_ref[block] = out[:, :HD]
        kv_ref[1, block] = out[:, HD:]
        for copy in halo(block):
            copy.start()

    def count(step):
        slot = step % 2

        @pl.when(step >= 2)
        def _():
            count_out(step - 2).wait()

        here = pl.ds(pl.multiple_of(step * depth, depth), depth)

        def put(g, t, found):
            tiles[slot, g * GROUP : (g + 1) * GROUP, t * 256 : (t + 1) * 256] = found

        count_tile(bands[:, here], spots[:, here], put, tiles.shape[2] // 256)
        count_out(step).start()

    def count_out(step):
        return pltpu.make_async_copy(
            tiles.at[step % 2],
            count_ref.at[pl.ds(pl.multiple_of(step * depth, depth), depth)],
            out_sems.at[step % 2],
        )

    project(head)
    total = nodes * groups
    relative = nbr_ref[...] - node * nodes + nodes
    relative = jnp.where(relative >= total, relative - total, relative)
    relative = jnp.where(relative < 0, relative + total, relative)
    live = lax.broadcasted_iota(jnp.int32, relative.shape, 0) < live_ref[...]
    bands[...] = jnp.where(live, relative >> 8, -1).astype(f32).astype(bf16)
    spots[...] = (relative & 255).astype(f32).astype(bf16)
    each(steps // 4, count, 0)
    norms.hand_on(0)
    norms.hand_on(1)
    each(steps * 3 // 8, count, steps // 4)
    for side in range(2):
        norms.arrived(side)
        project(norms.near[side])
    each(steps * 5 // 8, count, steps * 3 // 8)
    norms.arrived_across()
    project(norms.across)
    each(steps, count, steps * 5 // 8)
    each(steps, lambda step: count_out(step).wait(), steps - 2)
    stats.all("arrived")
    sum_ref[...] = sum(jnp.where(t == node, stat_own[...], stat_box[t]) for t in range(groups))

    def finish(block):
        for copy in halo(block):
            copy.wait()

    each(heads, finish, 0)
    norms.sent()
    stats.all("sent")


def open_nodes(node_in, w_enc, modulation, stat, w_attn, neighbours, live, heads, groups):
    rows, width = node_in.shape[0], w_enc.shape[1]
    depth = 8 * GROUP
    reach = 3 * heads * rows
    block = lambda w: jax.ShapeDtypeStruct((heads, rows, w), bf16)
    return pl.pallas_call(
        open_kernel,
        in_specs=[vmem()] * 7,
        out_specs=[vmem()] * 5 + [pl.BlockSpec(memory_space=pl.ANY)],
        out_shape=[
            jax.ShapeDtypeStruct((rows, width), f32),
            block(width),
            block(HD),
            jax.ShapeDtypeStruct((3, heads, rows, 2 * HD), bf16),
            jax.ShapeDtypeStruct((SLIM, 128), f32),
            jax.ShapeDtypeStruct((heads * rows, reach), bf16),
        ],
        scratch_shapes=[
            pltpu.VMEM((SLIM, 128), f32),
            pltpu.VMEM((groups, SLIM, 128), f32),
            pltpu.VMEM((NBR, heads * rows), bf16),
            pltpu.VMEM((NBR, heads * rows), bf16),
            pltpu.VMEM((2, depth, reach), bf16),
            pltpu.SemaphoreType.DMA((2, 3, 2)),
            pltpu.SemaphoreType.DMA((2, groups)),
            pltpu.SemaphoreType.DMA((4, heads)),
            pltpu.SemaphoreType.DMA((2,)),
        ],
        compiler_params=remote(56, 3),
        name="open_nodes",
    )(node_in, w_enc, modulation, stat, w_attn, neighbours, live)


def attend_kernel(
    q_ref, kv_ref, count_ref, column_ref, ffn_ref, e_ref, mix_ref, out_ref, attn_out, ffn_out, s_scr, own, box, attn_all, ffn_all, sems,
    attn_sems, column_sems, ffn_sems, pair_sems, local_sems, chunk
):
    step = pl.program_id(0)
    steps = pl.num_programs(0)
    head = lax.axis_index("head")
    tile = q_ref.shape[0]
    per = box.shape[1] // tile

    def copy(target, source, part):
        at = pl.ds(pl.multiple_of(part * tile, tile), tile)
        return pltpu.make_async_remote_copy(
            src_ref=own.at[target, at],
            dst_ref=box.at[source, at],
            send_sem=sems.at[0, target, part],
            recv_sem=sems.at[1, source, part],
            device_id={"head": target},
        )

    within, across = pairs()
    place, pair = within[1], across[1]
    ffn_pairs = Spread(
        across, lambda _: ffn_ref, lambda i: ffn_all.at[head, i, place], column_sems.at[0], column_sems.at[1]
    )
    count = across[0]

    def half_of(array):
        return lambda slot, half: array.at[slot, pl.ds(half * (count // 2), count // 2), place]

    attn_heads = Relay(half_of(attn_all), attn_sems)
    ffn_heads = Relay(half_of(ffn_all), ffn_sems)
    stay = [
        pltpu.make_async_copy(column_ref, attn_all.at[head, :, place], local_sems.at[0]),
        pltpu.make_async_copy(ffn_ref, ffn_all.at[head, pair, place], local_sems.at[1]),
    ]

    def swap(h, which, side):
        array = (attn_all, ffn_all)[which]
        return pltpu.make_async_remote_copy(
            src_ref=array.at[h, :, side],
            dst_ref=array.at[h, :, side],
            send_sem=pair_sems.at[0, which, h],
            recv_sem=pair_sems.at[1, which, h],
            device_id=within[2](1 - place),
        )

    @pl.when(step == 0)
    def _():
        for copy in stay:
            copy.start()
        meet(["head", "node"])
        ffn_pairs.all("start")
        for copy in stay:
            copy.wait()
        attn_heads.start()

    @pl.when(step == 5)
    def _():
        attn_heads.hand_on(0)
        attn_heads.hand_on(1)

    @pl.when(step == 5)
    def _():
        ffn_pairs.all("arrived")
        ffn_heads.start()

    @pl.when(step == 12)
    def _():
        ffn_heads.hand_on(0)
        ffn_heads.hand_on(1)

    @pl.when(step == 15)
    def _():
        for heads_of in (attn_heads, ffn_heads):
            for side in range(2):
                heads_of.arrived(side)
            heads_of.arrived_across()

        def begin(h):
            for which in range(2):
                swap(h, which, place).start()

        each(box.shape[0], begin, 0)

    nodes = kv_ref.shape[1]
    q = q_ref[...]
    top = jnp.full((tile, 128), -1e30, f32)
    for b in range(3):
        for at in range(0, nodes, chunk):
            cols = slice(b * nodes + at, b * nodes + at + chunk)
            s = contract(q, kv_ref[b, at : at + chunk, :HD], 1, 1)
            s = jnp.where(count_ref[:, cols].astype(f32) > 0, s, -1e30)
            s_scr[:, cols] = s
            top = jnp.maximum(top, fold_lanes(s, jnp.maximum))
    top = jnp.max(top, 1, keepdims=True)
    factor = math.log2(math.e) / math.sqrt(HD)
    total = jnp.zeros((tile, 128), f32)
    mixed = jnp.zeros((tile, HD), f32)
    for b in range(3):
        for at in range(0, nodes, chunk):
            cols = slice(b * nodes + at, b * nodes + at + chunk)
            e = count_ref[:, cols].astype(f32) * jnp.exp2((s_scr[:, cols] - top) * factor)
            total += fold_lanes(e)
            e = e.astype(bf16)
            e_ref[:, cols] = e
            mixed += contract(e, kv_ref[b, at : at + chunk, HD:], 1, 0)
    inverse = 1.0 / jnp.sum(total, 1, keepdims=True)
    mixed = mixed * inverse
    mix_ref[:, :HD] = mixed
    mix_ref[:, HD:] = jnp.broadcast_to(inverse, (tile, HD))
    target, part = step // per, step % per
    at = pl.ds(pl.multiple_of(part * tile, tile), tile)
    low = mixed.astype(bf16)
    own[target, at] = low

    @pl.when(target == head)
    def _():
        box[head, at] = low

    @pl.when(target != head)
    def _():
        copy(target, head, part).start()

    @pl.when(step == steps - 1)
    def _():
        heads = box.shape[0]

        def finish(off):
            other = (head + off) % heads
            for p in range(per):
                copy(other, other, p).wait_recv()
                copy(other, head, p).wait_send()

        each(heads, finish)
        out_ref[...] = box[...]

        def end(h):
            for which in range(2):
                swap(h, which, place).wait_send()
                swap(h, which, 1 - place).wait_recv()

        each(heads, end, 0)
        outs = [
            pltpu.make_async_copy(attn_all, attn_out, local_sems.at[0]),
            pltpu.make_async_copy(ffn_all, ffn_out, local_sems.at[1]),
        ]
        for put in outs:
            put.start()
        for put in outs:
            put.wait()
        ffn_pairs.all("sent")
        attn_heads.sent()
        ffn_heads.sent()


def attend(query, keyval, counts, column, ffn_share, heads, tile, chunk):
    nodes, reach = counts.shape
    rows = nodes // heads
    count = column.shape[0]
    dma = lambda *shape: pltpu.SemaphoreType.DMA(shape)
    row = lambda width: pl.BlockSpec((tile, width), lambda i: (i, 0))
    return pl.pallas_call(
        functools.partial(attend_kernel, chunk=chunk),
        grid=(nodes // tile,),
        in_specs=[row(HD), whole(keyval.shape), row(reach), hbm(), hbm()],
        out_specs=[row(reach), row(2 * HD), whole((heads, rows, HD)), hbm(), hbm()],
        out_shape=[
            jax.ShapeDtypeStruct((nodes, reach), bf16),
            jax.ShapeDtypeStruct((nodes, 2 * HD), f32),
            jax.ShapeDtypeStruct((heads, rows, HD), bf16),
            jax.ShapeDtypeStruct((heads, count, 2, *column.shape[1:]), bf16),
            jax.ShapeDtypeStruct((heads, count, 2, *ffn_share.shape), bf16),
        ],
        scratch_shapes=[
            pltpu.VMEM((tile, reach), f32),
            pltpu.VMEM((heads, rows, HD), bf16),
            pltpu.VMEM((heads, rows, HD), bf16),
            pltpu.VMEM((heads, count, 2, *column.shape[1:]), bf16),
            pltpu.VMEM((heads, count, 2, *ffn_share.shape), bf16),
            dma(2, heads, rows // tile),
            dma(2, 3, 2),
            dma(2, count),
            dma(2, 3, 2),
            dma(2, 2, heads),
            dma(2),
        ],
        compiler_params=remote(60, 4),
        name="attend",
    )(query, keyval, counts, column, ffn_share)


def attend_back_kernel(
    q_ref, d_ref, mix_ref, e_ref, kv_ref, norm_ref, pair_sum,
    dq_ref, dkv_ref, grad_ref, share_ref, full_ref,
    dk, dv, dq, low_own, high_own, low_box, high_box, dq_own, dq_box, dkv_own, dkv_box,
    head_box, across_own, across_box, share_low, full,
    halo_sems, dq_sems, dkv_sems, pair_sems, head_sems, across_sems, full_sems,
    chunk,
):
    turn, part = pl.program_id(0), pl.program_id(1)
    parts = pl.num_programs(1)
    step = turn * parts + part
    tile = q_ref.shape[0]
    nodes = kv_ref.shape[1]
    heads, rows, _ = dq_box.shape
    per = rows // tile
    head, node, groups = lax.axis_index("head"), lax.axis_index("node"), lax.axis_size("node")
    within, across = pairs()
    last = part == parts - 1

    place, pair = within[1], across[1]
    over_heads = Spread(
        along("head"), lambda o: pair_sum.at[o], lambda i: head_box.at[i], head_sems.at[0], head_sems.at[1]
    )
    over_pairs = Spread(
        across, lambda o: across_own.at[o], lambda i: across_box.at[i], across_sems.at[0], across_sems.at[1]
    )
    over_full = Spread(
        across, lambda _: share_low, lambda i: full.at[place, i], full_sems.at[0], full_sems.at[1]
    )
    count = across[0]

    def swap(side):
        return pltpu.make_async_remote_copy(
            src_ref=full.at[side],
            dst_ref=full.at[side],
            send_sem=pair_sems.at[0],
            recv_sem=pair_sems.at[1],
            device_id=within[2](1 - place),
        )

    def halo(own, box, side, by):
        return pltpu.make_async_remote_copy(
            src_ref=own,
            dst_ref=box,
            send_sem=halo_sems.at[0, side],
            recv_sem=halo_sems.at[1, side],
            device_id={"node": (node + by) % groups},
        )

    to_below = halo(low_own, low_box, 0, groups - 1)
    to_above = halo(high_own, high_box, 1, 1)

    def dq_copy(target, source, piece):
        at = pl.ds(pl.multiple_of(piece * tile, tile), tile)
        return pltpu.make_async_remote_copy(
            src_ref=dq_own.at[target, at],
            dst_ref=dq_box.at[source, at],
            send_sem=dq_sems.at[0, target, piece],
            recv_sem=dq_sems.at[1, source, piece],
            device_id={"head": target},
        )

    dkv_spread = Spread(
        along("head"), lambda o: dkv_own.at[o], lambda i: dkv_box.at[i], dkv_sems.at[0], dkv_sems.at[1]
    )

    @pl.when(step == 0)
    def _():
        meet(["head", "node"])
        over_heads.all("start")
        head_box[head] = pair_sum[head]

    @pl.when(step == HEAD_STEP)
    def _():
        over_heads.all("arrived")

        def add(z):
            across_own[z] = sum(head_box[h, z].astype(f32) for h in range(heads)).astype(bf16)

        each(count, add, 0)
        over_pairs.all("start")
        across_box[across[1]] = across_own[across[1]]

    @pl.when(part == 0)
    def _():
        dk[...] = jnp.zeros_like(dk)
        dv[...] = jnp.zeros_like(dv)

    grad = d_ref[...]
    wide = grad.astype(f32)
    inverse = mix_ref[:, HD : HD + 1]
    delta = jnp.sum(wide * mix_ref[:, :HD], 1, keepdims=True)
    gain = inverse * (1.0 / math.sqrt(HD))
    q_turned = q_ref[...].T
    d_turned = (wide * inverse).astype(bf16).T
    here = pl.ds(pl.multiple_of(part * tile, tile), tile)
    dq_here = jnp.where(turn == 0, 0.0, dq[here])
    for at in range(0, nodes, chunk):
        cols = slice(at, at + chunk)
        dp = contract(grad, kv_ref[0, cols, HD:], 1, 1)
        e = e_ref[:, cols]
        ds = (e.astype(f32) * ((dp - delta) * gain)).astype(bf16)
        dq_here += contract(ds, kv_ref[0, cols, :HD], 1, 0)
        dk[:, cols] += contract(q_turned, ds, 1, 0)
        dv[:, cols] += contract(d_turned, e, 1, 0)
    dq[here] = dq_here

    for which, own, copy in ((0, low_own, to_below), (1, high_own, to_above)):

        @pl.when(last & (turn == which))
        def _(own=own, copy=copy):
            own[:HD] = dk[...].astype(bf16)
            own[HD:] = dv[...].astype(bf16)
            copy.start()

    @pl.when(turn == 2)
    def _():
        target, piece = part // per, part % per
        at = pl.ds(pl.multiple_of(piece * tile, tile), tile)
        low = dq_here.astype(bf16)
        dq_own[target, at] = low

        @pl.when(target == head)
        def _():
            dq_box[head, at] = low

        @pl.when(target != head)
        def _():
            dq_copy(target, head, piece).start()

    @pl.when(last & (turn == 2))
    def _():
        to_below.wait()
        to_above.wait()
        for h in range(heads):
            cols = slice(h * rows, (h + 1) * rows)
            for half, acc in enumerate((dk, dv)):
                lines = slice(half * HD, (half + 1) * HD)
                total = acc[:, cols] + low_box[lines, cols].astype(f32) + high_box[lines, cols].astype(f32)
                dkv_own[h, lines] = total.astype(bf16)
        dkv_spread.all("start")
        dkv_box[head] = dkv_own[head]
        over_pairs.all("arrived")
        total = sum(across_box[z].astype(f32) for z in range(count))
        share_ref[...] = total
        share_low[...] = total.astype(bf16)
        over_full.all("start")
        full[place, pair] = total.astype(bf16)
        grad_q = sum(
            contract(norm_ref[h * rows : (h + 1) * rows], dq_own[h], 0, 0) for h in range(heads)
        )
        grad_kv = sum(
            contract(dkv_own[h], norm_ref[h * rows : (h + 1) * rows], 1, 0) for h in range(heads)
        )
        grad_ref[:, :HD] = grad_q
        grad_ref[:, HD:] = grad_kv.T

        def finish(off):
            other = (head + off) % heads
            for p in range(per):
                dq_copy(other, other, p).wait_recv()
                dq_copy(other, head, p).wait_send()

        each(heads, finish)
        over_full.all("arrived")
        swap(place).start()
        dkv_spread.all("arrived")
        dq_ref[...] = dq_box[...]
        dkv_ref[...] = dkv_box[...]
        swap(place).wait_send()
        swap(1 - place).wait_recv()
        for c in range(2):
            for z in range(count):
                full_ref[z, c] = full[c, z]
        for spread in (dkv_spread, over_heads, over_pairs, over_full):
            spread.all("sent")


def attend_back(query, grad, mix, e, keyval, norm_all, pair_sum, heads, tile, chunk):
    nodes, reach = e.shape
    rows, width = nodes // heads, norm_all.shape[1]
    parts = nodes // tile
    _, count, share, across = pair_sum.shape
    row = lambda width: pl.BlockSpec((tile, width), lambda j, i: (i, 0))
    pair = (heads, count, share, across)
    dma = lambda *shape: pltpu.SemaphoreType.DMA(shape)
    order = lambda j: 2 * j % 3
    return pl.pallas_call(
        functools.partial(attend_back_kernel, chunk=chunk),
        grid=(3, parts),
        in_specs=[
            row(HD),
            row(HD),
            row(2 * HD),
            pl.BlockSpec((tile, nodes), lambda j, i: (i, order(j))),
            pl.BlockSpec((1, nodes, 2 * HD), lambda j, i: (order(j), 0, 0)),
            vmem(),
            vmem(),
        ],
        out_specs=[
            whole((heads, rows, HD)),
            whole((heads, 2 * HD, rows)),
            whole((width, 3 * HD)),
            whole((share, across)),
            whole((count, 2, share, across)),
        ],
        out_shape=[
            jax.ShapeDtypeStruct((heads, rows, HD), bf16),
            jax.ShapeDtypeStruct((heads, 2 * HD, rows), bf16),
            jax.ShapeDtypeStruct((width, 3 * HD), f32),
            jax.ShapeDtypeStruct((share, across), f32),
            jax.ShapeDtypeStruct((count, 2, share, across), bf16),
        ],
        scratch_shapes=[
            pltpu.VMEM((HD, nodes), f32),
            pltpu.VMEM((HD, nodes), f32),
            pltpu.VMEM((nodes, HD), f32),
            *[pltpu.VMEM((2 * HD, nodes), bf16)] * 4,
            *[pltpu.VMEM((heads, rows, HD), bf16)] * 2,
            *[pltpu.VMEM((heads, 2 * HD, rows), bf16)] * 2,
            pltpu.VMEM(pair, bf16),
            *[pltpu.VMEM(pair[1:], bf16)] * 2,
            pltpu.VMEM((share, across), bf16),
            pltpu.VMEM((2, *pair[1:]), bf16),
            dma(2, 2),
            dma(2, heads, rows // tile),
            dma(2, heads),
            dma(2),
            dma(2, heads),
            dma(2, count),
            dma(2, count),
        ],
        compiler_params=remote(60, 5),
        name="attend_back",
    )(query, grad, mix, e, keyval, norm_all, pair_sum)


def middle_kernel(
    place_ref, scale_ref, mixed_ref, zero_ref, wa_ref, wf_ref, mod_ref, wdec_ref, stat_ref,
    node_ref, read_ref, target_ref, eps_ref,
    done_ref, dmix_ref, pair_ref, gdec_ref, gmod_ref, loss_ref,
    one_scr, two_scr, norm_scr, up_scr, act_scr, dec_box, hits, turned, total,
    d_own, d_box, dmix_own, dmix_box, grad, big, pair_box,
    dec_sems, d_sems, dmix_sems, pair_sems, out_sems,
    node_tiles, pixel_tiles,
):
    step = pl.program_id(0)
    heads, rows, _ = mixed_ref.shape
    width = zero_ref.shape[1]
    tile = rows // node_tiles
    head = lax.axis_index("head")
    within, _ = pairs()
    place = within[1]
    count, share = pair_ref.shape[1:3]
    pixel_end = node_tiles + pixel_tiles
    others = nearest_first(head, heads)

    decs = Relay(lambda slot, half: dec_box.at[slot, :, pl.ds(half * tile, tile)], dec_sems)

    d_spread = Spread(along("head"), lambda o: d_own.at[o], lambda i: d_box.at[i], d_sems.at[0], d_sems.at[1])

    def dmix_copy(other, slot, t):
        lines = pl.ds(t * tile, tile)
        return pltpu.make_async_remote_copy(
            src_ref=dmix_own.at[other, lines],
            dst_ref=dmix_box.at[slot, lines],
            send_sem=dmix_sems.at[0, other, t],
            recv_sem=dmix_sems.at[1, slot, t],
            device_id={"head": other},
        )

    def pair_copy(h, part):
        cols = (pl.ds(0, 2 * width), pl.ds(2 * width, HD))[part]
        return pltpu.make_async_remote_copy(
            src_ref=big.at[1 - place, h, :, :, cols],
            dst_ref=pair_box.at[h, :, :, cols],
            send_sem=pair_sems.at[0, part, h],
            recv_sem=pair_sems.at[1, part, h],
            device_id=within[2](1 - place),
        )

    def pack(h, cols):
        for c in range(2):
            for z in range(count):
                at = (2 * z + c) * share
                big[c, h, z, :, cols] = grad[h, at : at + share, cols].astype(bf16)

    @pl.when(step == 0)
    def _():
        meet(["head", "node"])
        turned[...] = jnp.zeros_like(turned)
        total[...] = jnp.zeros_like(total)
        loss_ref[...] = jnp.zeros_like(loss_ref)
        gdec_ref[...] = jnp.zeros_like(gdec_ref)
        gmod_ref[...] = jnp.zeros_like(gmod_ref)

    for t in range(node_tiles):

        @pl.when(step == t)
        def _(t=t, lines=slice(t * tile, (t + 1) * tile)):
            h_one = zero_ref[lines] + sum(
                contract(mixed_ref[h, lines], wa_ref[h, :, 3 * HD :], 1, 1) for h in range(heads)
            )
            one_scr[lines] = h_one
            normed, _ = standardize(h_one)
            norm_two = (normed * (1 + mod_ref[2:3]) + mod_ref[3:4]).astype(bf16)
            norm_scr[lines] = norm_two
            h_two = h_one
            for h in range(heads):
                up = contract(norm_two, wf_ref[h, :, :width], 1, 0)
                up_scr[h, lines] = up
                act = (up * jax.nn.sigmoid(up)).astype(bf16)
                act_scr[h, lines] = act
                h_two = h_two + contract(act, wf_ref[h, :, width:], 1, 1)
            two_scr[lines] = h_two
            final = standardize(h_two)[0].astype(bf16)
            high, low = halves(contract(wdec_ref[...], final, 1, 1))
            dec_box[head, :SLIM, lines] = high
            dec_box[head, SLIM:, lines] = low
            decs.start(((0, t), (1, t)))
            if t == 1:
                decs.hand_on(0)

    @pl.when((step >= node_tiles) & (step < pixel_end))
    def _():
        reads = read_ref[...] - place_ref[0]
        pixels = target_ref.shape[1]
        for h in range(heads):
            spot = lax.broadcasted_iota(jnp.int32, (rows, pixels), 0) + h * rows
            hit = sum((spot == reads[k : k + 1]).astype(f32) for k in range(3)).astype(bf16)
            hits[h * rows : (h + 1) * rows] = hit

        @pl.when(step == node_tiles)
        def _():
            decs.hand_on(1)
            for side in range(2):
                decs.arrived(side)
            decs.arrived_across()

        field = sum(contract(dec_box[h], hits[h * rows : (h + 1) * rows], 1, 0) for h in range(heads))
        field = (field[:VARS] + field[SLIM : SLIM + VARS]) / 3.0
        target = target_ref[...]
        noisy = target + scale_ref[0] * eps_ref[...]
        error = scale_ref[2] * noisy + scale_ref[3] * field - target
        valid = (node_ref[...] - place_ref[0] < place_ref[2]).astype(f32)
        valid_pixels = stat_ref[SLIM - 1 : SLIM, 0:1]
        weighted = valid * (scale_ref[4] / (stat_ref[:VARS, 0:1] / valid_pixels + norm_eps))
        loss_ref[:VARS] += fold_lanes(weighted * error * error)
        high, low = halves(scale_ref[3] * (2.0 / (valid_pixels * VARS)) / 3.0 * weighted * error)
        turned[:VARS] = high
        turned[SLOT : SLOT + VARS] = low
        total[...] += contract(hits[...], turned[...], 1, 1)

    @pl.when(step == pixel_end - 1)
    def _():
        for h in range(heads):
            lines = slice(h * rows, (h + 1) * rows)
            d_own[h] = (total[lines, :SLOT] + total[lines, SLOT:]).astype(bf16)
        for other in others:
            d_spread.copy(other, head).start()
        d_box[head] = d_own[head]

    for t in range(node_tiles):
        final_tile = t == node_tiles - 1

        @pl.when(step == pixel_end + t)
        def _(t=t, lines=slice(t * tile, (t + 1) * tile), final_tile=final_tile):
            normed_two, inv_two = standardize(two_scr[lines])
            final = normed_two.astype(bf16)
            normed_one, inv_one = standardize(one_scr[lines])
            if t == 0:
                for other in others:
                    d_spread.copy(other, other).wait_recv()
            d_dec = sum(d_box[h, lines].astype(f32) for h in range(heads)).astype(bf16)[:, :SLIM]
            gdec_ref[...] += contract(d_dec, final, 0, 0)
            d_two = norm_back(normed_two, inv_two, contract(d_dec, wdec_ref[...], 1, 0))
            d_low = d_two.astype(bf16)
            norm_two = norm_scr[lines]
            d_mid = jnp.zeros_like(d_two)

            def add(h, cols, value):
                if t == 0:
                    grad[h, :, cols] = value
                else:
                    grad[h, :, cols] += value

            for h in range(heads):
                up = up_scr[h, lines]
                d_act = contract(d_low, wf_ref[h, :, width:], 1, 0)
                gating = jax.nn.sigmoid(up)
                d_up = (d_act * gating * (1 + up * (1 - gating))).astype(bf16)
                add(h, slice(0, width), contract(norm_two, d_up, 0, 0))
                add(h, slice(width, 2 * width), contract(d_low, act_scr[h, lines], 0, 0))
                if final_tile:
                    pack(h, slice(0, 2 * width))
                    pair_copy(h, 0).start()
                d_mid += contract(d_up, wf_ref[h, :, :width], 1, 1)
            gmod_ref[0:1] += jnp.sum(d_mid * normed_one, 0, keepdims=True)
            gmod_ref[1:2] += jnp.sum(d_mid, 0, keepdims=True)
            d_one = d_two + norm_back(normed_one, inv_one, d_mid * (1 + mod_ref[2:3]))
            done_ref[lines] = d_one
            one_low = d_one.astype(bf16)
            for h in range(heads):
                dmix_own[h, lines] = contract(one_low, wa_ref[h, :, 3 * HD :], 1, 0).astype(bf16)
            for other in others:
                dmix_copy(other, head, t).start()
            dmix_box[head, lines] = dmix_own[head, lines]
            for h in range(heads):
                add(h, slice(2 * width, 2 * width + HD), contract(one_low, mixed_ref[h, lines], 0, 0))
                if final_tile:
                    pack(h, slice(2 * width, 2 * width + HD))
                    pair_copy(h, 1).start()
            if final_tile:
                for h in range(heads):
                    for part in range(2):
                        pair_copy(h, part).wait_recv()
                    for z in range(count):
                        pair_ref[h, z] = (
                            big[place, h, z].astype(f32) + pair_box[h, z].astype(f32)
                        ).astype(bf16)
                for other in others:
                    for u in range(node_tiles):
                        dmix_copy(other, other, u).wait_recv()
                dmix_ref[...] = dmix_box[...]
                for other in others:
                    d_spread.copy(other, head).wait_send()
                    for u in range(node_tiles):
                        dmix_copy(other, head, u).wait_send()
                decs.sent()
                for h in range(heads):
                    for part in range(2):
                        pair_copy(h, part).wait_send()


def middle(place, scales, mixed, h_zero, w_attn, w_ffn, modulation, w_dec, stat, node_row, read_rows, target, eps, groups):
    heads, rows, _ = mixed.shape
    width = h_zero.shape[1]
    node_tiles, pixels = 2, target.shape[1] // heads
    tile = 512
    pixel_tiles = pixels // tile
    share, count = width // groups, groups // 2
    grads = 2 * width + HD
    pair = (heads, count, share, grads)
    low = lambda *shape: pltpu.VMEM(shape, bf16)
    full = lambda *shape: pltpu.VMEM(shape, f32)
    dma = lambda *shape: pltpu.SemaphoreType.DMA(shape)

    def at(i):
        part = jnp.clip(i - node_tiles, 0, pixel_tiles - 1)
        return 0, lax.axis_index("head") * pixel_tiles + part

    piece = lambda lines: pl.BlockSpec((lines, tile), at)
    return pl.pallas_call(
        functools.partial(middle_kernel, node_tiles=node_tiles, pixel_tiles=pixel_tiles),
        grid=(2 * node_tiles + pixel_tiles,),
        in_specs=[smem(), smem()] + [vmem()] * 7 + [piece(1), piece(3), piece(VARS), piece(VARS)],
        out_specs=[
            whole((rows, width)),
            whole((heads, rows, HD)),
            whole(pair),
            whole((SLIM, width)),
            whole((8, width)),
            whole((SLIM, 128)),
        ],
        out_shape=[
            jax.ShapeDtypeStruct((rows, width), f32),
            jax.ShapeDtypeStruct((heads, rows, HD), bf16),
            jax.ShapeDtypeStruct(pair, bf16),
            jax.ShapeDtypeStruct((SLIM, width), f32),
            jax.ShapeDtypeStruct((8, width), f32),
            jax.ShapeDtypeStruct((SLIM, 128), f32),
        ],
        scratch_shapes=[
            full(rows, width),
            full(rows, width),
            low(rows, width),
            full(heads, rows, width),
            low(heads, rows, width),
            low(heads, 2 * SLIM, rows),
            low(heads * rows, tile),
            low(2 * SLOT, tile),
            full(heads * rows, 2 * SLOT),
            low(heads, rows, SLOT),
            low(heads, rows, SLOT),
            low(heads, rows, HD),
            low(heads, rows, HD),
            full(heads, width, grads),
            low(2, *pair),
            low(*pair),
            dma(2, 3, 2),
            dma(2, heads),
            dma(2, heads, node_tiles),
            dma(2, 2, heads),
            dma(2, heads),
        ],
        compiler_params=remote(62, 7),
        name="middle",
    )(
        place, scales, mixed, h_zero, w_attn, w_ffn, modulation, w_dec, stat, node_row, read_rows, target, eps
    )


def settle_kernel(
    feat_ref, dq_ref, dkv_ref, w_ref, zero_ref, done_ref, in_ref, mod_ref, gdec_ref, gmod_ref, qkv_ref, big_ref, loss_ref,
    small_ref, share_ref, full_ref, sums_ref,
    q_low, q_pair, q_sum, q_box, q_share, q_full,
    parts, part_box, part_sum, part_own, pay, heard, tally, tallies,
    pair_sems, q_sems, f_sems, a_sems, n_sems, b_sems, t_sems, s_sems,
):
    heads, width = w_ref.shape[0], w_ref.shape[1]
    share_rows = share_ref.shape[0]
    head, node = lax.axis_index("head"), lax.axis_index("node")
    groups = heard.shape[0]
    within, across = pairs()
    place, pair, count = within[1], across[1], across[0]

    def to_other(source, target, index):
        return pltpu.make_async_remote_copy(
            src_ref=source,
            dst_ref=target,
            send_sem=pair_sems.at[0, index],
            recv_sem=pair_sems.at[1, index],
            device_id=within[2](1 - place),
        )

    for c in range(2):
        for z in range(count):
            at = (2 * z + c) * share_rows
            q_low[c, z] = qkv_ref[at : at + share_rows].astype(bf16)
    meet(["head", "node"])
    q_pairs = to_other(q_low.at[1 - place], q_pair, 0)
    q_pairs.start()

    d_norm = sum(
        contract(dq_ref[h], w_ref[h, :, :HD], 1, 1)
        + contract(dkv_ref[h], w_ref[h, :, HD : 3 * HD], 0, 1)
        for h in range(heads)
    )
    normed, inv = standardize(zero_ref[...])
    d_zero = done_ref[...] + norm_back(normed, inv, d_norm * (1 + mod_ref[0:1]))

    q_pairs.wait()
    for z in range(count):
        q_sum[z] = (q_low[place, z].astype(f32) + q_pair[z].astype(f32)).astype(bf16)
    q_over = Spread(across, lambda o: q_sum.at[o], lambda i: q_box.at[i], q_sems.at[0], q_sems.at[1])
    q_over.all("start")
    q_box[pair] = q_sum[pair]

    g_enc = contract(in_ref[...].T, d_zero, 1, 0, highest)
    parts[...] = jnp.zeros_like(parts)
    flat = parts.reshape(parts.shape[0] * parts.shape[1], width)
    flat[:VARS] = g_enc[:VARS]
    flat[VARS : 2 * VARS] = g_enc[SLOT : SLOT + VARS]
    flat[2 * VARS : 3 * VARS] = gdec_ref[:VARS]
    at = 3 * VARS
    flat[at : at + 1] = jnp.sum(d_norm * normed, 0, keepdims=True)
    flat[at + 1 : at + 2] = jnp.sum(d_norm, 0, keepdims=True)
    flat[at + 2 : at + 4] = gmod_ref[0:2]
    over_heads = Spread(
        along("head"), lambda o: parts.at[o], lambda i: part_box.at[i], a_sems.at[0], a_sems.at[1]
    )
    over_heads.all("start")
    part_box[head] = parts[head]

    q_over.all("arrived")
    share = sum(q_box[z].astype(f32) for z in range(count))
    share_ref[...] = share
    q_share[...] = share.astype(bf16)
    q_full[place, pair] = share.astype(bf16)
    f_over = Spread(
        across, lambda _: q_share, lambda i: q_full.at[place, i], f_sems.at[0], f_sems.at[1]
    )
    f_over.all("start")

    over_heads.all("arrived")
    total = sum(part_box[h] for h in range(heads))
    for t in range(groups):
        part_sum[t] = total[8 * t : 8 * t + 8]
    over_nodes = Spread(
        along("node"), lambda o: part_sum.at[o], lambda i: part_own.at[i], n_sems.at[0], n_sems.at[1]
    )
    over_nodes.all("start")
    part_own[node] = part_sum[node]

    squares = jnp.sum(share * share) + jnp.sum(big_ref[...] * big_ref[...])
    loss = jnp.sum(loss_ref[:VARS])
    over_nodes.all("arrived")
    own = sum(part_own[t] for t in range(groups))
    row = lax.broadcasted_iota(jnp.int32, own.shape, 0) + 8 * (head * groups + node)
    squares += jnp.sum(own * own * jnp.where(row >= 3 * VARS, feat_ref[0], 1.0))
    line = lax.broadcasted_iota(jnp.int32, (8, 128), 0)
    pay[:, :width] = own
    pay[:, width:] = jnp.where(line == 0, squares, jnp.where(line == 1, loss, 0.0))
    back = Spread(along("node"), lambda _: pay, lambda i: heard.at[i], b_sems.at[0], b_sems.at[1])
    back.all("start")
    heard[node] = pay[...]

    f_over.all("arrived")
    q_rest = to_other(q_full.at[place], q_full.at[place], 1)
    q_rest.start()

    back.all("arrived")
    tally[...] = sum(heard[t, :, width:] for t in range(groups))
    tell = Spread(along("head"), lambda _: tally, lambda i: tallies.at[i], t_sems.at[0], t_sems.at[1])
    tell.all("start")
    tallies[head] = tally[...]
    for t in range(groups):
        small_ref[head, 8 * t : 8 * t + 8] = heard[t, :, :width]
    smalls = Spread(
        along("head"), lambda _: small_ref.at[head], lambda i: small_ref.at[i], s_sems.at[0], s_sems.at[1]
    )
    smalls.all("start")
    tell.all("arrived")
    sums_ref[...] = sum(tallies[h] for h in range(heads))

    q_rest.wait_send()
    to_other(q_full.at[1 - place], q_full.at[1 - place], 1).wait_recv()
    for c in range(2):
        for z in range(count):
            full_ref[2 * z + c] = q_full[c, z]
    smalls.all("arrived")
    for spread in (q_over, over_heads, f_over, over_nodes, back, tell, smalls):
        spread.all("sent")


def settle(feat_sq, dq, dkv, w_attn, h_zero, d_one, node_in, modulation, grad_dec, gmod_two, grad_qkv, big_share, loss, groups):
    heads, rows, _ = dq.shape
    width = h_zero.shape[1]
    count = groups // 2
    share = (grad_qkv.shape[0] // groups, grad_qkv.shape[1])
    low = lambda *shape: pltpu.VMEM(shape, bf16)
    full = lambda *shape: pltpu.VMEM(shape, f32)
    dma = lambda *shape: pltpu.SemaphoreType.DMA(shape)
    return pl.pallas_call(
        settle_kernel,
        in_specs=[smem()] + [vmem()] * 12,
        out_specs=[vmem()] * 4,
        out_shape=[
            jax.ShapeDtypeStruct((heads, 8 * groups, width), f32),
            jax.ShapeDtypeStruct(share, f32),
            jax.ShapeDtypeStruct((groups, *share), bf16),
            jax.ShapeDtypeStruct((8, 128), f32),
        ],
        scratch_shapes=[
            low(2, count, *share),
            low(count, *share),
            low(count, *share),
            low(count, *share),
            low(*share),
            low(2, count, *share),
            full(heads, 8 * groups, width),
            full(heads, 8 * groups, width),
            full(groups, 8, width),
            full(groups, 8, width),
            full(8, width + 128),
            full(groups, 8, width + 128),
            full(8, 128),
            full(heads, 8, 128),
            dma(2, 2),
            dma(2, count),
            dma(2, count),
            dma(2, heads),
            dma(2, groups),
            dma(2, groups),
            dma(2, heads),
            dma(2, heads),
        ],
        compiler_params=remote(56, 1),
        name="settle",
    )(feat_sq, dq, dkv, w_attn, h_zero, d_one, node_in, modulation, grad_dec, gmod_two, grad_qkv, big_share, loss)


def eliminate(work, done):
    count = work.shape[0]
    lane = lax.broadcasted_iota(jnp.int32, (1, BLOCK), 1)
    sub = lax.broadcasted_iota(jnp.int32, (STRIP, BLOCK), 0)
    pivots = [jnp.ones((1, BLOCK), f32) for _ in range(count)]
    both = lambda x: jnp.concatenate([x, x], 1)
    for at in range(0, BLOCK, STRIP):
        strip = slice(at, at + STRIP)
        rows = [work[m, strip] for m in range(count)]
        columns = [
            [jnp.broadcast_to(rows[m][:, at + k : at + k + 1], (STRIP, BLOCK)) for k in range(STRIP)]
            for m in range(count)
        ]
        scale = [jnp.ones((STRIP, BLOCK), f32) for _ in range(count)]
        for r in range(STRIP):
            for m in range(count):
                column = columns[m][r]
                pivot = jnp.broadcast_to(column[r : r + 1], (STRIP, BLOCK))
                factor = jnp.where(sub > r, column * (1.0 / pivot), 0.0)
                scale[m] = jnp.where(sub == r, pivot, scale[m])
                for k in range(r + 1, STRIP):
                    columns[m][k] = columns[m][k] - factor * columns[m][k][r : r + 1]
                pivots[m] = jnp.where(lane == at + r, pivot[:1], pivots[m])
                rows[m] = rows[m] - both(factor) * rows[m][r : r + 1]
        for m in range(count):
            done[m, strip] = rows[m][:, BLOCK:]
            if at + STRIP < BLOCK:
                high, mid, low = thirds(rows[m] * both(lax.rsqrt(scale[m])))
                left = jnp.concatenate([high, high, mid, mid, high, low], 0)[:, :BLOCK]
                right = jnp.concatenate([high, mid, high, mid, low, high], 0)
                rest = slice(at + STRIP, BLOCK)
                work[m, rest] -= contract(left, right, 0, 0)[rest]
    return pivots


def finish_kernel(
    sums_ref, small_ref, qkv_share_ref, big_share_ref, qkv_ref, big_ref, stats_ref, basis_ref,
    layer_ref, first_ref, second_ref, feat_ref,
    enc_ref, enc1_ref, enc2_ref, cond_ref, cond1_ref, cond2_ref, dec_ref, dec1_ref, dec2_ref,
    out_ref, stats_out, layer_out, first_out, second_out,
    enc_out, enc1_out, enc2_out, cond_out, cond1_out, cond2_out, dec_out, dec1_out, dec2_out,
    gram, both, work, done, shares,
):
    count, size = stats_ref.shape[:2]
    k = pl.program_id(0)
    clip = clip_limit / jnp.maximum(jnp.sqrt(sums_ref[0:1, 0:1]), clip_limit)

    @pl.when(k == 0)
    def _():
        cuts = [slice(0, size), slice(size, 2 * size), slice(2 * size, 3 * size)]
        shares[0] = jnp.concatenate([qkv_share_ref[...], big_share_ref[:, cuts[2].start :]], 1)
        grads = [jnp.concatenate([qkv_ref[...], big_ref[:, cuts[2].start :]], 1)]
        for m in (1, 2):
            shares[m] = big_share_ref[:, cuts[m - 1]]
            grads.append(big_ref[:, cuts[m - 1]])
        for m in range(count):
            raw = contract(grads[m], grads[m], 0, 0)
            new = beta_stats * stats_ref[m] + (1 - beta_stats) * (clip * (clip * raw))
            stats_out[m] = new
            product = contract(new, basis_ref[m], 1, 0, highest)
            both[m] = product
            gram[m] = contract(product, product, 0, 0, highest)

    i = jnp.minimum(k, count - 1)
    rotated = contract(clip * shares[i], basis_ref[i], 1, 0, highest)
    first_new = beta_first * first_ref[i] + (1 - beta_first) * rotated
    second_new = beta_second * second_ref[i] + (1 - beta_second) * rotated * rotated
    first_out[i] = first_new
    second_out[i] = second_new
    direction = (
        first_new
        / (1 - beta_first**STEP)
        / (jnp.sqrt(second_new / (1 - beta_second**STEP)) + adam_epsilon)
    )
    layer_out[i] = layer_ref[i] - rate_layer * (
        contract(direction, basis_ref[i], 1, 1, highest) + decay_rate * layer_ref[i]
    )

    at = pl.ds(pl.multiple_of(k * BLOCK, BLOCK), BLOCK)
    unit = lax.broadcasted_iota(jnp.int32, (BLOCK, BLOCK), 0) == lax.broadcasted_iota(
        jnp.int32, (BLOCK, BLOCK), 1
    )
    for m in range(count):
        work[m, :, :BLOCK] = gram[m, at, at]
        work[m, :, BLOCK:] = unit.astype(f32)
    roots = [lax.rsqrt(p) for p in eliminate(work, done)]
    for step in range(size // BLOCK):

        @pl.when(k == step)
        def _(here=slice(step * BLOCK, (step + 1) * BLOCK), rest=(step + 1) * BLOCK):
            for m in range(count):
                factor = done[m]
                panel = contract(both[m, :, here], factor, 1, 1, highest) * roots[m]
                out_ref[m] = panel
                if rest < size:
                    left = contract(gram[m, rest:, here], factor, 1, 1, highest) * roots[m]
                    both[m, :, rest:] -= contract(panel, left, 1, 1, highest)
                    gram[m, rest:, rest:] -= contract(left, left, 1, 1, highest)

    @pl.when(k == pl.num_programs(0) - 1)
    def _():
        flat = clip * small_ref[...]

        def adam(grad, cols, refs, outs):
            for out, new in zip(outs, adam_small(refs[0][:, cols], grad, refs[1][:, cols], refs[2][:, cols])):
                out[:, cols] = new

        every = slice(None)
        adam(flat[: 2 * VARS], every, (enc_ref, enc1_ref, enc2_ref), (enc_out, enc1_out, enc2_out))
        adam(flat[2 * VARS : 3 * VARS], every, (dec_ref, dec1_ref, dec2_ref), (dec_out, dec1_out, dec2_out))
        width = flat.shape[1]
        for j in range(4):
            grad = feat_ref[:, 0:1] * flat[3 * VARS + j : 3 * VARS + j + 1]
            adam(
                grad,
                slice(j * width, (j + 1) * width),
                (cond_ref, cond1_ref, cond2_ref),
                (cond_out, cond1_out, cond2_out),
            )


def finish(sums, small, qkv_share, big_share, qkv_full, big_full, stats, basis, layers, feat, enc, cond, dec):
    count, size = stats.shape[:2]
    inputs = (sums, small, qkv_share, big_share, qkv_full, big_full, stats, basis, *layers, feat, *enc, *cond, *dec)
    like = lambda x: jax.ShapeDtypeStruct(x.shape, f32)
    outs = [stats, *layers, *enc, *cond, *dec]
    return pl.pallas_call(
        finish_kernel,
        grid=(size // BLOCK,),
        in_specs=[whole(x.shape) for x in inputs],
        out_specs=[pl.BlockSpec((count, size, BLOCK), lambda k: (0, 0, k))] + [whole(x.shape) for x in outs],
        out_shape=[like(stats)] + [like(x) for x in outs],
        scratch_shapes=[
            pltpu.VMEM((count, size, size), f32),
            pltpu.VMEM((count, size, size), f32),
            pltpu.VMEM((count, BLOCK, 2 * BLOCK), f32),
            pltpu.VMEM((count, BLOCK, BLOCK), f32),
            pltpu.VMEM(layers[0].shape, f32),
        ],
        compiler_params=params(60),
        name="finish",
    )(*inputs)


def local(
    prev_state,
    target,
    noise_eps,
    noise_level,
    valid_count,
    neighbours,
    nbr_count,
    pix_node,
    pix_read,
    w_enc,
    w_cond,
    w_dec,
    layer_w,
    soap_first,
    soap_second,
    soap_basis,
    soap_stats,
    enc_first,
    enc_second,
    cond_first,
    cond_second,
    dec_first,
    dec_second,
):
    nodes = nbr_count.shape[0]
    groups = lax.axis_size("node")
    heads = lax.axis_size("head")
    rows = nodes // heads
    block_start = lax.axis_index("node") * nodes
    quarter = lax.axis_index("head")
    width = w_enc.shape[1]
    both = ("head", "node")

    low_w = layer_w.astype(bf16)
    ffn_share = jnp.concatenate([low_w[1], low_w[2]], 1)
    noise_sigma, noise_feat = noise_terms(noise_level)
    sig_sq = noise_sigma * noise_sigma
    input_scale = lax.rsqrt(sig_sq + 1.0)
    skip_scale = 1.0 / (sig_sq + 1.0)
    output_scale = noise_sigma * lax.rsqrt(sig_sq + 1.0)
    loss_scale = (sig_sq + 1.0) / sig_sq
    modulation = jnp.dot(noise_feat[None, :], w_cond, precision=highest).reshape(4, width)

    prev_t, target_t, eps_t = prev_state.T, target.T, noise_eps.T
    node_row = pix_node.reshape(1, -1)
    read_rows = pix_read.T
    place = jnp.stack([block_start, quarter * rows, valid_count[0], quarter]).astype(jnp.int32)
    node_in, stat, column, w_attn = encode(
        place, jnp.stack([noise_sigma, input_scale]), node_row, prev_t, target_t, eps_t, low_w[0],
        rows, 1024, groups
    )
    w_attn = w_attn.reshape(width, -1)

    pad_enc = jnp.zeros((2, SLOT, width), bf16)
    pad_enc = pad_enc.at[:, :VARS].set(w_enc.astype(bf16).reshape(2, VARS, width))
    h_zero, norm_all, query, keyval, stat, counts = open_nodes(
        node_in, pad_enc.reshape(2 * SLOT, width), modulation, stat, w_attn, neighbours.T,
        nbr_count.reshape(1, -1), heads, groups,
    )
    norm_all, query = norm_all.reshape(nodes, -1), query.reshape(nodes, -1)
    keyval = keyval.reshape(3, nodes, -1)
    loss_count = stat[SLIM - 1, 0] * VARS
    e, mix, mixed, attn_all, ffn_all = attend(query, keyval, counts, column, ffn_share, heads, 128, 512)
    attn_all = attn_all.reshape(heads, width, -1)
    ffn_all = ffn_all.reshape(heads, width, -1)

    w_dec_t = jnp.zeros((SLIM, width), bf16).at[:VARS].set(w_dec.T.astype(bf16))
    scales = jnp.stack([noise_sigma, input_scale, skip_scale, output_scale, loss_scale])
    d_one, d_mixed, pair_sum, grad_dec, gmod_two, loss_part = middle(
        place, scales, mixed, h_zero, attn_all, ffn_all, modulation, w_dec_t, stat, node_row, read_rows,
        target_t, eps_t, groups,
    )
    d_mixed = d_mixed.reshape(nodes, HD)
    dq, dkv, grad_qkv, big_share, big_full = attend_back(
        query, d_mixed, mix, e, keyval, norm_all, pair_sum, heads, 256, 512
    )
    feat_sq = jnp.sum(noise_feat * noise_feat).reshape(1)
    small, qkv_share, qkv_full, sums = settle(
        feat_sq, dq, dkv, attn_all, h_zero, d_one, node_in, modulation, grad_dec, gmod_two, grad_qkv, big_share,
        loss_part, groups,
    )
    basis_new, stats_new, layer_new, first_new, second_new, *small_new = finish(
        sums,
        small.reshape(-1, width),
        qkv_share,
        big_share,
        qkv_full.reshape(width, -1),
        big_full.reshape(width, -1),
        soap_stats[:, 0],
        soap_basis[:, 0],
        (layer_w, soap_first, soap_second),
        jnp.broadcast_to(noise_feat[:, None], (NF, 128)),
        (w_enc, enc_first, enc_second),
        (w_cond, cond_first, cond_second),
        (w_dec.T, dec_first.T, dec_second.T),
    )
    return (
        jnp.reshape(sums[1, 0], (1,)),
        jnp.reshape(loss_count, (1,)),
        jnp.reshape(jnp.sqrt(sums[0, 0]), (1,)),
        layer_new,
        first_new,
        second_new,
        basis_new[:, None],
        stats_new[:, None],
        *small_new[:6],
        *(x.T for x in small_new[6:]),
    )


def solution(mesh):
    pixel = P("node", None)
    layer = P(None, "node", "head")
    basis = P(None, "head", None, None)
    placed = (
        *(pixel,) * 3,
        P(),
        P("node"),
        P("node", None),
        P("node"),
        P("node"),
        P("node", None),
        *(P(),) * 3,
        *(layer,) * 3,
        *(basis,) * 2,
        *(P(),) * 6,
    )
    return jax.shard_map(
        local,
        mesh=mesh,
        in_specs=placed,
        out_specs=(*(P(),) * 3, *(layer,) * 3, *(basis,) * 2, *(P(),) * 9),
        check_vma=False,
    )
```

```python
import functools
import math

import jax
import jax.numpy as jnp
from jax import lax
from jax.experimental import pallas as pl
from jax.experimental.pallas import tpu as pltpu
from jax.sharding import PartitionSpec as P

HD = 128
VARS = 84
NF = 32
NBR = 16
LEVELS = 1000
STEP = 10

SLOT = 128
SLIM = 96
GROUP = 256 // NBR
BLOCK = 128
STRIP = 16
HEAD_STEP = 8

highest = lax.Precision.HIGHEST
clip_limit = 0.01
beta_first = 0.9
beta_second = 0.95
beta_stats = 0.95
adam_epsilon = 1e-08
rate_layer = 0.02
rate_small = 0.05
decay_rate = 0.1
norm_eps = 1e-05

f32 = jnp.float32
bf16 = jnp.bfloat16
MIB = 2**20


def passed_along(x, axis, by):
    length = lax.axis_size(axis)
    return lax.ppermute(x, axis, [(i, (i + by) % length) for i in range(length)])


def noise_terms(noise_level):
    level_frac = noise_level[0].astype(f32) / (LEVELS - 1)
    noise_sigma = 0.05 * jnp.exp(level_frac * math.log(40.0))
    frequency = 1.0 + jnp.arange(NF // 2).astype(f32)
    phase_angle = jnp.log(noise_sigma) * frequency
    return (noise_sigma, jnp.concatenate([jnp.sin(phase_angle), jnp.cos(phase_angle)]))


def standardize(values_in):
    row_mean = jnp.mean(values_in, -1, keepdims=True)
    centered = values_in - row_mean
    inv_std = lax.rsqrt(jnp.mean(centered * centered, -1, keepdims=True) + norm_eps)
    return (centered * inv_std, inv_std)


def norm_back(normed, inv_std, grad_in):
    return inv_std * (
        grad_in
        - jnp.mean(grad_in, -1, keepdims=True)
        - normed * jnp.mean(grad_in * normed, -1, keepdims=True)
    )


def contract(left, right, left_dim, right_dim, precision=None):
    return lax.dot_general(
        left,
        right,
        (((left_dim,), (right_dim,)), ((), ())),
        preferred_element_type=f32,
        precision=precision,
    )


def halves(x):
    high = x.astype(bf16)
    return high, (x - high.astype(f32)).astype(bf16)


def thirds(x):
    high = x.astype(bf16)
    rest = x - high.astype(f32)
    return (high, *halves(rest))


def fold_lanes(x, op=jnp.add):
    parts = [x[:, i : i + 128] for i in range(0, x.shape[1], 128)]
    while len(parts) > 1:
        parts = [op(*parts[i : i + 2]) if i + 1 < len(parts) else parts[i] for i in range(0, len(parts), 2)]
    return parts[0]


def adam_small(weight, grad_item, first, second):
    first_new = beta_first * first + (1 - beta_first) * grad_item
    second_new = beta_second * second + (1 - beta_second) * grad_item * grad_item
    ratio = (
        first_new
        / (1 - beta_first**STEP)
        / (jnp.sqrt(second_new / (1 - beta_second**STEP)) + adam_epsilon)
    )
    return (weight - rate_small * (ratio + decay_rate * weight), first_new, second_new)


def smem():
    return pl.BlockSpec(memory_space=pltpu.SMEM)


def whole(shape):
    zeros = (0,) * len(shape)
    return pl.BlockSpec(tuple(shape), lambda *_: zeros)


def params(mib=48):
    return pltpu.CompilerParams(vmem_limit_bytes=mib * MIB)


def remote(mib, identity):
    return pltpu.CompilerParams(
        vmem_limit_bytes=mib * MIB, collective_id=identity, has_side_effects=True
    )


def vmem():
    return pl.BlockSpec(memory_space=pltpu.VMEM)


def hbm():
    return pl.BlockSpec(memory_space=pl.ANY)


def each(count, act, start=1):
    def body(off, carry):
        act(off)
        return carry

    lax.fori_loop(start, count, body, 0)


def meet(axes):
    barrier = pltpu.get_barrier_semaphore()
    total = 0
    for axis in axes:
        count, me = lax.axis_size(axis), lax.axis_index(axis)
        total += count - 1
        each(
            count,
            lambda off: pl.semaphore_signal(barrier, inc=1, device_id={axis: (me + off) % count}),
        )
    pl.semaphore_wait(barrier, total)


class Spread:
    def __init__(self, group, source, target, sends, receives):
        self.count, self.me, self.where = group
        self.source, self.target = source, target
        self.sends, self.receives = sends, receives

    def copy(self, other, slot):
        return pltpu.make_async_remote_copy(
            src_ref=self.source(other),
            dst_ref=self.target(slot),
            send_sem=self.sends.at[other],
            recv_sem=self.receives.at[slot],
            device_id=self.where(other),
        )

    def other(self, off):
        return (self.me + off) % self.count

    def start(self, off):
        self.copy(self.other(off), self.me).start()

    def arrived(self, off):
        self.copy(self.other(off), self.other(off)).wait_recv()

    def sent(self, off):
        self.copy(self.other(off), self.me).wait_send()

    def all(self, act):
        each(self.count, getattr(self, act))


def along(axis):
    return lax.axis_size(axis), lax.axis_index(axis), lambda other: {axis: other}


def pairs():
    node = lax.axis_index("node")
    place, pair = node % 2, node // 2
    within = (2, place, lambda other: {"node": 2 * pair + other})
    across = (lax.axis_size("node") // 2, pair, lambda other: {"node": 2 * other + place})
    return within, across


class Relay:
    def __init__(self, part, sems):
        me = lax.axis_index("head")
        self.me, self.near, self.across = me, (me + 1 - 2 * (me % 2), (me + 2) % 4), 3 - me
        self.part, self.sems = part, sems

    def copy(self, kind, target, slot, half):
        return pltpu.make_async_remote_copy(
            src_ref=self.part(slot, half),
            dst_ref=self.part(slot, half),
            send_sem=self.sems.at[0, kind, half],
            recv_sem=self.sems.at[1, kind, half],
            device_id={"head": target},
        )

    def start(self, halves=((0, 0), (1, 1), (0, 1), (1, 0))):
        for side, half in halves:
            self.copy(side, self.near[side], self.me, half).start()

    def hand_on(self, side):
        self.copy(side, self.near[side], self.near[side], side).wait_recv()
        self.copy(2, self.near[1 - side], self.near[side], side).start()

    def arrived(self, side):
        self.copy(side, self.near[side], self.near[side], 1 - side).wait_recv()

    def arrived_across(self):
        for half in range(2):
            self.copy(2, self.near[half], self.across, half).wait_recv()

    def sent(self):
        for half in range(2):
            for side in range(2):
                self.copy(side, self.near[side], self.me, half).wait_send()
            self.copy(2, self.near[1 - half], self.near[half], half).wait_send()


def count_tile(band_rows, spot_rows, put, bands):
    lane = lax.broadcasted_iota(jnp.int32, (GROUP, 256), 1)
    sub = lax.broadcasted_iota(jnp.int32, (GROUP, 256), 0)
    own = lane % GROUP == sub
    widen = (lane // GROUP == sub).astype(f32).astype(bf16)
    all_bands = contract(band_rows, widen, 0, 0)
    all_spots = contract(spot_rows, widen, 0, 0)
    spot = lax.broadcasted_iota(jnp.int32, (256, 256), 0).astype(f32)
    for g in range(band_rows.shape[1] // GROUP):
        nodes = slice(g * GROUP, (g + 1) * GROUP)
        band = jnp.where(own, all_bands[nodes], -1.0)
        left = jnp.concatenate([(band == t).astype(f32).astype(bf16) for t in range(bands)], 0)
        row = jnp.sum(jnp.where(own, all_spots[nodes], 0.0), 0, keepdims=True)
        right = (spot == row).astype(f32).astype(bf16)
        found = contract(left, right, 1, 1).astype(bf16)
        for t in range(bands):
            put(g, t, found[t * GROUP : (t + 1) * GROUP])


def nearest_first(me, count):
    if count == 4:
        return [me + 1 - 2 * (me % 2), (me + 2) % 4, 3 - me]
    return [(me + k) % count for k in range(1, count)]


def enter_kernel(
    place_ref, scale_ref, node_ref, prev_ref, target_ref, eps_ref, share_ref, wenc_ref, mod_ref, nbr_ref, live_ref,
    in_ref, own_ref, zero_ref, sum_ref, norm_out, q_out, kv_out, count_ref,
    pix, box, pair_box, gathered, w_flat, stat_ref, stat_own, stat_box, norm_ref, q_ref, kv_ref, bands, spots, tiles,
    weight_sems, swap_sems, head_sems, stat_sems, halo_sems, out_sems, put_sems,
):
    step = pl.program_id(0)
    last = pl.num_programs(0) - 1
    within, across = pairs()
    place = within[1]
    weights = Spread(across, lambda _: share_ref, lambda i: box.at[i], weight_sems.at[0], weight_sems.at[1])
    swap = pltpu.make_async_remote_copy(
        src_ref=box,
        dst_ref=pair_box,
        send_sem=swap_sems.at[0],
        recv_sem=swap_sems.at[1],
        device_id=within[2](1 - place),
    )

    @pl.when(step == 0)
    def _():
        meet(["head", "node"])
        weights.all("start")
        box[weights.me] = share_ref[...]
        pix[...] = jnp.zeros_like(pix)
        in_ref[...] = jnp.zeros_like(in_ref)
        stat_ref[...] = jnp.zeros_like(stat_ref)

    @pl.when(step == last - 1)
    def _():
        weights.all("arrived")
        swap.start()

    @pl.when(step < last)
    def _():
        rows, tile = in_ref.shape[0], node_ref.shape[1]
        prev = prev_ref[...]
        target = target_ref[...]
        noisy = target + scale_ref[0] * eps_ref[...]
        pix[:VARS] = prev.astype(bf16)
        pix[SLOT : SLOT + VARS] = (scale_ref[1] * noisy).astype(bf16)
        node = node_ref[...] - place_ref[0]
        mine = node - place_ref[1]
        spot = lax.broadcasted_iota(jnp.int32, (rows, tile), 0)
        onehot = (spot == mine).astype(f32).astype(bf16)
        in_ref[...] += contract(onehot, pix[...], 1, 1)
        valid = (node < place_ref[2]).astype(f32)
        residual = target - prev
        stat_ref[:VARS] += fold_lanes(valid * residual * residual)
        stat_ref[SLIM - 1 : SLIM] += fold_lanes(valid)

    @pl.when(step == last)
    def _():
        heads, rows, _ = norm_ref.shape
        head, node = lax.axis_index("head"), lax.axis_index("node")
        groups = lax.axis_size("node")
        depth = tiles.shape[1]
        nodes = count_ref.shape[0]
        steps = nodes // depth
        stat_own[...] = jnp.broadcast_to(jnp.sum(stat_ref[...], 1, keepdims=True), stat_own.shape)
        stats = Spread(along("node"), lambda _: stat_own, lambda i: stat_box.at[i], stat_sems.at[0], stat_sems.at[1])
        stats.all("start")
        w_enc = wenc_ref[...]
        h_zero = sum(contract(part, w_enc, 1, 0) for part in thirds(in_ref[...]))
        zero_ref[...] = h_zero
        normed, _ = standardize(h_zero)
        norm_ref[head] = (normed * (1 + mod_ref[0:1]) + mod_ref[1:2]).astype(bf16)
        half_rows = rows // 2
        norms = Relay(lambda slot, half: norm_ref.at[slot, pl.ds(half * half_rows, half_rows)], head_sems)
        norms.start()

        def halo(block):
            return [
                pltpu.make_async_remote_copy(
                    src_ref=kv_ref.at[1, block],
                    dst_ref=kv_ref.at[2 * side, block],
                    send_sem=halo_sems.at[2 * side, block],
                    recv_sem=halo_sems.at[2 * side + 1, block],
                    device_id={"node": (node + by) % groups},
                )
                for side, by in enumerate((1, groups - 1))
            ]

        def project(block):
            out = contract(norm_ref[block], w_flat[...], 1, 0).astype(bf16)
            q_ref[block] = out[:, :HD]
            kv_ref[1, block] = out[:, HD:]
            for copy in halo(block):
                copy.start()

        def count(step):
            slot = step % 2

            @pl.when(step >= 2)
            def _():
                count_out(step - 2).wait()

            here = pl.ds(pl.multiple_of(step * depth, depth), depth)

            def put(g, t, found):
                tiles[slot, g * GROUP : (g + 1) * GROUP, t * 256 : (t + 1) * 256] = found

            count_tile(bands[:, here], spots[:, here], put, tiles.shape[2] // 256)
            count_out(step).start()

        def count_out(step):
            return pltpu.make_async_copy(
                tiles.at[step % 2],
                count_ref.at[pl.ds(pl.multiple_of(step * depth, depth), depth)],
                out_sems.at[step % 2],
            )

        swap.wait()
        gathered[:, place] = box[...]
        gathered[:, 1 - place] = pair_box[...]
        flat = gathered[...].astype(f32).reshape(w_flat.shape[0], -1)
        w_flat[...] = flat[:, : 3 * HD].astype(bf16)
        own_ref[...] = box[...]
        project(head)
        total = nodes * groups
        relative = nbr_ref[...] - node * nodes + nodes
        relative = jnp.where(relative >= total, relative - total, relative)
        relative = jnp.where(relative < 0, relative + total, relative)
        live = lax.broadcasted_iota(jnp.int32, relative.shape, 0) < live_ref[...]
        bands[...] = jnp.where(live, relative >> 8, -1).astype(f32).astype(bf16)
        spots[...] = (relative & 255).astype(f32).astype(bf16)
        each(steps // 4, count, 0)
        norms.hand_on(0)
        norms.hand_on(1)
        each(steps * 3 // 8, count, steps // 4)
        for side in range(2):
            norms.arrived(side)
            project(norms.near[side])
        each(steps * 5 // 8, count, steps * 3 // 8)
        norms.arrived_across()
        project(norms.across)
        each(steps, count, steps * 5 // 8)
        each(steps, lambda step: count_out(step).wait(), steps - 2)
        stats.all("arrived")
        sum_ref[...] = sum(jnp.where(t == node, stat_own[...], stat_box[t]) for t in range(groups))

        def finish(block):
            for copy in halo(block):
                copy.wait()

        each(heads, finish, 0)
        norms.sent()
        stats.all("sent")
        outs = [
            pltpu.make_async_copy(source, target, put_sems.at[i])
            for i, (source, target) in enumerate(((norm_ref, norm_out), (q_ref, q_out), (kv_ref, kv_out)))
        ]
        for put in outs:
            put.start()
        for put in outs:
            put.wait()
        weights.all("sent")


def enter(
    place, scales, node_row, prev, target, eps, w_share, w_enc, modulation, neighbours, live, rows, tile, heads, groups
):
    steps = prev.shape[1] // tile
    width = w_enc.shape[1]
    depth = 8 * GROUP
    nodes = heads * rows
    reach = 3 * nodes
    column = (groups // 2, *w_share.shape)
    gathered = (groups // 2, 2, *w_share.shape)
    at = lambda i: (0, jnp.minimum(i, steps - 1))
    pixel_block = pl.BlockSpec((VARS, tile), at)
    full = lambda *shape: (shape, f32)
    low = lambda *shape: (shape, bf16)
    kept = [low(heads, rows, width), low(heads, rows, HD), low(3, heads, rows, 2 * HD)]
    blocks = [full(rows, 2 * SLOT), low(*column), full(rows, width), full(SLIM, 128)]
    dma = lambda *shape: pltpu.SemaphoreType.DMA(shape)
    return pl.pallas_call(
        enter_kernel,
        grid=(steps + 1,),
        in_specs=[smem(), smem(), pl.BlockSpec((1, tile), at)] + [pixel_block] * 3 + [vmem()] * 5,
        out_specs=[whole(shape) for shape, _ in blocks] + [hbm()] * 4,
        out_shape=[jax.ShapeDtypeStruct(*x) for x in blocks + kept + [low(nodes, reach)]],
        scratch_shapes=[
            pltpu.VMEM((2 * SLOT, tile), bf16),
            pltpu.VMEM(column, bf16),
            pltpu.VMEM(column, bf16),
            pltpu.VMEM(gathered, bf16),
            pltpu.VMEM((width, 3 * HD), bf16),
            pltpu.VMEM((SLIM, 128), f32),
            pltpu.VMEM((SLIM, 128), f32),
            pltpu.VMEM((groups, SLIM, 128), f32),
            *[pltpu.VMEM(*x) for x in kept],
            pltpu.VMEM((NBR, nodes), bf16),
            pltpu.VMEM((NBR, nodes), bf16),
            pltpu.VMEM((2, depth, reach), bf16),
            dma(2, groups // 2),
            dma(2),
            dma(2, 3, 2),
            dma(2, groups),
            dma(4, heads),
            dma(2),
            dma(3),
        ],
        compiler_params=remote(56, 3),
        name="enter",
    )(place, scales, node_row, prev, target, eps, w_share, w_enc, modulation, neighbours, live)


def attend_kernel(
    q_ref, kv_ref, count_ref, column_ref, ffn_ref, e_ref, mix_ref, out_ref, attn_out, ffn_out, s_scr, own, box, attn_all, ffn_all, sems,
    attn_sems, column_sems, ffn_sems, pair_sems, local_sems, put_sems, chunk
):
    step = pl.program_id(0)
    steps = pl.num_programs(0)
    head = lax.axis_index("head")
    tile = q_ref.shape[0]
    per = box.shape[1] // tile

    def copy(target, source, part):
        at = pl.ds(pl.multiple_of(part * tile, tile), tile)
        return pltpu.make_async_remote_copy(
            src_ref=own.at[target, at],
            dst_ref=box.at[source, at],
            send_sem=sems.at[0, target, part],
            recv_sem=sems.at[1, source, part],
            device_id={"head": target},
        )

    within, across = pairs()
    place, pair = within[1], across[1]
    ffn_pairs = Spread(
        across, lambda _: ffn_ref, lambda i: ffn_all.at[head, i, place], column_sems.at[0], column_sems.at[1]
    )
    count = across[0]

    def half_of(array):
        return lambda slot, half: array.at[slot, pl.ds(half * (count // 2), count // 2), place]

    attn_heads = Relay(half_of(attn_all), attn_sems)
    ffn_heads = Relay(half_of(ffn_all), ffn_sems)
    stay = [
        pltpu.make_async_copy(column_ref, attn_all.at[head, :, place], local_sems.at[0]),
        pltpu.make_async_copy(ffn_ref, ffn_all.at[head, pair, place], local_sems.at[1]),
    ]

    def swap(h, which, side):
        array = (attn_all, ffn_all)[which]
        return pltpu.make_async_remote_copy(
            src_ref=array.at[h, :, side],
            dst_ref=array.at[h, :, side],
            send_sem=pair_sems.at[0, which, h],
            recv_sem=pair_sems.at[1, which, h],
            device_id=within[2](1 - place),
        )

    @pl.when(step == 0)
    def _():
        for copy in stay:
            copy.start()
        meet(["head", "node"])
        ffn_pairs.all("start")
        for copy in stay:
            copy.wait()
        attn_heads.start()

    def exchange(which, blocks):
        for h in blocks:
            swap(h, which, place).start()

    def put(which, h):
        array, out = ((attn_all, attn_out), (ffn_all, ffn_out))[which]
        return pltpu.make_async_copy(array.at[h], out.at[h], put_sems.at[which, h])

    def put_all(which, blocks):
        for h in blocks:
            swap(h, which, 1 - place).wait_recv()
            put(which, h).start()

    near, beyond = list(attn_heads.near), attn_heads.across

    @pl.when(step == 5)
    def _():
        attn_heads.hand_on(0)
        attn_heads.hand_on(1)
        ffn_pairs.all("arrived")
        ffn_heads.start()
        exchange(0, [head])
        exchange(1, [head])

    @pl.when(step == 8)
    def _():
        for side in range(2):
            attn_heads.arrived(side)
        attn_heads.arrived_across()
        exchange(0, near + [beyond])

    @pl.when(step == 11)
    def _():
        for side in range(2):
            ffn_heads.hand_on(side)
        for side in range(2):
            ffn_heads.arrived(side)
        exchange(1, near)
        put_all(0, [head, *near, beyond])
        put_all(1, [head])

    @pl.when(step == 14)
    def _():
        ffn_heads.arrived_across()
        exchange(1, [beyond])
        put_all(1, near)

    @pl.when(step == 15)
    def _():
        put_all(1, [beyond])

    nodes = kv_ref.shape[1]
    q = q_ref[...]
    top = jnp.full((tile, 128), -1e30, f32)
    for b in range(3):
        for at in range(0, nodes, chunk):
            cols = slice(b * nodes + at, b * nodes + at + chunk)
            s = contract(q, kv_ref[b, at : at + chunk, :HD], 1, 1)
            s = jnp.where(count_ref[:, cols].astype(f32) > 0, s, -1e30)
            s_scr[:, cols] = s
            top = jnp.maximum(top, fold_lanes(s, jnp.maximum))
    top = jnp.max(top, 1, keepdims=True)
    factor = math.log2(math.e) / math.sqrt(HD)
    total = jnp.zeros((tile, 128), f32)
    mixed = jnp.zeros((tile, HD), f32)
    for b in range(3):
        for at in range(0, nodes, chunk):
            cols = slice(b * nodes + at, b * nodes + at + chunk)
            e = count_ref[:, cols].astype(f32) * jnp.exp2((s_scr[:, cols] - top) * factor)
            total += fold_lanes(e)
            e = e.astype(bf16)
            e_ref[:, cols] = e
            mixed += contract(e, kv_ref[b, at : at + chunk, HD:], 1, 0)
    inverse = 1.0 / jnp.sum(total, 1, keepdims=True)
    mixed = mixed * inverse
    mix_ref[:, :HD] = mixed
    mix_ref[:, HD:] = jnp.broadcast_to(inverse, (tile, HD))
    target, part = step // per, step % per
    at = pl.ds(pl.multiple_of(part * tile, tile), tile)
    low = mixed.astype(bf16)
    own[target, at] = low

    @pl.when(target == head)
    def _():
        box[head, at] = low

    @pl.when(target != head)
    def _():
        copy(target, head, part).start()

    @pl.when(step == steps - 1)
    def _():
        heads = box.shape[0]

        def finish(off):
            other = (head + off) % heads
            for p in range(per):
                copy(other, other, p).wait_recv()
                copy(other, head, p).wait_send()

        each(heads, finish)
        out_ref[...] = box[...]

        def end(h):
            for which in range(2):
                put(which, h).wait()
                swap(h, which, place).wait_send()

        each(heads, end, 0)
        ffn_pairs.all("sent")
        attn_heads.sent()
        ffn_heads.sent()


def attend(query, keyval, counts, column, ffn_share, heads, tile, chunk):
    nodes, reach = counts.shape
    rows = nodes // heads
    count = column.shape[0]
    dma = lambda *shape: pltpu.SemaphoreType.DMA(shape)
    row = lambda width: pl.BlockSpec((tile, width), lambda i: (i, 0))
    return pl.pallas_call(
        functools.partial(attend_kernel, chunk=chunk),
        grid=(nodes // tile,),
        in_specs=[row(HD), whole(keyval.shape), row(reach), hbm(), hbm()],
        out_specs=[row(reach), row(2 * HD), whole((heads, rows, HD)), hbm(), hbm()],
        out_shape=[
            jax.ShapeDtypeStruct((nodes, reach), bf16),
            jax.ShapeDtypeStruct((nodes, 2 * HD), f32),
            jax.ShapeDtypeStruct((heads, rows, HD), bf16),
            jax.ShapeDtypeStruct((heads, count, 2, *column.shape[1:]), bf16),
            jax.ShapeDtypeStruct((heads, count, 2, *ffn_share.shape), bf16),
        ],
        scratch_shapes=[
            pltpu.VMEM((tile, reach), f32),
            pltpu.VMEM((heads, rows, HD), bf16),
            pltpu.VMEM((heads, rows, HD), bf16),
            pltpu.VMEM((heads, count, 2, *column.shape[1:]), bf16),
            pltpu.VMEM((heads, count, 2, *ffn_share.shape), bf16),
            dma(2, heads, rows // tile),
            dma(2, 3, 2),
            dma(2, count),
            dma(2, 3, 2),
            dma(2, 2, heads),
            dma(2),
            dma(2, heads),
        ],
        compiler_params=remote(60, 4),
        name="attend",
    )(query, keyval, counts, column, ffn_share)


def attend_back_kernel(
    q_ref, d_ref, mix_ref, e_ref, kv_ref, norm_ref, pair_sum,
    dq_ref, dkv_ref, grad_ref, share_ref, full_ref,
    dk, dv, dq, low_own, high_own, low_box, high_box, dq_own, dq_box, dkv_own, dkv_box,
    head_box, across_own, across_box, share_low, full,
    halo_sems, dq_sems, dkv_sems, pair_sems, head_sems, across_sems, full_sems,
    chunk,
):
    turn, part = pl.program_id(0), pl.program_id(1)
    parts = pl.num_programs(1)
    step = turn * parts + part
    tile = q_ref.shape[0]
    nodes = kv_ref.shape[1]
    heads, rows, _ = dq_box.shape
    per = rows // tile
    head, node, groups = lax.axis_index("head"), lax.axis_index("node"), lax.axis_size("node")
    within, across = pairs()
    last = part == parts - 1

    place, pair = within[1], across[1]
    over_heads = Spread(
        along("head"), lambda o: pair_sum.at[o], lambda i: head_box.at[i], head_sems.at[0], head_sems.at[1]
    )
    over_pairs = Spread(
        across, lambda o: across_own.at[o], lambda i: across_box.at[i], across_sems.at[0], across_sems.at[1]
    )
    over_full = Spread(
        across, lambda _: share_low, lambda i: full.at[place, i], full_sems.at[0], full_sems.at[1]
    )
    count = across[0]

    def swap(side):
        return pltpu.make_async_remote_copy(
            src_ref=full.at[side],
            dst_ref=full.at[side],
            send_sem=pair_sems.at[0],
            recv_sem=pair_sems.at[1],
            device_id=within[2](1 - place),
        )

    def halo(own, box, side, by):
        return pltpu.make_async_remote_copy(
            src_ref=own,
            dst_ref=box,
            send_sem=halo_sems.at[0, side],
            recv_sem=halo_sems.at[1, side],
            device_id={"node": (node + by) % groups},
        )

    to_below = halo(low_own, low_box, 0, groups - 1)
    to_above = halo(high_own, high_box, 1, 1)

    def dq_copy(target, source, piece):
        at = pl.ds(pl.multiple_of(piece * tile, tile), tile)
        return pltpu.make_async_remote_copy(
            src_ref=dq_own.at[target, at],
            dst_ref=dq_box.at[source, at],
            send_sem=dq_sems.at[0, target, piece],
            recv_sem=dq_sems.at[1, source, piece],
            device_id={"head": target},
        )

    dkv_spread = Spread(
        along("head"), lambda o: dkv_own.at[o], lambda i: dkv_box.at[i], dkv_sems.at[0], dkv_sems.at[1]
    )

    @pl.when(step == 0)
    def _():
        meet(["head", "node"])
        over_heads.all("start")
        head_box[head] = pair_sum[head]

    @pl.when(step == HEAD_STEP)
    def _():
        over_heads.all("arrived")

        def add(z):
            across_own[z] = sum(head_box[h, z].astype(f32) for h in range(heads)).astype(bf16)

        each(count, add, 0)
        over_pairs.all("start")
        across_box[across[1]] = across_own[across[1]]

    @pl.when(part == 0)
    def _():
        dk[...] = jnp.zeros_like(dk)
        dv[...] = jnp.zeros_like(dv)

    grad = d_ref[...]
    wide = grad.astype(f32)
    inverse = mix_ref[:, HD : HD + 1]
    delta = jnp.sum(wide * mix_ref[:, :HD], 1, keepdims=True)
    gain = inverse * (1.0 / math.sqrt(HD))
    q_turned = q_ref[...].T
    d_turned = (wide * inverse).astype(bf16).T
    here = pl.ds(pl.multiple_of(part * tile, tile), tile)
    dq_here = jnp.where(turn == 0, 0.0, dq[here])
    for at in range(0, nodes, chunk):
        cols = slice(at, at + chunk)
        dp = contract(grad, kv_ref[0, cols, HD:], 1, 1)
        e = e_ref[:, cols]
        ds = (e.astype(f32) * ((dp - delta) * gain)).astype(bf16)
        dq_here += contract(ds, kv_ref[0, cols, :HD], 1, 0)
        dk[:, cols] += contract(q_turned, ds, 1, 0)
        dv[:, cols] += contract(d_turned, e, 1, 0)
    dq[here] = dq_here

    for which, own, copy in ((0, low_own, to_below), (1, high_own, to_above)):

        @pl.when(last & (turn == which))
        def _(own=own, copy=copy):
            own[:HD] = dk[...].astype(bf16)
            own[HD:] = dv[...].astype(bf16)
            copy.start()

    @pl.when(turn == 2)
    def _():
        target, piece = part // per, part % per
        at = pl.ds(pl.multiple_of(piece * tile, tile), tile)
        low = dq_here.astype(bf16)
        dq_own[target, at] = low

        @pl.when(target == head)
        def _():
            dq_box[head, at] = low

        @pl.when(target != head)
        def _():
            dq_copy(target, head, piece).start()

    @pl.when(last & (turn == 2))
    def _():
        to_below.wait()
        to_above.wait()
        for h in range(heads):
            cols = slice(h * rows, (h + 1) * rows)
            for half, acc in enumerate((dk, dv)):
                lines = slice(half * HD, (half + 1) * HD)
                total = acc[:, cols] + low_box[lines, cols].astype(f32) + high_box[lines, cols].astype(f32)
                dkv_own[h, lines] = total.astype(bf16)
        dkv_spread.all("start")
        dkv_box[head] = dkv_own[head]
        over_pairs.all("arrived")
        total = sum(across_box[z].astype(f32) for z in range(count))
        share_ref[...] = total
        share_low[...] = total.astype(bf16)
        over_full.all("start")
        full[place, pair] = total.astype(bf16)
        grad_q = sum(
            contract(norm_ref[h * rows : (h + 1) * rows], dq_own[h], 0, 0) for h in range(heads)
        )
        grad_kv = sum(
            contract(dkv_own[h], norm_ref[h * rows : (h + 1) * rows], 1, 0) for h in range(heads)
        )
        grad_ref[:, :HD] = grad_q
        grad_ref[:, HD:] = grad_kv.T

        def finish(off):
            other = (head + off) % heads
            for p in range(per):
                dq_copy(other, other, p).wait_recv()
                dq_copy(other, head, p).wait_send()

        each(heads, finish)
        over_full.all("arrived")
        swap(place).start()
        dkv_spread.all("arrived")
        dq_ref[...] = dq_box[...]
        dkv_ref[...] = dkv_box[...]
        swap(place).wait_send()
        swap(1 - place).wait_recv()
        for c in range(2):
            for z in range(count):
                full_ref[z, c] = full[c, z]
        for spread in (dkv_spread, over_heads, over_pairs, over_full):
            spread.all("sent")


def attend_back(query, grad, mix, e, keyval, norm_all, pair_sum, heads, tile, chunk):
    nodes, reach = e.shape
    rows, width = nodes // heads, norm_all.shape[1]
    parts = nodes // tile
    _, count, share, across = pair_sum.shape
    row = lambda width: pl.BlockSpec((tile, width), lambda j, i: (i, 0))
    pair = (heads, count, share, across)
    dma = lambda *shape: pltpu.SemaphoreType.DMA(shape)
    order = lambda j: 2 * j % 3
    return pl.pallas_call(
        functools.partial(attend_back_kernel, chunk=chunk),
        grid=(3, parts),
        in_specs=[
            row(HD),
            row(HD),
            row(2 * HD),
            pl.BlockSpec((tile, nodes), lambda j, i: (i, order(j))),
            pl.BlockSpec((1, nodes, 2 * HD), lambda j, i: (order(j), 0, 0)),
            vmem(),
            vmem(),
        ],
        out_specs=[
            whole((heads, rows, HD)),
            whole((heads, 2 * HD, rows)),
            whole((width, 3 * HD)),
            whole((share, across)),
            whole((count, 2, share, across)),
        ],
        out_shape=[
            jax.ShapeDtypeStruct((heads, rows, HD), bf16),
            jax.ShapeDtypeStruct((heads, 2 * HD, rows), bf16),
            jax.ShapeDtypeStruct((width, 3 * HD), f32),
            jax.ShapeDtypeStruct((share, across), f32),
            jax.ShapeDtypeStruct((count, 2, share, across), bf16),
        ],
        scratch_shapes=[
            pltpu.VMEM((HD, nodes), f32),
            pltpu.VMEM((HD, nodes), f32),
            pltpu.VMEM((nodes, HD), f32),
            *[pltpu.VMEM((2 * HD, nodes), bf16)] * 4,
            *[pltpu.VMEM((heads, rows, HD), bf16)] * 2,
            *[pltpu.VMEM((heads, 2 * HD, rows), bf16)] * 2,
            pltpu.VMEM(pair, bf16),
            *[pltpu.VMEM(pair[1:], bf16)] * 2,
            pltpu.VMEM((share, across), bf16),
            pltpu.VMEM((2, *pair[1:]), bf16),
            dma(2, 2),
            dma(2, heads, rows // tile),
            dma(2, heads),
            dma(2),
            dma(2, heads),
            dma(2, count),
            dma(2, count),
        ],
        compiler_params=remote(60, 5),
        name="attend_back",
    )(query, grad, mix, e, keyval, norm_all, pair_sum)


def middle_kernel(
    place_ref, scale_ref, mixed_ref, zero_ref, wa_ref, wf_ref, mod_ref, wdec_ref, stat_ref,
    node_ref, read_ref, target_ref, eps_ref,
    done_ref, dmix_ref, pair_ref, gdec_ref, gmod_ref, loss_ref,
    one_scr, two_scr, norm_scr, up_scr, act_scr, dec_box, hits, turned, total,
    d_own, d_box, dmix_own, dmix_box, grad, big, pair_box,
    dec_sems, d_sems, dmix_sems, pair_sems, out_sems,
    node_tiles, pixel_tiles,
):
    step = pl.program_id(0)
    heads, rows, _ = mixed_ref.shape
    width = zero_ref.shape[1]
    tile = rows // node_tiles
    head = lax.axis_index("head")
    within, _ = pairs()
    place = within[1]
    count, share = pair_ref.shape[1:3]
    pixel_end = node_tiles + pixel_tiles
    others = nearest_first(head, heads)

    decs = Relay(lambda slot, half: dec_box.at[slot, :, pl.ds(half * tile, tile)], dec_sems)

    d_spread = Spread(along("head"), lambda o: d_own.at[o], lambda i: d_box.at[i], d_sems.at[0], d_sems.at[1])

    def dmix_copy(other, slot, t):
        lines = pl.ds(t * tile, tile)
        return pltpu.make_async_remote_copy(
            src_ref=dmix_own.at[other, lines],
            dst_ref=dmix_box.at[slot, lines],
            send_sem=dmix_sems.at[0, other, t],
            recv_sem=dmix_sems.at[1, slot, t],
            device_id={"head": other},
        )

    def pair_copy(h, part):
        cols = (pl.ds(0, 2 * width), pl.ds(2 * width, HD))[part]
        return pltpu.make_async_remote_copy(
            src_ref=big.at[1 - place, h, :, :, cols],
            dst_ref=pair_box.at[h, :, :, cols],
            send_sem=pair_sems.at[0, part, h],
            recv_sem=pair_sems.at[1, part, h],
            device_id=within[2](1 - place),
        )

    def pack(h, cols):
        for c in range(2):
            for z in range(count):
                at = (2 * z + c) * share
                big[c, h, z, :, cols] = grad[h, at : at + share, cols].astype(bf16)

    @pl.when(step == 0)
    def _():
        meet(["head", "node"])
        turned[...] = jnp.zeros_like(turned)
        total[...] = jnp.zeros_like(total)
        loss_ref[...] = jnp.zeros_like(loss_ref)
        gdec_ref[...] = jnp.zeros_like(gdec_ref)
        gmod_ref[...] = jnp.zeros_like(gmod_ref)

    for t in range(node_tiles):

        @pl.when(step == t)
        def _(t=t, lines=slice(t * tile, (t + 1) * tile)):
            h_one = zero_ref[lines] + sum(
                contract(mixed_ref[h, lines], wa_ref[h, :, 3 * HD :], 1, 1) for h in range(heads)
            )
            one_scr[lines] = h_one
            normed, _ = standardize(h_one)
            norm_two = (normed * (1 + mod_ref[2:3]) + mod_ref[3:4]).astype(bf16)
            norm_scr[lines] = norm_two
            h_two = h_one
            for h in range(heads):
                up = contract(norm_two, wf_ref[h, :, :width], 1, 0)
                up_scr[h, lines] = up
                act = (up * jax.nn.sigmoid(up)).astype(bf16)
                act_scr[h, lines] = act
                h_two = h_two + contract(act, wf_ref[h, :, width:], 1, 1)
            two_scr[lines] = h_two
            final = standardize(h_two)[0].astype(bf16)
            high, low = halves(contract(wdec_ref[...], final, 1, 1))
            dec_box[head, :SLIM, lines] = high
            dec_box[head, SLIM:, lines] = low
            decs.start(((0, t), (1, t)))
            if t == 1:
                decs.hand_on(0)

    @pl.when((step >= node_tiles) & (step < pixel_end))
    def _():
        reads = read_ref[...] - place_ref[0]
        pixels = target_ref.shape[1]
        for h in range(heads):
            spot = lax.broadcasted_iota(jnp.int32, (rows, pixels), 0) + h * rows
            hit = sum((spot == reads[k : k + 1]).astype(f32) for k in range(3)).astype(bf16)
            hits[h * rows : (h + 1) * rows] = hit

        @pl.when(step == node_tiles)
        def _():
            decs.hand_on(1)
            for side in range(2):
                decs.arrived(side)
            decs.arrived_across()

        field = sum(contract(dec_box[h], hits[h * rows : (h + 1) * rows], 1, 0) for h in range(heads))
        field = (field[:VARS] + field[SLIM : SLIM + VARS]) / 3.0
        target = target_ref[...]
        noisy = target + scale_ref[0] * eps_ref[...]
        error = scale_ref[2] * noisy + scale_ref[3] * field - target
        valid = (node_ref[...] - place_ref[0] < place_ref[2]).astype(f32)
        valid_pixels = stat_ref[SLIM - 1 : SLIM, 0:1]
        weighted = valid * (scale_ref[4] / (stat_ref[:VARS, 0:1] / valid_pixels + norm_eps))
        loss_ref[:VARS] += fold_lanes(weighted * error * error)
        high, low = halves(scale_ref[3] * (2.0 / (valid_pixels * VARS)) / 3.0 * weighted * error)
        turned[:VARS] = high
        turned[SLOT : SLOT + VARS] = low
        total[...] += contract(hits[...], turned[...], 1, 1)

    @pl.when(step == pixel_end - 1)
    def _():
        for h in range(heads):
            lines = slice(h * rows, (h + 1) * rows)
            d_own[h] = (total[lines, :SLOT] + total[lines, SLOT:]).astype(bf16)
        for other in others:
            d_spread.copy(other, head).start()
        d_box[head] = d_own[head]

    for t in range(node_tiles):
        final_tile = t == node_tiles - 1

        @pl.when(step == pixel_end + t)
        def _(t=t, lines=slice(t * tile, (t + 1) * tile), final_tile=final_tile):
            normed_two, inv_two = standardize(two_scr[lines])
            final = normed_two.astype(bf16)
            normed_one, inv_one = standardize(one_scr[lines])
            if t == 0:
                for other in others:
                    d_spread.copy(other, other).wait_recv()
            d_dec = sum(d_box[h, lines].astype(f32) for h in range(heads)).astype(bf16)[:, :SLIM]
            gdec_ref[...] += contract(d_dec, final, 0, 0)
            d_two = norm_back(normed_two, inv_two, contract(d_dec, wdec_ref[...], 1, 0))
            d_low = d_two.astype(bf16)
            norm_two = norm_scr[lines]
            d_mid = jnp.zeros_like(d_two)

            def add(h, cols, value):
                if t == 0:
                    grad[h, :, cols] = value
                else:
                    grad[h, :, cols] += value

            for h in range(heads):
                up = up_scr[h, lines]
                d_act = contract(d_low, wf_ref[h, :, width:], 1, 0)
                gating = jax.nn.sigmoid(up)
                d_up = (d_act * gating * (1 + up * (1 - gating))).astype(bf16)
                add(h, slice(0, width), contract(norm_two, d_up, 0, 0))
                add(h, slice(width, 2 * width), contract(d_low, act_scr[h, lines], 0, 0))
                if final_tile:
                    pack(h, slice(0, 2 * width))
                    pair_copy(h, 0).start()
                d_mid += contract(d_up, wf_ref[h, :, :width], 1, 1)
            gmod_ref[0:1] += jnp.sum(d_mid * normed_one, 0, keepdims=True)
            gmod_ref[1:2] += jnp.sum(d_mid, 0, keepdims=True)
            d_one = d_two + norm_back(normed_one, inv_one, d_mid * (1 + mod_ref[2:3]))
            done_ref[lines] = d_one
            one_low = d_one.astype(bf16)
            for h in range(heads):
                dmix_own[h, lines] = contract(one_low, wa_ref[h, :, 3 * HD :], 1, 0).astype(bf16)
            for other in others:
                dmix_copy(other, head, t).start()
            dmix_box[head, lines] = dmix_own[head, lines]
            for h in range(heads):
                add(h, slice(2 * width, 2 * width + HD), contract(one_low, mixed_ref[h, lines], 0, 0))
                if final_tile:
                    pack(h, slice(2 * width, 2 * width + HD))
                    pair_copy(h, 1).start()
            if final_tile:
                for h in range(heads):
                    for part in range(2):
                        pair_copy(h, part).wait_recv()
                    for z in range(count):
                        pair_ref[h, z] = (
                            big[place, h, z].astype(f32) + pair_box[h, z].astype(f32)
                        ).astype(bf16)
                for other in others:
                    for u in range(node_tiles):
                        dmix_copy(other, other, u).wait_recv()
                dmix_ref[...] = dmix_box[...]
                for other in others:
                    d_spread.copy(other, head).wait_send()
                    for u in range(node_tiles):
                        dmix_copy(other, head, u).wait_send()
                decs.sent()
                for h in range(heads):
                    for part in range(2):
                        pair_copy(h, part).wait_send()


def middle(place, scales, mixed, h_zero, w_attn, w_ffn, modulation, w_dec, stat, node_row, read_rows, target, eps, groups):
    heads, rows, _ = mixed.shape
    width = h_zero.shape[1]
    node_tiles, pixels = 2, target.shape[1] // heads
    tile = 1536
    pixel_tiles = pixels // tile
    share, count = width // groups, groups // 2
    grads = 2 * width + HD
    pair = (heads, count, share, grads)
    low = lambda *shape: pltpu.VMEM(shape, bf16)
    full = lambda *shape: pltpu.VMEM(shape, f32)
    dma = lambda *shape: pltpu.SemaphoreType.DMA(shape)

    def at(i):
        part = jnp.clip(i - node_tiles, 0, pixel_tiles - 1)
        return 0, lax.axis_index("head") * pixel_tiles + part

    piece = lambda lines: pl.BlockSpec((lines, tile), at)
    return pl.pallas_call(
        functools.partial(middle_kernel, node_tiles=node_tiles, pixel_tiles=pixel_tiles),
        grid=(2 * node_tiles + pixel_tiles,),
        in_specs=[smem(), smem()] + [vmem()] * 7 + [piece(1), piece(3), piece(VARS), piece(VARS)],
        out_specs=[
            whole((rows, width)),
            whole((heads, rows, HD)),
            whole(pair),
            whole((SLIM, width)),
            whole((8, width)),
            whole((SLIM, 128)),
        ],
        out_shape=[
            jax.ShapeDtypeStruct((rows, width), f32),
            jax.ShapeDtypeStruct((heads, rows, HD), bf16),
            jax.ShapeDtypeStruct(pair, bf16),
            jax.ShapeDtypeStruct((SLIM, width), f32),
            jax.ShapeDtypeStruct((8, width), f32),
            jax.ShapeDtypeStruct((SLIM, 128), f32),
        ],
        scratch_shapes=[
            full(rows, width),
            full(rows, width),
            low(rows, width),
            full(heads, rows, width),
            low(heads, rows, width),
            low(heads, 2 * SLIM, rows),
            low(heads * rows, tile),
            low(2 * SLOT, tile),
            full(heads * rows, 2 * SLOT),
            low(heads, rows, SLOT),
            low(heads, rows, SLOT),
            low(heads, rows, HD),
            low(heads, rows, HD),
            full(heads, width, grads),
            low(2, *pair),
            low(*pair),
            dma(2, 3, 2),
            dma(2, heads),
            dma(2, heads, node_tiles),
            dma(2, 2, heads),
            dma(2, heads),
        ],
        compiler_params=remote(62, 7),
        name="middle",
    )(
        place, scales, mixed, h_zero, w_attn, w_ffn, modulation, w_dec, stat, node_row, read_rows, target, eps
    )


def settle_kernel(
    feat_ref, dq_ref, dkv_ref, w_ref, zero_ref, done_ref, in_ref, mod_ref, gdec_ref, gmod_ref, qkv_ref, big_ref, loss_ref,
    small_ref, share_ref, full_ref, sums_ref,
    q_low, q_pair, q_sum, q_box, q_share, q_full,
    parts, part_box, part_sum, part_own, pay, heard, tally, tallies,
    pair_sems, q_sems, f_sems, a_sems, n_sems, b_sems, t_sems, s_sems,
):
    heads, width = w_ref.shape[0], w_ref.shape[1]
    share_rows = share_ref.shape[0]
    head, node = lax.axis_index("head"), lax.axis_index("node")
    groups = heard.shape[0]
    within, across = pairs()
    place, pair, count = within[1], across[1], across[0]

    def to_other(source, target, index):
        return pltpu.make_async_remote_copy(
            src_ref=source,
            dst_ref=target,
            send_sem=pair_sems.at[0, index],
            recv_sem=pair_sems.at[1, index],
            device_id=within[2](1 - place),
        )

    for c in range(2):
        for z in range(count):
            at = (2 * z + c) * share_rows
            q_low[c, z] = qkv_ref[at : at + share_rows].astype(bf16)
    meet(["head", "node"])
    q_pairs = to_other(q_low.at[1 - place], q_pair, 0)
    q_pairs.start()

    d_norm = sum(
        contract(dq_ref[h], w_ref[h, :, :HD], 1, 1)
        + contract(dkv_ref[h], w_ref[h, :, HD : 3 * HD], 0, 1)
        for h in range(heads)
    )
    normed, inv = standardize(zero_ref[...])
    d_zero = done_ref[...] + norm_back(normed, inv, d_norm * (1 + mod_ref[0:1]))

    q_pairs.wait()
    for z in range(count):
        q_sum[z] = (q_low[place, z].astype(f32) + q_pair[z].astype(f32)).astype(bf16)
    q_over = Spread(across, lambda o: q_sum.at[o], lambda i: q_box.at[i], q_sems.at[0], q_sems.at[1])
    q_over.all("start")
    q_box[pair] = q_sum[pair]

    g_enc = contract(in_ref[...].T, d_zero, 1, 0, highest)
    parts[...] = jnp.zeros_like(parts)
    flat = parts.reshape(parts.shape[0] * parts.shape[1], width)
    flat[:VARS] = g_enc[:VARS]
    flat[VARS : 2 * VARS] = g_enc[SLOT : SLOT + VARS]
    flat[2 * VARS : 3 * VARS] = gdec_ref[:VARS]
    at = 3 * VARS
    flat[at : at + 1] = jnp.sum(d_norm * normed, 0, keepdims=True)
    flat[at + 1 : at + 2] = jnp.sum(d_norm, 0, keepdims=True)
    flat[at + 2 : at + 4] = gmod_ref[0:2]
    over_heads = Spread(
        along("head"), lambda o: parts.at[o], lambda i: part_box.at[i], a_sems.at[0], a_sems.at[1]
    )
    over_heads.all("start")
    part_box[head] = parts[head]

    q_over.all("arrived")
    share = sum(q_box[z].astype(f32) for z in range(count))
    share_ref[...] = share
    q_share[...] = share.astype(bf16)
    q_full[place, pair] = share.astype(bf16)
    f_over = Spread(
        across, lambda _: q_share, lambda i: q_full.at[place, i], f_sems.at[0], f_sems.at[1]
    )
    f_over.all("start")

    over_heads.all("arrived")
    total = sum(part_box[h] for h in range(heads))
    for t in range(groups):
        part_sum[t] = total[8 * t : 8 * t + 8]
    over_nodes = Spread(
        along("node"), lambda o: part_sum.at[o], lambda i: part_own.at[i], n_sems.at[0], n_sems.at[1]
    )
    over_nodes.all("start")
    part_own[node] = part_sum[node]

    squares = jnp.sum(share * share) + jnp.sum(big_ref[...] * big_ref[...])
    loss = jnp.sum(loss_ref[:VARS])
    over_nodes.all("arrived")
    own = sum(part_own[t] for t in range(groups))
    row = lax.broadcasted_iota(jnp.int32, own.shape, 0) + 8 * (head * groups + node)
    squares += jnp.sum(own * own * jnp.where(row >= 3 * VARS, feat_ref[0], 1.0))
    line = lax.broadcasted_iota(jnp.int32, (8, 128), 0)
    pay[:, :width] = own
    pay[:, width:] = jnp.where(line == 0, squares, jnp.where(line == 1, loss, 0.0))
    back = Spread(along("node"), lambda _: pay, lambda i: heard.at[i], b_sems.at[0], b_sems.at[1])
    back.all("start")
    heard[node] = pay[...]

    f_over.all("arrived")
    q_rest = to_other(q_full.at[place], q_full.at[place], 1)
    q_rest.start()

    back.all("arrived")
    tally[...] = sum(heard[t, :, width:] for t in range(groups))
    tell = Spread(along("head"), lambda _: tally, lambda i: tallies.at[i], t_sems.at[0], t_sems.at[1])
    tell.all("start")
    tallies[head] = tally[...]
    for t in range(groups):
        small_ref[head, 8 * t : 8 * t + 8] = heard[t, :, :width]
    smalls = Spread(
        along("head"), lambda _: small_ref.at[head], lambda i: small_ref.at[i], s_sems.at[0], s_sems.at[1]
    )
    smalls.all("start")
    tell.all("arrived")
    sums_ref[...] = sum(tallies[h] for h in range(heads))

    q_rest.wait_send()
    to_other(q_full.at[1 - place], q_full.at[1 - place], 1).wait_recv()
    for c in range(2):
        for z in range(count):
            full_ref[2 * z + c] = q_full[c, z]
    smalls.all("arrived")
    for spread in (q_over, over_heads, f_over, over_nodes, back, tell, smalls):
        spread.all("sent")


def settle(feat_sq, dq, dkv, w_attn, h_zero, d_one, node_in, modulation, grad_dec, gmod_two, grad_qkv, big_share, loss, groups):
    heads, rows, _ = dq.shape
    width = h_zero.shape[1]
    count = groups // 2
    share = (grad_qkv.shape[0] // groups, grad_qkv.shape[1])
    low = lambda *shape: pltpu.VMEM(shape, bf16)
    full = lambda *shape: pltpu.VMEM(shape, f32)
    dma = lambda *shape: pltpu.SemaphoreType.DMA(shape)
    return pl.pallas_call(
        settle_kernel,
        in_specs=[smem()] + [vmem()] * 12,
        out_specs=[vmem()] * 4,
        out_shape=[
            jax.ShapeDtypeStruct((heads, 8 * groups, width), f32),
            jax.ShapeDtypeStruct(share, f32),
            jax.ShapeDtypeStruct((groups, *share), bf16),
            jax.ShapeDtypeStruct((8, 128), f32),
        ],
        scratch_shapes=[
            low(2, count, *share),
            low(count, *share),
            low(count, *share),
            low(count, *share),
            low(*share),
            low(2, count, *share),
            full(heads, 8 * groups, width),
            full(heads, 8 * groups, width),
            full(groups, 8, width),
            full(groups, 8, width),
            full(8, width + 128),
            full(groups, 8, width + 128),
            full(8, 128),
            full(heads, 8, 128),
            dma(2, 2),
            dma(2, count),
            dma(2, count),
            dma(2, heads),
            dma(2, groups),
            dma(2, groups),
            dma(2, heads),
            dma(2, heads),
        ],
        compiler_params=remote(56, 1),
        name="settle",
    )(feat_sq, dq, dkv, w_attn, h_zero, d_one, node_in, modulation, grad_dec, gmod_two, grad_qkv, big_share, loss)


def eliminate(work, done):
    count = work.shape[0]
    lane = lax.broadcasted_iota(jnp.int32, (1, BLOCK), 1)
    sub = lax.broadcasted_iota(jnp.int32, (STRIP, BLOCK), 0)
    pivots = [jnp.ones((1, BLOCK), f32) for _ in range(count)]
    both = lambda x: jnp.concatenate([x, x], 1)
    for at in range(0, BLOCK, STRIP):
        strip = slice(at, at + STRIP)
        rows = [work[m, strip] for m in range(count)]
        columns = [
            [jnp.broadcast_to(rows[m][:, at + k : at + k + 1], (STRIP, BLOCK)) for k in range(STRIP)]
            for m in range(count)
        ]
        scale = [jnp.ones((STRIP, BLOCK), f32) for _ in range(count)]
        for r in range(STRIP):
            for m in range(count):
                column = columns[m][r]
                pivot = jnp.broadcast_to(column[r : r + 1], (STRIP, BLOCK))
                factor = jnp.where(sub > r, column * (1.0 / pivot), 0.0)
                scale[m] = jnp.where(sub == r, pivot, scale[m])
                for k in range(r + 1, STRIP):
                    columns[m][k] = columns[m][k] - factor * columns[m][k][r : r + 1]
                pivots[m] = jnp.where(lane == at + r, pivot[:1], pivots[m])
                rows[m] = rows[m] - both(factor) * rows[m][r : r + 1]
        for m in range(count):
            done[m, strip] = rows[m][:, BLOCK:]
            if at + STRIP < BLOCK:
                high, mid, low = thirds(rows[m] * both(lax.rsqrt(scale[m])))
                left = jnp.concatenate([high, high, mid, mid, high, low], 0)[:, :BLOCK]
                right = jnp.concatenate([high, mid, high, mid, low, high], 0)
                rest = slice(at + STRIP, BLOCK)
                work[m, rest] -= contract(left, right, 0, 0)[rest]
    return pivots


def finish_kernel(
    sums_ref, small_ref, qkv_share_ref, big_share_ref, qkv_ref, big_ref, stats_ref, basis_ref,
    layer_ref, first_ref, second_ref, feat_ref,
    enc_ref, enc1_ref, enc2_ref, cond_ref, cond1_ref, cond2_ref, dec_ref, dec1_ref, dec2_ref,
    out_ref, stats_out, layer_out, first_out, second_out,
    enc_out, enc1_out, enc2_out, cond_out, cond1_out, cond2_out, dec_out, dec1_out, dec2_out,
    gram, both, work, done, shares,
):
    count, size = stats_ref.shape[:2]
    k = pl.program_id(0)
    clip = clip_limit / jnp.maximum(jnp.sqrt(sums_ref[0:1, 0:1]), clip_limit)

    @pl.when(k == 0)
    def _():
        cuts = [slice(0, size), slice(size, 2 * size), slice(2 * size, 3 * size)]
        shares[0] = jnp.concatenate([qkv_share_ref[...], big_share_ref[:, cuts[2].start :]], 1)
        grads = [jnp.concatenate([qkv_ref[...], big_ref[:, cuts[2].start :]], 1)]
        for m in (1, 2):
            shares[m] = big_share_ref[:, cuts[m - 1]]
            grads.append(big_ref[:, cuts[m - 1]])
        for m in range(count):
            raw = contract(grads[m], grads[m], 0, 0)
            new = beta_stats * stats_ref[m] + (1 - beta_stats) * (clip * (clip * raw))
            stats_out[m] = new
            product = contract(new, basis_ref[m], 1, 0, highest)
            both[m] = product
            gram[m] = contract(product, product, 0, 0, highest)

    i = jnp.minimum(k, count - 1)
    rotated = contract(clip * shares[i], basis_ref[i], 1, 0, highest)
    first_new = beta_first * first_ref[i] + (1 - beta_first) * rotated
    second_new = beta_second * second_ref[i] + (1 - beta_second) * rotated * rotated
    first_out[i] = first_new
    second_out[i] = second_new
    direction = (
        first_new
        / (1 - beta_first**STEP)
        / (jnp.sqrt(second_new / (1 - beta_second**STEP)) + adam_epsilon)
    )
    layer_out[i] = layer_ref[i] - rate_layer * (
        contract(direction, basis_ref[i], 1, 1, highest) + decay_rate * layer_ref[i]
    )

    at = pl.ds(pl.multiple_of(k * BLOCK, BLOCK), BLOCK)
    unit = lax.broadcasted_iota(jnp.int32, (BLOCK, BLOCK), 0) == lax.broadcasted_iota(
        jnp.int32, (BLOCK, BLOCK), 1
    )
    for m in range(count):
        work[m, :, :BLOCK] = gram[m, at, at]
        work[m, :, BLOCK:] = unit.astype(f32)
    roots = [lax.rsqrt(p) for p in eliminate(work, done)]
    for step in range(size // BLOCK):

        @pl.when(k == step)
        def _(here=slice(step * BLOCK, (step + 1) * BLOCK), rest=(step + 1) * BLOCK):
            for m in range(count):
                factor = done[m]
                panel = contract(both[m, :, here], factor, 1, 1, highest) * roots[m]
                out_ref[m] = panel
                if rest < size:
                    left = contract(gram[m, rest:, here], factor, 1, 1, highest) * roots[m]
                    both[m, :, rest:] -= contract(panel, left, 1, 1, highest)
                    gram[m, rest:, rest:] -= contract(left, left, 1, 1, highest)

    @pl.when(k == pl.num_programs(0) - 1)
    def _():
        flat = clip * small_ref[...]

        def adam(grad, cols, refs, outs):
            for out, new in zip(outs, adam_small(refs[0][:, cols], grad, refs[1][:, cols], refs[2][:, cols])):
                out[:, cols] = new

        every = slice(None)
        adam(flat[: 2 * VARS], every, (enc_ref, enc1_ref, enc2_ref), (enc_out, enc1_out, enc2_out))
        adam(flat[2 * VARS : 3 * VARS], every, (dec_ref, dec1_ref, dec2_ref), (dec_out, dec1_out, dec2_out))
        width = flat.shape[1]
        for j in range(4):
            grad = feat_ref[:, 0:1] * flat[3 * VARS + j : 3 * VARS + j + 1]
            adam(
                grad,
                slice(j * width, (j + 1) * width),
                (cond_ref, cond1_ref, cond2_ref),
                (cond_out, cond1_out, cond2_out),
            )


def finish(sums, small, qkv_share, big_share, qkv_full, big_full, stats, basis, layers, feat, enc, cond, dec):
    count, size = stats.shape[:2]
    inputs = (sums, small, qkv_share, big_share, qkv_full, big_full, stats, basis, *layers, feat, *enc, *cond, *dec)
    like = lambda x: jax.ShapeDtypeStruct(x.shape, f32)
    outs = [stats, *layers, *enc, *cond, *dec]
    return pl.pallas_call(
        finish_kernel,
        grid=(size // BLOCK,),
        in_specs=[whole(x.shape) for x in inputs],
        out_specs=[pl.BlockSpec((count, size, BLOCK), lambda k: (0, 0, k))] + [whole(x.shape) for x in outs],
        out_shape=[like(stats)] + [like(x) for x in outs],
        scratch_shapes=[
            pltpu.VMEM((count, size, size), f32),
            pltpu.VMEM((count, size, size), f32),
            pltpu.VMEM((count, BLOCK, 2 * BLOCK), f32),
            pltpu.VMEM((count, BLOCK, BLOCK), f32),
            pltpu.VMEM(layers[0].shape, f32),
        ],
        compiler_params=params(60),
        name="finish",
    )(*inputs)


def local(
    prev_state,
    target,
    noise_eps,
    noise_level,
    valid_count,
    neighbours,
    nbr_count,
    pix_node,
    pix_read,
    w_enc,
    w_cond,
    w_dec,
    layer_w,
    soap_first,
    soap_second,
    soap_basis,
    soap_stats,
    enc_first,
    enc_second,
    cond_first,
    cond_second,
    dec_first,
    dec_second,
):
    nodes = nbr_count.shape[0]
    groups = lax.axis_size("node")
    heads = lax.axis_size("head")
    rows = nodes // heads
    block_start = lax.axis_index("node") * nodes
    quarter = lax.axis_index("head")
    width = w_enc.shape[1]
    both = ("head", "node")

    low_w = layer_w.astype(bf16)
    ffn_share = jnp.concatenate([low_w[1], low_w[2]], 1)
    noise_sigma, noise_feat = noise_terms(noise_level)
    sig_sq = noise_sigma * noise_sigma
    input_scale = lax.rsqrt(sig_sq + 1.0)
    skip_scale = 1.0 / (sig_sq + 1.0)
    output_scale = noise_sigma * lax.rsqrt(sig_sq + 1.0)
    loss_scale = (sig_sq + 1.0) / sig_sq
    modulation = jnp.dot(noise_feat[None, :], w_cond, precision=highest).reshape(4, width)

    prev_t, target_t, eps_t = prev_state.T, target.T, noise_eps.T
    node_row = pix_node.reshape(1, -1)
    read_rows = pix_read.T
    place = jnp.stack([block_start, quarter * rows, valid_count[0], quarter]).astype(jnp.int32)
    pad_enc = jnp.zeros((2, SLOT, width), bf16)
    pad_enc = pad_enc.at[:, :VARS].set(w_enc.astype(bf16).reshape(2, VARS, width))
    node_in, column, h_zero, stat, norm_all, query, keyval, counts = enter(
        place, jnp.stack([noise_sigma, input_scale]), node_row, prev_t, target_t, eps_t, low_w[0],
        pad_enc.reshape(2 * SLOT, width), modulation, neighbours.T, nbr_count.reshape(1, -1), rows, 2048, heads, groups,
    )
    norm_all, query = norm_all.reshape(nodes, -1), query.reshape(nodes, -1)
    keyval = keyval.reshape(3, nodes, -1)
    loss_count = stat[SLIM - 1, 0] * VARS
    e, mix, mixed, attn_all, ffn_all = attend(query, keyval, counts, column, ffn_share, heads, 128, 512)
    attn_all = attn_all.reshape(heads, width, -1)
    ffn_all = ffn_all.reshape(heads, width, -1)

    w_dec_t = jnp.zeros((SLIM, width), bf16).at[:VARS].set(w_dec.T.astype(bf16))
    scales = jnp.stack([noise_sigma, input_scale, skip_scale, output_scale, loss_scale])
    d_one, d_mixed, pair_sum, grad_dec, gmod_two, loss_part = middle(
        place, scales, mixed, h_zero, attn_all, ffn_all, modulation, w_dec_t, stat, node_row, read_rows,
        target_t, eps_t, groups,
    )
    d_mixed = d_mixed.reshape(nodes, HD)
    dq, dkv, grad_qkv, big_share, big_full = attend_back(
        query, d_mixed, mix, e, keyval, norm_all, pair_sum, heads, 512, 1024
    )
    feat_sq = jnp.sum(noise_feat * noise_feat).reshape(1)
    small, qkv_share, qkv_full, sums = settle(
        feat_sq, dq, dkv, attn_all, h_zero, d_one, node_in, modulation, grad_dec, gmod_two, grad_qkv, big_share,
        loss_part, groups,
    )
    basis_new, stats_new, layer_new, first_new, second_new, *small_new = finish(
        sums,
        small.reshape(-1, width),
        qkv_share,
        big_share,
        qkv_full.reshape(width, -1),
        big_full.reshape(width, -1),
        soap_stats[:, 0],
        soap_basis[:, 0],
        (layer_w, soap_first, soap_second),
        jnp.broadcast_to(noise_feat[:, None], (NF, 128)),
        (w_enc, enc_first, enc_second),
        (w_cond, cond_first, cond_second),
        (w_dec.T, dec_first.T, dec_second.T),
    )
    return (
        jnp.reshape(sums[1, 0], (1,)),
        jnp.reshape(loss_count, (1,)),
        jnp.reshape(jnp.sqrt(sums[0, 0]), (1,)),
        layer_new,
        first_new,
        second_new,
        basis_new[:, None],
        stats_new[:, None],
        *small_new[:6],
        *(x.T for x in small_new[6:]),
    )


def solution(mesh):
    pixel = P("node", None)
    layer = P(None, "node", "head")
    basis = P(None, "head", None, None)
    placed = (
        *(pixel,) * 3,
        P(),
        P("node"),
        P("node", None),
        P("node"),
        P("node"),
        P("node", None),
        *(P(),) * 3,
        *(layer,) * 3,
        *(basis,) * 2,
        *(P(),) * 6,
    )
    return jax.shard_map(
        local,
        mesh=mesh,
        in_specs=placed,
        out_specs=(*(P(),) * 3, *(layer,) * 3, *(basis,) * 2, *(P(),) * 9),
        check_vma=False,
    )
```

```python
import functools
import math

import jax
import jax.numpy as jnp
from jax import lax
from jax.experimental import pallas as pl
from jax.experimental.pallas import tpu as pltpu
from jax.sharding import PartitionSpec as P

HD = 128
VARS = 84
NF = 32
NBR = 16
LEVELS = 1000
STEP = 10

SLOT = 128
SLIM = 96
GROUP = 256 // NBR
BLOCK = 128
STRIP = 16
HEAD_STEP = 8

highest = lax.Precision.HIGHEST
clip_limit = 0.01
beta_first = 0.9
beta_second = 0.95
beta_stats = 0.95
adam_epsilon = 1e-08
rate_layer = 0.02
rate_small = 0.05
decay_rate = 0.1
norm_eps = 1e-05

f32 = jnp.float32
bf16 = jnp.bfloat16
MIB = 2**20


def passed_along(x, axis, by):
    length = lax.axis_size(axis)
    return lax.ppermute(x, axis, [(i, (i + by) % length) for i in range(length)])


def noise_terms(noise_level):
    level_frac = noise_level[0].astype(f32) / (LEVELS - 1)
    noise_sigma = 0.05 * jnp.exp(level_frac * math.log(40.0))
    frequency = 1.0 + jnp.arange(NF // 2).astype(f32)
    phase_angle = jnp.log(noise_sigma) * frequency
    return (noise_sigma, jnp.concatenate([jnp.sin(phase_angle), jnp.cos(phase_angle)]))


def standardize(values_in):
    row_mean = jnp.mean(values_in, -1, keepdims=True)
    centered = values_in - row_mean
    inv_std = lax.rsqrt(jnp.mean(centered * centered, -1, keepdims=True) + norm_eps)
    return (centered * inv_std, inv_std)


def norm_back(normed, inv_std, grad_in):
    return inv_std * (
        grad_in
        - jnp.mean(grad_in, -1, keepdims=True)
        - normed * jnp.mean(grad_in * normed, -1, keepdims=True)
    )


def contract(left, right, left_dim, right_dim, precision=None):
    return lax.dot_general(
        left,
        right,
        (((left_dim,), (right_dim,)), ((), ())),
        preferred_element_type=f32,
        precision=precision,
    )


def halves(x):
    high = x.astype(bf16)
    return high, (x - high.astype(f32)).astype(bf16)


def thirds(x):
    high = x.astype(bf16)
    rest = x - high.astype(f32)
    return (high, *halves(rest))


def fold_lanes(x, op=jnp.add):
    parts = [x[:, i : i + 128] for i in range(0, x.shape[1], 128)]
    while len(parts) > 1:
        parts = [op(*parts[i : i + 2]) if i + 1 < len(parts) else parts[i] for i in range(0, len(parts), 2)]
    return parts[0]


def adam_small(weight, grad_item, first, second):
    first_new = beta_first * first + (1 - beta_first) * grad_item
    second_new = beta_second * second + (1 - beta_second) * grad_item * grad_item
    ratio = (
        first_new
        / (1 - beta_first**STEP)
        / (jnp.sqrt(second_new / (1 - beta_second**STEP)) + adam_epsilon)
    )
    return (weight - rate_small * (ratio + decay_rate * weight), first_new, second_new)


def smem():
    return pl.BlockSpec(memory_space=pltpu.SMEM)


def whole(shape):
    zeros = (0,) * len(shape)
    return pl.BlockSpec(tuple(shape), lambda *_: zeros)


def params(mib=48):
    return pltpu.CompilerParams(vmem_limit_bytes=mib * MIB)


def remote(mib, identity):
    return pltpu.CompilerParams(
        vmem_limit_bytes=mib * MIB, collective_id=identity, has_side_effects=True
    )


def vmem():
    return pl.BlockSpec(memory_space=pltpu.VMEM)


def hbm():
    return pl.BlockSpec(memory_space=pl.ANY)


def each(count, act, start=1):
    def body(off, carry):
        act(off)
        return carry

    lax.fori_loop(start, count, body, 0)


def meet(axes):
    barrier = pltpu.get_barrier_semaphore()
    total = 0
    for axis in axes:
        count, me = lax.axis_size(axis), lax.axis_index(axis)
        total += count - 1
        each(
            count,
            lambda off: pl.semaphore_signal(barrier, inc=1, device_id={axis: (me + off) % count}),
        )
    pl.semaphore_wait(barrier, total)


class Spread:
    def __init__(self, group, source, target, sends, receives):
        self.count, self.me, self.where = group
        self.source, self.target = source, target
        self.sends, self.receives = sends, receives

    def copy(self, other, slot):
        return pltpu.make_async_remote_copy(
            src_ref=self.source(other),
            dst_ref=self.target(slot),
            send_sem=self.sends.at[other],
            recv_sem=self.receives.at[slot],
            device_id=self.where(other),
        )

    def other(self, off):
        return (self.me + off) % self.count

    def start(self, off):
        self.copy(self.other(off), self.me).start()

    def arrived(self, off):
        self.copy(self.other(off), self.other(off)).wait_recv()

    def sent(self, off):
        self.copy(self.other(off), self.me).wait_send()

    def all(self, act):
        each(self.count, getattr(self, act))


def along(axis):
    return lax.axis_size(axis), lax.axis_index(axis), lambda other: {axis: other}


def pairs():
    node = lax.axis_index("node")
    place, pair = node % 2, node // 2
    within = (2, place, lambda other: {"node": 2 * pair + other})
    across = (lax.axis_size("node") // 2, pair, lambda other: {"node": 2 * other + place})
    return within, across


class Relay:
    def __init__(self, part, sems):
        me = lax.axis_index("head")
        self.me, self.near, self.across = me, (me + 1 - 2 * (me % 2), (me + 2) % 4), 3 - me
        self.part, self.sems = part, sems

    def copy(self, kind, target, slot, half):
        return pltpu.make_async_remote_copy(
            src_ref=self.part(slot, half),
            dst_ref=self.part(slot, half),
            send_sem=self.sems.at[0, kind, half],
            recv_sem=self.sems.at[1, kind, half],
            device_id={"head": target},
        )

    def start(self, halves=((0, 0), (1, 1), (0, 1), (1, 0))):
        for side, half in halves:
            self.copy(side, self.near[side], self.me, half).start()

    def hand_on(self, side):
        self.copy(side, self.near[side], self.near[side], side).wait_recv()
        self.copy(2, self.near[1 - side], self.near[side], side).start()

    def arrived(self, side):
        self.copy(side, self.near[side], self.near[side], 1 - side).wait_recv()

    def arrived_across(self):
        for half in range(2):
            self.copy(2, self.near[half], self.across, half).wait_recv()

    def sent(self):
        for half in range(2):
            for side in range(2):
                self.copy(side, self.near[side], self.me, half).wait_send()
            self.copy(2, self.near[1 - half], self.near[half], half).wait_send()


def count_tile(band_rows, spot_rows, put, bands):
    lane = lax.broadcasted_iota(jnp.int32, (GROUP, 256), 1)
    sub = lax.broadcasted_iota(jnp.int32, (GROUP, 256), 0)
    own = lane % GROUP == sub
    widen = (lane // GROUP == sub).astype(f32).astype(bf16)
    all_bands = contract(band_rows, widen, 0, 0)
    all_spots = contract(spot_rows, widen, 0, 0)
    spot = lax.broadcasted_iota(jnp.int32, (256, 256), 0).astype(f32)
    for g in range(band_rows.shape[1] // GROUP):
        nodes = slice(g * GROUP, (g + 1) * GROUP)
        band = jnp.where(own, all_bands[nodes], -1.0)
        left = jnp.concatenate([(band == t).astype(f32).astype(bf16) for t in range(bands)], 0)
        row = jnp.sum(jnp.where(own, all_spots[nodes], 0.0), 0, keepdims=True)
        right = (spot == row).astype(f32).astype(bf16)
        found = contract(left, right, 1, 1).astype(bf16)
        for t in range(bands):
            put(g, t, found[t * GROUP : (t + 1) * GROUP])


def nearest_first(me, count):
    if count == 4:
        return [me + 1 - 2 * (me % 2), (me + 2) % 4, 3 - me]
    return [(me + k) % count for k in range(1, count)]


def enter_kernel(
    place_ref, scale_ref, node_ref, prev_ref, target_ref, eps_ref, share_ref, wenc_ref, mod_ref, nbr_ref, live_ref,
    in_ref, own_ref, zero_ref, sum_ref, norm_out, q_out, kv_out, count_ref,
    pix, box, pair_box, gathered, w_flat, wenc_low, stat_ref, stat_own, stat_box, norm_ref, q_ref, kv_ref, bands, spots, tiles,
    weight_sems, swap_sems, head_sems, stat_sems, halo_sems, out_sems, put_sems,
):
    step = pl.program_id(0)
    last = pl.num_programs(0) - 1
    within, across = pairs()
    place = within[1]
    weights = Spread(across, lambda _: share_ref, lambda i: box.at[i], weight_sems.at[0], weight_sems.at[1])
    swap = pltpu.make_async_remote_copy(
        src_ref=box,
        dst_ref=pair_box,
        send_sem=swap_sems.at[0],
        recv_sem=swap_sems.at[1],
        device_id=within[2](1 - place),
    )

    @pl.when(step == 0)
    def _():
        meet(["head", "node"])
        weights.all("start")
        box[weights.me] = share_ref[...]
        pix[...] = jnp.zeros_like(pix)
        in_ref[...] = jnp.zeros_like(in_ref)
        stat_ref[...] = jnp.zeros_like(stat_ref)

    @pl.when(step == last - 1)
    def _():
        weights.all("arrived")
        swap.start()

    @pl.when(step < last)
    def _():
        rows, tile = in_ref.shape[0], node_ref.shape[1]
        prev = prev_ref[...]
        target = target_ref[...]
        noisy = target + scale_ref[0] * eps_ref[...]
        pix[:VARS] = prev.astype(bf16)
        pix[SLOT : SLOT + VARS] = (scale_ref[1] * noisy).astype(bf16)
        node = node_ref[...] - place_ref[0]
        mine = node - place_ref[1]
        spot = lax.broadcasted_iota(jnp.int32, (rows, tile), 0)
        onehot = (spot == mine).astype(f32).astype(bf16)
        in_ref[...] += contract(onehot, pix[...], 1, 1)
        valid = (node < place_ref[2]).astype(f32)
        residual = target - prev
        stat_ref[:VARS] += fold_lanes(valid * residual * residual)
        stat_ref[SLIM - 1 : SLIM] += fold_lanes(valid)

    @pl.when(step == last)
    def _():
        heads, rows, _ = norm_ref.shape
        head, node = lax.axis_index("head"), lax.axis_index("node")
        groups = lax.axis_size("node")
        depth = tiles.shape[1]
        nodes = count_ref.shape[0]
        steps = nodes // depth
        stat_own[...] = jnp.broadcast_to(jnp.sum(stat_ref[...], 1, keepdims=True), stat_own.shape)
        stats = Spread(along("node"), lambda _: stat_own, lambda i: stat_box.at[i], stat_sems.at[0], stat_sems.at[1])
        stats.all("start")
        wenc_low[...] = jnp.zeros_like(wenc_low)
        wenc_low[:VARS] = wenc_ref[:VARS].astype(bf16)
        wenc_low[SLOT : SLOT + VARS] = wenc_ref[VARS : 2 * VARS].astype(bf16)
        w_enc = wenc_low[...]
        h_zero = sum(contract(part, w_enc, 1, 0) for part in thirds(in_ref[...]))
        zero_ref[...] = h_zero
        normed, _ = standardize(h_zero)
        norm_ref[head] = (normed * (1 + mod_ref[0:1]) + mod_ref[1:2]).astype(bf16)
        half_rows = rows // 2
        norms = Relay(lambda slot, half: norm_ref.at[slot, pl.ds(half * half_rows, half_rows)], head_sems)
        norms.start()

        def halo(block):
            return [
                pltpu.make_async_remote_copy(
                    src_ref=kv_ref.at[1, block],
                    dst_ref=kv_ref.at[2 * side, block],
                    send_sem=halo_sems.at[2 * side, block],
                    recv_sem=halo_sems.at[2 * side + 1, block],
                    device_id={"node": (node + by) % groups},
                )
                for side, by in enumerate((1, groups - 1))
            ]

        def project(block):
            out = contract(norm_ref[block], w_flat[...], 1, 0).astype(bf16)
            q_ref[block] = out[:, :HD]
            kv_ref[1, block] = out[:, HD:]
            for copy in halo(block):
                copy.start()

        def count(step):
            slot = step % 2

            @pl.when(step >= 2)
            def _():
                count_out(step - 2).wait()

            here = pl.ds(pl.multiple_of(step * depth, depth), depth)

            def put(g, t, found):
                tiles[slot, g * GROUP : (g + 1) * GROUP, t * 256 : (t + 1) * 256] = found

            count_tile(bands[:, here], spots[:, here], put, tiles.shape[2] // 256)
            count_out(step).start()

        def count_out(step):
            return pltpu.make_async_copy(
                tiles.at[step % 2],
                count_ref.at[pl.ds(pl.multiple_of(step * depth, depth), depth)],
                out_sems.at[step % 2],
            )

        swap.wait()
        gathered[:, place] = box[...]
        gathered[:, 1 - place] = pair_box[...]
        flat = gathered[...].astype(f32).reshape(w_flat.shape[0], -1)
        w_flat[...] = flat[:, : 3 * HD].astype(bf16)
        own_ref[...] = box[...]
        project(head)
        total = nodes * groups
        relative = nbr_ref[...] - node * nodes + nodes
        relative = jnp.where(relative >= total, relative - total, relative)
        relative = jnp.where(relative < 0, relative + total, relative)
        live = lax.broadcasted_iota(jnp.int32, relative.shape, 0) < live_ref[...]
        bands[...] = jnp.where(live, relative >> 8, -1).astype(f32).astype(bf16)
        spots[...] = (relative & 255).astype(f32).astype(bf16)
        each(steps // 4, count, 0)
        norms.hand_on(0)
        norms.hand_on(1)
        each(steps * 3 // 8, count, steps // 4)
        for side in range(2):
            norms.arrived(side)
            project(norms.near[side])
        each(steps * 5 // 8, count, steps * 3 // 8)
        norms.arrived_across()
        project(norms.across)
        each(steps, count, steps * 5 // 8)
        each(steps, lambda step: count_out(step).wait(), steps - 2)
        stats.all("arrived")
        sum_ref[...] = sum(jnp.where(t == node, stat_own[...], stat_box[t]) for t in range(groups))

        def finish(block):
            for copy in halo(block):
                copy.wait()

        each(heads, finish, 0)
        norms.sent()
        stats.all("sent")
        outs = [
            pltpu.make_async_copy(source, target, put_sems.at[i])
            for i, (source, target) in enumerate(((norm_ref, norm_out), (q_ref, q_out), (kv_ref, kv_out)))
        ]
        for put in outs:
            put.start()
        for put in outs:
            put.wait()
        weights.all("sent")


def enter(
    place, scales, node_row, prev, target, eps, w_share, w_enc, modulation, neighbours, live, rows, tile, heads, groups
):
    steps = prev.shape[1] // tile
    width = w_enc.shape[1]
    depth = 8 * GROUP
    nodes = heads * rows
    reach = 3 * nodes
    column = (groups // 2, *w_share.shape)
    gathered = (groups // 2, 2, *w_share.shape)
    at = lambda i: (0, jnp.minimum(i, steps - 1))
    pixel_block = pl.BlockSpec((VARS, tile), at)
    full = lambda *shape: (shape, f32)
    low = lambda *shape: (shape, bf16)
    kept = [low(heads, rows, width), low(heads, rows, HD), low(3, heads, rows, 2 * HD)]
    blocks = [full(rows, 2 * SLOT), low(*column), full(rows, width), full(SLIM, 128)]
    dma = lambda *shape: pltpu.SemaphoreType.DMA(shape)
    return pl.pallas_call(
        enter_kernel,
        grid=(steps + 1,),
        in_specs=[smem(), smem(), pl.BlockSpec((1, tile), at)] + [pixel_block] * 3 + [vmem()] * 5,
        out_specs=[whole(shape) for shape, _ in blocks] + [hbm()] * 4,
        out_shape=[jax.ShapeDtypeStruct(*x) for x in blocks + kept + [low(nodes, reach)]],
        scratch_shapes=[
            pltpu.VMEM((2 * SLOT, tile), bf16),
            pltpu.VMEM(column, bf16),
            pltpu.VMEM(column, bf16),
            pltpu.VMEM(gathered, bf16),
            pltpu.VMEM((width, 3 * HD), bf16),
            pltpu.VMEM((2 * SLOT, width), bf16),
            pltpu.VMEM((SLIM, 128), f32),
            pltpu.VMEM((SLIM, 128), f32),
            pltpu.VMEM((groups, SLIM, 128), f32),
            *[pltpu.VMEM(*x) for x in kept],
            pltpu.VMEM((NBR, nodes), bf16),
            pltpu.VMEM((NBR, nodes), bf16),
            pltpu.VMEM((2, depth, reach), bf16),
            dma(2, groups // 2),
            dma(2),
            dma(2, 3, 2),
            dma(2, groups),
            dma(4, heads),
            dma(2),
            dma(3),
        ],
        compiler_params=remote(56, 3),
        name="enter",
    )(place, scales, node_row, prev, target, eps, w_share, w_enc, modulation, neighbours, live)


def attend_kernel(
    q_ref, kv_ref, count_ref, column_ref, ffn_ref, e_ref, mix_ref, out_ref, attn_out, ffn_out, s_scr, own, box, attn_all, ffn_all, sems,
    attn_sems, column_sems, ffn_sems, pair_sems, local_sems, put_sems, chunk
):
    step = pl.program_id(0)
    steps = pl.num_programs(0)
    head = lax.axis_index("head")
    tile = q_ref.shape[0]
    per = box.shape[1] // tile

    def copy(target, source, part):
        at = pl.ds(pl.multiple_of(part * tile, tile), tile)
        return pltpu.make_async_remote_copy(
            src_ref=own.at[target, at],
            dst_ref=box.at[source, at],
            send_sem=sems.at[0, target, part],
            recv_sem=sems.at[1, source, part],
            device_id={"head": target},
        )

    within, across = pairs()
    place, pair = within[1], across[1]
    ffn_pairs = Spread(
        across, lambda _: ffn_ref, lambda i: ffn_all.at[head, i, place], column_sems.at[0], column_sems.at[1]
    )
    count = across[0]

    def half_of(array):
        return lambda slot, half: array.at[slot, pl.ds(half * (count // 2), count // 2), place]

    attn_heads = Relay(half_of(attn_all), attn_sems)
    ffn_heads = Relay(half_of(ffn_all), ffn_sems)
    stay = [
        pltpu.make_async_copy(column_ref, attn_all.at[head, :, place], local_sems.at[0]),
        pltpu.make_async_copy(ffn_ref, ffn_all.at[head, pair, place], local_sems.at[1]),
    ]

    def swap(h, which, side):
        array = (attn_all, ffn_all)[which]
        return pltpu.make_async_remote_copy(
            src_ref=array.at[h, :, side],
            dst_ref=array.at[h, :, side],
            send_sem=pair_sems.at[0, which, h],
            recv_sem=pair_sems.at[1, which, h],
            device_id=within[2](1 - place),
        )

    @pl.when(step == 0)
    def _():
        for copy in stay:
            copy.start()
        meet(["head", "node"])
        ffn_pairs.all("start")
        for copy in stay:
            copy.wait()
        attn_heads.start()

    def exchange(which, blocks):
        for h in blocks:
            swap(h, which, place).start()

    def put(which, h):
        array, out = ((attn_all, attn_out), (ffn_all, ffn_out))[which]
        return pltpu.make_async_copy(array.at[h], out.at[h], put_sems.at[which, h])

    def put_all(which, blocks):
        for h in blocks:
            swap(h, which, 1 - place).wait_recv()
            put(which, h).start()

    near, beyond = list(attn_heads.near), attn_heads.across

    @pl.when(step == 6)
    def _():
        ffn_pairs.all("arrived")
        ffn_heads.start()
        exchange(0, [head])
        exchange(1, [head])

    @pl.when(step == 4)
    def _():
        attn_heads.hand_on(0)
        attn_heads.hand_on(1)

    @pl.when(step == 8)
    def _():
        for side in range(2):
            attn_heads.arrived(side)
        attn_heads.arrived_across()
        exchange(0, near + [beyond])

    @pl.when(step == 12)
    def _():
        for side in range(2):
            ffn_heads.hand_on(side)
        for side in range(2):
            ffn_heads.arrived(side)
        exchange(1, near)
        put_all(0, [head, *near, beyond])
        put_all(1, [head])

    @pl.when(step == 14)
    def _():
        ffn_heads.arrived_across()
        exchange(1, [beyond])
        put_all(1, near)

    @pl.when(step == 15)
    def _():
        put_all(1, [beyond])

    nodes = kv_ref.shape[1]
    q = q_ref[...]
    top = jnp.full((tile, 128), -1e30, f32)
    for b in range(3):
        for at in range(0, nodes, chunk):
            cols = slice(b * nodes + at, b * nodes + at + chunk)
            s = contract(q, kv_ref[b, at : at + chunk, :HD], 1, 1)
            s = jnp.where(count_ref[:, cols].astype(f32) > 0, s, -1e30)
            s_scr[:, cols] = s
            top = jnp.maximum(top, fold_lanes(s, jnp.maximum))
    top = jnp.max(top, 1, keepdims=True)
    factor = math.log2(math.e) / math.sqrt(HD)
    total = jnp.zeros((tile, 128), f32)
    mixed = jnp.zeros((tile, HD), f32)
    for b in range(3):
        for at in range(0, nodes, chunk):
            cols = slice(b * nodes + at, b * nodes + at + chunk)
            e = count_ref[:, cols].astype(f32) * jnp.exp2((s_scr[:, cols] - top) * factor)
            total += fold_lanes(e)
            e = e.astype(bf16)
            e_ref[:, cols] = e
            mixed += contract(e, kv_ref[b, at : at + chunk, HD:], 1, 0)
    inverse = 1.0 / jnp.sum(total, 1, keepdims=True)
    mixed = mixed * inverse
    mix_ref[:, :HD] = mixed
    mix_ref[:, HD:] = jnp.broadcast_to(inverse, (tile, HD))
    target, part = step // per, step % per
    at = pl.ds(pl.multiple_of(part * tile, tile), tile)
    low = mixed.astype(bf16)
    own[target, at] = low

    @pl.when(target == head)
    def _():
        box[head, at] = low

    @pl.when(target != head)
    def _():
        copy(target, head, part).start()

    @pl.when(step == steps - 1)
    def _():
        heads = box.shape[0]

        def finish(off):
            other = (head + off) % heads
            for p in range(per):
                copy(other, other, p).wait_recv()
                copy(other, head, p).wait_send()

        each(heads, finish)
        out_ref[...] = box[...]

        def end(h):
            for which in range(2):
                put(which, h).wait()
                swap(h, which, place).wait_send()

        each(heads, end, 0)
        ffn_pairs.all("sent")
        attn_heads.sent()
        ffn_heads.sent()


def attend(query, keyval, counts, column, ffn_share, heads, tile, chunk):
    nodes, reach = counts.shape
    rows = nodes // heads
    count = column.shape[0]
    dma = lambda *shape: pltpu.SemaphoreType.DMA(shape)
    row = lambda width: pl.BlockSpec((tile, width), lambda i: (i, 0))
    return pl.pallas_call(
        functools.partial(attend_kernel, chunk=chunk),
        grid=(nodes // tile,),
        in_specs=[row(HD), whole(keyval.shape), row(reach), hbm(), hbm()],
        out_specs=[row(reach), row(2 * HD), whole((heads, rows, HD)), hbm(), hbm()],
        out_shape=[
            jax.ShapeDtypeStruct((nodes, reach), bf16),
            jax.ShapeDtypeStruct((nodes, 2 * HD), f32),
            jax.ShapeDtypeStruct((heads, rows, HD), bf16),
            jax.ShapeDtypeStruct((heads, count, 2, *column.shape[1:]), bf16),
            jax.ShapeDtypeStruct((heads, count, 2, *ffn_share.shape), bf16),
        ],
        scratch_shapes=[
            pltpu.VMEM((tile, reach), f32),
            pltpu.VMEM((heads, rows, HD), bf16),
            pltpu.VMEM((heads, rows, HD), bf16),
            pltpu.VMEM((heads, count, 2, *column.shape[1:]), bf16),
            pltpu.VMEM((heads, count, 2, *ffn_share.shape), bf16),
            dma(2, heads, rows // tile),
            dma(2, 3, 2),
            dma(2, count),
            dma(2, 3, 2),
            dma(2, 2, heads),
            dma(2),
            dma(2, heads),
        ],
        compiler_params=remote(60, 4),
        name="attend",
    )(query, keyval, counts, column, ffn_share)


def attend_back_kernel(
    q_ref, d_ref, mix_ref, e_ref, kv_ref, norm_ref, pair_sum,
    dq_ref, dkv_ref, grad_ref, share_ref, full_ref,
    dk, dv, dq, low_own, high_own, low_box, high_box, dq_own, dq_box, dkv_own, dkv_box,
    head_box, across_own, across_box, share_low, full,
    halo_sems, dq_sems, dkv_sems, pair_sems, head_sems, across_sems, full_sems,
    chunk,
):
    turn, part = pl.program_id(0), pl.program_id(1)
    parts = pl.num_programs(1)
    step = turn * parts + part
    tile = q_ref.shape[0]
    nodes = kv_ref.shape[1]
    heads, rows, _ = dq_box.shape
    per = rows // tile
    head, node, groups = lax.axis_index("head"), lax.axis_index("node"), lax.axis_size("node")
    within, across = pairs()
    last = part == parts - 1

    place, pair = within[1], across[1]
    over_heads = Spread(
        along("head"), lambda o: pair_sum.at[o], lambda i: head_box.at[i], head_sems.at[0], head_sems.at[1]
    )
    over_pairs = Spread(
        across, lambda o: across_own.at[o], lambda i: across_box.at[i], across_sems.at[0], across_sems.at[1]
    )
    over_full = Spread(
        across, lambda _: share_low, lambda i: full.at[place, i], full_sems.at[0], full_sems.at[1]
    )
    count = across[0]

    def swap(side):
        return pltpu.make_async_remote_copy(
            src_ref=full.at[side],
            dst_ref=full.at[side],
            send_sem=pair_sems.at[0],
            recv_sem=pair_sems.at[1],
            device_id=within[2](1 - place),
        )

    def halo(own, box, side, by):
        return pltpu.make_async_remote_copy(
            src_ref=own,
            dst_ref=box,
            send_sem=halo_sems.at[0, side],
            recv_sem=halo_sems.at[1, side],
            device_id={"node": (node + by) % groups},
        )

    to_below = halo(low_own, low_box, 0, groups - 1)
    to_above = halo(high_own, high_box, 1, 1)

    def dq_copy(target, source, piece):
        at = pl.ds(pl.multiple_of(piece * tile, tile), tile)
        return pltpu.make_async_remote_copy(
            src_ref=dq_own.at[target, at],
            dst_ref=dq_box.at[source, at],
            send_sem=dq_sems.at[0, target, piece],
            recv_sem=dq_sems.at[1, source, piece],
            device_id={"head": target},
        )

    dkv_spread = Spread(
        along("head"), lambda o: dkv_own.at[o], lambda i: dkv_box.at[i], dkv_sems.at[0], dkv_sems.at[1]
    )

    @pl.when(step == 0)
    def _():
        meet(["head", "node"])
        over_heads.all("start")
        head_box[head] = pair_sum[head]

    @pl.when(step == HEAD_STEP)
    def _():
        over_heads.all("arrived")

        def add(z):
            across_own[z] = sum(head_box[h, z].astype(f32) for h in range(heads)).astype(bf16)

        each(count, add, 0)
        over_pairs.all("start")
        across_box[across[1]] = across_own[across[1]]

    @pl.when(part == 0)
    def _():
        dk[...] = jnp.zeros_like(dk)
        dv[...] = jnp.zeros_like(dv)

    grad = d_ref[...]
    wide = grad.astype(f32)
    inverse = mix_ref[:, HD : HD + 1]
    delta = jnp.sum(wide * mix_ref[:, :HD], 1, keepdims=True)
    gain = inverse * (1.0 / math.sqrt(HD))
    q_turned = q_ref[...].T
    d_turned = (wide * inverse).astype(bf16).T
    here = pl.ds(pl.multiple_of(part * tile, tile), tile)
    dq_here = jnp.where(turn == 0, 0.0, dq[here])
    for at in range(0, nodes, chunk):
        cols = slice(at, at + chunk)
        dp = contract(grad, kv_ref[0, cols, HD:], 1, 1)
        e = e_ref[:, cols]
        ds = (e.astype(f32) * ((dp - delta) * gain)).astype(bf16)
        dq_here += contract(ds, kv_ref[0, cols, :HD], 1, 0)
        dk[:, cols] += contract(q_turned, ds, 1, 0)
        dv[:, cols] += contract(d_turned, e, 1, 0)
    dq[here] = dq_here

    for which, own, copy in ((0, low_own, to_below), (1, high_own, to_above)):

        @pl.when(last & (turn == which))
        def _(own=own, copy=copy):
            own[:HD] = dk[...].astype(bf16)
            own[HD:] = dv[...].astype(bf16)
            copy.start()

    @pl.when(turn == 2)
    def _():
        target, piece = part // per, part % per
        at = pl.ds(pl.multiple_of(piece * tile, tile), tile)
        low = dq_here.astype(bf16)
        dq_own[target, at] = low

        @pl.when(target == head)
        def _():
            dq_box[head, at] = low

        @pl.when(target != head)
        def _():
            dq_copy(target, head, piece).start()

    @pl.when(last & (turn == 2))
    def _():
        to_below.wait()
        to_above.wait()
        for h in range(heads):
            cols = slice(h * rows, (h + 1) * rows)
            for half, acc in enumerate((dk, dv)):
                lines = slice(half * HD, (half + 1) * HD)
                total = acc[:, cols] + low_box[lines, cols].astype(f32) + high_box[lines, cols].astype(f32)
                dkv_own[h, lines] = total.astype(bf16)
        dkv_spread.all("start")
        dkv_box[head] = dkv_own[head]
        over_pairs.all("arrived")
        total = sum(across_box[z].astype(f32) for z in range(count))
        share_ref[...] = total
        share_low[...] = total.astype(bf16)
        over_full.all("start")
        full[place, pair] = total.astype(bf16)
        grad_q = sum(
            contract(norm_ref[h * rows : (h + 1) * rows], dq_own[h], 0, 0) for h in range(heads)
        )
        grad_kv = sum(
            contract(dkv_own[h], norm_ref[h * rows : (h + 1) * rows], 1, 0) for h in range(heads)
        )
        grad_ref[:, :HD] = grad_q
        grad_ref[:, HD:] = grad_kv.T

        def finish(off):
            other = (head + off) % heads
            for p in range(per):
                dq_copy(other, other, p).wait_recv()
                dq_copy(other, head, p).wait_send()

        each(heads, finish)
        over_full.all("arrived")
        swap(place).start()
        dkv_spread.all("arrived")
        dq_ref[...] = dq_box[...]
        dkv_ref[...] = dkv_box[...]
        swap(place).wait_send()
        swap(1 - place).wait_recv()
        for c in range(2):
            for z in range(count):
                full_ref[z, c] = full[c, z]
        for spread in (dkv_spread, over_heads, over_pairs, over_full):
            spread.all("sent")


def attend_back(query, grad, mix, e, keyval, norm_all, pair_sum, heads, tile, chunk):
    nodes, reach = e.shape
    rows, width = nodes // heads, norm_all.shape[1]
    parts = nodes // tile
    _, count, share, across = pair_sum.shape
    row = lambda width: pl.BlockSpec((tile, width), lambda j, i: (i, 0))
    pair = (heads, count, share, across)
    dma = lambda *shape: pltpu.SemaphoreType.DMA(shape)
    order = lambda j: 2 * j % 3
    return pl.pallas_call(
        functools.partial(attend_back_kernel, chunk=chunk),
        grid=(3, parts),
        in_specs=[
            row(HD),
            row(HD),
            row(2 * HD),
            pl.BlockSpec((tile, nodes), lambda j, i: (i, order(j))),
            pl.BlockSpec((1, nodes, 2 * HD), lambda j, i: (order(j), 0, 0)),
            vmem(),
            vmem(),
        ],
        out_specs=[
            whole((heads, rows, HD)),
            whole((heads, 2 * HD, rows)),
            whole((width, 3 * HD)),
            whole((share, across)),
            whole((count, 2, share, across)),
        ],
        out_shape=[
            jax.ShapeDtypeStruct((heads, rows, HD), bf16),
            jax.ShapeDtypeStruct((heads, 2 * HD, rows), bf16),
            jax.ShapeDtypeStruct((width, 3 * HD), f32),
            jax.ShapeDtypeStruct((share, across), f32),
            jax.ShapeDtypeStruct((count, 2, share, across), bf16),
        ],
        scratch_shapes=[
            pltpu.VMEM((HD, nodes), f32),
            pltpu.VMEM((HD, nodes), f32),
            pltpu.VMEM((nodes, HD), f32),
            *[pltpu.VMEM((2 * HD, nodes), bf16)] * 4,
            *[pltpu.VMEM((heads, rows, HD), bf16)] * 2,
            *[pltpu.VMEM((heads, 2 * HD, rows), bf16)] * 2,
            pltpu.VMEM(pair, bf16),
            *[pltpu.VMEM(pair[1:], bf16)] * 2,
            pltpu.VMEM((share, across), bf16),
            pltpu.VMEM((2, *pair[1:]), bf16),
            dma(2, 2),
            dma(2, heads, rows // tile),
            dma(2, heads),
            dma(2),
            dma(2, heads),
            dma(2, count),
            dma(2, count),
        ],
        compiler_params=remote(60, 5),
        name="attend_back",
    )(query, grad, mix, e, keyval, norm_all, pair_sum)


def middle_kernel(
    place_ref, scale_ref, mixed_ref, zero_ref, wa_ref, wf_ref, mod_ref, wdec_ref, stat_ref,
    node_ref, read_ref, target_ref, eps_ref,
    done_ref, dmix_ref, pair_ref, gdec_ref, gmod_ref, loss_ref,
    wdec_low, one_scr, two_scr, norm_scr, up_scr, act_scr, dec_box, hits, turned, total,
    d_own, d_box, dmix_own, dmix_box, grad, big, pair_box,
    dec_sems, d_sems, dmix_sems, pair_sems, out_sems,
    node_tiles, pixel_tiles,
):
    step = pl.program_id(0)
    heads, rows, _ = mixed_ref.shape
    width = zero_ref.shape[1]
    tile = rows // node_tiles
    head = lax.axis_index("head")
    within, _ = pairs()
    place = within[1]
    count, share = pair_ref.shape[1:3]
    pixel_end = node_tiles + pixel_tiles
    others = nearest_first(head, heads)

    decs = Relay(lambda slot, half: dec_box.at[slot, :, pl.ds(half * tile, tile)], dec_sems)

    d_spread = Spread(along("head"), lambda o: d_own.at[o], lambda i: d_box.at[i], d_sems.at[0], d_sems.at[1])

    def dmix_copy(other, slot, t):
        lines = pl.ds(t * tile, tile)
        return pltpu.make_async_remote_copy(
            src_ref=dmix_own.at[other, lines],
            dst_ref=dmix_box.at[slot, lines],
            send_sem=dmix_sems.at[0, other, t],
            recv_sem=dmix_sems.at[1, slot, t],
            device_id={"head": other},
        )

    def pair_copy(h, part):
        cols = (pl.ds(0, 2 * width), pl.ds(2 * width, HD))[part]
        return pltpu.make_async_remote_copy(
            src_ref=big.at[1 - place, h, :, :, cols],
            dst_ref=pair_box.at[h, :, :, cols],
            send_sem=pair_sems.at[0, part, h],
            recv_sem=pair_sems.at[1, part, h],
            device_id=within[2](1 - place),
        )

    def pack(h, cols):
        for c in range(2):
            for z in range(count):
                at = (2 * z + c) * share
                big[c, h, z, :, cols] = grad[h, at : at + share, cols].astype(bf16)

    @pl.when(step == 0)
    def _():
        meet(["head", "node"])
        wdec_low[...] = jnp.zeros_like(wdec_low)
        wdec_low[:VARS] = wdec_ref[...].astype(bf16)
        turned[...] = jnp.zeros_like(turned)
        total[...] = jnp.zeros_like(total)
        loss_ref[...] = jnp.zeros_like(loss_ref)
        gdec_ref[...] = jnp.zeros_like(gdec_ref)
        gmod_ref[...] = jnp.zeros_like(gmod_ref)

    for t in range(node_tiles):

        @pl.when(step == t)
        def _(t=t, lines=slice(t * tile, (t + 1) * tile)):
            h_one = zero_ref[lines] + sum(
                contract(mixed_ref[h, lines], wa_ref[h, :, 3 * HD :], 1, 1) for h in range(heads)
            )
            one_scr[lines] = h_one
            normed, _ = standardize(h_one)
            norm_two = (normed * (1 + mod_ref[2:3]) + mod_ref[3:4]).astype(bf16)
            norm_scr[lines] = norm_two
            h_two = h_one
            for h in range(heads):
                up = contract(norm_two, wf_ref[h, :, :width], 1, 0)
                up_scr[h, lines] = up
                act = (up * jax.nn.sigmoid(up)).astype(bf16)
                act_scr[h, lines] = act
                h_two = h_two + contract(act, wf_ref[h, :, width:], 1, 1)
            two_scr[lines] = h_two
            final = standardize(h_two)[0].astype(bf16)
            high, low = halves(contract(wdec_low[...], final, 1, 1))
            dec_box[head, :SLIM, lines] = high
            dec_box[head, SLIM:, lines] = low
            decs.start(((0, t), (1, t)))
            if t == 1:
                decs.hand_on(0)

    @pl.when((step >= node_tiles) & (step < pixel_end))
    def _():
        reads = read_ref[...] - place_ref[0]
        pixels = target_ref.shape[1]
        for h in range(heads):
            spot = lax.broadcasted_iota(jnp.int32, (rows, pixels), 0) + h * rows
            hit = sum((spot == reads[k : k + 1]).astype(f32) for k in range(3)).astype(bf16)
            hits[h * rows : (h + 1) * rows] = hit

        @pl.when(step == node_tiles)
        def _():
            decs.hand_on(1)
            for side in range(2):
                decs.arrived(side)
            decs.arrived_across()

        field = sum(contract(dec_box[h], hits[h * rows : (h + 1) * rows], 1, 0) for h in range(heads))
        field = (field[:VARS] + field[SLIM : SLIM + VARS]) / 3.0
        target = target_ref[...]
        noisy = target + scale_ref[0] * eps_ref[...]
        error = scale_ref[2] * noisy + scale_ref[3] * field - target
        valid = (node_ref[...] - place_ref[0] < place_ref[2]).astype(f32)
        valid_pixels = stat_ref[SLIM - 1 : SLIM, 0:1]
        weighted = valid * (scale_ref[4] / (stat_ref[:VARS, 0:1] / valid_pixels + norm_eps))
        loss_ref[:VARS] += fold_lanes(weighted * error * error)
        high, low = halves(scale_ref[3] * (2.0 / (valid_pixels * VARS)) / 3.0 * weighted * error)
        turned[:VARS] = high
        turned[SLOT : SLOT + VARS] = low
        total[...] += contract(hits[...], turned[...], 1, 1)

    @pl.when(step == pixel_end - 1)
    def _():
        for h in range(heads):
            lines = slice(h * rows, (h + 1) * rows)
            d_own[h] = (total[lines, :SLOT] + total[lines, SLOT:]).astype(bf16)
        for other in others:
            d_spread.copy(other, head).start()
        d_box[head] = d_own[head]

    for t in range(node_tiles):
        final_tile = t == node_tiles - 1

        @pl.when(step == pixel_end + t)
        def _(t=t, lines=slice(t * tile, (t + 1) * tile), final_tile=final_tile):
            normed_two, inv_two = standardize(two_scr[lines])
            final = normed_two.astype(bf16)
            normed_one, inv_one = standardize(one_scr[lines])
            if t == 0:
                for other in others:
                    d_spread.copy(other, other).wait_recv()
            d_dec = sum(d_box[h, lines].astype(f32) for h in range(heads)).astype(bf16)[:, :SLIM]
            gdec_ref[...] += contract(d_dec, final, 0, 0)
            d_two = norm_back(normed_two, inv_two, contract(d_dec, wdec_low[...], 1, 0))
            d_low = d_two.astype(bf16)
            norm_two = norm_scr[lines]
            d_mid = jnp.zeros_like(d_two)

            def add(h, cols, value):
                if t == 0:
                    grad[h, :, cols] = value
                else:
                    grad[h, :, cols] += value

            for h in range(heads):
                up = up_scr[h, lines]
                d_act = contract(d_low, wf_ref[h, :, width:], 1, 0)
                gating = jax.nn.sigmoid(up)
                d_up = (d_act * gating * (1 + up * (1 - gating))).astype(bf16)
                add(h, slice(0, width), contract(norm_two, d_up, 0, 0))
                add(h, slice(width, 2 * width), contract(d_low, act_scr[h, lines], 0, 0))
                if final_tile:
                    pack(h, slice(0, 2 * width))
                    pair_copy(h, 0).start()
                d_mid += contract(d_up, wf_ref[h, :, :width], 1, 1)
            gmod_ref[0:1] += jnp.sum(d_mid * normed_one, 0, keepdims=True)
            gmod_ref[1:2] += jnp.sum(d_mid, 0, keepdims=True)
            d_one = d_two + norm_back(normed_one, inv_one, d_mid * (1 + mod_ref[2:3]))
            done_ref[lines] = d_one
            one_low = d_one.astype(bf16)
            for h in range(heads):
                dmix_own[h, lines] = contract(one_low, wa_ref[h, :, 3 * HD :], 1, 0).astype(bf16)
            for other in others:
                dmix_copy(other, head, t).start()
            dmix_box[head, lines] = dmix_own[head, lines]
            for h in range(heads):
                add(h, slice(2 * width, 2 * width + HD), contract(one_low, mixed_ref[h, lines], 0, 0))
                if final_tile:
                    pack(h, slice(2 * width, 2 * width + HD))
                    pair_copy(h, 1).start()
            if final_tile:
                for h in range(heads):
                    for part in range(2):
                        pair_copy(h, part).wait_recv()
                    for z in range(count):
                        pair_ref[h, z] = (
                            big[place, h, z].astype(f32) + pair_box[h, z].astype(f32)
                        ).astype(bf16)
                for other in others:
                    for u in range(node_tiles):
                        dmix_copy(other, other, u).wait_recv()
                dmix_ref[...] = dmix_box[...]
                for other in others:
                    d_spread.copy(other, head).wait_send()
                    for u in range(node_tiles):
                        dmix_copy(other, head, u).wait_send()
                decs.sent()
                for h in range(heads):
                    for part in range(2):
                        pair_copy(h, part).wait_send()


def middle(place, scales, mixed, h_zero, w_attn, w_ffn, modulation, w_dec, stat, node_row, read_rows, target, eps, groups):
    heads, rows, _ = mixed.shape
    width = h_zero.shape[1]
    node_tiles, pixels = 2, target.shape[1] // heads
    tile = 1536
    pixel_tiles = pixels // tile
    share, count = width // groups, groups // 2
    grads = 2 * width + HD
    pair = (heads, count, share, grads)
    low = lambda *shape: pltpu.VMEM(shape, bf16)
    full = lambda *shape: pltpu.VMEM(shape, f32)
    dma = lambda *shape: pltpu.SemaphoreType.DMA(shape)

    def at(i):
        part = jnp.clip(i - node_tiles, 0, pixel_tiles - 1)
        return 0, lax.axis_index("head") * pixel_tiles + part

    piece = lambda lines: pl.BlockSpec((lines, tile), at)
    return pl.pallas_call(
        functools.partial(middle_kernel, node_tiles=node_tiles, pixel_tiles=pixel_tiles),
        grid=(2 * node_tiles + pixel_tiles,),
        in_specs=[smem(), smem()] + [vmem()] * 7 + [piece(1), piece(3), piece(VARS), piece(VARS)],
        out_specs=[
            whole((rows, width)),
            whole((heads, rows, HD)),
            whole(pair),
            whole((SLIM, width)),
            whole((8, width)),
            whole((SLIM, 128)),
        ],
        out_shape=[
            jax.ShapeDtypeStruct((rows, width), f32),
            jax.ShapeDtypeStruct((heads, rows, HD), bf16),
            jax.ShapeDtypeStruct(pair, bf16),
            jax.ShapeDtypeStruct((SLIM, width), f32),
            jax.ShapeDtypeStruct((8, width), f32),
            jax.ShapeDtypeStruct((SLIM, 128), f32),
        ],
        scratch_shapes=[
            low(SLIM, width),
            full(rows, width),
            full(rows, width),
            low(rows, width),
            full(heads, rows, width),
            low(heads, rows, width),
            low(heads, 2 * SLIM, rows),
            low(heads * rows, tile),
            low(2 * SLOT, tile),
            full(heads * rows, 2 * SLOT),
            low(heads, rows, SLOT),
            low(heads, rows, SLOT),
            low(heads, rows, HD),
            low(heads, rows, HD),
            full(heads, width, grads),
            low(2, *pair),
            low(*pair),
            dma(2, 3, 2),
            dma(2, heads),
            dma(2, heads, node_tiles),
            dma(2, 2, heads),
            dma(2, heads),
        ],
        compiler_params=remote(62, 7),
        name="middle",
    )(
        place, scales, mixed, h_zero, w_attn, w_ffn, modulation, w_dec, stat, node_row, read_rows, target, eps
    )


def settle_kernel(
    feat_ref, dq_ref, dkv_ref, w_ref, zero_ref, done_ref, in_ref, mod_ref, gdec_ref, gmod_ref, qkv_ref, big_ref, loss_ref,
    small_ref, share_ref, full_ref, sums_ref,
    q_low, q_pair, q_sum, q_box, q_share, q_full,
    parts, part_box, part_sum, part_own, pay, heard, tally, tallies,
    pair_sems, q_sems, f_sems, a_sems, n_sems, b_sems, t_sems, s_sems,
):
    heads, width = w_ref.shape[0], w_ref.shape[1]
    share_rows = share_ref.shape[0]
    head, node = lax.axis_index("head"), lax.axis_index("node")
    groups = heard.shape[0]
    within, across = pairs()
    place, pair, count = within[1], across[1], across[0]

    def to_other(source, target, index):
        return pltpu.make_async_remote_copy(
            src_ref=source,
            dst_ref=target,
            send_sem=pair_sems.at[0, index],
            recv_sem=pair_sems.at[1, index],
            device_id=within[2](1 - place),
        )

    for c in range(2):
        for z in range(count):
            at = (2 * z + c) * share_rows
            q_low[c, z] = qkv_ref[at : at + share_rows].astype(bf16)
    meet(["head", "node"])
    q_pairs = to_other(q_low.at[1 - place], q_pair, 0)
    q_pairs.start()

    d_norm = sum(
        contract(dq_ref[h], w_ref[h, :, :HD], 1, 1)
        + contract(dkv_ref[h], w_ref[h, :, HD : 3 * HD], 0, 1)
        for h in range(heads)
    )
    normed, inv = standardize(zero_ref[...])
    d_zero = done_ref[...] + norm_back(normed, inv, d_norm * (1 + mod_ref[0:1]))

    q_pairs.wait()
    for z in range(count):
        q_sum[z] = (q_low[place, z].astype(f32) + q_pair[z].astype(f32)).astype(bf16)
    q_over = Spread(across, lambda o: q_sum.at[o], lambda i: q_box.at[i], q_sems.at[0], q_sems.at[1])
    q_over.all("start")
    q_box[pair] = q_sum[pair]

    g_enc = contract(in_ref[...].T, d_zero, 1, 0, highest)
    parts[...] = jnp.zeros_like(parts)
    flat = parts.reshape(parts.shape[0] * parts.shape[1], width)
    flat[:VARS] = g_enc[:VARS]
    flat[VARS : 2 * VARS] = g_enc[SLOT : SLOT + VARS]
    flat[2 * VARS : 3 * VARS] = gdec_ref[:VARS]
    at = 3 * VARS
    flat[at : at + 1] = jnp.sum(d_norm * normed, 0, keepdims=True)
    flat[at + 1 : at + 2] = jnp.sum(d_norm, 0, keepdims=True)
    flat[at + 2 : at + 4] = gmod_ref[0:2]
    over_heads = Spread(
        along("head"), lambda o: parts.at[o], lambda i: part_box.at[i], a_sems.at[0], a_sems.at[1]
    )
    over_heads.all("start")
    part_box[head] = parts[head]

    q_over.all("arrived")
    share = sum(q_box[z].astype(f32) for z in range(count))
    share_ref[...] = share
    q_share[...] = share.astype(bf16)
    q_full[place, pair] = share.astype(bf16)
    f_over = Spread(
        across, lambda _: q_share, lambda i: q_full.at[place, i], f_sems.at[0], f_sems.at[1]
    )
    f_over.all("start")

    over_heads.all("arrived")
    total = sum(part_box[h] for h in range(heads))
    for t in range(groups):
        part_sum[t] = total[8 * t : 8 * t + 8]
    over_nodes = Spread(
        along("node"), lambda o: part_sum.at[o], lambda i: part_own.at[i], n_sems.at[0], n_sems.at[1]
    )
    over_nodes.all("start")
    part_own[node] = part_sum[node]

    squares = jnp.sum(share * share) + jnp.sum(big_ref[...] * big_ref[...])
    loss = jnp.sum(loss_ref[:VARS])
    over_nodes.all("arrived")
    own = sum(part_own[t] for t in range(groups))
    row = lax.broadcasted_iota(jnp.int32, own.shape, 0) + 8 * (head * groups + node)
    squares += jnp.sum(own * own * jnp.where(row >= 3 * VARS, feat_ref[0], 1.0))
    line = lax.broadcasted_iota(jnp.int32, (8, 128), 0)
    pay[:, :width] = own
    pay[:, width:] = jnp.where(line == 0, squares, jnp.where(line == 1, loss, 0.0))
    back = Spread(along("node"), lambda _: pay, lambda i: heard.at[i], b_sems.at[0], b_sems.at[1])
    back.all("start")
    heard[node] = pay[...]

    f_over.all("arrived")
    q_rest = to_other(q_full.at[place], q_full.at[place], 1)
    q_rest.start()

    back.all("arrived")
    tally[...] = sum(heard[t, :, width:] for t in range(groups))
    tell = Spread(along("head"), lambda _: tally, lambda i: tallies.at[i], t_sems.at[0], t_sems.at[1])
    tell.all("start")
    tallies[head] = tally[...]
    for t in range(groups):
        small_ref[head, 8 * t : 8 * t + 8] = heard[t, :, :width]
    smalls = Spread(
        along("head"), lambda _: small_ref.at[head], lambda i: small_ref.at[i], s_sems.at[0], s_sems.at[1]
    )
    smalls.all("start")
    tell.all("arrived")
    sums_ref[...] = sum(tallies[h] for h in range(heads))

    q_rest.wait_send()
    to_other(q_full.at[1 - place], q_full.at[1 - place], 1).wait_recv()
    for c in range(2):
        for z in range(count):
            full_ref[2 * z + c] = q_full[c, z]
    smalls.all("arrived")
    for spread in (q_over, over_heads, f_over, over_nodes, back, tell, smalls):
        spread.all("sent")


def settle(feat_sq, dq, dkv, w_attn, h_zero, d_one, node_in, modulation, grad_dec, gmod_two, grad_qkv, big_share, loss, groups):
    heads, rows, _ = dq.shape
    width = h_zero.shape[1]
    count = groups // 2
    share = (grad_qkv.shape[0] // groups, grad_qkv.shape[1])
    low = lambda *shape: pltpu.VMEM(shape, bf16)
    full = lambda *shape: pltpu.VMEM(shape, f32)
    dma = lambda *shape: pltpu.SemaphoreType.DMA(shape)
    return pl.pallas_call(
        settle_kernel,
        in_specs=[smem()] + [vmem()] * 12,
        out_specs=[vmem()] * 4,
        out_shape=[
            jax.ShapeDtypeStruct((heads, 8 * groups, width), f32),
            jax.ShapeDtypeStruct(share, f32),
            jax.ShapeDtypeStruct((groups, *share), bf16),
            jax.ShapeDtypeStruct((8, 128), f32),
        ],
        scratch_shapes=[
            low(2, count, *share),
            low(count, *share),
            low(count, *share),
            low(count, *share),
            low(*share),
            low(2, count, *share),
            full(heads, 8 * groups, width),
            full(heads, 8 * groups, width),
            full(groups, 8, width),
            full(groups, 8, width),
            full(8, width + 128),
            full(groups, 8, width + 128),
            full(8, 128),
            full(heads, 8, 128),
            dma(2, 2),
            dma(2, count),
            dma(2, count),
            dma(2, heads),
            dma(2, groups),
            dma(2, groups),
            dma(2, heads),
            dma(2, heads),
        ],
        compiler_params=remote(56, 1),
        name="settle",
    )(feat_sq, dq, dkv, w_attn, h_zero, d_one, node_in, modulation, grad_dec, gmod_two, grad_qkv, big_share, loss)


def eliminate(work, done):
    count = work.shape[0]
    lane = lax.broadcasted_iota(jnp.int32, (1, BLOCK), 1)
    sub = lax.broadcasted_iota(jnp.int32, (STRIP, BLOCK), 0)
    pivots = [jnp.ones((1, BLOCK), f32) for _ in range(count)]
    both = lambda x: jnp.concatenate([x, x], 1)
    for at in range(0, BLOCK, STRIP):
        strip = slice(at, at + STRIP)
        rows = [work[m, strip] for m in range(count)]
        columns = [
            [jnp.broadcast_to(rows[m][:, at + k : at + k + 1], (STRIP, BLOCK)) for k in range(STRIP)]
            for m in range(count)
        ]
        scale = [jnp.ones((STRIP, BLOCK), f32) for _ in range(count)]
        for r in range(STRIP):
            for m in range(count):
                column = columns[m][r]
                pivot = jnp.broadcast_to(column[r : r + 1], (STRIP, BLOCK))
                factor = jnp.where(sub > r, column * (1.0 / pivot), 0.0)
                scale[m] = jnp.where(sub == r, pivot, scale[m])
                for k in range(r + 1, STRIP):
                    columns[m][k] = columns[m][k] - factor * columns[m][k][r : r + 1]
                pivots[m] = jnp.where(lane == at + r, pivot[:1], pivots[m])
                rows[m] = rows[m] - both(factor) * rows[m][r : r + 1]
        for m in range(count):
            done[m, strip] = rows[m][:, BLOCK:]
            if at + STRIP < BLOCK:
                high, mid, low = thirds(rows[m] * both(lax.rsqrt(scale[m])))
                left = jnp.concatenate([high, high, mid, mid, high, low], 0)[:, :BLOCK]
                right = jnp.concatenate([high, mid, high, mid, low, high], 0)
                rest = slice(at + STRIP, BLOCK)
                work[m, rest] -= contract(left, right, 0, 0)[rest]
    return pivots


def finish_kernel(
    sums_ref, small_ref, qkv_share_ref, big_share_ref, qkv_ref, big_ref, stats_ref, basis_ref,
    layer_ref, first_ref, second_ref, feat_ref,
    enc_ref, enc1_ref, enc2_ref, cond_ref, cond1_ref, cond2_ref, dec_ref, dec1_ref, dec2_ref,
    out_ref, stats_out, layer_out, first_out, second_out,
    enc_out, enc1_out, enc2_out, cond_out, cond1_out, cond2_out, dec_out, dec1_out, dec2_out,
    gram, both, work, done, shares,
):
    count, size = stats_ref.shape[:2]
    k = pl.program_id(0)
    clip = clip_limit / jnp.maximum(jnp.sqrt(sums_ref[0:1, 0:1]), clip_limit)

    @pl.when(k == 0)
    def _():
        cuts = [slice(0, size), slice(size, 2 * size), slice(2 * size, 3 * size)]
        shares[0] = jnp.concatenate([qkv_share_ref[...], big_share_ref[:, cuts[2].start :]], 1)
        grads = [jnp.concatenate([qkv_ref[...], big_ref[:, cuts[2].start :]], 1)]
        for m in (1, 2):
            shares[m] = big_share_ref[:, cuts[m - 1]]
            grads.append(big_ref[:, cuts[m - 1]])
        for m in range(count):
            raw = contract(grads[m], grads[m], 0, 0)
            new = beta_stats * stats_ref[m] + (1 - beta_stats) * (clip * (clip * raw))
            stats_out[m] = new
            product = contract(new, basis_ref[m], 1, 0, highest)
            both[m] = product
            half = size // 2
            gram[m, :half, :half] = contract(product[:, :half], product[:, :half], 0, 0, highest)
            gram[m, half:] = contract(product[:, half:], product, 0, 0, highest)

    i = jnp.minimum(k, count - 1)
    rotated = contract(clip * shares[i], basis_ref[i], 1, 0, highest)
    first_new = beta_first * first_ref[i] + (1 - beta_first) * rotated
    second_new = beta_second * second_ref[i] + (1 - beta_second) * rotated * rotated
    first_out[i] = first_new
    second_out[i] = second_new
    direction = (
        first_new
        / (1 - beta_first**STEP)
        / (jnp.sqrt(second_new / (1 - beta_second**STEP)) + adam_epsilon)
    )
    layer_out[i] = layer_ref[i] - rate_layer * (
        contract(direction, basis_ref[i], 1, 1, highest) + decay_rate * layer_ref[i]
    )

    at = pl.ds(pl.multiple_of(k * BLOCK, BLOCK), BLOCK)
    unit = lax.broadcasted_iota(jnp.int32, (BLOCK, BLOCK), 0) == lax.broadcasted_iota(
        jnp.int32, (BLOCK, BLOCK), 1
    )
    for m in range(count):
        work[m, :, :BLOCK] = gram[m, at, at]
        work[m, :, BLOCK:] = unit.astype(f32)
    roots = [lax.rsqrt(p) for p in eliminate(work, done)]
    for step in range(size // BLOCK):

        @pl.when(k == step)
        def _(here=slice(step * BLOCK, (step + 1) * BLOCK), rest=(step + 1) * BLOCK):
            for m in range(count):
                factor = done[m]
                panel = contract(both[m, :, here], factor, 1, 1, highest) * roots[m]
                out_ref[m] = panel
                if rest < size:
                    left = contract(gram[m, rest:, here], factor, 1, 1, highest) * roots[m]
                    both[m, :, rest:] -= contract(panel, left, 1, 1, highest)
                    gram[m, rest:, rest:] -= contract(left, left, 1, 1, highest)

    @pl.when(k == pl.num_programs(0) - 1)
    def _():
        flat = clip * small_ref[...]

        def adam(grad, cols, refs, outs):
            for out, new in zip(outs, adam_small(refs[0][:, cols], grad, refs[1][:, cols], refs[2][:, cols])):
                out[:, cols] = new

        every = slice(None)
        adam(flat[: 2 * VARS], every, (enc_ref, enc1_ref, enc2_ref), (enc_out, enc1_out, enc2_out))
        adam(flat[2 * VARS : 3 * VARS], every, (dec_ref, dec1_ref, dec2_ref), (dec_out, dec1_out, dec2_out))
        width = flat.shape[1]
        for j in range(4):
            grad = feat_ref[:, 0:1] * flat[3 * VARS + j : 3 * VARS + j + 1]
            adam(
                grad,
                slice(j * width, (j + 1) * width),
                (cond_ref, cond1_ref, cond2_ref),
                (cond_out, cond1_out, cond2_out),
            )


def finish(sums, small, qkv_share, big_share, qkv_full, big_full, stats, basis, layers, feat, enc, cond, dec):
    count, size = stats.shape[:2]
    inputs = (sums, small, qkv_share, big_share, qkv_full, big_full, stats, basis, *layers, feat, *enc, *cond, *dec)
    like = lambda x: jax.ShapeDtypeStruct(x.shape, f32)
    outs = [stats, *layers, *enc, *cond, *dec]
    return pl.pallas_call(
        finish_kernel,
        grid=(size // BLOCK,),
        in_specs=[whole(x.shape) for x in inputs],
        out_specs=[pl.BlockSpec((count, size, BLOCK), lambda k: (0, 0, k))] + [whole(x.shape) for x in outs],
        out_shape=[like(stats)] + [like(x) for x in outs],
        scratch_shapes=[
            pltpu.VMEM((count, size, size), f32),
            pltpu.VMEM((count, size, size), f32),
            pltpu.VMEM((count, BLOCK, 2 * BLOCK), f32),
            pltpu.VMEM((count, BLOCK, BLOCK), f32),
            pltpu.VMEM(layers[0].shape, f32),
        ],
        compiler_params=params(60),
        name="finish",
    )(*inputs)


def local(
    prev_state,
    target,
    noise_eps,
    noise_level,
    valid_count,
    neighbours,
    nbr_count,
    pix_node,
    pix_read,
    w_enc,
    w_cond,
    w_dec,
    layer_w,
    soap_first,
    soap_second,
    soap_basis,
    soap_stats,
    enc_first,
    enc_second,
    cond_first,
    cond_second,
    dec_first,
    dec_second,
):
    nodes = nbr_count.shape[0]
    groups = lax.axis_size("node")
    heads = lax.axis_size("head")
    rows = nodes // heads
    block_start = lax.axis_index("node") * nodes
    quarter = lax.axis_index("head")
    width = w_enc.shape[1]
    both = ("head", "node")

    low_w = layer_w.astype(bf16)
    ffn_share = jnp.concatenate([low_w[1], low_w[2]], 1)
    noise_sigma, noise_feat = noise_terms(noise_level)
    sig_sq = noise_sigma * noise_sigma
    input_scale = lax.rsqrt(sig_sq + 1.0)
    skip_scale = 1.0 / (sig_sq + 1.0)
    output_scale = noise_sigma * lax.rsqrt(sig_sq + 1.0)
    loss_scale = (sig_sq + 1.0) / sig_sq
    modulation = jnp.dot(noise_feat[None, :], w_cond, precision=highest).reshape(4, width)

    prev_t, target_t, eps_t = prev_state.T, target.T, noise_eps.T
    node_row = pix_node.reshape(1, -1)
    read_rows = pix_read.T
    place = jnp.stack([block_start, quarter * rows, valid_count[0], quarter]).astype(jnp.int32)
    node_in, column, h_zero, stat, norm_all, query, keyval, counts = enter(
        place, jnp.stack([noise_sigma, input_scale]), node_row, prev_t, target_t, eps_t, low_w[0],
        w_enc, modulation, neighbours.T, nbr_count.reshape(1, -1), rows, 2048, heads, groups,
    )
    norm_all, query = norm_all.reshape(nodes, -1), query.reshape(nodes, -1)
    keyval = keyval.reshape(3, nodes, -1)
    loss_count = stat[SLIM - 1, 0] * VARS
    e, mix, mixed, attn_all, ffn_all = attend(query, keyval, counts, column, ffn_share, heads, 128, 512)
    attn_all = attn_all.reshape(heads, width, -1)
    ffn_all = ffn_all.reshape(heads, width, -1)

    scales = jnp.stack([noise_sigma, input_scale, skip_scale, output_scale, loss_scale])
    d_one, d_mixed, pair_sum, grad_dec, gmod_two, loss_part = middle(
        place, scales, mixed, h_zero, attn_all, ffn_all, modulation, w_dec.T, stat, node_row, read_rows,
        target_t, eps_t, groups,
    )
    d_mixed = d_mixed.reshape(nodes, HD)
    dq, dkv, grad_qkv, big_share, big_full = attend_back(
        query, d_mixed, mix, e, keyval, norm_all, pair_sum, heads, 512, 1024
    )
    feat_sq = jnp.sum(noise_feat * noise_feat).reshape(1)
    small, qkv_share, qkv_full, sums = settle(
        feat_sq, dq, dkv, attn_all, h_zero, d_one, node_in, modulation, grad_dec, gmod_two, grad_qkv, big_share,
        loss_part, groups,
    )
    basis_new, stats_new, layer_new, first_new, second_new, *small_new = finish(
        sums,
        small.reshape(-1, width),
        qkv_share,
        big_share,
        qkv_full.reshape(width, -1),
        big_full.reshape(width, -1),
        soap_stats[:, 0],
        soap_basis[:, 0],
        (layer_w, soap_first, soap_second),
        jnp.broadcast_to(noise_feat[:, None], (NF, 128)),
        (w_enc, enc_first, enc_second),
        (w_cond, cond_first, cond_second),
        (w_dec.T, dec_first.T, dec_second.T),
    )
    return (
        jnp.reshape(sums[1, 0], (1,)),
        jnp.reshape(loss_count, (1,)),
        jnp.reshape(jnp.sqrt(sums[0, 0]), (1,)),
        layer_new,
        first_new,
        second_new,
        basis_new[:, None],
        stats_new[:, None],
        *small_new[:6],
        *(x.T for x in small_new[6:]),
    )


def solution(mesh):
    pixel = P("node", None)
    layer = P(None, "node", "head")
    basis = P(None, "head", None, None)
    placed = (
        *(pixel,) * 3,
        P(),
        P("node"),
        P("node", None),
        P("node"),
        P("node"),
        P("node", None),
        *(P(),) * 3,
        *(layer,) * 3,
        *(basis,) * 2,
        *(P(),) * 6,
    )
    return jax.shard_map(
        local,
        mesh=mesh,
        in_specs=placed,
        out_specs=(*(P(),) * 3, *(layer,) * 3, *(basis,) * 2, *(P(),) * 9),
        check_vma=False,
    )
```
